32 devices in a mesh: wide: 16 (over z, y, core), tensor: 2 (over x).
Axes of the slice: x: 2, y: 2, z: 4, core: 2. Of those that a mesh axis runs over, the one named last changes fastest.
Arguments:
- tokens_in: bfloat16 [18432, 512], P('wide'), may hold values from -6 to 6
- pre_gain: float32 [512], replicated, may hold values from 0.5 to 1.5
- pre_shift: float32 [512], replicated, may hold values from -0.5 to 0.5
- qkv_weight: bfloat16 [512, 3, 512], P(None, None, 'tensor'), may hold values from -0.25 to 0.25
- qv_bias: float32 [2, 512], P(None, 'tensor'), may hold values from -0.5 to 0.5
- proj_weight: bfloat16 [512, 512], P('tensor'), may hold values from -1.5 to 1.5
- proj_bias: float32 [512], replicated, may hold values from -0.5 to 0.5
- mid_gain: float32 [512], replicated, may hold values from 0.5 to 1.5
- mid_shift: float32 [512], replicated, may hold values from -0.5 to 0.5
- hidden_weight: bfloat16 [512, 2048], P(None, 'tensor'), may hold values from -0.25 to 0.25
- hidden_bias: float32 [2048], P('tensor'), may hold values from -0.5 to 0.5
- output_weight: bfloat16 [2048, 512], P('tensor'), may hold values from -0.125 to 0.125
- output_bias: float32 [512], replicated, may hold values from -0.5 to 0.5
- moe_gain: float32 [512], replicated, may hold values from 0.5 to 1.5
- moe_shift: float32 [512], replicated, may hold values from -0.5 to 0.5
- router_weight: float32 [512, 16], replicated, may hold values from -0.1875 to 0.1875
- expert_in: bfloat16 [16, 512, 2048], P('wide', None, 'tensor'), may hold values from -0.25 to 0.25
- expert_in_bias: float32 [16, 2048], P('wide', 'tensor'), may hold values from -0.5 to 0.5
- expert_out: bfloat16 [16, 2048, 512], P('wide', 'tensor'), may hold values from -2 to 2
- expert_out_bias: float32 [16, 512], P('wide'), may hold values from -5 to 5
- expert_ids: int32 [18432, 2], P('wide'), may hold values from 0 to 15, all different within a row
- priority: int32 [16, 1152], P('wide'), may hold values from 0 to 1151, each once within a row
- cotangent: float32 [18432, 512], P('wide'), may hold values from -6 to 6
Outputs:
- block_out: bfloat16 [18432, 512], P('wide')
- tokens_grad: float32 [18432, 512], P('wide')
- pre_gain_grad: float32 [512], replicated
- pre_shift_grad: float32 [512], replicated
- qkv_weight_grad: float32 [512, 3, 512], P(None, None, 'tensor')
- qv_bias_grad: float32 [2, 512], P(None, 'tensor')
- proj_weight_grad: float32 [512, 512], P('tensor')
- proj_bias_grad: float32 [512], replicated
- mid_gain_grad: float32 [512], replicated
- mid_shift_grad: float32 [512], replicated
- hidden_weight_grad: float32 [512, 2048], P(None, 'tensor')
- hidden_bias_grad: float32 [2048], P('tensor')
- output_weight_grad: float32 [2048, 512], P('tensor')
- output_bias_grad: float32 [512], replicated
- moe_gain_grad: float32 [512], replicated
- moe_shift_grad: float32 [512], replicated
- router_weight_grad: float32 [512, 16], replicated
- expert_in_grad: float32 [16, 512, 2048], P('wide', None, 'tensor')
- expert_in_bias_grad: float32 [16, 2048], P('wide', 'tensor')
- expert_out_grad: float32 [16, 2048, 512], P('wide', 'tensor')
- expert_out_bias_grad: float32 [16, 512], P('wide')
The draws below stay inside these ranges and needn't reach their ends.
Inputs may be any that keep to these rules, and one draw needn't show every extreme that they name: `priority`: each row is a permutation of the 1152 ranks: the order in which one index's tokens claim expert slots. `expert_ids`: a token's two experts differ.
All inputs are finite; a program needn't handle non-finite values.
Results may differ from the reference program's by a relative error of at most 0.022.
Values may be sent and summed in bfloat16 or wider, within the bound.
A program may use at most 128 MiB of HBM per device.

```python
import jax
import jax.numpy as jnp
from jax import lax

D = 512
HEADS = 8
HEAD_DIM = 64
FF = 2048
PATCHES = 144
IMG_DEV = 8
EXPERTS = 16
TOK_DEV = 1152
TOKENS = 18432
CAP = 72
N_WIDE = 16


def level_of(key, dims, split, smallest, high):
    level, own = 1.0, jax.random.fold_in(key, 6)
    for dim, blocks in split:
        heights = jnp.exp(jax.random.uniform(jax.random.fold_in(own, dim), (blocks,), jnp.float32, smallest / len(split), high / len(split)))
        level = level * jnp.repeat(heights, dims[dim] // blocks).reshape([-1 if axis == dim else 1 for axis in range(len(dims))])
    return level


def choose_distinct(own_key, rows, count, top, lift):
    sequence = jax.random.permutation(jax.random.fold_in(own_key, 1), count)
    pull = sequence
    for power in range(3):
        pull = pull * pull // count
    pull = pull * lift // count
    lots = jax.random.randint(jax.random.fold_in(own_key, 2), (rows, count), 0, 4096) + pull
    fixed_rows = jax.random.permutation(jax.random.fold_in(own_key, 3), rows)[jnp.arange(count) % rows]
    lots = jnp.where(jnp.arange(rows)[:, None] == fixed_rows[None, :], 1 << 14, lots)
    score = lots * count + jnp.arange(count)
    return lax.top_k(score.astype(jnp.int32), top)[1].astype(jnp.int32)


def noise(key, dims, deviation, limit, split=(), kind=jnp.bfloat16):
    entries = deviation * jax.random.normal(key, dims, jnp.float32)
    if split:
        entries = entries * level_of(key, dims, split, -0.22, 0.18)
    return jnp.clip(entries, -limit, limit).astype(kind)


def setup_inputs(seed: int = 0) -> dict:
    key_of = jax.random.split(jax.random.key(seed), 24)
    tokens_in = noise(key_of[0], (TOKENS, D), 1.0, 6.0, ((0, 16),))
    pre_gain = jnp.clip(1.0 + 0.1 * jax.random.normal(key_of[1], (D,), jnp.float32), 0.5, 1.5)
    pre_shift = noise(key_of[2], (D,), 0.1, 0.5, (), jnp.float32)
    qkv_weight = noise(key_of[3], (D, 3, D), D ** -0.5, 0.25, ((2, 2),))
    qv_bias = noise(key_of[4], (2, D), 0.1, 0.5, ((1, 2),), jnp.float32)
    proj_weight = noise(key_of[5], (D, D), (max(D // 32, 2)) ** -0.5, 1.5, ((0, 2),))
    proj_bias = noise(key_of[6], (D,), 0.1, 0.5, (), jnp.float32)
    mid_gain = jnp.clip(1.0 + 0.1 * jax.random.normal(key_of[7], (D,), jnp.float32), 0.5, 1.5)
    mid_shift = noise(key_of[8], (D,), 0.1, 0.5, (), jnp.float32)
    hidden_weight = noise(key_of[9], (D, FF), D ** -0.5, 0.25, ((1, 2),))
    hidden_bias = noise(key_of[10], (FF,), 0.1, 0.5, ((0, 2),), jnp.float32)
    output_weight = noise(key_of[11], (FF, D), FF ** -0.5, 0.125, ((0, 2),))
    output_bias = noise(key_of[12], (D,), 0.1, 0.5, (), jnp.float32)
    moe_gain = jnp.clip(1.0 + 0.1 * jax.random.normal(key_of[13], (D,), jnp.float32), 0.5, 1.5)
    moe_shift = noise(key_of[14], (D,), 0.1, 0.5, (), jnp.float32)
    router_weight = noise(key_of[15], (D, EXPERTS), (2 * D) ** -0.5, 0.1875, (), jnp.float32)
    expert_in = noise(key_of[16], (EXPERTS, D, FF), D ** -0.5, 0.25, ((0, 16), (2, 2)))
    expert_in_bias = noise(key_of[17], (EXPERTS, FF), 0.1, 0.5, ((0, 16), (1, 2)), jnp.float32)
    expert_out = noise(key_of[18], (EXPERTS, FF, D), (max(FF // 256, 2)) ** -0.5, 2.0, ((0, 16), (1, 2)))
    expert_out_bias = noise(key_of[19], (EXPERTS, D), 1.0, 5.0, ((0, 16),), jnp.float32)
    expert_ids = choose_distinct(key_of[20], TOKENS, EXPERTS, 2, 1024)
    priority = jax.vmap(lambda own: jax.random.permutation(own, TOK_DEV))(jax.random.split(key_of[21], N_WIDE)).reshape((N_WIDE, TOK_DEV)).astype(jnp.int32)
    cotangent = noise(key_of[22], (TOKENS, D), 1.0, 6.0, ((0, 16),), jnp.float32)
    return dict(tokens_in=tokens_in, pre_gain=pre_gain, pre_shift=pre_shift, qkv_weight=qkv_weight, qv_bias=qv_bias, proj_weight=proj_weight, proj_bias=proj_bias, mid_gain=mid_gain, mid_shift=mid_shift, hidden_weight=hidden_weight, hidden_bias=hidden_bias, output_weight=output_weight, output_bias=output_bias, moe_gain=moe_gain, moe_shift=moe_shift, router_weight=router_weight, expert_in=expert_in, expert_in_bias=expert_in_bias, expert_out=expert_out, expert_out_bias=expert_out_bias, expert_ids=expert_ids, priority=priority, cotangent=cotangent)


@jax.custom_vjp
def low(v):
    return lax.optimization_barrier(v.astype(jnp.bfloat16)).astype(jnp.float32)

@jax.custom_vjp
def low_back(v):
    return v

def low_keep(v):
    return (low(v), None)

def low_pass(kept, grad):
    return (grad,)

def back_keep(v):
    return (v, None)

def back_low(kept, grad):
    return (low(grad),)
low.defvjp(low_keep, low_pass)
low_back.defvjp(back_keep, back_low)

def product(form, left, right):
    return jnp.einsum(form, left, right, precision=lax.Precision.HIGHEST)

def layer_norm(values, gain, shift):
    centered = values - lax.optimization_barrier(jnp.mean(values, axis=-1, keepdims=True))
    variance = lax.optimization_barrier(jnp.mean(centered * centered, axis=-1, keepdims=True))
    return centered * lax.rsqrt(variance + 1e-06) * gain + shift

def slot_tables(choice_ids, ranks, capacity, experts):
    count = choice_ids.shape[0]
    order_keys = jnp.concatenate([ranks, ranks + count]).astype(jnp.int32)
    flat_ids = jnp.concatenate([choice_ids[:, 0], choice_ids[:, 1]]).astype(jnp.int32)
    earlier = (order_keys[None, :] < order_keys[:, None]) & (flat_ids[None, :] == flat_ids[:, None])
    position = lax.optimization_barrier(jnp.sum(earlier.astype(jnp.int32), axis=1)).astype(jnp.int32)
    kept = position < capacity
    position = position.reshape(2, count)
    kept = kept.reshape(2, count)
    columns = jnp.arange(experts * capacity, dtype=jnp.int32)
    target = (choice_ids.T.astype(jnp.int32) * capacity + position).astype(jnp.int32)
    tables = (target[:, :, None] == columns[None, None, :]) & kept[:, :, None]
    return (tables, kept)

def attention_block(qkv_rows):
    grid = qkv_rows.reshape(IMG_DEV, PATCHES, 3, HEADS, HEAD_DIM)
    query, keys, values = (grid[:, :, 0], grid[:, :, 1], grid[:, :, 2])
    scale = float(HEAD_DIM) ** (-0.5)
    scores = low_back(product('bqhd,bkhd->bhqk', query, keys) * scale)
    weights = jax.nn.softmax(scores, axis=-1)
    context = product('bhqk,bkhd->bqhd', low(weights), values)
    return context.reshape(TOK_DEV, D)

def reference(tokens_in, pre_gain, pre_shift, qkv_weight, qv_bias, proj_weight, proj_bias, mid_gain, mid_shift, hidden_weight, hidden_bias, output_weight, output_bias, moe_gain, moe_shift, router_weight, expert_in, expert_in_bias, expert_out, expert_out_bias, expert_ids, priority, cotangent):

    def device_tables(pair):
        return slot_tables(pair[0], pair[1], CAP, EXPERTS)
    tables, kept = lax.map(device_tables, (expert_ids.reshape(N_WIDE, TOK_DEV, 2), priority))
    tables = tables.transpose(1, 0, 2, 3).astype(jnp.float32)
    dispatch = tables[0] + tables[1]
    keep_rows = kept.transpose(0, 2, 1).reshape(TOKENS, 2).astype(jnp.float32)

    def forward(params):
        tokens, pre_g, pre_s, qkv_w, qv_b, proj_w, proj_b, mid_g, mid_s, hidden_w, hidden_b, output_w, output_b, moe_g, moe_s, router_w, exp_in, exp_in_b, exp_out, exp_out_b = params
        normed = layer_norm(tokens, pre_g, pre_s)
        blank = jnp.zeros_like(qv_b[0])
        qkv_shift = jnp.stack([qv_b[0], blank, qv_b[1]])
        qkv = low(low_back(product('td,dsk->tsk', low(normed), qkv_w) + qkv_shift))
        context = lax.map(jax.checkpoint(attention_block), qkv.reshape(N_WIDE, TOK_DEV, 3, D)).reshape(TOKENS, D)
        context = low(low_back(context))
        branch = low_back(product('td,de->te', context, proj_w))
        first = tokens + branch + proj_b
        normed = layer_norm(first, mid_g, mid_s)
        inner = low_back(product('td,df->tf', low(normed), hidden_w) + hidden_b)
        branch = low_back(product('tf,fd->td', low(jax.nn.gelu(inner)), output_w))
        second = first + branch + output_b
        normed = layer_norm(second, moe_g, moe_s)
        route = jax.nn.softmax(product('td,de->te', normed, router_w), axis=-1)
        sent = low(normed).reshape(N_WIDE, TOK_DEV, D)
        buffers = low_back(product('wtk,wtd->wkd', dispatch, sent))
        rows = buffers.reshape(N_WIDE, EXPERTS, CAP, D).transpose(1, 0, 2, 3).reshape(EXPERTS, N_WIDE * CAP, D)
        exp_inner = low_back(product('erd,edf->erf', rows, exp_in) + exp_in_b[:, None, :])
        result = product('erf,efd->erd', low(jax.nn.gelu(exp_inner)), exp_out) + exp_out_b[:, None, :]
        result = low(low_back(result))
        returned = result.reshape(EXPERTS, N_WIDE, CAP, D).transpose(1, 0, 2, 3).reshape(N_WIDE, EXPERTS * CAP, D)
        picked = product('jwtk,wkd->jwtd', tables, returned).reshape(2, TOKENS, D)
        gates = jnp.take_along_axis(route, expert_ids, axis=1) * keep_rows
        mixture = gates[:, 0, None] * picked[0] + gates[:, 1, None] * picked[1]
        return second + mixture
    floats = (tokens_in, pre_gain, pre_shift, qkv_weight, qv_bias, proj_weight, proj_bias, mid_gain, mid_shift, hidden_weight, hidden_bias, output_weight, output_bias, moe_gain, moe_shift, router_weight, expert_in, expert_in_bias, expert_out, expert_out_bias)
    params = tuple((value.astype(jnp.float32) for value in floats))
    result, pullback = jax.vjp(forward, params)
    grads = pullback(cotangent.astype(jnp.float32))[0]
    return (result.astype(jnp.bfloat16), grads[0], grads[1], grads[2], grads[3], grads[4], grads[5], grads[6], grads[7], grads[8], grads[9], grads[10], grads[11], grads[12], grads[13], grads[14], grads[15], grads[16], grads[17], grads[18], grads[19])
```

```python
import functools

import jax
import jax.numpy as jnp
from jax import lax
from jax.experimental import pallas as pl
from jax.experimental.pallas import tpu as pltpu
from jax.sharding import PartitionSpec as P

HEAD_DIM = 64
PATCHES = 144
BF16 = jnp.bfloat16
F32 = jnp.float32
HIGHEST = lax.Precision.HIGHEST
VMEM_BYTES = 48 * 1024 * 1024


def dot(left, right):
    return jnp.dot(left, right, preferred_element_type=F32)


def dot_rows(left, right):
    return lax.dot_general(left, right, (((1,), (1,)), ((), ())), preferred_element_type=F32)


def dot_columns(left, right, precision=None):
    return lax.dot_general(
        left, right, (((0,), (0,)), ((), ())), precision=precision, preferred_element_type=F32
    )


def normalized(values):
    centered = values - jnp.mean(values, axis=-1, keepdims=True)
    variance = jnp.mean(centered * centered, axis=-1, keepdims=True)
    scale = lax.rsqrt(variance + 1e-06)
    return centered * scale, scale


def norm_back(rows, scale, gain, upstream):
    scaled = upstream * gain
    inward = jnp.mean(scaled, axis=-1, keepdims=True)
    along = jnp.mean(scaled * rows, axis=-1, keepdims=True)
    return scale * (scaled - inward - rows * along)


def gelu_parts(inner):
    square = inner * inner
    bend = jnp.tanh(0.7978845608028654 * inner * (1.0 + 0.044715 * square))
    half = 0.5 * (1.0 + bend)
    slope = half + (0.5 * 0.7978845608028654) * inner * (1.0 - bend * bend) * (
        1.0 + 0.134145 * square
    )
    return inner * half, slope


def gelu(inner):
    return inner * (0.5 * (1.0 + jnp.tanh(0.7978845608028654 * inner * (1.0 + 0.044715 * inner * inner))))


def softmax_rows(scores, scale):
    peak = jnp.max(scores, axis=-1, keepdims=True)
    weights = jnp.exp((scores - peak) * scale)
    return weights * (1.0 / jnp.sum(weights, axis=-1, keepdims=True))


def call(kernel, steps, ins, outs, name):
    def spec(shape, rows, first):
        if rows is None:
            return pl.BlockSpec(shape, lambda i: (0,) * len(shape))
        return pl.BlockSpec((rows,) + tuple(shape[1:]), lambda i: (i + first,) + (0,) * (len(shape) - 1))

    in_specs = []
    for array, rows, first in ins:
        if rows == "scalar":
            in_specs.append(pl.BlockSpec(memory_space=pltpu.SMEM))
        else:
            in_specs.append(spec(array.shape, rows, first))
    return pl.pallas_call(
        kernel,
        grid=(steps,),
        in_specs=in_specs,
        out_specs=[spec(shape, rows, 0) for shape, _, rows in outs],
        out_shape=[jax.ShapeDtypeStruct(shape, dtype) for shape, dtype, _ in outs],
        compiler_params=pltpu.CompilerParams(vmem_limit_bytes=VMEM_BYTES),
        name=name,
    )(*[array for array, _, _ in ins])


def attend(heads, tokens, gain, shift, weight, bias, qkv_out, context_out):
    rows, _ = normalized(tokens[...].astype(F32))
    lowered = (rows * gain[...] + shift[...]).astype(BF16)
    qkv = (dot(lowered, weight[...]) + bias[...]).astype(BF16)
    qkv_out[...] = qkv
    width = heads * HEAD_DIM
    for image in range(qkv.shape[0] // PATCHES):
        block = qkv[image * PATCHES : (image + 1) * PATCHES]
        parts = []
        for head in range(heads):
            at = head * HEAD_DIM
            query = block[:, at : at + HEAD_DIM]
            keys = block[:, width + at : width + at + HEAD_DIM]
            values = block[:, 2 * width + at : 2 * width + at + HEAD_DIM]
            probs = softmax_rows(dot_rows(query, keys), HEAD_DIM**-0.5)
            parts.append(dot(probs.astype(BF16), values))
        context = jnp.concatenate(parts, axis=1).astype(BF16)
        context_out[image * PATCHES : (image + 1) * PATCHES, :] = context


def feed(
    pairs, tokens, proj_bias, gain, shift, hidden, hidden_bias, output, *rest
):
    contexts, projections = rest[:pairs], rest[pairs : 2 * pairs]
    first_out, partial_out = rest[2 * pairs :]
    branch = dot(contexts[0][...], projections[0][...])
    if pairs == 2:
        branch = branch + dot(contexts[1][...], projections[1][...])
    first = tokens[...].astype(F32) + branch + proj_bias[...]
    first_out[...] = first
    rows, _ = normalized(first)
    lowered = (rows * gain[...] + shift[...]).astype(BF16)
    activated = gelu(dot(lowered, hidden[...]) + hidden_bias[...]).astype(BF16)
    partial_out[...] = dot(activated, output[...]).astype(BF16)


def total(parts):
    value = parts[0][...].astype(F32)
    for part in parts[1:]:
        value = value + part[...].astype(F32)
    return value


def router(pairs, first, bias, gain, shift, weight, marks, *rest):
    second_out, lowered_out, route_out, gates_out = rest[pairs:]
    second = first[...] + total(rest[:pairs]) + bias[...]
    second_out[...] = second
    rows, _ = normalized(second)
    normed = rows * gain[...] + shift[...]
    lowered_out[...] = normed.astype(BF16)
    logits = jnp.dot(normed, weight[...], precision=HIGHEST, preferred_element_type=F32)
    grown = jnp.exp(logits - jnp.max(logits, axis=-1, keepdims=True))
    route = grown / jnp.sum(grown, axis=-1, keepdims=True)
    route_out[...] = route
    expert = lax.broadcasted_iota(jnp.int32, route.shape, 1)
    gates = [
        jnp.sum(jnp.where(expert == marks[:, j : j + 1], route, 0.0), axis=1, keepdims=True)
        for j in range(2)
    ]
    gates_out[...] = jnp.concatenate(gates, axis=1)


def slot_hits(targets, rows):
    first = pl.program_id(0) * rows
    slot = first + lax.broadcasted_iota(jnp.int32, (rows, targets.shape[1]), 0)
    return [slot == targets[j : j + 1, :] for j in range(2)]


def thirds(values):
    high = values.astype(BF16)
    rest = values - high.astype(F32)
    middle = rest.astype(BF16)
    low = (rest - middle.astype(F32)).astype(BF16)
    return high, middle, low


def place(parts, targets, *rest):
    sources, out = rest[:parts], rest[parts]
    hits = slot_hits(targets, out.shape[0])
    table = (hits[0] | hits[1]).astype(BF16)
    rows = jnp.zeros(out.shape, F32)
    at = 0
    for source in sources:
        rows = rows + dot(table[:, at : at + source.shape[0]], source[...].astype(BF16))
        at += source.shape[0]
    out[...] = rows.astype(BF16)


def place_gated(parts, targets, *rest):
    sources, gates, out, gates_out = rest[:parts], rest[parts : 2 * parts], rest[2 * parts], rest[2 * parts + 1]
    hits = slot_hits(targets, out.shape[0])
    table = (hits[0] | hits[1]).astype(BF16)
    tables = [hit.astype(BF16) for hit in hits]
    rows = jnp.zeros(out.shape, F32)
    slot_gates = jnp.zeros(gates_out.shape, F32)
    at = 0
    for source, gate in zip(sources, gates):
        end = at + source.shape[0]
        rows = rows + dot(table[:, at:end], source[...])
        for j in range(2):
            terms = jnp.concatenate(thirds(gate[:, j : j + 1]), axis=1)
            slot_gates = slot_gates + jnp.sum(dot(tables[j][:, at:end], terms), axis=1, keepdims=True)
        at = end
    out[...] = rows.astype(BF16)
    gates_out[...] = slot_gates


def expert(
    plane, arrived, upstream, gates, weight_in, bias_in, weight_out, bias_out,
    result_out, grad_out, gate_out, act_out, inner_out, slot_out,
):
    rows = arrived[...]
    inner = dot(rows, weight_in[...]) + bias_in[...]
    act, slope = gelu_parts(inner)
    act = act.astype(BF16)
    act_out[...] = act
    result = dot(act, weight_out[...])
    result_out[...] = result.astype(BF16)
    raised = upstream[...].astype(F32)
    once = jnp.where(plane[0] == 0, 1.0, 0.0)
    gate_out[...] = jnp.sum(raised * (result + bias_out[...] * once), axis=1, keepdims=True)
    slot_grad = (raised * gates[...]).astype(BF16)
    slot_out[...] = slot_grad
    inner_grad = (dot_rows(slot_grad, weight_out[...]) * slope).astype(BF16)
    inner_out[...] = inner_grad
    grad_out[...] = dot_rows(inner_grad, weight_in[...]).astype(BF16)


def token_hits(targets, slots):
    slot = lax.broadcasted_iota(jnp.int32, (targets.shape[0], slots), 1)
    return [slot == targets[:, j : j + 1] for j in range(2)]


def ordered(plane, parts):
    if len(parts) == 1:
        return parts[0]
    own, peer = parts
    flipped = plane[0] != 0
    return jnp.concatenate([jnp.where(flipped, peer, own), jnp.where(flipped, own, peer)], axis=1)


def settle(
    pairs, plane, second, cotangent, route, gain, shift, router_weight, marks, targets, slot_grads, *rest
):
    pieces = rest[:pairs]
    second_out, lowered_out, sums_out, router_out = rest[pairs:]

    @pl.when(pl.program_id(0) == 0)
    def _():
        sums_out[...] = jnp.zeros_like(sums_out)
        router_out[...] = jnp.zeros_like(router_out)

    hits = token_hits(targets, slot_grads.shape[1])
    table = (hits[0] | hits[1]).astype(BF16)
    moe_grad = ordered(plane, [dot(table, piece[...]) for piece in pieces])
    chances = route[...]
    number = lax.broadcasted_iota(jnp.int32, chances.shape, 1)
    route_grad = jnp.zeros_like(chances)
    for j in range(2):
        gate_grad = jnp.sum(jnp.where(hits[j], slot_grads[...], 0.0), axis=1, keepdims=True)
        route_grad = route_grad + jnp.where(number == marks[:, j : j + 1], gate_grad, 0.0)
    logit_grad = chances * (route_grad - jnp.sum(chances * route_grad, axis=1, keepdims=True))
    rows, scale = normalized(second[...])
    normed = rows * gain[...] + shift[...]
    router_out[...] += dot_columns(normed, logit_grad, HIGHEST)
    moe_grad = moe_grad + lax.dot_general(
        logit_grad, router_weight[...], (((1,), (1,)), ((), ())), precision=HIGHEST, preferred_element_type=F32
    )
    grad = cotangent[...] + norm_back(rows, scale, gain[...], moe_grad)
    second_out[...] = grad
    lowered_out[...] = grad.astype(BF16)
    sums_out[0:1, :] += jnp.sum(moe_grad * rows, axis=0, keepdims=True)
    sums_out[1:2, :] += jnp.sum(moe_grad, axis=0, keepdims=True)
    sums_out[2:3, :] += jnp.sum(grad, axis=0, keepdims=True)


def feed_back(
    first, second_grad, gain, shift, hidden, hidden_bias, output,
    act_out, inner_out, lowered_out, partial_out, sums_out,
):
    @pl.when(pl.program_id(0) == 0)
    def _():
        sums_out[...] = jnp.zeros_like(sums_out)

    rows, _ = normalized(first[...])
    lowered = (rows * gain[...] + shift[...]).astype(BF16)
    lowered_out[...] = lowered
    act, slope = gelu_parts(dot(lowered, hidden[...]) + hidden_bias[...])
    act_out[...] = act.astype(BF16)
    inner_grad = (dot_rows(second_grad[...], output[...]) * slope).astype(BF16)
    inner_out[...] = inner_grad
    partial_out[...] = dot_rows(inner_grad, hidden[...]).astype(BF16)
    sums_out[0:1, :] += jnp.sum(inner_grad.astype(F32), axis=0, keepdims=True)


def attend_back(
    pairs, heads, first, second_grad, gain, projection, qkv, weight, tokens, pre_gain, pre_shift, *rest
):
    first_out, branch_out, qkv_out, lowered_out, partial_out, sums_out, qkv_sums_out = rest[pairs:]

    @pl.when(pl.program_id(0) == 0)
    def _():
        sums_out[...] = jnp.zeros_like(sums_out)
        qkv_sums_out[...] = jnp.zeros_like(qkv_sums_out)

    mid_grad = total(rest[:pairs])
    rows, scale = normalized(first[...])
    first_grad = second_grad[...] + norm_back(rows, scale, gain[...], mid_grad)
    first_out[...] = first_grad
    branch = first_grad.astype(BF16)
    branch_out[...] = branch
    sums_out[0:1, :] += jnp.sum(mid_grad * rows, axis=0, keepdims=True)
    sums_out[1:2, :] += jnp.sum(mid_grad, axis=0, keepdims=True)
    sums_out[2:3, :] += jnp.sum(first_grad, axis=0, keepdims=True)
    rows, _ = normalized(tokens[...].astype(F32))
    lowered_out[...] = (rows * pre_gain[...] + pre_shift[...]).astype(BF16)
    context_grad = dot_rows(branch, projection[...]).astype(BF16)
    width = heads * HEAD_DIM
    scale = HEAD_DIM**-0.5
    for image in range(qkv.shape[0] // PATCHES):
        at = image * PATCHES
        block = qkv[at : at + PATCHES, :]
        grad = context_grad[at : at + PATCHES]
        parts = [[], [], []]
        for head in range(heads):
            h = head * HEAD_DIM
            query = block[:, h : h + HEAD_DIM]
            keys = block[:, width + h : width + h + HEAD_DIM]
            values = block[:, 2 * width + h : 2 * width + h + HEAD_DIM]
            upstream = grad[:, h : h + HEAD_DIM]
            probs = softmax_rows(dot_rows(query, keys), scale)
            prob_grad = dot_rows(upstream, values)
            inward = jnp.sum(probs * prob_grad, axis=-1, keepdims=True)
            score_grad = (probs * (prob_grad - inward)).astype(BF16)
            parts[0].append(dot(score_grad, keys) * scale)
            parts[1].append(dot_columns(score_grad, query) * scale)
            parts[2].append(dot_columns(probs.astype(BF16), upstream))
        qkv_grad = jnp.concatenate(parts[0] + parts[1] + parts[2], axis=1).astype(BF16)
        qkv_out[at : at + PATCHES, :] = qkv_grad
        partial_out[at : at + PATCHES, :] = dot_rows(qkv_grad, weight[...]).astype(BF16)
        qkv_sums_out[0:1, :] += jnp.sum(qkv_grad.astype(F32), axis=0, keepdims=True)


def finish(pairs, tokens, gain, first_grad, *rest):
    grad_out, sums_out = rest[pairs:]

    @pl.when(pl.program_id(0) == 0)
    def _():
        sums_out[...] = jnp.zeros_like(sums_out)

    upstream = total(rest[:pairs])
    rows, scale = normalized(tokens[...].astype(F32))
    grad_out[...] = first_grad[...] + norm_back(rows, scale, gain[...], upstream)
    sums_out[0:1, :] += jnp.sum(upstream * rows, axis=0, keepdims=True)
    sums_out[1:2, :] += jnp.sum(upstream, axis=0, keepdims=True)


def blend(pairs, plane, second, gates, targets, *rest):
    pieces, out = rest[:pairs], rest[pairs]
    slots = pieces[0].shape[0]
    mixture = jnp.zeros(out.shape, F32)
    for j, hit in enumerate(token_hits(targets, slots)):
        table = hit.astype(BF16)
        picked = ordered(plane, [dot(table, piece[...]) for piece in pieces])
        mixture = mixture + gates[:, j : j + 1] * picked
    out[...] = (second[...] + mixture).astype(BF16)


def slot_targets(choice_ids, ranks, capacity):
    count = choice_ids.shape[0]
    order_keys = jnp.concatenate([ranks, ranks + count])
    flat_ids = jnp.concatenate([choice_ids[:, 0], choice_ids[:, 1]])
    earlier = (order_keys[None, :] < order_keys[:, None]) & (flat_ids[None, :] == flat_ids[:, None])
    position = jnp.sum(earlier.astype(jnp.int32), axis=1).reshape(2, count)
    kept = position < capacity
    targets = jnp.where(kept, choice_ids.T * capacity + position, -1)
    marks = jnp.where(kept, choice_ids.T, -1)
    return targets, marks


def shards(
    planes,
    tokens_in, pre_gain, pre_shift, qkv_weight, qv_bias, proj_weight, proj_bias, mid_gain, mid_shift,
    hidden_weight, hidden_bias, output_weight, output_bias, moe_gain, moe_shift, router_weight,
    expert_in, expert_in_bias, expert_out, expert_out_bias, expert_ids, priority, cotangent,
):
    tokens, model = tokens_in.shape
    width = qkv_weight.shape[2]
    heads = width // HEAD_DIM
    hidden = hidden_weight.shape[1]
    experts = router_weight.shape[1]
    capacity = tokens // experts
    slots = experts * capacity
    step = 2 * PATCHES
    parts = 2
    part_rows = tokens // parts
    part_steps = part_rows // step
    two = planes == 2
    pairs = 2 if two else 1
    plane = lax.axis_index("tensor").astype(jnp.int32).reshape(1)

    def swap(value):
        return lax.ppermute(value, "tensor", [(0, 1), (1, 0)])

    def summands(value):
        if two:
            return [value, swap(value)]
        return [lax.psum(value.astype(F32), "tensor").astype(BF16)]

    def row(vector):
        return vector.reshape(1, -1)

    pre_gain, pre_shift, proj_bias = row(pre_gain), row(pre_shift), row(proj_bias)
    mid_gain, mid_shift, hidden_bias = row(mid_gain), row(mid_shift), row(hidden_bias)
    output_bias, moe_gain, moe_shift = row(output_bias), row(moe_gain), row(moe_shift)
    weight_qkv = qkv_weight.reshape(model, 3 * width)
    qkv_bias = jnp.concatenate([qv_bias[0], jnp.zeros_like(qv_bias[0]), qv_bias[1]]).reshape(1, 3 * width)
    if two:
        projections = [proj_weight, swap(proj_weight)]
    else:
        projections = [lax.all_gather(proj_weight, "tensor", axis=0, tiled=True)]

    targets, marks = slot_targets(expert_ids, priority[0], capacity)
    targets_by_token, marks = targets.T, marks.T
    upstream_rows = call(
        functools.partial(place, 1), slots // step,
        [(targets, None, 0), (cotangent, None, 0)],
        [((slots, model), BF16, step)], "place_cotangent",
    )[0]

    def to_experts(rows):
        wide = rows.reshape(experts, capacity, rows.shape[1])
        return lax.all_to_all(wide, "wide", split_axis=0, concat_axis=0, tiled=True).reshape(rows.shape)

    upstream = to_experts(upstream_rows)

    qkv, firsts, seconds, lowered, routes, gates = [], [], [], [], [], []
    contexts = []
    for part in range(parts):
        first_step = part * part_steps
        qkv_part, context = call(
            functools.partial(attend, heads), part_steps,
            [(tokens_in, step, first_step), (pre_gain, None, 0), (pre_shift, None, 0), (weight_qkv, None, 0), (qkv_bias, None, 0)],
            [((part_rows, 3 * width), BF16, step), ((part_rows, width), BF16, step)], "attend",
        )
        qkv.append(qkv_part)
        contexts.append(context)
    gathered = [
        [context, swap(context)] if two else [lax.all_gather(context, "tensor", axis=1, tiled=True)]
        for context in contexts
    ]
    partials = []
    for part in range(parts):
        first_step = part * part_steps
        first, partial = call(
            functools.partial(feed, pairs), part_steps,
            [(tokens_in, step, first_step), (proj_bias, None, 0), (mid_gain, None, 0), (mid_shift, None, 0),
             (hidden_weight, None, 0), (hidden_bias, None, 0), (output_weight, None, 0)]
            + [(context, step, 0) for context in gathered[part]]
            + [(projection, None, 0) for projection in projections],
            [((part_rows, model), F32, step), ((part_rows, model), BF16, step)], "feed",
        )
        firsts.append(first)
        partials.append(summands(partial))
    for part in range(parts):
        first_step = part * part_steps
        second, low, route, gate = call(
            functools.partial(router, pairs), part_steps,
            [(firsts[part], step, 0), (output_bias, None, 0), (moe_gain, None, 0), (moe_shift, None, 0),
             (router_weight, None, 0), (marks, step, first_step)]
            + [(partial, step, 0) for partial in partials[part]],
            [((part_rows, model), F32, step), ((part_rows, model), BF16, step),
             ((part_rows, experts), F32, step), ((part_rows, 2), F32, step)], "router",
        )
        seconds.append(second)
        lowered.append(low)
        routes.append(route)
        gates.append(gate)

    buffers, slot_gates = call(
        functools.partial(place_gated, parts), slots // step,
        [(targets, None, 0)] + [(low, None, 0) for low in lowered] + [(gate, None, 0) for gate in gates],
        [((slots, model), BF16, step), ((slots, 1), F32, step)], "place_tokens",
    )
    arrived = to_experts(buffers)
    arrived_gates = lax.all_to_all(
        slot_gates.reshape(experts, capacity), "wide", split_axis=0, concat_axis=0, tiled=True
    ).reshape(slots, 1)
    result, arrived_grad, gate_grad, expert_act, expert_inner_grad, slot_grad = call(
        expert, slots // step,
        [(plane, "scalar", 0), (arrived, step, 0), (upstream, step, 0), (arrived_gates, step, 0),
         (expert_in[0], None, 0), (expert_in_bias, None, 0), (expert_out[0], None, 0), (expert_out_bias, None, 0)],
        [((slots, model), BF16, step), ((slots, model), BF16, step), ((slots, 1), F32, step),
         ((slots, hidden), BF16, step), ((slots, hidden), BF16, step), ((slots, model), BF16, step)], "expert",
    )

    def home(partial, bias):
        if not two:
            rows = lax.psum(partial.astype(F32), "tensor")
            if bias is not None:
                rows = rows + bias
            return [to_experts(rows.astype(BF16))]
        half = model // 2
        low, high = partial[:, :half], partial[:, half:]
        flipped = plane[0] != 0
        kept = jnp.where(flipped, high, low)
        other = swap(jnp.where(flipped, low, high))
        rows = kept.astype(F32) + other.astype(F32)
        if bias is not None:
            rows = rows + jnp.where(flipped, bias[:, half:], bias[:, :half])
        own = to_experts(rows.astype(BF16))
        return [own, swap(own)]

    row_pieces = home(arrived_grad, None)
    gate_home = lax.all_to_all(
        gate_grad.reshape(experts, capacity), "wide", split_axis=0, concat_axis=0, tiled=True
    ).reshape(1, slots)
    gate_home = lax.psum(gate_home, "tensor") if not two else gate_home + swap(gate_home)
    second_grads, lowered_seconds = [], []
    moe_sums, router_sums = [], []
    for part in range(parts):
        first_step = part * part_steps
        grad, low, sums, router_sum = call(
            functools.partial(settle, pairs), part_steps,
            [(plane, "scalar", 0), (seconds[part], step, 0), (cotangent, step, first_step), (routes[part], step, 0),
             (moe_gain, None, 0), (moe_shift, None, 0), (router_weight, None, 0),
             (marks, step, first_step), (targets_by_token, step, first_step), (gate_home, None, 0)]
            + [(piece, None, 0) for piece in row_pieces],
            [((part_rows, model), F32, step), ((part_rows, model), BF16, step), ((8, model), F32, None),
             ((model, experts), F32, None)], "settle",
        )
        second_grads.append(grad)
        lowered_seconds.append(low)
        moe_sums.append(sums)
        router_sums.append(router_sum)
    acts, inner_grads, lowered_mids, mid_parts, hidden_sums = [], [], [], [], []
    for part in range(parts):
        act, inner_grad, low, partial, sums = call(
            feed_back, part_steps,
            [(firsts[part], step, 0), (lowered_seconds[part], step, 0), (mid_gain, None, 0), (mid_shift, None, 0),
             (hidden_weight, None, 0), (hidden_bias, None, 0), (output_weight, None, 0)],
            [((part_rows, hidden), BF16, step), ((part_rows, hidden), BF16, step), ((part_rows, model), BF16, step),
             ((part_rows, model), BF16, step), ((8, hidden), F32, None)], "feed_back",
        )
        acts.append(act)
        inner_grads.append(inner_grad)
        lowered_mids.append(low)
        mid_parts.append(summands(partial))
        hidden_sums.append(sums)

    def weight_grad(lefts, rights):
        return sum(dot_columns(left, right) for left, right in zip(lefts, rights))

    output_weight_grad = weight_grad(acts, lowered_seconds)
    hidden_weight_grad = weight_grad(lowered_mids, inner_grads)
    first_grads, branch_grads, qkv_grads, lowered_pres, pre_parts, mid_sums, qkv_sums = [], [], [], [], [], [], []
    for part in range(parts):
        first_step = part * part_steps
        first_grad, branch, qkv_grad, low, partial, sums, qkv_sum = call(
            functools.partial(attend_back, pairs, heads), part_steps,
            [(firsts[part], step, 0), (second_grads[part], step, 0), (mid_gain, None, 0), (proj_weight, None, 0),
             (qkv[part], step, 0), (weight_qkv, None, 0), (tokens_in, step, first_step),
             (pre_gain, None, 0), (pre_shift, None, 0)]
            + [(partial, step, 0) for partial in mid_parts[part]],
            [((part_rows, model), F32, step), ((part_rows, model), BF16, step), ((part_rows, 3 * width), BF16, step),
             ((part_rows, model), BF16, step), ((part_rows, model), BF16, step), ((8, model), F32, None),
             ((8, 3 * width), F32, None)], "attend_back",
        )
        first_grads.append(first_grad)
        branch_grads.append(branch)
        qkv_grads.append(qkv_grad)
        lowered_pres.append(low)
        pre_parts.append(summands(partial))
        mid_sums.append(sums)
        qkv_sums.append(qkv_sum)
    proj_weight_grad = weight_grad(contexts, branch_grads)
    qkv_weight_grad = weight_grad(lowered_pres, qkv_grads)
    token_grads, pre_sums = [], []
    for part in range(parts):
        first_step = part * part_steps
        grad, sums = call(
            functools.partial(finish, pairs), part_steps,
            [(tokens_in, step, first_step), (pre_gain, None, 0), (first_grads[part], step, 0)]
            + [(partial, step, 0) for partial in pre_parts[part]],
            [((part_rows, model), F32, step), ((8, model), F32, None)], "finish",
        )
        token_grads.append(grad)
        pre_sums.append(sums)
    tokens_grad = jnp.concatenate(token_grads)

    result_pieces = home(result, expert_out_bias)
    outs = []
    for part in range(parts):
        first_step = part * part_steps
        outs.append(
            call(
                functools.partial(blend, pairs), part_steps,
                [(plane, "scalar", 0), (seconds[part], step, 0), (gates[part], step, 0), (targets_by_token, step, first_step)]
                + [(piece, None, 0) for piece in result_pieces],
                [((part_rows, model), BF16, step)], "blend",
            )[0]
        )
    block_out = jnp.concatenate(outs)

    expert_out_grad = dot_columns(expert_act, slot_grad)[None]
    expert_in_grad = dot_columns(arrived, expert_inner_grad)[None]
    expert_out_bias_grad = jnp.sum(slot_grad.astype(F32), axis=0, keepdims=True)
    expert_in_bias_grad = jnp.sum(expert_inner_grad.astype(F32), axis=0, keepdims=True)

    pre, mid, moe, hid, qks = (sum(group) for group in (pre_sums, mid_sums, moe_sums, hidden_sums, qkv_sums))
    qks = qks[0].reshape(3, width)
    vectors = [pre[0], pre[1], qks[0], qks[2], mid[2], mid[0], mid[1], hid[0], moe[2], moe[0], moe[1], sum(router_sums).reshape(-1)]
    sizes = [vector.size for vector in vectors]
    small = lax.psum(jnp.concatenate(vectors).astype(BF16), "wide").astype(F32)
    ends = [sum(sizes[: i + 1]) for i in range(len(sizes))]
    (pre_gain_g, pre_shift_g, q_bias_g, v_bias_g, proj_bias_g, mid_gain_g, mid_shift_g, hidden_bias_g,
     output_bias_g, moe_gain_g, moe_shift_g, router_g) = [small[end - size : end] for size, end in zip(sizes, ends)]

    def over_wide(value):
        return lax.psum(value.astype(BF16), "wide").astype(F32)

    return (
        block_out,
        tokens_grad,
        pre_gain_g,
        pre_shift_g,
        over_wide(qkv_weight_grad).reshape(model, 3, width),
        jnp.stack([q_bias_g, v_bias_g]),
        over_wide(proj_weight_grad),
        proj_bias_g,
        mid_gain_g,
        mid_shift_g,
        over_wide(hidden_weight_grad),
        hidden_bias_g,
        over_wide(output_weight_grad),
        output_bias_g,
        moe_gain_g,
        moe_shift_g,
        router_g.reshape(model, experts),
        expert_in_grad,
        expert_in_bias_grad,
        expert_out_grad,
        expert_out_bias_grad,
    )


def solution(mesh):
    return jax.shard_map(
        functools.partial(shards, mesh.shape["tensor"]),
        mesh=mesh,
        in_specs=(
            P("wide", None), P(), P(), P(None, None, "tensor"), P(None, "tensor"), P("tensor", None), P(), P(), P(),
            P(None, "tensor"), P("tensor"), P("tensor", None), P(), P(), P(), P(),
            P("wide", None, "tensor"), P("wide", "tensor"), P("wide", "tensor", None), P("wide", None),
            P("wide", None), P("wide", None), P("wide", None),
        ),
        out_specs=(
            P("wide", None), P("wide", None), P(), P(), P(None, None, "tensor"), P(None, "tensor"), P("tensor", None),
            P(), P(), P(), P(None, "tensor"), P("tensor"), P("tensor", None), P(), P(), P(), P(),
            P("wide", None, "tensor"), P("wide", "tensor"), P("wide", "tensor", None), P("wide", None),
        ),
        check_vma=False,
    )
```

```python
import functools

import jax
import jax.numpy as jnp
from jax import lax
from jax.experimental import pallas as pl
from jax.experimental.pallas import tpu as pltpu
from jax.sharding import PartitionSpec as P

HEAD_DIM = 64
PATCHES = 144
BF16 = jnp.bfloat16
F32 = jnp.float32
HIGHEST = lax.Precision.HIGHEST
VMEM_BYTES = 48 * 1024 * 1024


def dot(left, right):
    return jnp.dot(left, right, preferred_element_type=F32)


def dot_rows(left, right):
    return lax.dot_general(left, right, (((1,), (1,)), ((), ())), preferred_element_type=F32)


def dot_columns(left, right, precision=None):
    return lax.dot_general(
        left, right, (((0,), (0,)), ((), ())), precision=precision, preferred_element_type=F32
    )


def normalized(values):
    centered = values - jnp.mean(values, axis=-1, keepdims=True)
    variance = jnp.mean(centered * centered, axis=-1, keepdims=True)
    scale = lax.rsqrt(variance + 1e-06)
    return centered * scale, scale


def norm_back(rows, scale, gain, upstream):
    scaled = upstream * gain
    inward = jnp.mean(scaled, axis=-1, keepdims=True)
    along = jnp.mean(scaled * rows, axis=-1, keepdims=True)
    return scale * (scaled - inward - rows * along)


def gelu_parts(inner):
    square = inner * inner
    bend = jnp.tanh(0.7978845608028654 * inner * (1.0 + 0.044715 * square))
    half = 0.5 * (1.0 + bend)
    slope = half + (0.5 * 0.7978845608028654) * inner * (1.0 - bend * bend) * (
        1.0 + 0.134145 * square
    )
    return inner * half, slope


def gelu(inner):
    return inner * (0.5 * (1.0 + jnp.tanh(0.7978845608028654 * inner * (1.0 + 0.044715 * inner * inner))))


def softmax_rows(scores, scale):
    peak = jnp.max(scores, axis=-1, keepdims=True)
    weights = jnp.exp((scores - peak) * scale)
    return weights * (1.0 / jnp.sum(weights, axis=-1, keepdims=True))


def call(kernel, steps, ins, outs, name):
    def spec(shape, rows, first):
        if rows is None:
            return pl.BlockSpec(shape, lambda i: (0,) * len(shape))
        return pl.BlockSpec((rows,) + tuple(shape[1:]), lambda i: (i + first,) + (0,) * (len(shape) - 1))

    in_specs = []
    for array, rows, first in ins:
        if rows == "scalar":
            in_specs.append(pl.BlockSpec(memory_space=pltpu.SMEM))
        else:
            in_specs.append(spec(array.shape, rows, first))
    return pl.pallas_call(
        kernel,
        grid=(steps,),
        in_specs=in_specs,
        out_specs=[spec(shape, rows, 0) for shape, _, rows in outs],
        out_shape=[jax.ShapeDtypeStruct(shape, dtype) for shape, dtype, _ in outs],
        compiler_params=pltpu.CompilerParams(vmem_limit_bytes=VMEM_BYTES),
        name=name,
    )(*[array for array, _, _ in ins])


def attend(heads, tokens, gain, shift, weight, bias, qkv_out, context_out):
    rows, _ = normalized(tokens[...].astype(F32))
    lowered = (rows * gain[...] + shift[...]).astype(BF16)
    qkv = (dot(lowered, weight[...]) + bias[...]).astype(BF16)
    qkv_out[...] = qkv
    width = heads * HEAD_DIM
    for image in range(qkv.shape[0] // PATCHES):
        block = qkv[image * PATCHES : (image + 1) * PATCHES]
        parts = []
        for head in range(heads):
            at = head * HEAD_DIM
            query = block[:, at : at + HEAD_DIM]
            keys = block[:, width + at : width + at + HEAD_DIM]
            values = block[:, 2 * width + at : 2 * width + at + HEAD_DIM]
            probs = softmax_rows(dot_rows(query, keys), HEAD_DIM**-0.5)
            parts.append(dot(probs.astype(BF16), values))
        context = jnp.concatenate(parts, axis=1).astype(BF16)
        context_out[image * PATCHES : (image + 1) * PATCHES, :] = context


def feed(
    pairs, tokens, proj_bias, gain, shift, hidden, hidden_bias, output, *rest
):
    contexts, projections = rest[:pairs], rest[pairs : 2 * pairs]
    first_out, partial_out = rest[2 * pairs :]
    branch = dot(contexts[0][...], projections[0][...])
    if pairs == 2:
        branch = branch + dot(contexts[1][...], projections[1][...])
    first = tokens[...].astype(F32) + branch + proj_bias[...]
    first_out[...] = first
    rows, _ = normalized(first)
    lowered = (rows * gain[...] + shift[...]).astype(BF16)
    activated = gelu(dot(lowered, hidden[...]) + hidden_bias[...]).astype(BF16)
    partial_out[...] = dot(activated, output[...]).astype(BF16)


def total(parts):
    value = parts[0][...].astype(F32)
    for part in parts[1:]:
        value = value + part[...].astype(F32)
    return value


def router(pairs, first, bias, gain, shift, weight, marks, *rest):
    second_out, lowered_out, route_out, gates_out = rest[pairs:]
    second = first[...] + total(rest[:pairs]) + bias[...]
    second_out[...] = second
    rows, _ = normalized(second)
    normed = rows * gain[...] + shift[...]
    lowered_out[...] = normed.astype(BF16)
    logits = jnp.dot(normed, weight[...], precision=HIGHEST, preferred_element_type=F32)
    grown = jnp.exp(logits - jnp.max(logits, axis=-1, keepdims=True))
    route = grown / jnp.sum(grown, axis=-1, keepdims=True)
    route_out[...] = route
    expert = lax.broadcasted_iota(jnp.int32, route.shape, 1)
    gates = [
        jnp.sum(jnp.where(expert == marks[:, j : j + 1], route, 0.0), axis=1, keepdims=True)
        for j in range(2)
    ]
    gates_out[...] = jnp.concatenate(gates, axis=1)


def slot_hits(targets, rows):
    first = pl.program_id(0) * rows
    slot = first + lax.broadcasted_iota(jnp.int32, (rows, targets.shape[1]), 0)
    return [slot == targets[j : j + 1, :] for j in range(2)]


def thirds(values):
    high = values.astype(BF16)
    rest = values - high.astype(F32)
    middle = rest.astype(BF16)
    low = (rest - middle.astype(F32)).astype(BF16)
    return high, middle, low


def place(parts, targets, *rest):
    sources, out = rest[:parts], rest[parts]
    hits = slot_hits(targets, out.shape[0])
    table = (hits[0] | hits[1]).astype(BF16)
    rows = jnp.zeros(out.shape, F32)
    at = 0
    for source in sources:
        rows = rows + dot(table[:, at : at + source.shape[0]], source[...].astype(BF16))
        at += source.shape[0]
    out[...] = rows.astype(BF16)


def place_gated(parts, targets, *rest):
    sources, gates, out, gates_out = rest[:parts], rest[parts : 2 * parts], rest[2 * parts], rest[2 * parts + 1]
    hits = slot_hits(targets, out.shape[0])
    table = (hits[0] | hits[1]).astype(BF16)
    tables = [hit.astype(BF16) for hit in hits]
    rows = jnp.zeros(out.shape, F32)
    slot_gates = jnp.zeros(gates_out.shape, F32)
    at = 0
    for source, gate in zip(sources, gates):
        end = at + source.shape[0]
        rows = rows + dot(table[:, at:end], source[...])
        for j in range(2):
            terms = jnp.concatenate(thirds(gate[:, j : j + 1]), axis=1)
            slot_gates = slot_gates + jnp.sum(dot(tables[j][:, at:end], terms), axis=1, keepdims=True)
        at = end
    out[...] = rows.astype(BF16)
    gates_out[...] = slot_gates


def expert(
    plane, arrived, upstream, gates, weight_in, bias_in, weight_out, bias_out,
    result_out, grad_out, gate_out, act_out, inner_out, slot_out,
):
    rows = arrived[...]
    inner = dot(rows, weight_in[...]) + bias_in[...]
    act, slope = gelu_parts(inner)
    act = act.astype(BF16)
    act_out[...] = act
    result = dot(act, weight_out[...])
    result_out[...] = result.astype(BF16)
    raised = upstream[...].astype(F32)
    once = jnp.where(plane[0] == 0, 1.0, 0.0)
    gate_out[...] = jnp.sum(raised * (result + bias_out[...] * once), axis=1, keepdims=True)
    slot_grad = (raised * gates[...]).astype(BF16)
    slot_out[...] = slot_grad
    inner_grad = (dot_rows(slot_grad, weight_out[...]) * slope).astype(BF16)
    inner_out[...] = inner_grad
    grad_out[...] = dot_rows(inner_grad, weight_in[...]).astype(BF16)


def token_hits(targets, slots):
    slot = lax.broadcasted_iota(jnp.int32, (targets.shape[0], slots), 1)
    return [slot == targets[:, j : j + 1] for j in range(2)]


def ordered(plane, parts):
    if len(parts) == 1:
        return parts[0]
    own, peer = parts
    flipped = plane[0] != 0
    return jnp.concatenate([jnp.where(flipped, peer, own), jnp.where(flipped, own, peer)], axis=1)


def settle(
    pairs, plane, second, cotangent, route, gain, shift, router_weight, marks, targets, slot_grads, *rest
):
    pieces = rest[:pairs]
    second_out, lowered_out, sums_out, router_out = rest[pairs:]

    @pl.when(pl.program_id(0) == 0)
    def _():
        sums_out[...] = jnp.zeros_like(sums_out)
        router_out[...] = jnp.zeros_like(router_out)

    hits = token_hits(targets, slot_grads.shape[1])
    table = (hits[0] | hits[1]).astype(BF16)
    moe_grad = ordered(plane, [dot(table, piece[...]) for piece in pieces])
    chances = route[...]
    number = lax.broadcasted_iota(jnp.int32, chances.shape, 1)
    route_grad = jnp.zeros_like(chances)
    for j in range(2):
        gate_grad = jnp.sum(jnp.where(hits[j], slot_grads[...], 0.0), axis=1, keepdims=True)
        route_grad = route_grad + jnp.where(number == marks[:, j : j + 1], gate_grad, 0.0)
    logit_grad = chances * (route_grad - jnp.sum(chances * route_grad, axis=1, keepdims=True))
    rows, scale = normalized(second[...])
    normed = rows * gain[...] + shift[...]
    router_out[...] += dot_columns(logit_grad, normed, HIGHEST)
    moe_grad = moe_grad + lax.dot_general(
        logit_grad, router_weight[...], (((1,), (1,)), ((), ())), precision=HIGHEST, preferred_element_type=F32
    )
    grad = cotangent[...] + norm_back(rows, scale, gain[...], moe_grad)
    second_out[...] = grad
    lowered_out[...] = grad.astype(BF16)
    sums_out[0:1, :] += jnp.sum(moe_grad * rows, axis=0, keepdims=True)
    sums_out[1:2, :] += jnp.sum(moe_grad, axis=0, keepdims=True)
    sums_out[2:3, :] += jnp.sum(grad, axis=0, keepdims=True)


def feed_back(
    first, second_grad, gain, shift, hidden, hidden_bias, output,
    act_out, inner_out, lowered_out, partial_out, sums_out,
):
    @pl.when(pl.program_id(0) == 0)
    def _():
        sums_out[...] = jnp.zeros_like(sums_out)

    rows, _ = normalized(first[...])
    lowered = (rows * gain[...] + shift[...]).astype(BF16)
    lowered_out[...] = lowered
    act, slope = gelu_parts(dot(lowered, hidden[...]) + hidden_bias[...])
    act_out[...] = act.astype(BF16)
    inner_grad = (dot_rows(second_grad[...], output[...]) * slope).astype(BF16)
    inner_out[...] = inner_grad
    partial_out[...] = dot_rows(inner_grad, hidden[...]).astype(BF16)
    sums_out[0:1, :] += jnp.sum(inner_grad.astype(F32), axis=0, keepdims=True)


def attend_back(
    pairs, heads, first, second_grad, gain, projection, qkv, weight, tokens, pre_gain, pre_shift, *rest
):
    first_out, branch_out, qkv_out, lowered_out, partial_out, sums_out, qkv_sums_out = rest[pairs:]

    @pl.when(pl.program_id(0) == 0)
    def _():
        sums_out[...] = jnp.zeros_like(sums_out)
        qkv_sums_out[...] = jnp.zeros_like(qkv_sums_out)

    mid_grad = total(rest[:pairs])
    rows, scale = normalized(first[...])
    first_grad = second_grad[...] + norm_back(rows, scale, gain[...], mid_grad)
    first_out[...] = first_grad
    branch = first_grad.astype(BF16)
    branch_out[...] = branch
    sums_out[0:1, :] += jnp.sum(mid_grad * rows, axis=0, keepdims=True)
    sums_out[1:2, :] += jnp.sum(mid_grad, axis=0, keepdims=True)
    sums_out[2:3, :] += jnp.sum(first_grad, axis=0, keepdims=True)
    rows, _ = normalized(tokens[...].astype(F32))
    lowered_out[...] = (rows * pre_gain[...] + pre_shift[...]).astype(BF16)
    context_grad = dot_rows(branch, projection[...]).astype(BF16)
    width = heads * HEAD_DIM
    scale = HEAD_DIM**-0.5
    for image in range(qkv.shape[0] // PATCHES):
        at = image * PATCHES
        block = qkv[at : at + PATCHES, :]
        grad = context_grad[at : at + PATCHES]
        parts = [[], [], []]
        for head in range(heads):
            h = head * HEAD_DIM
            query = block[:, h : h + HEAD_DIM]
            keys = block[:, width + h : width + h + HEAD_DIM]
            values = block[:, 2 * width + h : 2 * width + h + HEAD_DIM]
            upstream = grad[:, h : h + HEAD_DIM]
            probs = softmax_rows(dot_rows(query, keys), scale)
            prob_grad = dot_rows(upstream, values)
            inward = jnp.sum(probs * prob_grad, axis=-1, keepdims=True)
            score_grad = (probs * (prob_grad - inward)).astype(BF16)
            parts[0].append(dot(score_grad, keys) * scale)
            parts[1].append(dot_columns(score_grad, query) * scale)
            parts[2].append(dot_columns(probs.astype(BF16), upstream))
        qkv_grad = jnp.concatenate(parts[0] + parts[1] + parts[2], axis=1).astype(BF16)
        qkv_out[at : at + PATCHES, :] = qkv_grad
        partial_out[at : at + PATCHES, :] = dot_rows(qkv_grad, weight[...]).astype(BF16)
        qkv_sums_out[0:1, :] += jnp.sum(qkv_grad.astype(F32), axis=0, keepdims=True)


def finish(pairs, tokens, gain, first_grad, *rest):
    grad_out, sums_out = rest[pairs:]

    @pl.when(pl.program_id(0) == 0)
    def _():
        sums_out[...] = jnp.zeros_like(sums_out)

    upstream = total(rest[:pairs])
    rows, scale = normalized(tokens[...].astype(F32))
    grad_out[...] = first_grad[...] + norm_back(rows, scale, gain[...], upstream)
    sums_out[0:1, :] += jnp.sum(upstream * rows, axis=0, keepdims=True)
    sums_out[1:2, :] += jnp.sum(upstream, axis=0, keepdims=True)


def blend(pairs, plane, second, gates, targets, *rest):
    pieces, out = rest[:pairs], rest[pairs]
    slots = pieces[0].shape[0]
    mixture = jnp.zeros(out.shape, F32)
    for j, hit in enumerate(token_hits(targets, slots)):
        table = hit.astype(BF16)
        picked = ordered(plane, [dot(table, piece[...]) for piece in pieces])
        mixture = mixture + gates[:, j : j + 1] * picked
    out[...] = (second[...] + mixture).astype(BF16)


def slot_targets(choice_ids, ranks, capacity):
    count = choice_ids.shape[0]
    order_keys = jnp.concatenate([ranks, ranks + count])
    flat_ids = jnp.concatenate([choice_ids[:, 0], choice_ids[:, 1]])
    earlier = (order_keys[None, :] < order_keys[:, None]) & (flat_ids[None, :] == flat_ids[:, None])
    position = jnp.sum(earlier.astype(jnp.int32), axis=1).reshape(2, count)
    kept = position < capacity
    targets = jnp.where(kept, choice_ids.T * capacity + position, -1)
    marks = jnp.where(kept, choice_ids.T, -1)
    return targets, marks


MESH = pl.DeviceIdType.MESH


def bits_of(index, wide):
    return [lax.rem(lax.div(index, 1 << k), 2) for k in range(wide.bit_length() - 1)]


def sum_wide(wide, orders, totals, sends, lands, gathers, send_sems, recv_sems):
    me, plane = lax.axis_index("wide"), lax.axis_index("tensor")
    bits = bits_of(me, wide)
    partners = [me + (1 - 2 * bit) * (1 << k) for k, bit in enumerate(bits)]
    steps = len(bits)
    count = len(totals)

    def piece(i, step):
        rows = totals[i].shape[0]
        base = 0
        for s in range(step):
            base = base + bits[orders[i][s]] * (rows >> (s + 1))
        length = rows >> (step + 1)
        bit = bits[orders[i][step]]
        return pl.multiple_of(base + bit * length, 16), pl.multiple_of(base + (1 - bit) * length, 16), length

    def move(i, slot, source, target, step):
        return pltpu.make_async_remote_copy(
            source, target, send_sems.at[i, slot], recv_sems.at[i, slot],
            device_id=(partners[orders[i][step]], plane), device_id_type=MESH,
        )

    def scatter(i, step):
        _, other, length = piece(i, step)
        at = totals[i].shape[0] - (totals[i].shape[0] >> step)
        sends[i][at : at + length, :] = totals[i][pl.ds(other, length), :].astype(BF16)
        return move(i, step, sends[i].at[pl.ds(at, length)], lands[i].at[pl.ds(at, length)], step)

    def spread(i, step):
        kept, _, length = piece(i, step)
        block = gathers[i].at[pl.ds(kept, length)]
        return move(i, steps + step, block, block, step)

    copies = [scatter(i, 0) for i in range(count)]
    for copy in copies:
        copy.start()
    for step in range(steps):
        for i in range(count):
            copies[i].wait()
            kept, _, length = piece(i, step)
            at = totals[i].shape[0] - (totals[i].shape[0] >> step)
            totals[i][pl.ds(kept, length), :] += lands[i][at : at + length, :].astype(F32)
            if step + 1 < steps:
                copies[i] = scatter(i, step + 1)
            else:
                gathers[i][pl.ds(kept, length), :] = totals[i][pl.ds(kept, length), :].astype(BF16)
                copies[i] = spread(i, step)
            copies[i].start()
    for step in range(steps - 2, -1, -1):
        for i in range(count):
            copies[i].wait()
            copies[i] = spread(i, step)
            copies[i].start()
    for i in range(count):
        copies[i].wait()
        totals[i][...] = gathers[i][...].astype(F32)


def greet(wide):
    me, plane = lax.axis_index("wide"), lax.axis_index("tensor")
    barrier = pltpu.get_barrier_semaphore()
    bits = bits_of(me, wide)
    for k, bit in enumerate(bits):
        pl.semaphore_signal(
            barrier, inc=1, device_id=(me + (1 - 2 * bit) * (1 << k), plane), device_id_type=MESH
        )
    pl.semaphore_wait(barrier, len(bits))


def fold_scratch(shapes, steps):
    kept = [pltpu.VMEM(shape, BF16) for shape in shapes]
    sems = pltpu.SemaphoreType.DMA((len(shapes), 2 * steps))
    return kept * 3 + [sems, sems]


def put_row(small, at, row):
    for c in range(row.shape[1] // 128):
        small[at + c : at + c + 1, :] = row[:, 128 * c : 128 * (c + 1)]
    return at + row.shape[1] // 128


def get_row(small, at, width):
    return jnp.concatenate([small[at + c : at + c + 1, :] for c in range(width // 128)], axis=1)


def last_sums(wide, parts, layout, orders, *refs):
    lowered, qkv_grads, contexts, branches = (refs[i * parts : (i + 1) * parts] for i in range(4))
    at = 4 * parts
    vectors = refs[at : at + len(layout) * parts]
    at += len(layout) * parts
    qkv_out, proj_out = refs[at : at + 2]
    vectors_out = refs[at + 2 : at + 2 + len(layout)]
    scratch = refs[at + 2 + len(layout) :]
    totals, buffers = scratch[:4], scratch[4:]
    left, right, proj, small = totals
    greet(wide)
    half = left.shape[1]
    for p in range(parts):
        grad = dot_columns(lowered[p][...], qkv_grads[p][...])
        side = dot_columns(contexts[p][...], branches[p][...])
        if p == 0:
            left[...], right[...], proj[...] = grad[:, :half], grad[:, half:], side
        else:
            left[...] += grad[:, :half]
            right[...] += grad[:, half:]
            proj[...] += side
    small[...] = jnp.zeros_like(small)
    at = 0
    for v, rows in enumerate(layout):
        group = vectors[v * parts : (v + 1) * parts]
        for r in rows:
            at = put_row(small, at, sum(part[r : r + 1, :] for part in group))
    count = len(totals)
    sum_wide(wide, orders, totals, buffers[:count], buffers[count : 2 * count], buffers[2 * count : 3 * count], *buffers[3 * count :])
    qkv_out[:, :half] = left[...]
    qkv_out[:, half:] = right[...]
    proj_out[...] = proj[...]
    at = 0
    for v, rows in enumerate(layout):
        out = vectors_out[v]
        for i in range(len(rows)):
            out[i : i + 1, :] = get_row(small, at, out.shape[1])
            at += out.shape[1] // 128


def shards(
    wide, planes,
    tokens_in, pre_gain, pre_shift, qkv_weight, qv_bias, proj_weight, proj_bias, mid_gain, mid_shift,
    hidden_weight, hidden_bias, output_weight, output_bias, moe_gain, moe_shift, router_weight,
    expert_in, expert_in_bias, expert_out, expert_out_bias, expert_ids, priority, cotangent,
):
    tokens, model = tokens_in.shape
    width = qkv_weight.shape[2]
    heads = width // HEAD_DIM
    hidden = hidden_weight.shape[1]
    experts = router_weight.shape[1]
    capacity = tokens // experts
    slots = experts * capacity
    step = 2 * PATCHES
    parts = 2
    part_rows = tokens // parts
    part_steps = part_rows // step
    two = planes == 2
    pairs = 2 if two else 1
    plane = lax.axis_index("tensor").astype(jnp.int32).reshape(1)

    def swap(value):
        return lax.ppermute(value, "tensor", [(0, 1), (1, 0)])

    def summands(value):
        if two:
            return [value, swap(value)]
        return [lax.psum(value.astype(F32), "tensor").astype(BF16)]

    def row(vector):
        return vector.reshape(1, -1)

    pre_gain, pre_shift, proj_bias = row(pre_gain), row(pre_shift), row(proj_bias)
    mid_gain, mid_shift, hidden_bias = row(mid_gain), row(mid_shift), row(hidden_bias)
    output_bias, moe_gain, moe_shift = row(output_bias), row(moe_gain), row(moe_shift)
    weight_qkv = qkv_weight.reshape(model, 3 * width)
    qkv_bias = jnp.concatenate([qv_bias[0], jnp.zeros_like(qv_bias[0]), qv_bias[1]]).reshape(1, 3 * width)
    if two:
        projections = [proj_weight, swap(proj_weight)]
    else:
        projections = [lax.all_gather(proj_weight, "tensor", axis=0, tiled=True)]

    targets, marks = slot_targets(expert_ids, priority[0], capacity)
    targets_by_token, marks = targets.T, marks.T
    upstream_rows = call(
        functools.partial(place, 1), slots // step,
        [(targets, None, 0), (cotangent, None, 0)],
        [((slots, model), BF16, step)], "place_cotangent",
    )[0]

    def to_experts(rows):
        grouped = rows.reshape(experts, capacity, rows.shape[1])
        return lax.all_to_all(grouped, "wide", split_axis=0, concat_axis=0, tiled=True).reshape(rows.shape)

    tokens_in, upstream_rows = lax.optimization_barrier((tokens_in, upstream_rows))
    upstream = to_experts(upstream_rows)

    qkv, firsts, seconds, lowered, routes, gates = [], [], [], [], [], []
    contexts = []
    for part in range(parts):
        first_step = part * part_steps
        qkv_part, context = call(
            functools.partial(attend, heads), part_steps,
            [(tokens_in, step, first_step), (pre_gain, None, 0), (pre_shift, None, 0), (weight_qkv, None, 0), (qkv_bias, None, 0)],
            [((part_rows, 3 * width), BF16, step), ((part_rows, width), BF16, step)], "attend",
        )
        qkv.append(qkv_part)
        contexts.append(context)
    gathered = [
        [context, swap(context)] if two else [lax.all_gather(context, "tensor", axis=1, tiled=True)]
        for context in contexts
    ]
    partials = []
    for part in range(parts):
        first_step = part * part_steps
        first, partial = call(
            functools.partial(feed, pairs), part_steps,
            [(tokens_in, step, first_step), (proj_bias, None, 0), (mid_gain, None, 0), (mid_shift, None, 0),
             (hidden_weight, None, 0), (hidden_bias, None, 0), (output_weight, None, 0)]
            + [(context, step, 0) for context in gathered[part]]
            + [(projection, None, 0) for projection in projections],
            [((part_rows, model), F32, step), ((part_rows, model), BF16, step)], "feed",
        )
        firsts.append(first)
        partials.append(summands(partial))
    for part in range(parts):
        first_step = part * part_steps
        second, low, route, gate = call(
            functools.partial(router, pairs), part_steps,
            [(firsts[part], step, 0), (output_bias, None, 0), (moe_gain, None, 0), (moe_shift, None, 0),
             (router_weight, None, 0), (marks, step, first_step)]
            + [(partial, step, 0) for partial in partials[part]],
            [((part_rows, model), F32, step), ((part_rows, model), BF16, step),
             ((part_rows, experts), F32, step), ((part_rows, 2), F32, step)], "router",
        )
        seconds.append(second)
        lowered.append(low)
        routes.append(route)
        gates.append(gate)

    buffers, slot_gates = call(
        functools.partial(place_gated, parts), slots // step,
        [(targets, None, 0)] + [(low, None, 0) for low in lowered] + [(gate, None, 0) for gate in gates],
        [((slots, model), BF16, step), ((slots, 1), F32, step)], "place_tokens",
    )
    arrived = to_experts(buffers)
    arrived_gates = lax.all_to_all(
        slot_gates.reshape(experts, capacity), "wide", split_axis=0, concat_axis=0, tiled=True
    ).reshape(slots, 1)
    result, arrived_grad, gate_grad, expert_act, expert_inner_grad, slot_grad = call(
        expert, slots // step,
        [(plane, "scalar", 0), (arrived, step, 0), (upstream, step, 0), (arrived_gates, step, 0),
         (expert_in[0], None, 0), (expert_in_bias, None, 0), (expert_out[0], None, 0), (expert_out_bias, None, 0)],
        [((slots, model), BF16, step), ((slots, model), BF16, step), ((slots, 1), F32, step),
         ((slots, hidden), BF16, step), ((slots, hidden), BF16, step), ((slots, model), BF16, step)], "expert",
    )

    def home(partial, bias):
        if not two:
            rows = lax.psum(partial.astype(F32), "tensor")
            if bias is not None:
                rows = rows + bias
            return [to_experts(rows.astype(BF16))]
        half = model // 2
        low, high = partial[:, :half], partial[:, half:]
        flipped = plane[0] != 0
        kept = jnp.where(flipped, high, low)
        other = swap(jnp.where(flipped, low, high))
        rows = kept.astype(F32) + other.astype(F32)
        if bias is not None:
            rows = rows + jnp.where(flipped, bias[:, half:], bias[:, :half])
        own = to_experts(rows.astype(BF16))
        return [own, swap(own)]

    row_pieces = home(arrived_grad, None)
    gate_home = lax.all_to_all(
        gate_grad.reshape(experts, capacity), "wide", split_axis=0, concat_axis=0, tiled=True
    ).reshape(1, slots)
    gate_home = lax.psum(gate_home, "tensor") if not two else gate_home + swap(gate_home)
    second_grads, lowered_seconds = [], []
    moe_sums, router_sums = [], []
    for part in range(parts):
        first_step = part * part_steps
        grad, low, sums, router_sum = call(
            functools.partial(settle, pairs), part_steps,
            [(plane, "scalar", 0), (seconds[part], step, 0), (cotangent, step, first_step), (routes[part], step, 0),
             (moe_gain, None, 0), (moe_shift, None, 0), (router_weight, None, 0),
             (marks, step, first_step), (targets_by_token, step, first_step), (gate_home, None, 0)]
            + [(piece, None, 0) for piece in row_pieces],
            [((part_rows, model), F32, step), ((part_rows, model), BF16, step), ((8, model), F32, None),
             ((experts, model), F32, None)], "settle",
        )
        second_grads.append(grad)
        lowered_seconds.append(low)
        moe_sums.append(sums)
        router_sums.append(router_sum)
    acts, inner_grads, lowered_mids, mid_parts, hidden_sums = [], [], [], [], []
    for part in range(parts):
        act, inner_grad, low, partial, sums = call(
            feed_back, part_steps,
            [(firsts[part], step, 0), (lowered_seconds[part], step, 0), (mid_gain, None, 0), (mid_shift, None, 0),
             (hidden_weight, None, 0), (hidden_bias, None, 0), (output_weight, None, 0)],
            [((part_rows, hidden), BF16, step), ((part_rows, hidden), BF16, step), ((part_rows, model), BF16, step),
             ((part_rows, model), BF16, step), ((8, hidden), F32, None)], "feed_back",
        )
        acts.append(act)
        inner_grads.append(inner_grad)
        lowered_mids.append(low)
        mid_parts.append(summands(partial))
        hidden_sums.append(sums)

    def weight_grad(lefts, rights):
        return sum(dot_columns(left, right) for left, right in zip(lefts, rights))

    output_weight_grad = weight_grad(acts, lowered_seconds)
    hidden_weight_grad = weight_grad(lowered_mids, inner_grads)
    first_grads, branch_grads, qkv_grads, lowered_pres, pre_parts, mid_sums, qkv_sums = [], [], [], [], [], [], []
    for part in range(parts):
        first_step = part * part_steps
        first_grad, branch, qkv_grad, low, partial, sums, qkv_sum = call(
            functools.partial(attend_back, pairs, heads), part_steps,
            [(firsts[part], step, 0), (second_grads[part], step, 0), (mid_gain, None, 0), (proj_weight, None, 0),
             (qkv[part], step, 0), (weight_qkv, None, 0), (tokens_in, step, first_step),
             (pre_gain, None, 0), (pre_shift, None, 0)]
            + [(partial, step, 0) for partial in mid_parts[part]],
            [((part_rows, model), F32, step), ((part_rows, model), BF16, step), ((part_rows, 3 * width), BF16, step),
             ((part_rows, model), BF16, step), ((part_rows, model), BF16, step), ((8, model), F32, None),
             ((8, 3 * width), F32, None)], "attend_back",
        )
        first_grads.append(first_grad)
        branch_grads.append(branch)
        qkv_grads.append(qkv_grad)
        lowered_pres.append(low)
        pre_parts.append(summands(partial))
        mid_sums.append(sums)
        qkv_sums.append(qkv_sum)
    token_grads, pre_sums = [], []
    for part in range(parts):
        first_step = part * part_steps
        grad, sums = call(
            functools.partial(finish, pairs), part_steps,
            [(tokens_in, step, first_step), (pre_gain, None, 0), (first_grads[part], step, 0)]
            + [(partial, step, 0) for partial in pre_parts[part]],
            [((part_rows, model), F32, step), ((8, model), F32, None)], "finish",
        )
        token_grads.append(grad)
        pre_sums.append(sums)
    tokens_grad = jnp.concatenate(token_grads)

    result_pieces = home(result, expert_out_bias)
    outs = []
    for part in range(parts):
        first_step = part * part_steps
        outs.append(
            call(
                functools.partial(blend, pairs), part_steps,
                [(plane, "scalar", 0), (seconds[part], step, 0), (gates[part], step, 0), (targets_by_token, step, first_step)]
                + [(piece, None, 0) for piece in result_pieces],
                [((part_rows, model), BF16, step)], "blend",
            )[0]
        )
    block_out = jnp.concatenate(outs)

    expert_out_grad = dot_columns(expert_act, slot_grad)[None]
    expert_in_grad = dot_columns(arrived, expert_inner_grad)[None]
    expert_out_bias_grad = jnp.sum(slot_grad.astype(F32), axis=0, keepdims=True)
    expert_in_bias_grad = jnp.sum(expert_inner_grad.astype(F32), axis=0, keepdims=True)

    lanes = 3 * width
    layout = [(0, 1), (0, 1, 2), (0, 1, 2), (0,), (0,), tuple(range(experts))]
    groups = [pre_sums, mid_sums, moe_sums, hidden_sums, qkv_sums, router_sums]
    vector_shapes = [(max(8, len(rows)), group[0].shape[1]) for rows, group in zip(layout, groups)]
    if two:
        steps = wide.bit_length() - 1
        near, far = tuple(range(steps)), (0,) + tuple(range(2, steps)) + (1,)
        shapes = [(model, lanes // 2), (model, lanes // 2), (width, model), (16 * wide, 128)]
        qkv_weight_g, proj_weight_g, pre, mid, moe, hid, qks, router_g = pl.pallas_call(
            functools.partial(last_sums, wide, parts, layout, (near, far, near, far)),
            out_shape=[jax.ShapeDtypeStruct(shape, F32) for shape in [(model, lanes), (width, model)] + vector_shapes],
            in_specs=[pl.BlockSpec(memory_space=pltpu.VMEM)] * (parts * (4 + len(groups))),
            out_specs=[pl.BlockSpec(memory_space=pltpu.VMEM)] * (2 + len(groups)),
            scratch_shapes=[pltpu.VMEM(shape, F32) for shape in shapes] + fold_scratch(shapes, steps),
            compiler_params=pltpu.CompilerParams(
                vmem_limit_bytes=VMEM_BYTES, collective_id=1, has_side_effects=True
            ),
            name="last_sums",
        )(*lowered_pres, *qkv_grads, *contexts, *branch_grads, *[part for group in groups for part in group])
    else:
        sums = [sum(group) for group in groups]
        terms = [weight_grad(lowered_pres, qkv_grads), weight_grad(contexts, branch_grads)] + sums
        qkv_weight_g, proj_weight_g, pre, mid, moe, hid, qks, router_g = (
            lax.psum(term.astype(BF16), "wide").astype(F32) for term in terms
        )
    qks, router_g = qks[0].reshape(3, width), router_g[:experts]

    def over_wide(value):
        return lax.psum(value.astype(BF16), "wide").astype(F32)

    return (
        block_out,
        tokens_grad,
        pre[0],
        pre[1],
        qkv_weight_g.reshape(model, 3, width),
        jnp.stack([qks[0], qks[2]]),
        proj_weight_g,
        mid[2],
        mid[0],
        mid[1],
        over_wide(hidden_weight_grad),
        hid[0],
        over_wide(output_weight_grad),
        moe[2],
        moe[0],
        moe[1],
        router_g.T,
        expert_in_grad,
        expert_in_bias_grad,
        expert_out_grad,
        expert_out_bias_grad,
    )


def solution(mesh):
    return jax.shard_map(
        functools.partial(shards, mesh.shape["wide"], mesh.shape["tensor"]),
        mesh=mesh,
        in_specs=(
            P("wide", None), P(), P(), P(None, None, "tensor"), P(None, "tensor"), P("tensor", None), P(), P(), P(),
            P(None, "tensor"), P("tensor"), P("tensor", None), P(), P(), P(), P(),
            P("wide", None, "tensor"), P("wide", "tensor"), P("wide", "tensor", None), P("wide", None),
            P("wide", None), P("wide", None), P("wide", None),
        ),
        out_specs=(
            P("wide", None), P("wide", None), P(), P(), P(None, None, "tensor"), P(None, "tensor"), P("tensor", None),
            P(), P(), P(), P(None, "tensor"), P("tensor"), P("tensor", None), P(), P(), P(), P(),
            P("wide", None, "tensor"), P("wide", "tensor"), P("wide", "tensor", None), P("wide", None),
        ),
        check_vma=False,
    )
```

```python
import functools

import jax
import jax.numpy as jnp
from jax import lax
from jax.experimental import pallas as pl
from jax.experimental.pallas import tpu as pltpu
from jax.sharding import PartitionSpec as P

HEAD_DIM = 64
PATCHES = 144
BF16 = jnp.bfloat16
F32 = jnp.float32
HIGHEST = lax.Precision.HIGHEST
VMEM_BYTES = 48 * 1024 * 1024
BIG_VMEM_BYTES = 60 * 1024 * 1024


def dot(left, right):
    return jnp.dot(left, right, preferred_element_type=F32)


def dot_rows(left, right):
    return lax.dot_general(left, right, (((1,), (1,)), ((), ())), preferred_element_type=F32)


def dot_columns(left, right, precision=None):
    return lax.dot_general(
        left, right, (((0,), (0,)), ((), ())), precision=precision, preferred_element_type=F32
    )


def normalized(values):
    centered = values - jnp.mean(values, axis=-1, keepdims=True)
    variance = jnp.mean(centered * centered, axis=-1, keepdims=True)
    scale = lax.rsqrt(variance + 1e-06)
    return centered * scale, scale


def norm_back(rows, scale, gain, upstream):
    scaled = upstream * gain
    inward = jnp.mean(scaled, axis=-1, keepdims=True)
    along = jnp.mean(scaled * rows, axis=-1, keepdims=True)
    return scale * (scaled - inward - rows * along)


def gelu_parts(inner):
    square = inner * inner
    bend = jnp.tanh(0.7978845608028654 * inner * (1.0 + 0.044715 * square))
    half = 0.5 * (1.0 + bend)
    slope = half + (0.5 * 0.7978845608028654) * inner * (1.0 - bend * bend) * (
        1.0 + 0.134145 * square
    )
    return inner * half, slope


def gelu(inner):
    return inner * (0.5 * (1.0 + jnp.tanh(0.7978845608028654 * inner * (1.0 + 0.044715 * inner * inner))))


def softmax_rows(scores, scale):
    peak = jnp.max(scores, axis=-1, keepdims=True)
    weights = jnp.exp((scores - peak) * scale)
    return weights * (1.0 / jnp.sum(weights, axis=-1, keepdims=True))


def call(kernel, steps, ins, outs, name):
    def spec(shape, rows, first):
        if rows is None:
            return pl.BlockSpec(shape, lambda i: (0,) * len(shape))
        return pl.BlockSpec((rows,) + tuple(shape[1:]), lambda i: (i + first,) + (0,) * (len(shape) - 1))

    in_specs = []
    for array, rows, first in ins:
        if rows == "scalar":
            in_specs.append(pl.BlockSpec(memory_space=pltpu.SMEM))
        else:
            in_specs.append(spec(array.shape, rows, first))
    return pl.pallas_call(
        kernel,
        grid=(steps,),
        in_specs=in_specs,
        out_specs=[spec(shape, rows, 0) for shape, _, rows in outs],
        out_shape=[jax.ShapeDtypeStruct(shape, dtype) for shape, dtype, _ in outs],
        compiler_params=pltpu.CompilerParams(vmem_limit_bytes=VMEM_BYTES),
        name=name,
    )(*[array for array, _, _ in ins])


def attend(heads, tokens, gain, shift, weight, bias, qkv_out, context_out):
    rows, _ = normalized(tokens[...].astype(F32))
    lowered = (rows * gain[...] + shift[...]).astype(BF16)
    qkv = (dot(lowered, weight[...]) + bias[...]).astype(BF16)
    qkv_out[...] = qkv
    width = heads * HEAD_DIM
    for image in range(qkv.shape[0] // PATCHES):
        block = qkv[image * PATCHES : (image + 1) * PATCHES]
        parts = []
        for head in range(heads):
            at = head * HEAD_DIM
            query = block[:, at : at + HEAD_DIM]
            keys = block[:, width + at : width + at + HEAD_DIM]
            values = block[:, 2 * width + at : 2 * width + at + HEAD_DIM]
            probs = softmax_rows(dot_rows(query, keys), HEAD_DIM**-0.5)
            parts.append(dot(probs.astype(BF16), values))
        context = jnp.concatenate(parts, axis=1).astype(BF16)
        context_out[image * PATCHES : (image + 1) * PATCHES, :] = context


def feed(
    pairs, tokens, proj_bias, gain, shift, hidden, hidden_bias, output, *rest
):
    contexts, projections = rest[:pairs], rest[pairs : 2 * pairs]
    first_out, partial_out = rest[2 * pairs :]
    branch = dot(contexts[0][...], projections[0][...])
    if pairs == 2:
        branch = branch + dot(contexts[1][...], projections[1][...])
    first = tokens[...].astype(F32) + branch + proj_bias[...]
    first_out[...] = first
    rows, _ = normalized(first)
    lowered = (rows * gain[...] + shift[...]).astype(BF16)
    activated = gelu(dot(lowered, hidden[...]) + hidden_bias[...]).astype(BF16)
    partial_out[...] = dot(activated, output[...]).astype(BF16)


def total(parts):
    value = parts[0][...].astype(F32)
    for part in parts[1:]:
        value = value + part[...].astype(F32)
    return value


def router(pairs, first, bias, gain, shift, weight, marks, *rest):
    second_out, lowered_out, route_out, gates_out = rest[pairs:]
    second = first[...] + total(rest[:pairs]) + bias[...]
    second_out[...] = second
    rows, _ = normalized(second)
    normed = rows * gain[...] + shift[...]
    lowered_out[...] = normed.astype(BF16)
    logits = jnp.dot(normed, weight[...], precision=HIGHEST, preferred_element_type=F32)
    grown = jnp.exp(logits - jnp.max(logits, axis=-1, keepdims=True))
    route = grown / jnp.sum(grown, axis=-1, keepdims=True)
    route_out[...] = route
    expert = lax.broadcasted_iota(jnp.int32, route.shape, 1)
    gates = [
        jnp.sum(jnp.where(expert == marks[:, j : j + 1], route, 0.0), axis=1, keepdims=True)
        for j in range(2)
    ]
    gates_out[...] = jnp.concatenate(gates, axis=1)


def slot_hits(targets, rows):
    first = pl.program_id(0) * rows
    slot = first + lax.broadcasted_iota(jnp.int32, (rows, targets.shape[1]), 0)
    return [slot == targets[j : j + 1, :] for j in range(2)]


def thirds(values):
    high = values.astype(BF16)
    rest = values - high.astype(F32)
    middle = rest.astype(BF16)
    low = (rest - middle.astype(F32)).astype(BF16)
    return high, middle, low


def place(parts, targets, *rest):
    sources, out = rest[:parts], rest[parts]
    hits = slot_hits(targets, out.shape[0])
    table = (hits[0] | hits[1]).astype(BF16)
    rows = jnp.zeros(out.shape, F32)
    at = 0
    for source in sources:
        rows = rows + dot(table[:, at : at + source.shape[0]], source[...].astype(BF16))
        at += source.shape[0]
    out[...] = rows.astype(BF16)


def place_gated(parts, targets, *rest):
    sources, gates, out, gates_out = rest[:parts], rest[parts : 2 * parts], rest[2 * parts], rest[2 * parts + 1]
    hits = slot_hits(targets, out.shape[0])
    table = (hits[0] | hits[1]).astype(BF16)
    tables = [hit.astype(BF16) for hit in hits]
    rows = jnp.zeros(out.shape, F32)
    slot_gates = jnp.zeros(gates_out.shape, F32)
    at = 0
    for source, gate in zip(sources, gates):
        end = at + source.shape[0]
        rows = rows + dot(table[:, at:end], source[...])
        for j in range(2):
            terms = jnp.concatenate(thirds(gate[:, j : j + 1]), axis=1)
            slot_gates = slot_gates + jnp.sum(dot(tables[j][:, at:end], terms), axis=1, keepdims=True)
        at = end
    out[...] = rows.astype(BF16)
    gates_out[...] = slot_gates


def expert(
    plane, arrived, upstream, gates, weight_in, bias_in, weight_out, bias_out,
    result_out, grad_out, gate_out, act_out, inner_out, slot_out,
):
    rows = arrived[...]
    inner = dot(rows, weight_in[...]) + bias_in[...]
    act, slope = gelu_parts(inner)
    act = act.astype(BF16)
    act_out[...] = act
    result = dot(act, weight_out[...])
    result_out[...] = result.astype(BF16)
    raised = upstream[...].astype(F32)
    once = jnp.where(plane[0] == 0, 1.0, 0.0)
    gate_out[...] = jnp.sum(raised * (result + bias_out[...] * once), axis=1, keepdims=True)
    slot_grad = (raised * gates[...]).astype(BF16)
    slot_out[...] = slot_grad
    inner_grad = (dot_rows(slot_grad, weight_out[...]) * slope).astype(BF16)
    inner_out[...] = inner_grad
    grad_out[...] = dot_rows(inner_grad, weight_in[...]).astype(BF16)


def token_hits(targets, slots):
    slot = lax.broadcasted_iota(jnp.int32, (targets.shape[0], slots), 1)
    return [slot == targets[:, j : j + 1] for j in range(2)]


def ordered(plane, parts):
    if len(parts) == 1:
        return parts[0]
    own, peer = parts
    flipped = plane[0] != 0
    return jnp.concatenate([jnp.where(flipped, peer, own), jnp.where(flipped, own, peer)], axis=1)


def settle(
    pairs, plane, second, cotangent, route, gain, shift, router_weight, marks, targets, slot_grads, *rest
):
    pieces = rest[:pairs]
    second_out, lowered_out, sums_out, router_out = rest[pairs:]

    @pl.when(pl.program_id(0) == 0)
    def _():
        sums_out[...] = jnp.zeros_like(sums_out)
        router_out[...] = jnp.zeros_like(router_out)

    hits = token_hits(targets, slot_grads.shape[1])
    table = (hits[0] | hits[1]).astype(BF16)
    moe_grad = ordered(plane, [dot(table, piece[...]) for piece in pieces])
    chances = route[...]
    number = lax.broadcasted_iota(jnp.int32, chances.shape, 1)
    route_grad = jnp.zeros_like(chances)
    for j in range(2):
        gate_grad = jnp.sum(jnp.where(hits[j], slot_grads[...], 0.0), axis=1, keepdims=True)
        route_grad = route_grad + jnp.where(number == marks[:, j : j + 1], gate_grad, 0.0)
    logit_grad = chances * (route_grad - jnp.sum(chances * route_grad, axis=1, keepdims=True))
    rows, scale = normalized(second[...])
    normed = rows * gain[...] + shift[...]
    router_out[...] += dot_columns(logit_grad, normed, HIGHEST)
    moe_grad = moe_grad + lax.dot_general(
        logit_grad, router_weight[...], (((1,), (1,)), ((), ())), precision=HIGHEST, preferred_element_type=F32
    )
    grad = cotangent[...] + norm_back(rows, scale, gain[...], moe_grad)
    second_out[...] = grad
    lowered_out[...] = grad.astype(BF16)
    sums_out[0:1, :] += jnp.sum(moe_grad * rows, axis=0, keepdims=True)
    sums_out[1:2, :] += jnp.sum(moe_grad, axis=0, keepdims=True)
    sums_out[2:3, :] += jnp.sum(grad, axis=0, keepdims=True)


def feed_back(
    first, second_grad, gain, shift, hidden, hidden_bias, output,
    act_out, inner_out, lowered_out, partial_out, sums_out,
):
    @pl.when(pl.program_id(0) == 0)
    def _():
        sums_out[...] = jnp.zeros_like(sums_out)

    rows, _ = normalized(first[...])
    lowered = (rows * gain[...] + shift[...]).astype(BF16)
    lowered_out[...] = lowered
    act, slope = gelu_parts(dot(lowered, hidden[...]) + hidden_bias[...])
    act_out[...] = act.astype(BF16)
    inner_grad = (dot_rows(second_grad[...], output[...]) * slope).astype(BF16)
    inner_out[...] = inner_grad
    partial_out[...] = dot_rows(inner_grad, hidden[...]).astype(BF16)
    sums_out[0:1, :] += jnp.sum(inner_grad.astype(F32), axis=0, keepdims=True)


def attend_back(
    pairs, heads, first, second_grad, gain, projection, qkv, weight, tokens, pre_gain, pre_shift, *rest
):
    first_out, branch_out, qkv_out, lowered_out, partial_out, sums_out, qkv_sums_out = rest[pairs:]

    @pl.when(pl.program_id(0) == 0)
    def _():
        sums_out[...] = jnp.zeros_like(sums_out)
        qkv_sums_out[...] = jnp.zeros_like(qkv_sums_out)

    mid_grad = total(rest[:pairs])
    rows, scale = normalized(first[...])
    first_grad = second_grad[...] + norm_back(rows, scale, gain[...], mid_grad)
    first_out[...] = first_grad
    branch = first_grad.astype(BF16)
    branch_out[...] = branch
    sums_out[0:1, :] += jnp.sum(mid_grad * rows, axis=0, keepdims=True)
    sums_out[1:2, :] += jnp.sum(mid_grad, axis=0, keepdims=True)
    sums_out[2:3, :] += jnp.sum(first_grad, axis=0, keepdims=True)
    rows, _ = normalized(tokens[...].astype(F32))
    lowered_out[...] = (rows * pre_gain[...] + pre_shift[...]).astype(BF16)
    context_grad = dot_rows(branch, projection[...]).astype(BF16)
    width = heads * HEAD_DIM
    scale = HEAD_DIM**-0.5
    for image in range(qkv.shape[0] // PATCHES):
        at = image * PATCHES
        block = qkv[at : at + PATCHES, :]
        grad = context_grad[at : at + PATCHES]
        parts = [[], [], []]
        for head in range(heads):
            h = head * HEAD_DIM
            query = block[:, h : h + HEAD_DIM]
            keys = block[:, width + h : width + h + HEAD_DIM]
            values = block[:, 2 * width + h : 2 * width + h + HEAD_DIM]
            upstream = grad[:, h : h + HEAD_DIM]
            probs = softmax_rows(dot_rows(query, keys), scale)
            prob_grad = dot_rows(upstream, values)
            inward = jnp.sum(probs * prob_grad, axis=-1, keepdims=True)
            score_grad = (probs * (prob_grad - inward)).astype(BF16)
            parts[0].append(dot(score_grad, keys) * scale)
            parts[1].append(dot_columns(score_grad, query) * scale)
            parts[2].append(dot_columns(probs.astype(BF16), upstream))
        qkv_grad = jnp.concatenate(parts[0] + parts[1] + parts[2], axis=1).astype(BF16)
        qkv_out[at : at + PATCHES, :] = qkv_grad
        partial_out[at : at + PATCHES, :] = dot_rows(qkv_grad, weight[...]).astype(BF16)
        qkv_sums_out[0:1, :] += jnp.sum(qkv_grad.astype(F32), axis=0, keepdims=True)


def finish(pairs, tokens, gain, first_grad, *rest):
    grad_out, sums_out = rest[pairs:]

    @pl.when(pl.program_id(0) == 0)
    def _():
        sums_out[...] = jnp.zeros_like(sums_out)

    upstream = total(rest[:pairs])
    rows, scale = normalized(tokens[...].astype(F32))
    grad_out[...] = first_grad[...] + norm_back(rows, scale, gain[...], upstream)
    sums_out[0:1, :] += jnp.sum(upstream * rows, axis=0, keepdims=True)
    sums_out[1:2, :] += jnp.sum(upstream, axis=0, keepdims=True)


def blend(pairs, plane, second, gates, targets, *rest):
    pieces, out = rest[:pairs], rest[pairs]
    slots = pieces[0].shape[0]
    mixture = jnp.zeros(out.shape, F32)
    for j, hit in enumerate(token_hits(targets, slots)):
        table = hit.astype(BF16)
        picked = ordered(plane, [dot(table, piece[...]) for piece in pieces])
        mixture = mixture + gates[:, j : j + 1] * picked
    out[...] = (second[...] + mixture).astype(BF16)


def slot_targets(choice_ids, ranks, capacity):
    count = choice_ids.shape[0]
    order_keys = jnp.concatenate([ranks, ranks + count])
    flat_ids = jnp.concatenate([choice_ids[:, 0], choice_ids[:, 1]])
    earlier = (order_keys[None, :] < order_keys[:, None]) & (flat_ids[None, :] == flat_ids[:, None])
    position = jnp.sum(earlier.astype(jnp.int32), axis=1).reshape(2, count)
    kept = position < capacity
    targets = jnp.where(kept, choice_ids.T * capacity + position, -1)
    marks = jnp.where(kept, choice_ids.T, -1)
    return targets, marks


MESH = pl.DeviceIdType.MESH


def bits_of(index, wide):
    return [lax.rem(lax.div(index, 1 << k), 2) for k in range(wide.bit_length() - 1)]


class Sums:
    def __init__(self, wide, orders, totals, sends, lands, gathers, send_sems, recv_sems):
        me, self.plane = lax.axis_index("wide"), lax.axis_index("tensor")
        self.bits = bits_of(me, wide)
        self.partners = [me + (1 - 2 * bit) * (1 << k) for k, bit in enumerate(self.bits)]
        self.steps = len(self.bits)
        self.orders, self.totals, self.sends, self.lands, self.gathers = orders, totals, sends, lands, gathers
        self.send_sems, self.recv_sems = send_sems, recv_sems

    def piece(self, i, step):
        rows = self.gathers[i].shape[0]
        base = 0
        for s in range(step):
            base = base + self.bits[self.orders[i][s]] * (rows >> (s + 1))
        length = rows >> (step + 1)
        bit = self.bits[self.orders[i][step]]
        return pl.multiple_of(base + bit * length, 16), pl.multiple_of(base + (1 - bit) * length, 16), length

    def staged(self, i, step):
        rows = self.gathers[i].shape[0]
        return rows - (rows >> step)

    def transfer(self, i, k):
        step = k if k < self.steps else 2 * self.steps - 1 - k
        kept, _, length = self.piece(i, step)
        if k < self.steps:
            at = self.staged(i, step)
            source, target = self.sends[i].at[pl.ds(at, length)], self.lands[i].at[pl.ds(at, length)]
        else:
            source = target = self.gathers[i].at[pl.ds(kept, length)]
        return pltpu.make_async_remote_copy(
            source, target, self.send_sems.at[i, k], self.recv_sems.at[i, k],
            device_id=(self.partners[self.orders[i][step]], self.plane), device_id_type=MESH,
        )

    def begin(self, i, k):
        if k < self.steps:
            _, other, length = self.piece(i, k)
            at = self.staged(i, k)
            self.sends[i][at : at + length, :] = self.totals[i][pl.ds(other, length), :].astype(BF16)
        self.transfer(i, k).start()

    def advance(self, i, k):
        self.transfer(i, k).wait()
        if k < self.steps:
            kept, _, length = self.piece(i, k)
            at = self.staged(i, k)
            value = self.totals[i][pl.ds(kept, length), :] + self.lands[i][at : at + length, :].astype(F32)
            if k + 1 < self.steps:
                self.totals[i][pl.ds(kept, length), :] = value
            else:
                self.gathers[i][pl.ds(kept, length), :] = value.astype(BF16)
        if k + 1 < 2 * self.steps:
            self.begin(i, k + 1)


def greet(wide):
    me, plane = lax.axis_index("wide"), lax.axis_index("tensor")
    barrier = pltpu.get_barrier_semaphore()
    bits = bits_of(me, wide)
    for k, bit in enumerate(bits):
        pl.semaphore_signal(
            barrier, inc=1, device_id=(me + (1 - 2 * bit) * (1 << k), plane), device_id_type=MESH
        )
    pl.semaphore_signal(barrier, inc=1, device_id=(me, 1 - plane), device_id_type=MESH)
    pl.semaphore_wait(barrier, len(bits) + 1)


def put_row(small, at, row):
    for c in range(row.shape[1] // 128):
        small[at + c : at + c + 1, :] = row[:, 128 * c : 128 * (c + 1)]
    return at + row.shape[1] // 128


def get_row(small, at, width):
    return jnp.concatenate([small[at + c : at + c + 1, :] for c in range(width // 128)], axis=1)


def image_back(heads, qkv, context_grad):
    width = heads * HEAD_DIM
    scale = HEAD_DIM**-0.5
    parts = [[], [], []]
    for head in range(heads):
        h = head * HEAD_DIM
        query = qkv[:, h : h + HEAD_DIM]
        keys = qkv[:, width + h : width + h + HEAD_DIM]
        values = qkv[:, 2 * width + h : 2 * width + h + HEAD_DIM]
        upstream = context_grad[:, h : h + HEAD_DIM]
        probs = softmax_rows(dot_rows(query, keys), scale)
        prob_grad = dot_rows(upstream, values)
        inward = jnp.sum(probs * prob_grad, axis=-1, keepdims=True)
        score_grad = (probs * (prob_grad - inward)).astype(BF16)
        parts[0].append(dot(score_grad, keys) * scale)
        parts[1].append(dot_columns(score_grad, query) * scale)
        parts[2].append(dot_columns(probs.astype(BF16), upstream))
    return jnp.concatenate(parts[0] + parts[1] + parts[2], axis=1).astype(BF16)


def column_dots(left, right, put, tile=256):
    def body(i, carry):
        at = pl.multiple_of(i * tile, tile)
        put(at, tile, dot_columns(left[:, pl.ds(at, tile)], right[...]))
        return carry

    lax.fori_loop(0, left.shape[1] // tile, body, 0)


def backward(
    wide, heads, layout, orders, rows,
    second_grad, first, tokens, qkv, context, mid_gain, mid_shift, pre_gain, pre_shift,
    hidden, hidden_bias, output, projection, weight_qkv, moe_sums, router_sums,
    grad_out, hidden_out, output_out, left_out, right_out, proj_out, *rest,
):
    vectors_out, rest = rest[: len(layout)], rest[len(layout) :]
    (lowered_mid, act, inner_grad, mid_own, mid_peer, branch, qkv_grad, lowered_pre, pre_own, pre_peer,
     mid_sums, hidden_sums, qkv_sums, pre_sums, small_sums) = rest[:15]
    totals, sends, lands = rest[15:21], rest[21:27], rest[27:33]
    mid_sems, pre_sems, send_sems, recv_sems = rest[33:]
    gathers = (hidden_out, output_out, left_out, right_out, proj_out, small_sums)
    me, plane = lax.axis_index("wide"), lax.axis_index("tensor")
    chunks = tokens.shape[0] // rows
    greet(wide)
    sums = Sums(wide, orders, totals, sends, lands, gathers, send_sems, recv_sems)

    def across(own, peer, sems, chunk):
        at = pl.multiple_of(chunk * rows, rows)
        return pltpu.make_async_remote_copy(
            own.at[pl.ds(at, rows)], peer.at[pl.ds(at, rows)], sems.at[0, chunk], sems.at[1, chunk],
            device_id=(me, 1 - plane), device_id_type=MESH,
        )

    for vector in (mid_sums, hidden_sums, qkv_sums, pre_sums):
        vector[...] = jnp.zeros_like(vector)

    def feed_chunk(chunk, carry):
        here = pl.ds(pl.multiple_of(chunk * rows, rows), rows)
        normed, _ = normalized(first[here, :])
        lowered = (normed * mid_gain[...] + mid_shift[...]).astype(BF16)
        lowered_mid[here, :] = lowered
        acted, slope = gelu_parts(dot(lowered, hidden[...]) + hidden_bias[...])
        act[here, :] = acted.astype(BF16)
        upstream = second_grad[here, :].astype(BF16)
        branch[here, :] = upstream
        inward = (dot_rows(upstream, output[...]) * slope).astype(BF16)
        inner_grad[here, :] = inward
        hidden_sums[0:1, :] += jnp.sum(inward.astype(F32), axis=0, keepdims=True)
        mid_own[here, :] = dot_rows(inward, hidden[...]).astype(BF16)
        across(mid_own, mid_peer, mid_sems, chunk).start()
        return carry

    lax.fori_loop(0, chunks, feed_chunk, 0)

    def put_in(total):
        def put(at, tile, value):
            total[pl.ds(at, tile), :] = value

        return put

    column_dots(lowered_mid, inner_grad, put_in(totals[0]))
    sums.begin(0, 0)
    column_dots(act, branch, put_in(totals[1]))
    sums.begin(1, 0)

    def attend_chunk(chunk, carry):
        here = pl.ds(pl.multiple_of(chunk * rows, rows), rows)
        across(mid_own, mid_peer, mid_sems, chunk).wait()
        mid_grad = mid_own[here, :].astype(F32) + mid_peer[here, :].astype(F32)
        normed, scale = normalized(first[here, :])
        first_grad = second_grad[here, :] + norm_back(normed, scale, mid_gain[...], mid_grad)
        grad_out[here, :] = first_grad
        lowered_grad = first_grad.astype(BF16)
        branch[here, :] = lowered_grad
        mid_sums[0:1, :] += jnp.sum(mid_grad * normed, axis=0, keepdims=True)
        mid_sums[1:2, :] += jnp.sum(mid_grad, axis=0, keepdims=True)
        mid_sums[2:3, :] += jnp.sum(first_grad, axis=0, keepdims=True)
        normed, _ = normalized(tokens[here, :].astype(F32))
        lowered_pre[here, :] = (normed * pre_gain[...] + pre_shift[...]).astype(BF16)
        context_grad = dot_rows(lowered_grad, projection[...]).astype(BF16)
        for image in range(rows // PATCHES):
            at = pl.multiple_of(chunk * rows + image * PATCHES, PATCHES)
            block = qkv[pl.ds(at, PATCHES), :]
            grad = image_back(heads, block, context_grad[image * PATCHES : (image + 1) * PATCHES])
            qkv_grad[pl.ds(at, PATCHES), :] = grad
            pre_own[pl.ds(at, PATCHES), :] = dot_rows(grad, weight_qkv[...]).astype(BF16)
            qkv_sums[0:1, :] += jnp.sum(grad.astype(F32), axis=0, keepdims=True)
            for k in range(sums.steps):

                @pl.when(chunk == k)
                def _(i=image, k=k):
                    if i < 2:
                        sums.advance(i, k)

        across(pre_own, pre_peer, pre_sems, chunk).start()
        return carry

    lax.fori_loop(0, chunks, attend_chunk, 0)
    column_dots(context, branch, put_in(totals[4]))
    sums.begin(4, 0)

    def put_halves(at, tile, value):
        half = totals[2].shape[1]
        totals[2][pl.ds(at, tile), :] = value[:, :half]
        totals[3][pl.ds(at, tile), :] = value[:, half:]

    column_dots(lowered_pre, qkv_grad, put_halves)
    sums.begin(2, 0)
    sums.begin(3, 0)

    def finish_chunk(chunk, carry):
        here = pl.ds(pl.multiple_of(chunk * rows, rows), rows)
        across(pre_own, pre_peer, pre_sems, chunk).wait()
        upstream = pre_own[here, :].astype(F32) + pre_peer[here, :].astype(F32)
        normed, scale = normalized(tokens[here, :].astype(F32))
        grad_out[here, :] += norm_back(normed, scale, pre_gain[...], upstream)
        pre_sums[0:1, :] += jnp.sum(upstream * normed, axis=0, keepdims=True)
        pre_sums[1:2, :] += jnp.sum(upstream, axis=0, keepdims=True)
        return carry

    lax.fori_loop(0, chunks, finish_chunk, 0)
    small = totals[5]
    small[...] = jnp.zeros_like(small)
    at = 0
    for vector, picked in zip((pre_sums, mid_sums, moe_sums, hidden_sums, qkv_sums, router_sums), layout):
        for r in picked:
            at = put_row(small, at, vector[r : r + 1, :])
    sums.begin(5, 0)
    for k in range(2 * sums.steps):
        for i in (0, 1):
            if sums.steps + k < 2 * sums.steps:
                sums.advance(i, sums.steps + k)
        for i in (4, 2, 3, 5):
            sums.advance(i, k)
    at = 0
    for out, picked in zip(vectors_out, layout):
        for i in range(len(picked)):
            out[i : i + 1, :] = get_row(small_sums, at, out.shape[1]).astype(F32)
            at += out.shape[1] // 128


def shards(
    wide, planes,
    tokens_in, pre_gain, pre_shift, qkv_weight, qv_bias, proj_weight, proj_bias, mid_gain, mid_shift,
    hidden_weight, hidden_bias, output_weight, output_bias, moe_gain, moe_shift, router_weight,
    expert_in, expert_in_bias, expert_out, expert_out_bias, expert_ids, priority, cotangent,
):
    tokens, model = tokens_in.shape
    width = qkv_weight.shape[2]
    heads = width // HEAD_DIM
    hidden = hidden_weight.shape[1]
    experts = router_weight.shape[1]
    capacity = tokens // experts
    slots = experts * capacity
    step = 2 * PATCHES
    parts = 2
    part_rows = tokens // parts
    part_steps = part_rows // step
    two = planes == 2
    pairs = 2 if two else 1
    plane = lax.axis_index("tensor").astype(jnp.int32).reshape(1)

    def swap(value):
        return lax.ppermute(value, "tensor", [(0, 1), (1, 0)])

    def summands(value):
        if two:
            return [value, swap(value)]
        return [lax.psum(value.astype(F32), "tensor").astype(BF16)]

    def row(vector):
        return vector.reshape(1, -1)

    pre_gain, pre_shift, proj_bias = row(pre_gain), row(pre_shift), row(proj_bias)
    mid_gain, mid_shift, hidden_bias = row(mid_gain), row(mid_shift), row(hidden_bias)
    output_bias, moe_gain, moe_shift = row(output_bias), row(moe_gain), row(moe_shift)
    weight_qkv = qkv_weight.reshape(model, 3 * width)
    qkv_bias = jnp.concatenate([qv_bias[0], jnp.zeros_like(qv_bias[0]), qv_bias[1]]).reshape(1, 3 * width)
    if two:
        projections = [proj_weight, swap(proj_weight)]
    else:
        projections = [lax.all_gather(proj_weight, "tensor", axis=0, tiled=True)]

    targets, marks = slot_targets(expert_ids, priority[0], capacity)
    targets_by_token, marks = targets.T, marks.T
    upstream_rows = call(
        functools.partial(place, 1), slots // step,
        [(targets, None, 0), (cotangent, None, 0)],
        [((slots, model), BF16, step)], "place_cotangent",
    )[0]

    def to_experts(rows):
        grouped = rows.reshape(experts, capacity, rows.shape[1])
        return lax.all_to_all(grouped, "wide", split_axis=0, concat_axis=0, tiled=True).reshape(rows.shape)

    tokens_in, upstream_rows = lax.optimization_barrier((tokens_in, upstream_rows))
    upstream = to_experts(upstream_rows)

    qkv, firsts, seconds, lowered, routes, gates = [], [], [], [], [], []
    contexts = []
    for part in range(parts):
        first_step = part * part_steps
        qkv_part, context = call(
            functools.partial(attend, heads), part_steps,
            [(tokens_in, step, first_step), (pre_gain, None, 0), (pre_shift, None, 0), (weight_qkv, None, 0), (qkv_bias, None, 0)],
            [((part_rows, 3 * width), BF16, step), ((part_rows, width), BF16, step)], "attend",
        )
        qkv.append(qkv_part)
        contexts.append(context)
    gathered = [
        [context, swap(context)] if two else [lax.all_gather(context, "tensor", axis=1, tiled=True)]
        for context in contexts
    ]
    partials = []
    for part in range(parts):
        first_step = part * part_steps
        first, partial = call(
            functools.partial(feed, pairs), part_steps,
            [(tokens_in, step, first_step), (proj_bias, None, 0), (mid_gain, None, 0), (mid_shift, None, 0),
             (hidden_weight, None, 0), (hidden_bias, None, 0), (output_weight, None, 0)]
            + [(context, step, 0) for context in gathered[part]]
            + [(projection, None, 0) for projection in projections],
            [((part_rows, model), F32, step), ((part_rows, model), BF16, step)], "feed",
        )
        firsts.append(first)
        partials.append(summands(partial))
    for part in range(parts):
        first_step = part * part_steps
        second, low, route, gate = call(
            functools.partial(router, pairs), part_steps,
            [(firsts[part], step, 0), (output_bias, None, 0), (moe_gain, None, 0), (moe_shift, None, 0),
             (router_weight, None, 0), (marks, step, first_step)]
            + [(partial, step, 0) for partial in partials[part]],
            [((part_rows, model), F32, step), ((part_rows, model), BF16, step),
             ((part_rows, experts), F32, step), ((part_rows, 2), F32, step)], "router",
        )
        seconds.append(second)
        lowered.append(low)
        routes.append(route)
        gates.append(gate)

    buffers, slot_gates = call(
        functools.partial(place_gated, parts), slots // step,
        [(targets, None, 0)] + [(low, None, 0) for low in lowered] + [(gate, None, 0) for gate in gates],
        [((slots, model), BF16, step), ((slots, 1), F32, step)], "place_tokens",
    )
    arrived = to_experts(buffers)
    arrived_gates = lax.all_to_all(
        slot_gates.reshape(experts, capacity), "wide", split_axis=0, concat_axis=0, tiled=True
    ).reshape(slots, 1)
    result, arrived_grad, gate_grad, expert_act, expert_inner_grad, slot_grad = call(
        expert, slots // step,
        [(plane, "scalar", 0), (arrived, step, 0), (upstream, step, 0), (arrived_gates, step, 0),
         (expert_in[0], None, 0), (expert_in_bias, None, 0), (expert_out[0], None, 0), (expert_out_bias, None, 0)],
        [((slots, model), BF16, step), ((slots, model), BF16, step), ((slots, 1), F32, step),
         ((slots, hidden), BF16, step), ((slots, hidden), BF16, step), ((slots, model), BF16, step)], "expert",
    )

    def home(partial, bias):
        if not two:
            rows = lax.psum(partial.astype(F32), "tensor")
            if bias is not None:
                rows = rows + bias
            return [to_experts(rows.astype(BF16))]
        half = model // 2
        low, high = partial[:, :half], partial[:, half:]
        flipped = plane[0] != 0
        kept = jnp.where(flipped, high, low)
        other = swap(jnp.where(flipped, low, high))
        rows = kept.astype(F32) + other.astype(F32)
        if bias is not None:
            rows = rows + jnp.where(flipped, bias[:, half:], bias[:, :half])
        own = to_experts(rows.astype(BF16))
        return [own, swap(own)]

    row_pieces = home(arrived_grad, None)
    gate_home = lax.all_to_all(
        gate_grad.reshape(experts, capacity), "wide", split_axis=0, concat_axis=0, tiled=True
    ).reshape(1, slots)
    gate_home = lax.psum(gate_home, "tensor") if not two else gate_home + swap(gate_home)
    second_grads, lowered_seconds = [], []
    moe_sums, router_sums = [], []
    for part in range(parts):
        first_step = part * part_steps
        grad, low, sums, router_sum = call(
            functools.partial(settle, pairs), part_steps,
            [(plane, "scalar", 0), (seconds[part], step, 0), (cotangent, step, first_step), (routes[part], step, 0),
             (moe_gain, None, 0), (moe_shift, None, 0), (router_weight, None, 0),
             (marks, step, first_step), (targets_by_token, step, first_step), (gate_home, None, 0)]
            + [(piece, None, 0) for piece in row_pieces],
            [((part_rows, model), F32, step), ((part_rows, model), BF16, step), ((8, model), F32, None),
             ((experts, model), F32, None)], "settle",
        )
        second_grads.append(grad)
        lowered_seconds.append(low)
        moe_sums.append(sums)
        router_sums.append(router_sum)
    def over_wide(value):
        return lax.psum(value.astype(BF16), "wide").astype(F32)

    def plain_backward():
        acts, inner_grads, lowered_mids, mid_parts, hidden_sums = [], [], [], [], []
        for part in range(parts):
            act, inner_grad, low, partial, sums = call(
                feed_back, part_steps,
                [(firsts[part], step, 0), (lowered_seconds[part], step, 0), (mid_gain, None, 0), (mid_shift, None, 0),
                 (hidden_weight, None, 0), (hidden_bias, None, 0), (output_weight, None, 0)],
                [((part_rows, hidden), BF16, step), ((part_rows, hidden), BF16, step), ((part_rows, model), BF16, step),
                 ((part_rows, model), BF16, step), ((8, hidden), F32, None)], "feed_back",
            )
            acts.append(act)
            inner_grads.append(inner_grad)
            lowered_mids.append(low)
            mid_parts.append(summands(partial))
            hidden_sums.append(sums)

        def weight_grad(lefts, rights):
            return sum(dot_columns(left, right) for left, right in zip(lefts, rights))

        output_weight_grad = weight_grad(acts, lowered_seconds)
        hidden_weight_grad = weight_grad(lowered_mids, inner_grads)
        first_grads, branch_grads, qkv_grads, lowered_pres, pre_parts, mid_sums, qkv_sums = [], [], [], [], [], [], []
        for part in range(parts):
            first_step = part * part_steps
            first_grad, branch, qkv_grad, low, partial, sums, qkv_sum = call(
                functools.partial(attend_back, pairs, heads), part_steps,
                [(firsts[part], step, 0), (second_grads[part], step, 0), (mid_gain, None, 0), (proj_weight, None, 0),
                 (qkv[part], step, 0), (weight_qkv, None, 0), (tokens_in, step, first_step),
                 (pre_gain, None, 0), (pre_shift, None, 0)]
                + [(partial, step, 0) for partial in mid_parts[part]],
                [((part_rows, model), F32, step), ((part_rows, model), BF16, step), ((part_rows, 3 * width), BF16, step),
                 ((part_rows, model), BF16, step), ((part_rows, model), BF16, step), ((8, model), F32, None),
                 ((8, 3 * width), F32, None)], "attend_back",
            )
            first_grads.append(first_grad)
            branch_grads.append(branch)
            qkv_grads.append(qkv_grad)
            lowered_pres.append(low)
            pre_parts.append(summands(partial))
            mid_sums.append(sums)
            qkv_sums.append(qkv_sum)
        token_grads, pre_sums = [], []
        for part in range(parts):
            first_step = part * part_steps
            grad, sums = call(
                functools.partial(finish, pairs), part_steps,
                [(tokens_in, step, first_step), (pre_gain, None, 0), (first_grads[part], step, 0)]
                + [(partial, step, 0) for partial in pre_parts[part]],
                [((part_rows, model), F32, step), ((8, model), F32, None)], "finish",
            )
            token_grads.append(grad)
            pre_sums.append(sums)
        tokens_grad = jnp.concatenate(token_grads)

        groups = [pre_sums, mid_sums, moe_sums, hidden_sums, qkv_sums, router_sums]
        grads = [
            hidden_weight_grad, output_weight_grad, weight_grad(lowered_pres, qkv_grads),
            weight_grad(contexts, branch_grads),
        ]
        return [tokens_grad] + [over_wide(term) for term in grads + [sum(group) for group in groups]]

    def fused_backward():
        lanes = 3 * width
        layout = [(0, 1), (0, 1, 2), (0, 1, 2), (0,), (0,), tuple(range(experts))]
        vectors = [(8, model), (8, model), (8, model), (8, hidden), (8, lanes)]
        steps = wide.bit_length() - 1
        near, far = tuple(range(steps)), (0,) + tuple(range(2, steps)) + (1,)
        totals = [(model, hidden), (hidden, model), (model, lanes // 2), (model, lanes // 2), (width, model), (16 * wide, 128)]
        local = [
            ((tokens, model), BF16), ((tokens, hidden), BF16), ((tokens, hidden), BF16), ((tokens, model), BF16),
            ((tokens, model), BF16), ((tokens, model), BF16), ((tokens, lanes), BF16), ((tokens, model), BF16),
            ((tokens, model), BF16), ((tokens, model), BF16), ((8, model), F32), ((8, hidden), F32),
            ((8, lanes), F32), ((8, model), F32), (totals[-1], BF16),
        ]
        chunks = tokens // step
        outs = pl.pallas_call(
            functools.partial(backward, wide, heads, layout, (near, far, near, far, near, far), step),
            out_shape=[jax.ShapeDtypeStruct((tokens, model), F32)]
            + [jax.ShapeDtypeStruct(shape, BF16) for shape in totals[:-1]]
            + [jax.ShapeDtypeStruct(shape, F32) for shape in vectors + [(experts, model)]],
            in_specs=[pl.BlockSpec(memory_space=pltpu.VMEM)] * 16,
            out_specs=[pl.BlockSpec(memory_space=pltpu.VMEM)] * 12,
            scratch_shapes=[pltpu.VMEM(shape, dtype) for shape, dtype in local]
            + [pltpu.VMEM(shape, F32) for shape in totals]
            + [pltpu.VMEM(shape, BF16) for shape in totals] * 2
            + [pltpu.SemaphoreType.DMA((2, chunks))] * 2
            + [pltpu.SemaphoreType.DMA((len(totals), 2 * steps))] * 2,
            compiler_params=pltpu.CompilerParams(
                vmem_limit_bytes=BIG_VMEM_BYTES, collective_id=1, has_side_effects=True
            ),
            name="backward",
        )(
            jnp.concatenate(second_grads), jnp.concatenate(firsts), tokens_in, jnp.concatenate(qkv),
            jnp.concatenate(contexts), mid_gain, mid_shift, pre_gain, pre_shift, hidden_weight, hidden_bias,
            output_weight, proj_weight, weight_qkv, sum(moe_sums), sum(router_sums),
        )
        tokens_grad, hidden_g, output_g, left, right, proj_g = outs[:6]
        qkv_g = jnp.concatenate([left, right], axis=1)
        return [tokens_grad] + [grad.astype(F32) for grad in (hidden_g, output_g, qkv_g, proj_g)] + list(outs[6:])

    (tokens_grad, hidden_weight_g, output_weight_g, qkv_weight_g, proj_weight_g, pre, mid, moe, hid, qks, router_g) = (
        fused_backward() if two else plain_backward()
    )
    qks, router_g = qks[0].reshape(3, width), router_g[:experts]

    result_pieces = home(result, expert_out_bias)
    outs = []
    for part in range(parts):
        first_step = part * part_steps
        outs.append(
            call(
                functools.partial(blend, pairs), part_steps,
                [(plane, "scalar", 0), (seconds[part], step, 0), (gates[part], step, 0), (targets_by_token, step, first_step)]
                + [(piece, None, 0) for piece in result_pieces],
                [((part_rows, model), BF16, step)], "blend",
            )[0]
        )
    block_out = jnp.concatenate(outs)

    expert_out_grad = dot_columns(expert_act, slot_grad)[None]
    expert_in_grad = dot_columns(arrived, expert_inner_grad)[None]
    expert_out_bias_grad = jnp.sum(slot_grad.astype(F32), axis=0, keepdims=True)
    expert_in_bias_grad = jnp.sum(expert_inner_grad.astype(F32), axis=0, keepdims=True)

    return (
        block_out,
        tokens_grad,
        pre[0],
        pre[1],
        qkv_weight_g.reshape(model, 3, width),
        jnp.stack([qks[0], qks[2]]),
        proj_weight_g,
        mid[2],
        mid[0],
        mid[1],
        hidden_weight_g,
        hid[0],
        output_weight_g,
        moe[2],
        moe[0],
        moe[1],
        router_g.T,
        expert_in_grad,
        expert_in_bias_grad,
        expert_out_grad,
        expert_out_bias_grad,
    )


def solution(mesh):
    return jax.shard_map(
        functools.partial(shards, mesh.shape["wide"], mesh.shape["tensor"]),
        mesh=mesh,
        in_specs=(
            P("wide", None), P(), P(), P(None, None, "tensor"), P(None, "tensor"), P("tensor", None), P(), P(), P(),
            P(None, "tensor"), P("tensor"), P("tensor", None), P(), P(), P(), P(),
            P("wide", None, "tensor"), P("wide", "tensor"), P("wide", "tensor", None), P("wide", None),
            P("wide", None), P("wide", None), P("wide", None),
        ),
        out_specs=(
            P("wide", None), P("wide", None), P(), P(), P(None, None, "tensor"), P(None, "tensor"), P("tensor", None),
            P(), P(), P(), P(None, "tensor"), P("tensor"), P("tensor", None), P(), P(), P(), P(),
            P("wide", None, "tensor"), P("wide", "tensor"), P("wide", "tensor", None), P("wide", None),
        ),
        check_vma=False,
    )
```

```python
import functools

import jax
import jax.numpy as jnp
from jax import lax
from jax.experimental import pallas as pl
from jax.experimental.pallas import tpu as pltpu
from jax.sharding import PartitionSpec as P

HEAD_DIM = 64
PATCHES = 144
BF16 = jnp.bfloat16
F32 = jnp.float32
HIGHEST = lax.Precision.HIGHEST
VMEM_BYTES = 48 * 1024 * 1024
BIG_VMEM_BYTES = 60 * 1024 * 1024


def dot(left, right):
    return jnp.dot(left, right, preferred_element_type=F32)


def dot_rows(left, right):
    return lax.dot_general(left, right, (((1,), (1,)), ((), ())), preferred_element_type=F32)


def dot_columns(left, right, precision=None):
    return lax.dot_general(
        left, right, (((0,), (0,)), ((), ())), precision=precision, preferred_element_type=F32
    )


def normalized(values):
    centered = values - jnp.mean(values, axis=-1, keepdims=True)
    variance = jnp.mean(centered * centered, axis=-1, keepdims=True)
    scale = lax.rsqrt(variance + 1e-06)
    return centered * scale, scale


def norm_back(rows, scale, gain, upstream):
    scaled = upstream * gain
    inward = jnp.mean(scaled, axis=-1, keepdims=True)
    along = jnp.mean(scaled * rows, axis=-1, keepdims=True)
    return scale * (scaled - inward - rows * along)


def gelu_parts(inner):
    square = inner * inner
    bend = jnp.tanh(0.7978845608028654 * inner * (1.0 + 0.044715 * square))
    half = 0.5 * (1.0 + bend)
    slope = half + (0.5 * 0.7978845608028654) * inner * (1.0 - bend * bend) * (
        1.0 + 0.134145 * square
    )
    return inner * half, slope


def gelu(inner):
    return inner * (0.5 * (1.0 + jnp.tanh(0.7978845608028654 * inner * (1.0 + 0.044715 * inner * inner))))


def softmax_rows(scores, scale):
    peak = jnp.max(scores, axis=-1, keepdims=True)
    weights = jnp.exp((scores - peak) * scale)
    return weights * (1.0 / jnp.sum(weights, axis=-1, keepdims=True))


def call(kernel, steps, ins, outs, name):
    def spec(shape, rows, first):
        if rows is None:
            return pl.BlockSpec(shape, lambda i: (0,) * len(shape))
        return pl.BlockSpec((rows,) + tuple(shape[1:]), lambda i: (i + first,) + (0,) * (len(shape) - 1))

    in_specs = []
    for array, rows, first in ins:
        if rows == "scalar":
            in_specs.append(pl.BlockSpec(memory_space=pltpu.SMEM))
        else:
            in_specs.append(spec(array.shape, rows, first))
    return pl.pallas_call(
        kernel,
        grid=(steps,),
        in_specs=in_specs,
        out_specs=[spec(shape, rows, 0) for shape, _, rows in outs],
        out_shape=[jax.ShapeDtypeStruct(shape, dtype) for shape, dtype, _ in outs],
        compiler_params=pltpu.CompilerParams(vmem_limit_bytes=VMEM_BYTES),
        name=name,
    )(*[array for array, _, _ in ins])


def attend(heads, tokens, gain, shift, weight, bias, qkv_out, context_out):
    rows, _ = normalized(tokens[...].astype(F32))
    lowered = (rows * gain[...] + shift[...]).astype(BF16)
    qkv = (dot(lowered, weight[...]) + bias[...]).astype(BF16)
    qkv_out[...] = qkv
    width = heads * HEAD_DIM
    for image in range(qkv.shape[0] // PATCHES):
        block = qkv[image * PATCHES : (image + 1) * PATCHES]
        parts = []
        for head in range(heads):
            at = head * HEAD_DIM
            query = block[:, at : at + HEAD_DIM]
            keys = block[:, width + at : width + at + HEAD_DIM]
            values = block[:, 2 * width + at : 2 * width + at + HEAD_DIM]
            probs = softmax_rows(dot_rows(query, keys), HEAD_DIM**-0.5)
            parts.append(dot(probs.astype(BF16), values))
        context = jnp.concatenate(parts, axis=1).astype(BF16)
        context_out[image * PATCHES : (image + 1) * PATCHES, :] = context


def feed(
    pairs, tokens, proj_bias, gain, shift, hidden, hidden_bias, output, *rest
):
    contexts, projections = rest[:pairs], rest[pairs : 2 * pairs]
    first_out, partial_out = rest[2 * pairs :]
    branch = dot(contexts[0][...], projections[0][...])
    if pairs == 2:
        branch = branch + dot(contexts[1][...], projections[1][...])
    first = tokens[...].astype(F32) + branch + proj_bias[...]
    first_out[...] = first
    rows, _ = normalized(first)
    lowered = (rows * gain[...] + shift[...]).astype(BF16)
    activated = gelu(dot(lowered, hidden[...]) + hidden_bias[...]).astype(BF16)
    partial_out[...] = dot(activated, output[...]).astype(BF16)


def total(parts):
    value = parts[0][...].astype(F32)
    for part in parts[1:]:
        value = value + part[...].astype(F32)
    return value


def spots(places):
    lane = lax.broadcasted_iota(jnp.int32, (places.shape[0], 128), 1)
    return [(lane == places[:, j : j + 1]).astype(F32) for j in range(2)]


def router(pairs, first, bias, gain, shift, weight, choices, *rest):
    second_out, lowered_out, route_out, gates_out, table_out = rest[pairs:]

    @pl.when(pl.program_id(0) == 0)
    def _():
        table_out[...] = jnp.zeros_like(table_out)

    second = first[...] + total(rest[:pairs]) + bias[...]
    second_out[...] = second
    rows, _ = normalized(second)
    normed = rows * gain[...] + shift[...]
    lowered_out[...] = normed.astype(BF16)
    logits = jnp.dot(normed, weight[...], precision=HIGHEST, preferred_element_type=F32)
    grown = jnp.exp(logits - jnp.max(logits, axis=-1, keepdims=True))
    route = grown / jnp.sum(grown, axis=-1, keepdims=True)
    route_out[...] = route
    number = lax.broadcasted_iota(jnp.int32, route.shape, 1)
    chosen = [jnp.where(number == choices[:, 2 + j : 3 + j], route, 0.0) for j in range(2)]
    gates_out[...] = jnp.concatenate([jnp.sum(part, axis=1, keepdims=True) for part in chosen], axis=1)
    for part, spot in zip(chosen, spots(choices[:, 4:6])):
        table_out[...] += dot_columns(part, spot, HIGHEST)


def slot_hits(targets, rows):
    first = pl.program_id(0) * rows
    slot = first + lax.broadcasted_iota(jnp.int32, (rows, targets.shape[1]), 0)
    return [slot == targets[j : j + 1, :] for j in range(2)]


def place(parts, targets, *rest):
    sources, out = rest[:parts], rest[parts]
    hits = slot_hits(targets, out.shape[0])
    table = (hits[0] | hits[1]).astype(BF16)
    rows = jnp.zeros(out.shape, F32)
    at = 0
    for source in sources:
        rows = rows + dot(table[:, at : at + source.shape[0]], source[...].astype(BF16))
        at += source.shape[0]
    out[...] = rows.astype(BF16)


def expert(
    plane, arrived, upstream, gates, weight_in, bias_in, weight_out, bias_out,
    result_out, grad_out, gate_out, act_out, inner_out, slot_out,
):
    rows = arrived[...]
    inner = dot(rows, weight_in[...]) + bias_in[...]
    act, slope = gelu_parts(inner)
    act = act.astype(BF16)
    act_out[...] = act
    result = dot(act, weight_out[...])
    result_out[...] = result.astype(BF16)
    raised = upstream[...].astype(F32)
    once = jnp.where(plane[0] == 0, 1.0, 0.0)
    gate_out[...] = jnp.sum(raised * (result + bias_out[...] * once), axis=1, keepdims=True)
    slot_grad = (raised * gates[...]).astype(BF16)
    slot_out[...] = slot_grad
    inner_grad = (dot_rows(slot_grad, weight_out[...]) * slope).astype(BF16)
    inner_out[...] = inner_grad
    grad_out[...] = dot_rows(inner_grad, weight_in[...]).astype(BF16)


def token_hits(targets, slots):
    slot = lax.broadcasted_iota(jnp.int32, (targets.shape[0], slots), 1)
    return [slot == targets[:, j : j + 1] for j in range(2)]


def ordered(plane, parts):
    if len(parts) == 1:
        return parts[0]
    own, peer = parts
    flipped = plane[0] != 0
    return jnp.concatenate([jnp.where(flipped, peer, own), jnp.where(flipped, own, peer)], axis=1)


def settle(
    pairs, plane, second, cotangent, route, gain, shift, router_weight, choices, gate_grads, *rest
):
    pieces = rest[:pairs]
    second_out, lowered_out, sums_out, router_out = rest[pairs:]

    @pl.when(pl.program_id(0) == 0)
    def _():
        sums_out[...] = jnp.zeros_like(sums_out)
        router_out[...] = jnp.zeros_like(router_out)

    hits = token_hits(choices, pieces[0].shape[0])
    table = (hits[0] | hits[1]).astype(BF16)
    moe_grad = ordered(plane, [dot(table, piece[...]) for piece in pieces])
    chances = route[...]
    number = lax.broadcasted_iota(jnp.int32, chances.shape, 1)
    route_grad = jnp.zeros_like(chances)
    for j, spot in enumerate(spots(choices[:, 4:6])):
        at_place = lax.dot_general(
            spot, gate_grads[...], (((1,), (1,)), ((), ())), precision=HIGHEST, preferred_element_type=F32
        )
        route_grad = route_grad + jnp.where(number == choices[:, 2 + j : 3 + j], at_place, 0.0)
    logit_grad = chances * (route_grad - jnp.sum(chances * route_grad, axis=1, keepdims=True))
    rows, scale = normalized(second[...])
    normed = rows * gain[...] + shift[...]
    router_out[...] += dot_columns(logit_grad, normed, HIGHEST)
    moe_grad = moe_grad + lax.dot_general(
        logit_grad, router_weight[...], (((1,), (1,)), ((), ())), precision=HIGHEST, preferred_element_type=F32
    )
    grad = cotangent[...] + norm_back(rows, scale, gain[...], moe_grad)
    second_out[...] = grad
    lowered_out[...] = grad.astype(BF16)
    sums_out[0:1, :] += jnp.sum(moe_grad * rows, axis=0, keepdims=True)
    sums_out[1:2, :] += jnp.sum(moe_grad, axis=0, keepdims=True)
    sums_out[2:3, :] += jnp.sum(grad, axis=0, keepdims=True)


def feed_back(
    first, second_grad, gain, shift, hidden, hidden_bias, output,
    act_out, inner_out, lowered_out, partial_out, sums_out,
):
    @pl.when(pl.program_id(0) == 0)
    def _():
        sums_out[...] = jnp.zeros_like(sums_out)

    rows, _ = normalized(first[...])
    lowered = (rows * gain[...] + shift[...]).astype(BF16)
    lowered_out[...] = lowered
    act, slope = gelu_parts(dot(lowered, hidden[...]) + hidden_bias[...])
    act_out[...] = act.astype(BF16)
    inner_grad = (dot_rows(second_grad[...], output[...]) * slope).astype(BF16)
    inner_out[...] = inner_grad
    partial_out[...] = dot_rows(inner_grad, hidden[...]).astype(BF16)
    sums_out[0:1, :] += jnp.sum(inner_grad.astype(F32), axis=0, keepdims=True)


def attend_back(
    pairs, heads, first, second_grad, gain, projection, qkv, weight, tokens, pre_gain, pre_shift, *rest
):
    first_out, branch_out, qkv_out, lowered_out, partial_out, sums_out, qkv_sums_out = rest[pairs:]

    @pl.when(pl.program_id(0) == 0)
    def _():
        sums_out[...] = jnp.zeros_like(sums_out)
        qkv_sums_out[...] = jnp.zeros_like(qkv_sums_out)

    mid_grad = total(rest[:pairs])
    rows, scale = normalized(first[...])
    first_grad = second_grad[...] + norm_back(rows, scale, gain[...], mid_grad)
    first_out[...] = first_grad
    branch = first_grad.astype(BF16)
    branch_out[...] = branch
    sums_out[0:1, :] += jnp.sum(mid_grad * rows, axis=0, keepdims=True)
    sums_out[1:2, :] += jnp.sum(mid_grad, axis=0, keepdims=True)
    sums_out[2:3, :] += jnp.sum(first_grad, axis=0, keepdims=True)
    rows, _ = normalized(tokens[...].astype(F32))
    lowered_out[...] = (rows * pre_gain[...] + pre_shift[...]).astype(BF16)
    context_grad = dot_rows(branch, projection[...]).astype(BF16)
    width = heads * HEAD_DIM
    scale = HEAD_DIM**-0.5
    for image in range(qkv.shape[0] // PATCHES):
        at = image * PATCHES
        block = qkv[at : at + PATCHES, :]
        grad = context_grad[at : at + PATCHES]
        parts = [[], [], []]
        for head in range(heads):
            h = head * HEAD_DIM
            query = block[:, h : h + HEAD_DIM]
            keys = block[:, width + h : width + h + HEAD_DIM]
            values = block[:, 2 * width + h : 2 * width + h + HEAD_DIM]
            upstream = grad[:, h : h + HEAD_DIM]
            probs = softmax_rows(dot_rows(query, keys), scale)
            prob_grad = dot_rows(upstream, values)
            inward = jnp.sum(probs * prob_grad, axis=-1, keepdims=True)
            score_grad = (probs * (prob_grad - inward)).astype(BF16)
            parts[0].append(dot(score_grad, keys) * scale)
            parts[1].append(dot_columns(score_grad, query) * scale)
            parts[2].append(dot_columns(probs.astype(BF16), upstream))
        qkv_grad = jnp.concatenate(parts[0] + parts[1] + parts[2], axis=1).astype(BF16)
        qkv_out[at : at + PATCHES, :] = qkv_grad
        partial_out[at : at + PATCHES, :] = dot_rows(qkv_grad, weight[...]).astype(BF16)
        qkv_sums_out[0:1, :] += jnp.sum(qkv_grad.astype(F32), axis=0, keepdims=True)


def finish(pairs, tokens, gain, first_grad, *rest):
    grad_out, sums_out = rest[pairs:]

    @pl.when(pl.program_id(0) == 0)
    def _():
        sums_out[...] = jnp.zeros_like(sums_out)

    upstream = total(rest[:pairs])
    rows, scale = normalized(tokens[...].astype(F32))
    grad_out[...] = first_grad[...] + norm_back(rows, scale, gain[...], upstream)
    sums_out[0:1, :] += jnp.sum(upstream * rows, axis=0, keepdims=True)
    sums_out[1:2, :] += jnp.sum(upstream, axis=0, keepdims=True)


def blend(pairs, plane, second, gates, targets, *rest):
    pieces, out = rest[:pairs], rest[pairs]
    slots = pieces[0].shape[0]
    mixture = jnp.zeros(out.shape, F32)
    for j, hit in enumerate(token_hits(targets, slots)):
        table = hit.astype(BF16)
        picked = ordered(plane, [dot(table, piece[...]) for piece in pieces])
        mixture = mixture + gates[:, j : j + 1] * picked
    out[...] = (second[...] + mixture).astype(BF16)


def slot_targets(choice_ids, ranks, capacity, room):
    count = choice_ids.shape[0]
    order_keys = jnp.concatenate([ranks, ranks + count])
    flat_ids = jnp.concatenate([choice_ids[:, 0], choice_ids[:, 1]])
    earlier = (order_keys[None, :] < order_keys[:, None]) & (flat_ids[None, :] == flat_ids[:, None])
    position = jnp.sum(earlier.astype(jnp.int32), axis=1).reshape(2, count)
    kept = position < capacity
    targets = jnp.where(kept, choice_ids.T * room + position, -1)
    marks = jnp.where(kept, choice_ids.T, -1)
    places = jnp.where(kept, position, -1)
    return targets, jnp.concatenate([targets, marks, places]).T


MESH = pl.DeviceIdType.MESH


def bits_of(index, wide):
    return [lax.rem(lax.div(index, 1 << k), 2) for k in range(wide.bit_length() - 1)]


class Sums:
    def __init__(self, wide, orders, totals, sends, lands, gathers, send_sems, recv_sems):
        me, self.plane = lax.axis_index("wide"), lax.axis_index("tensor")
        self.bits = bits_of(me, wide)
        self.partners = [me + (1 - 2 * bit) * (1 << k) for k, bit in enumerate(self.bits)]
        self.steps = len(self.bits)
        self.orders, self.totals, self.sends, self.lands, self.gathers = orders, totals, sends, lands, gathers
        self.send_sems, self.recv_sems = send_sems, recv_sems

    def piece(self, i, step):
        rows = self.gathers[i].shape[0]
        base = 0
        for s in range(step):
            base = base + self.bits[self.orders[i][s]] * (rows >> (s + 1))
        length = rows >> (step + 1)
        bit = self.bits[self.orders[i][step]]
        return pl.multiple_of(base + bit * length, 16), pl.multiple_of(base + (1 - bit) * length, 16), length

    def staged(self, i, step):
        rows = self.gathers[i].shape[0]
        return rows - (rows >> step)

    def transfer(self, i, k):
        step = k if k < self.steps else 2 * self.steps - 1 - k
        kept, _, length = self.piece(i, step)
        if k < self.steps:
            at = self.staged(i, step)
            source, target = self.sends[i].at[pl.ds(at, length)], self.lands[i].at[pl.ds(at, length)]
        else:
            source = target = self.gathers[i].at[pl.ds(kept, length)]
        return pltpu.make_async_remote_copy(
            source, target, self.send_sems.at[i, k], self.recv_sems.at[i, k],
            device_id=(self.partners[self.orders[i][step]], self.plane), device_id_type=MESH,
        )

    def begin(self, i, k):
        if k < self.steps:
            _, other, length = self.piece(i, k)
            at = self.staged(i, k)
            self.sends[i][at : at + length, :] = self.totals[i][pl.ds(other, length), :].astype(BF16)
        self.transfer(i, k).start()

    def advance(self, i, k):
        self.transfer(i, k).wait()
        if k < self.steps:
            kept, _, length = self.piece(i, k)
            at = self.staged(i, k)
            value = self.totals[i][pl.ds(kept, length), :] + self.lands[i][at : at + length, :].astype(F32)
            if k + 1 < self.steps:
                self.totals[i][pl.ds(kept, length), :] = value
            else:
                self.gathers[i][pl.ds(kept, length), :] = value.astype(BF16)
        if k + 1 < 2 * self.steps:
            self.begin(i, k + 1)


def greet(wide):
    me, plane = lax.axis_index("wide"), lax.axis_index("tensor")
    barrier = pltpu.get_barrier_semaphore()
    bits = bits_of(me, wide)
    for k, bit in enumerate(bits):
        pl.semaphore_signal(
            barrier, inc=1, device_id=(me + (1 - 2 * bit) * (1 << k), plane), device_id_type=MESH
        )
    pl.semaphore_signal(barrier, inc=1, device_id=(me, 1 - plane), device_id_type=MESH)
    pl.semaphore_wait(barrier, len(bits) + 1)


def put_row(small, at, row):
    for c in range(row.shape[1] // 128):
        small[at + c : at + c + 1, :] = row[:, 128 * c : 128 * (c + 1)]
    return at + row.shape[1] // 128


def get_row(small, at, width):
    return jnp.concatenate([small[at + c : at + c + 1, :] for c in range(width // 128)], axis=1)


def image_back(heads, qkv, context_grad):
    width = heads * HEAD_DIM
    scale = HEAD_DIM**-0.5
    parts = [[], [], []]
    for head in range(heads):
        h = head * HEAD_DIM
        query = qkv[:, h : h + HEAD_DIM]
        keys = qkv[:, width + h : width + h + HEAD_DIM]
        values = qkv[:, 2 * width + h : 2 * width + h + HEAD_DIM]
        upstream = context_grad[:, h : h + HEAD_DIM]
        probs = softmax_rows(dot_rows(query, keys), scale)
        prob_grad = dot_rows(upstream, values)
        inward = jnp.sum(probs * prob_grad, axis=-1, keepdims=True)
        score_grad = (probs * (prob_grad - inward)).astype(BF16)
        parts[0].append(dot(score_grad, keys) * scale)
        parts[1].append(dot_columns(score_grad, query) * scale)
        parts[2].append(dot_columns(probs.astype(BF16), upstream))
    return jnp.concatenate(parts[0] + parts[1] + parts[2], axis=1).astype(BF16)


def column_dots(left, right, put, tile=256):
    def body(i, carry):
        at = pl.multiple_of(i * tile, tile)
        put(at, tile, dot_columns(left[:, pl.ds(at, tile)], right[...]))
        return carry

    lax.fori_loop(0, left.shape[1] // tile, body, 0)


def backward(
    wide, heads, layout, orders, rows,
    second_grad, first, tokens, qkv, context, mid_gain, mid_shift, pre_gain, pre_shift,
    hidden, hidden_bias, output, projection, weight_qkv, moe_sums, router_sums,
    grad_out, hidden_out, output_out, left_out, right_out, proj_out, *rest,
):
    vectors_out, rest = rest[: len(layout)], rest[len(layout) :]
    (lowered_mid, act, inner_grad, mid_own, mid_peer, branch, qkv_grad, lowered_pre, pre_own, pre_peer,
     mid_sums, hidden_sums, qkv_sums, pre_sums, small_sums) = rest[:15]
    totals, sends, lands = rest[15:21], rest[21:27], rest[27:33]
    mid_sems, pre_sems, send_sems, recv_sems = rest[33:]
    gathers = (hidden_out, output_out, left_out, right_out, proj_out, small_sums)
    me, plane = lax.axis_index("wide"), lax.axis_index("tensor")
    chunks = tokens.shape[0] // rows
    greet(wide)
    sums = Sums(wide, orders, totals, sends, lands, gathers, send_sems, recv_sems)

    def across(own, peer, sems, chunk):
        at = pl.multiple_of(chunk * rows, rows)
        return pltpu.make_async_remote_copy(
            own.at[pl.ds(at, rows)], peer.at[pl.ds(at, rows)], sems.at[0, chunk], sems.at[1, chunk],
            device_id=(me, 1 - plane), device_id_type=MESH,
        )

    for vector in (mid_sums, hidden_sums, qkv_sums, pre_sums):
        vector[...] = jnp.zeros_like(vector)

    def feed_chunk(chunk, carry):
        here = pl.ds(pl.multiple_of(chunk * rows, rows), rows)
        normed, _ = normalized(first[here, :])
        lowered = (normed * mid_gain[...] + mid_shift[...]).astype(BF16)
        lowered_mid[here, :] = lowered
        acted, slope = gelu_parts(dot(lowered, hidden[...]) + hidden_bias[...])
        act[here, :] = acted.astype(BF16)
        upstream = second_grad[here, :].astype(BF16)
        branch[here, :] = upstream
        inward = (dot_rows(upstream, output[...]) * slope).astype(BF16)
        inner_grad[here, :] = inward
        hidden_sums[0:1, :] += jnp.sum(inward.astype(F32), axis=0, keepdims=True)
        mid_own[here, :] = dot_rows(inward, hidden[...]).astype(BF16)
        across(mid_own, mid_peer, mid_sems, chunk).start()
        return carry

    lax.fori_loop(0, chunks, feed_chunk, 0)

    def put_in(total):
        def put(at, tile, value):
            total[pl.ds(at, tile), :] = value

        return put

    column_dots(lowered_mid, inner_grad, put_in(totals[0]))
    sums.begin(0, 0)
    column_dots(act, branch, put_in(totals[1]))
    sums.begin(1, 0)

    def attend_chunk(chunk, carry):
        here = pl.ds(pl.multiple_of(chunk * rows, rows), rows)
        across(mid_own, mid_peer, mid_sems, chunk).wait()
        mid_grad = mid_own[here, :].astype(F32) + mid_peer[here, :].astype(F32)
        normed, scale = normalized(first[here, :])
        first_grad = second_grad[here, :] + norm_back(normed, scale, mid_gain[...], mid_grad)
        grad_out[here, :] = first_grad
        lowered_grad = first_grad.astype(BF16)
        branch[here, :] = lowered_grad
        mid_sums[0:1, :] += jnp.sum(mid_grad * normed, axis=0, keepdims=True)
        mid_sums[1:2, :] += jnp.sum(mid_grad, axis=0, keepdims=True)
        mid_sums[2:3, :] += jnp.sum(first_grad, axis=0, keepdims=True)
        normed, _ = normalized(tokens[here, :].astype(F32))
        lowered_pre[here, :] = (normed * pre_gain[...] + pre_shift[...]).astype(BF16)
        context_grad = dot_rows(lowered_grad, projection[...]).astype(BF16)
        for image in range(rows // PATCHES):
            at = pl.multiple_of(chunk * rows + image * PATCHES, PATCHES)
            block = qkv[pl.ds(at, PATCHES), :]
            grad = image_back(heads, block, context_grad[image * PATCHES : (image + 1) * PATCHES])
            qkv_grad[pl.ds(at, PATCHES), :] = grad
            pre_own[pl.ds(at, PATCHES), :] = dot_rows(grad, weight_qkv[...]).astype(BF16)
            qkv_sums[0:1, :] += jnp.sum(grad.astype(F32), axis=0, keepdims=True)
            for k in range(sums.steps):

                @pl.when(chunk == k)
                def _(i=image, k=k):
                    if i < 2:
                        sums.advance(i, k)

        across(pre_own, pre_peer, pre_sems, chunk).start()
        return carry

    lax.fori_loop(0, chunks, attend_chunk, 0)
    column_dots(context, branch, put_in(totals[4]))
    sums.begin(4, 0)

    def put_halves(at, tile, value):
        half = totals[2].shape[1]
        totals[2][pl.ds(at, tile), :] = value[:, :half]
        totals[3][pl.ds(at, tile), :] = value[:, half:]

    column_dots(lowered_pre, qkv_grad, put_halves)
    sums.begin(2, 0)
    sums.begin(3, 0)

    def finish_chunk(chunk, carry):
        here = pl.ds(pl.multiple_of(chunk * rows, rows), rows)
        across(pre_own, pre_peer, pre_sems, chunk).wait()
        upstream = pre_own[here, :].astype(F32) + pre_peer[here, :].astype(F32)
        normed, scale = normalized(tokens[here, :].astype(F32))
        grad_out[here, :] += norm_back(normed, scale, pre_gain[...], upstream)
        pre_sums[0:1, :] += jnp.sum(upstream * normed, axis=0, keepdims=True)
        pre_sums[1:2, :] += jnp.sum(upstream, axis=0, keepdims=True)
        return carry

    lax.fori_loop(0, chunks, finish_chunk, 0)
    small = totals[5]
    small[...] = jnp.zeros_like(small)
    at = 0
    for vector, picked in zip((pre_sums, mid_sums, moe_sums, hidden_sums, qkv_sums, router_sums), layout):
        for r in picked:
            at = put_row(small, at, vector[r : r + 1, :])
    sums.begin(5, 0)
    for k in range(2 * sums.steps):
        for i in (0, 1):
            if sums.steps + k < 2 * sums.steps:
                sums.advance(i, sums.steps + k)
        for i in (4, 2, 3, 5):
            sums.advance(i, k)
    at = 0
    for out, picked in zip(vectors_out, layout):
        for i in range(len(picked)):
            out[i : i + 1, :] = get_row(small_sums, at, out.shape[1]).astype(F32)
            at += out.shape[1] // 128


def experts_kernel(
    wide, room, group,
    lowered_a, lowered_b, targets, table_a, table_b, upstream, weight_in, bias_in, weight_out, bias_out,
    own_home, peer_home, gate_home, result_out, in_grad, out_grad, in_bias_grad, out_bias_grad,
    placed, arrived, act, inner_grad, slot_grad, grad_kept, grad_sent, grad_landed, result_kept, result_sent,
    result_landed, grad_back, gate_sent, gate_arrived, gate_back, gate_own, gate_peer, sems,
):
    me, plane = lax.axis_index("wide"), lax.axis_index("tensor")
    groups = wide // group
    mine = lax.div(me, group)
    half = own_home.shape[1]
    block = group * room
    row_at, gate_at, home_at, back_at = 0, wide, 2 * wide, 3 * wide
    grad_at, result_at, share_at, table_at = 4 * wide, 4 * wide + groups, 4 * wide + 2 * groups, 4 * wide + 3 * groups

    barrier = pltpu.get_barrier_semaphore()

    def hail(d, carry):
        pl.semaphore_signal(barrier, inc=1, device_id=(lax.rem(me + d, wide), plane), device_id_type=MESH)
        return carry

    lax.fori_loop(1, wide, hail, 0)
    pl.semaphore_signal(barrier, inc=1, device_id=(me, 1 - plane), device_id_type=MESH)
    pl.semaphore_wait(barrier, wide)

    def rows_of(index):
        return pl.ds(pl.multiple_of(index * room, 16), room)

    def rows_of_group(index):
        return pl.ds(pl.multiple_of(index * block, 16), block)

    def move(source, target, base, sent, landed, device):
        return pltpu.make_async_remote_copy(
            source, target, sems.at[0, base + sent], sems.at[1, base + landed], device_id=device, device_id_type=MESH
        )

    def row_copy(other, sender):
        return move(placed.at[rows_of(other)], arrived.at[rows_of(sender)], row_at, other, sender, (other, plane))

    def gate_copy(other, sender):
        return move(gate_sent.at[other], gate_arrived.at[sender], gate_at, other, sender, (other, plane))

    def home_copy(other, sender):
        return move(grad_back.at[rows_of(other)], own_home.at[rows_of(sender)], home_at, other, sender, (other, plane))

    def back_copy(other, sender):
        return move(gate_back.at[other], gate_own.at[sender], back_at, other, sender, (other, plane))

    def across(source, target, base, index):
        there = rows_of_group(index)
        return move(source.at[there], target.at[there], base, index, index, (me, 1 - plane))

    table = table_a[...] + table_b[...]
    for e in range(wide):
        gate_sent[e] = jnp.broadcast_to(table[e : e + 1, :], gate_sent.shape[1:])
    in_bias_grad[...] = jnp.zeros_like(in_bias_grad)
    out_bias_grad[...] = jnp.zeros_like(out_bias_grad)

    def place_group(k, carry):
        q = lax.rem(mine + k, groups)
        slot = q * block + lax.broadcasted_iota(jnp.int32, (block, targets.shape[1]), 0)
        hits = ((slot == targets[0:1, :]) | (slot == targets[1:2, :])).astype(BF16)
        split = lowered_a.shape[0]
        rows = dot(hits[:, :split], lowered_a[...]) + dot(hits[:, split:], lowered_b[...])
        placed[rows_of_group(q), :] = rows.astype(BF16)
        for j in range(group):
            e = q * group + j

            @pl.when(e != me)
            def _(e=e):
                row_copy(e, me).start()
                gate_copy(e, me).start()

            @pl.when(e == me)
            def _(e=e):
                arrived[rows_of(e), :] = placed[rows_of(e), :]
                gate_arrived[e] = gate_sent[e]

        return carry

    lax.fori_loop(0, groups, place_group, 0)
    diagonal = lax.broadcasted_iota(jnp.int32, (room, 128), 0) == lax.broadcasted_iota(jnp.int32, (room, 128), 1)
    first_plane = plane == 0

    def give_back(p):
        across(grad_sent, grad_landed, grad_at, p).wait()
        there = rows_of_group(p)
        grad_back[there, :] = (grad_kept[there, :] + grad_landed[there, :].astype(F32)).astype(BF16)
        for j in range(group):
            w = p * group + j

            @pl.when(w != me)
            def _(w=w):
                home_copy(w, me).start()

            @pl.when(w == me)
            def _(w=w):
                own_home[rows_of(w), :] = grad_back[rows_of(w), :]

    def expert_group(k, carry):
        p = lax.rem(mine + groups - k, groups)
        there = rows_of_group(p)
        columns = []
        for j in range(group):
            w = p * group + j

            @pl.when(w != me)
            def _(w=w):
                row_copy(w, w).wait_recv()
                gate_copy(w, w).wait_recv()

            columns.append(jnp.sum(jnp.where(diagonal, gate_arrived[w][0:1, :], 0.0), axis=1, keepdims=True))
        gates = jnp.concatenate(columns, axis=0)
        inner = dot(arrived[there, :], weight_in[...]) + bias_in[...]
        acted, slope = gelu_parts(inner)
        acted = acted.astype(BF16)
        act[there, :] = acted
        result = dot(acted, weight_out[...])
        raised = upstream[there, :].astype(F32)
        slot = (raised * gates).astype(BF16)
        slot_grad[there, :] = slot
        out_bias_grad[0:1, :] += jnp.sum(slot.astype(F32), axis=0, keepdims=True)
        inward = (dot_rows(slot, weight_out[...]) * slope).astype(BF16)
        inner_grad[there, :] = inward
        in_bias_grad[0:1, :] += jnp.sum(inward.astype(F32), axis=0, keepdims=True)
        grad = dot_rows(inward, weight_in[...])
        low, high = grad[:, :half], grad[:, half:]
        grad_sent[there, :] = jnp.where(first_plane, high, low).astype(BF16)
        across(grad_sent, grad_landed, grad_at, p).start()
        grad_kept[there, :] = jnp.where(first_plane, low, high)
        biased = result + bias_out[...]
        low, high = biased[:, :half], biased[:, half:]
        result_kept[there, :] = jnp.where(first_plane, low, high)
        low, high = result[:, :half], result[:, half:]
        result_sent[there, :] = jnp.where(first_plane, high, low).astype(BF16)
        across(result_sent, result_landed, result_at, p).start()
        slopes = jnp.sum(raised * jnp.where(first_plane, biased, result), axis=1, keepdims=True)
        for j in range(group):
            w = p * group + j
            row = jnp.sum(
                jnp.where(diagonal, slopes[j * room : (j + 1) * room], 0.0), axis=0, keepdims=True
            )
            gate_back[w] = jnp.broadcast_to(row, gate_back.shape[1:])

            @pl.when(w != me)
            def _(w=w):
                back_copy(w, me).start()

            @pl.when(w == me)
            def _(w=w):
                gate_own[w] = gate_back[w]

        @pl.when(k > 0)
        def _():
            give_back(lax.rem(mine + groups - k + 1, groups))

        return carry

    lax.fori_loop(0, groups, expert_group, 0)
    give_back(lax.rem(mine + 1, groups))

    tile = act.shape[1] // groups

    def share_group(k, carry):
        at = pl.multiple_of(k * tile, 128)
        out_grad[pl.ds(at, tile), :] = dot_columns(act[:, pl.ds(at, tile)], slot_grad[...]).astype(BF16)
        q = lax.rem(mine + k, groups)
        for j in range(group):
            e = q * group + j

            @pl.when(e != me)
            def _(e=e):
                home_copy(e, e).wait_recv()

        across(own_home, peer_home, share_at, q).start()
        return carry

    lax.fori_loop(0, groups, share_group, 0)

    def take_gates(d, carry):
        back_copy(lax.rem(me + d, wide), lax.rem(me + d, wide)).wait_recv()
        return carry

    lax.fori_loop(1, wide, take_gates, 0)
    tables = move(gate_own, gate_peer, table_at, 0, 0, (me, 1 - plane))
    tables.start()

    def put(at, tile, value):
        in_grad[pl.ds(at, tile), :] = value.astype(BF16)

    column_dots(arrived, inner_grad, put)

    def take_result(p, carry):
        across(result_sent, result_landed, result_at, p).wait()
        there = rows_of_group(p)
        result_out[there, :] = (result_kept[there, :] + result_landed[there, :].astype(F32)).astype(BF16)
        return carry

    lax.fori_loop(0, groups, take_result, 0)

    def end_sends(d, carry):
        other = lax.rem(me + d, wide)
        row_copy(other, me).wait_send()
        gate_copy(other, me).wait_send()
        home_copy(other, me).wait_send()
        back_copy(other, me).wait_send()
        return carry

    lax.fori_loop(1, wide, end_sends, 0)
    tables.wait()
    for e in range(wide):
        gate_home[e : e + 1, :] = gate_own[e][0:1, :] + gate_peer[e][0:1, :]

    def end_share(q, carry):
        across(own_home, peer_home, share_at, q).wait()
        return carry

    lax.fori_loop(0, groups, end_share, 0)


def shards(
    wide, planes,
    tokens_in, pre_gain, pre_shift, qkv_weight, qv_bias, proj_weight, proj_bias, mid_gain, mid_shift,
    hidden_weight, hidden_bias, output_weight, output_bias, moe_gain, moe_shift, router_weight,
    expert_in, expert_in_bias, expert_out, expert_out_bias, expert_ids, priority, cotangent,
):
    tokens, model = tokens_in.shape
    width = qkv_weight.shape[2]
    heads = width // HEAD_DIM
    hidden = hidden_weight.shape[1]
    experts = router_weight.shape[1]
    capacity = tokens // experts
    room = -(-capacity // 16) * 16
    slots = experts * room
    slot_step = 4 * room
    step = 2 * PATCHES
    parts = 2
    part_rows = tokens // parts
    part_steps = part_rows // step
    two = planes == 2
    pairs = 2 if two else 1
    plane = lax.axis_index("tensor").astype(jnp.int32).reshape(1)

    def swap(value):
        return lax.ppermute(value, "tensor", [(0, 1), (1, 0)])

    def summands(value):
        if two:
            return [value, swap(value)]
        return [lax.psum(value.astype(F32), "tensor").astype(BF16)]

    def row(vector):
        return vector.reshape(1, -1)

    pre_gain, pre_shift, proj_bias = row(pre_gain), row(pre_shift), row(proj_bias)
    mid_gain, mid_shift, hidden_bias = row(mid_gain), row(mid_shift), row(hidden_bias)
    output_bias, moe_gain, moe_shift = row(output_bias), row(moe_gain), row(moe_shift)
    weight_qkv = qkv_weight.reshape(model, 3 * width)
    qkv_bias = jnp.concatenate([qv_bias[0], jnp.zeros_like(qv_bias[0]), qv_bias[1]]).reshape(1, 3 * width)
    if two:
        projections = [proj_weight, swap(proj_weight)]
    else:
        projections = [lax.all_gather(proj_weight, "tensor", axis=0, tiled=True)]

    targets, choices = slot_targets(expert_ids, priority[0], capacity, room)
    upstream_rows = call(
        functools.partial(place, 1), slots // slot_step,
        [(targets, None, 0), (cotangent, None, 0)],
        [((slots, model), BF16, slot_step)], "place_cotangent",
    )[0]

    def to_experts(rows):
        grouped = rows.reshape(experts, room, rows.shape[1])
        return lax.all_to_all(grouped, "wide", split_axis=0, concat_axis=0, tiled=True).reshape(rows.shape)

    tokens_in, upstream_rows = lax.optimization_barrier((tokens_in, upstream_rows))
    upstream = to_experts(upstream_rows)

    qkv, firsts, seconds, lowered, routes, gates, tables = [], [], [], [], [], [], []
    contexts = []
    for part in range(parts):
        first_step = part * part_steps
        qkv_part, context = call(
            functools.partial(attend, heads), part_steps,
            [(tokens_in, step, first_step), (pre_gain, None, 0), (pre_shift, None, 0), (weight_qkv, None, 0), (qkv_bias, None, 0)],
            [((part_rows, 3 * width), BF16, step), ((part_rows, width), BF16, step)], "attend",
        )
        qkv.append(qkv_part)
        contexts.append(context)
    gathered = [
        [context, swap(context)] if two else [lax.all_gather(context, "tensor", axis=1, tiled=True)]
        for context in contexts
    ]
    partials = []
    for part in range(parts):
        first_step = part * part_steps
        first, partial = call(
            functools.partial(feed, pairs), part_steps,
            [(tokens_in, step, first_step), (proj_bias, None, 0), (mid_gain, None, 0), (mid_shift, None, 0),
             (hidden_weight, None, 0), (hidden_bias, None, 0), (output_weight, None, 0)]
            + [(context, step, 0) for context in gathered[part]]
            + [(projection, None, 0) for projection in projections],
            [((part_rows, model), F32, step), ((part_rows, model), BF16, step)], "feed",
        )
        firsts.append(first)
        partials.append(summands(partial))
    for part in range(parts):
        first_step = part * part_steps
        second, low, route, gate, table = call(
            functools.partial(router, pairs), part_steps,
            [(firsts[part], step, 0), (output_bias, None, 0), (moe_gain, None, 0), (moe_shift, None, 0),
             (router_weight, None, 0), (choices, step, first_step)]
            + [(partial, step, 0) for partial in partials[part]],
            [((part_rows, model), F32, step), ((part_rows, model), BF16, step),
             ((part_rows, experts), F32, step), ((part_rows, 2), F32, step), ((experts, 128), F32, None)], "router",
        )
        tables.append(table)
        seconds.append(second)
        lowered.append(low)
        routes.append(route)
        gates.append(gate)

    def plain_experts():
        buffers = call(
            functools.partial(place, parts), slots // slot_step,
            [(targets, None, 0)] + [(low, None, 0) for low in lowered],
            [((slots, model), BF16, slot_step)], "place_tokens",
        )[0]
        arrived = to_experts(buffers)

        def turn(table):
            return lax.all_to_all(table, "wide", split_axis=0, concat_axis=0, tiled=True)

        arrived_gates = turn(sum(tables))[:, :room].reshape(slots, 1)
        result, arrived_grad, gate_grad, expert_act, expert_inner_grad, slot_grad = call(
            expert, slots // slot_step,
            [(plane, "scalar", 0), (arrived, slot_step, 0), (upstream, slot_step, 0), (arrived_gates, slot_step, 0),
             (expert_in[0], None, 0), (expert_in_bias, None, 0), (expert_out[0], None, 0), (expert_out_bias, None, 0)],
            [((slots, model), BF16, slot_step), ((slots, model), BF16, slot_step), ((slots, 1), F32, slot_step),
             ((slots, hidden), BF16, slot_step), ((slots, hidden), BF16, slot_step), ((slots, model), BF16, slot_step)],
            "expert",
        )
        rows = lax.psum(arrived_grad.astype(F32), "tensor").astype(BF16)
        results = (lax.psum(result.astype(F32), "tensor") + expert_out_bias).astype(BF16)
        gate_grads = jnp.pad(gate_grad.reshape(experts, room), ((0, 0), (0, 128 - room)))
        return (
            [to_experts(rows)], lax.psum(turn(gate_grads), "tensor"), [to_experts(results)],
            dot_columns(arrived, expert_inner_grad), dot_columns(expert_act, slot_grad),
            jnp.sum(expert_inner_grad.astype(F32), axis=0, keepdims=True),
            jnp.sum(slot_grad.astype(F32), axis=0, keepdims=True),
        )

    def fused_experts():
        group = 4
        half = model // 2
        table = ((experts, 8, 128), F32)
        outs = [
            ((slots, half), BF16), ((slots, half), BF16), ((experts, 128), F32), ((slots, half), BF16),
            ((model, hidden), BF16), ((hidden, model), BF16), ((8, hidden), F32), ((8, model), F32),
        ]
        local = [
            ((slots, model), BF16), ((slots, model), BF16), ((slots, hidden), BF16), ((slots, hidden), BF16),
            ((slots, model), BF16), ((slots, half), F32), ((slots, half), BF16), ((slots, half), BF16),
            ((slots, half), F32), ((slots, half), BF16), ((slots, half), BF16), ((slots, half), BF16),
            table, table, table, table, table,
        ]
        own, peer, gate_grads, result, in_grad, out_grad, in_bias, out_bias = pl.pallas_call(
            functools.partial(experts_kernel, wide, room, group),
            out_shape=[jax.ShapeDtypeStruct(shape, dtype) for shape, dtype in outs],
            in_specs=[pl.BlockSpec(memory_space=pltpu.VMEM)] * 10,
            out_specs=[pl.BlockSpec(memory_space=pltpu.VMEM)] * len(outs),
            scratch_shapes=[pltpu.VMEM(shape, dtype) for shape, dtype in local]
            + [pltpu.SemaphoreType.DMA((2, 4 * wide + 3 * (wide // group) + 1))],
            compiler_params=pltpu.CompilerParams(
                vmem_limit_bytes=BIG_VMEM_BYTES, collective_id=2, has_side_effects=True
            ),
            name="experts",
        )(*lowered, targets, *tables, upstream, expert_in[0], expert_in_bias, expert_out[0], expert_out_bias)
        home = to_experts(result)
        return (
            [own, peer], gate_grads, [home, swap(home)], in_grad.astype(F32), out_grad.astype(F32),
            in_bias[:1], out_bias[:1],
        )

    row_pieces, gate_grads, result_pieces, expert_in_grad, expert_out_grad, expert_in_bias_grad, expert_out_bias_grad = (
        fused_experts() if two else plain_experts()
    )
    second_grads, lowered_seconds = [], []
    moe_sums, router_sums = [], []
    for part in range(parts):
        first_step = part * part_steps
        grad, low, sums, router_sum = call(
            functools.partial(settle, pairs), part_steps,
            [(plane, "scalar", 0), (seconds[part], step, 0), (cotangent, step, first_step), (routes[part], step, 0),
             (moe_gain, None, 0), (moe_shift, None, 0), (router_weight, None, 0),
             (choices, step, first_step), (gate_grads, None, 0)]
            + [(piece, None, 0) for piece in row_pieces],
            [((part_rows, model), F32, step), ((part_rows, model), BF16, step), ((8, model), F32, None),
             ((experts, model), F32, None)], "settle",
        )
        second_grads.append(grad)
        lowered_seconds.append(low)
        moe_sums.append(sums)
        router_sums.append(router_sum)
    def over_wide(value):
        return lax.psum(value.astype(BF16), "wide").astype(F32)

    def plain_backward():
        acts, inner_grads, lowered_mids, mid_parts, hidden_sums = [], [], [], [], []
        for part in range(parts):
            act, inner_grad, low, partial, sums = call(
                feed_back, part_steps,
                [(firsts[part], step, 0), (lowered_seconds[part], step, 0), (mid_gain, None, 0), (mid_shift, None, 0),
                 (hidden_weight, None, 0), (hidden_bias, None, 0), (output_weight, None, 0)],
                [((part_rows, hidden), BF16, step), ((part_rows, hidden), BF16, step), ((part_rows, model), BF16, step),
                 ((part_rows, model), BF16, step), ((8, hidden), F32, None)], "feed_back",
            )
            acts.append(act)
            inner_grads.append(inner_grad)
            lowered_mids.append(low)
            mid_parts.append(summands(partial))
            hidden_sums.append(sums)

        def weight_grad(lefts, rights):
            return sum(dot_columns(left, right) for left, right in zip(lefts, rights))

        output_weight_grad = weight_grad(acts, lowered_seconds)
        hidden_weight_grad = weight_grad(lowered_mids, inner_grads)
        first_grads, branch_grads, qkv_grads, lowered_pres, pre_parts, mid_sums, qkv_sums = [], [], [], [], [], [], []
        for part in range(parts):
            first_step = part * part_steps
            first_grad, branch, qkv_grad, low, partial, sums, qkv_sum = call(
                functools.partial(attend_back, pairs, heads), part_steps,
                [(firsts[part], step, 0), (second_grads[part], step, 0), (mid_gain, None, 0), (proj_weight, None, 0),
                 (qkv[part], step, 0), (weight_qkv, None, 0), (tokens_in, step, first_step),
                 (pre_gain, None, 0), (pre_shift, None, 0)]
                + [(partial, step, 0) for partial in mid_parts[part]],
                [((part_rows, model), F32, step), ((part_rows, model), BF16, step), ((part_rows, 3 * width), BF16, step),
                 ((part_rows, model), BF16, step), ((part_rows, model), BF16, step), ((8, model), F32, None),
                 ((8, 3 * width), F32, None)], "attend_back",
            )
            first_grads.append(first_grad)
            branch_grads.append(branch)
            qkv_grads.append(qkv_grad)
            lowered_pres.append(low)
            pre_parts.append(summands(partial))
            mid_sums.append(sums)
            qkv_sums.append(qkv_sum)
        token_grads, pre_sums = [], []
        for part in range(parts):
            first_step = part * part_steps
            grad, sums = call(
                functools.partial(finish, pairs), part_steps,
                [(tokens_in, step, first_step), (pre_gain, None, 0), (first_grads[part], step, 0)]
                + [(partial, step, 0) for partial in pre_parts[part]],
                [((part_rows, model), F32, step), ((8, model), F32, None)], "finish",
            )
            token_grads.append(grad)
            pre_sums.append(sums)
        tokens_grad = jnp.concatenate(token_grads)

        groups = [pre_sums, mid_sums, moe_sums, hidden_sums, qkv_sums, router_sums]
        grads = [
            hidden_weight_grad, output_weight_grad, weight_grad(lowered_pres, qkv_grads),
            weight_grad(contexts, branch_grads),
        ]
        return [tokens_grad] + [over_wide(term) for term in grads + [sum(group) for group in groups]]

    def fused_backward():
        lanes = 3 * width
        layout = [(0, 1), (0, 1, 2), (0, 1, 2), (0,), (0,), tuple(range(experts))]
        vectors = [(8, model), (8, model), (8, model), (8, hidden), (8, lanes)]
        steps = wide.bit_length() - 1
        near, far = tuple(range(steps)), (0,) + tuple(range(2, steps)) + (1,)
        totals = [(model, hidden), (hidden, model), (model, lanes // 2), (model, lanes // 2), (width, model), (16 * wide, 128)]
        local = [
            ((tokens, model), BF16), ((tokens, hidden), BF16), ((tokens, hidden), BF16), ((tokens, model), BF16),
            ((tokens, model), BF16), ((tokens, model), BF16), ((tokens, lanes), BF16), ((tokens, model), BF16),
            ((tokens, model), BF16), ((tokens, model), BF16), ((8, model), F32), ((8, hidden), F32),
            ((8, lanes), F32), ((8, model), F32), (totals[-1], BF16),
        ]
        chunks = tokens // step
        outs = pl.pallas_call(
            functools.partial(backward, wide, heads, layout, (near, far, near, far, near, far), step),
            out_shape=[jax.ShapeDtypeStruct((tokens, model), F32)]
            + [jax.ShapeDtypeStruct(shape, BF16) for shape in totals[:-1]]
            + [jax.ShapeDtypeStruct(shape, F32) for shape in vectors + [(experts, model)]],
            in_specs=[pl.BlockSpec(memory_space=pltpu.VMEM)] * 16,
            out_specs=[pl.BlockSpec(memory_space=pltpu.VMEM)] * 12,
            scratch_shapes=[pltpu.VMEM(shape, dtype) for shape, dtype in local]
            + [pltpu.VMEM(shape, F32) for shape in totals]
            + [pltpu.VMEM(shape, BF16) for shape in totals] * 2
            + [pltpu.SemaphoreType.DMA((2, chunks))] * 2
            + [pltpu.SemaphoreType.DMA((len(totals), 2 * steps))] * 2,
            compiler_params=pltpu.CompilerParams(
                vmem_limit_bytes=BIG_VMEM_BYTES, collective_id=1, has_side_effects=True
            ),
            name="backward",
        )(
            jnp.concatenate(second_grads), jnp.concatenate(firsts), tokens_in, jnp.concatenate(qkv),
            jnp.concatenate(contexts), mid_gain, mid_shift, pre_gain, pre_shift, hidden_weight, hidden_bias,
            output_weight, proj_weight, weight_qkv, sum(moe_sums), sum(router_sums),
        )
        tokens_grad, hidden_g, output_g, left, right, proj_g = outs[:6]
        qkv_g = jnp.concatenate([left, right], axis=1)
        return [tokens_grad] + [grad.astype(F32) for grad in (hidden_g, output_g, qkv_g, proj_g)] + list(outs[6:])

    (tokens_grad, hidden_weight_g, output_weight_g, qkv_weight_g, proj_weight_g, pre, mid, moe, hid, qks, router_g) = (
        fused_backward() if two else plain_backward()
    )
    qks, router_g = qks[0].reshape(3, width), router_g[:experts]

    outs = []
    for part in range(parts):
        first_step = part * part_steps
        outs.append(
            call(
                functools.partial(blend, pairs), part_steps,
                [(plane, "scalar", 0), (seconds[part], step, 0), (gates[part], step, 0), (choices, step, first_step)]
                + [(piece, None, 0) for piece in result_pieces],
                [((part_rows, model), BF16, step)], "blend",
            )[0]
        )
    block_out = jnp.concatenate(outs)

    return (
        block_out,
        tokens_grad,
        pre[0],
        pre[1],
        qkv_weight_g.reshape(model, 3, width),
        jnp.stack([qks[0], qks[2]]),
        proj_weight_g,
        mid[2],
        mid[0],
        mid[1],
        hidden_weight_g,
        hid[0],
        output_weight_g,
        moe[2],
        moe[0],
        moe[1],
        router_g.T,
        expert_in_grad[None],
        expert_in_bias_grad,
        expert_out_grad[None],
        expert_out_bias_grad,
    )


def solution(mesh):
    return jax.shard_map(
        functools.partial(shards, mesh.shape["wide"], mesh.shape["tensor"]),
        mesh=mesh,
        in_specs=(
            P("wide", None), P(), P(), P(None, None, "tensor"), P(None, "tensor"), P("tensor", None), P(), P(), P(),
            P(None, "tensor"), P("tensor"), P("tensor", None), P(), P(), P(), P(),
            P("wide", None, "tensor"), P("wide", "tensor"), P("wide", "tensor", None), P("wide", None),
            P("wide", None), P("wide", None), P("wide", None),
        ),
        out_specs=(
            P("wide", None), P("wide", None), P(), P(), P(None, None, "tensor"), P(None, "tensor"), P("tensor", None),
            P(), P(), P(), P(None, "tensor"), P("tensor"), P("tensor", None), P(), P(), P(), P(),
            P("wide", None, "tensor"), P("wide", "tensor"), P("wide", "tensor", None), P("wide", None),
        ),
        check_vma=False,
    )
```

```python
import functools

import jax
import jax.numpy as jnp
from jax import lax
from jax.experimental import pallas as pl
from jax.experimental.pallas import tpu as pltpu
from jax.sharding import PartitionSpec as P

HEAD_DIM = 64
PATCHES = 144
BF16 = jnp.bfloat16
F32 = jnp.float32
HIGHEST = lax.Precision.HIGHEST
MESH = pl.DeviceIdType.MESH
VMEM_BYTES = 60 * 1024 * 1024


def dot(left, right):
    return jnp.dot(left, right, preferred_element_type=F32)


def dot_rows(left, right):
    return lax.dot_general(left, right, (((1,), (1,)), ((), ())), preferred_element_type=F32)


def dot_columns(left, right, precision=None):
    return lax.dot_general(
        left, right, (((0,), (0,)), ((), ())), precision=precision, preferred_element_type=F32
    )


def normalized(values):
    centered = values - jnp.mean(values, axis=-1, keepdims=True)
    variance = jnp.mean(centered * centered, axis=-1, keepdims=True)
    scale = lax.rsqrt(variance + 1e-06)
    return centered * scale, scale


def norm_back(rows, scale, gain, upstream):
    scaled = upstream * gain
    inward = jnp.mean(scaled, axis=-1, keepdims=True)
    along = jnp.mean(scaled * rows, axis=-1, keepdims=True)
    return scale * (scaled - inward - rows * along)


def gelu_parts(inner):
    square = inner * inner
    bend = jnp.tanh(0.7978845608028654 * inner * (1.0 + 0.044715 * square))
    half = 0.5 * (1.0 + bend)
    slope = half + (0.5 * 0.7978845608028654) * inner * (1.0 - bend * bend) * (
        1.0 + 0.134145 * square
    )
    return inner * half, slope


def gelu(inner):
    return inner * (0.5 * (1.0 + jnp.tanh(0.7978845608028654 * inner * (1.0 + 0.044715 * inner * inner))))


def softmax_rows(scores, scale):
    peak = jnp.max(scores, axis=-1, keepdims=True)
    weights = jnp.exp((scores - peak) * scale)
    return weights * (1.0 / jnp.sum(weights, axis=-1, keepdims=True))


def spots(places):
    lane = lax.broadcasted_iota(jnp.int32, (places.shape[0], 128), 1)
    return [(lane == places[:, j : j + 1]).astype(F32) for j in range(2)]


def bits_of(index, wide):
    return [lax.rem(lax.div(index, 1 << k), 2) for k in range(wide.bit_length() - 1)]


class Sums:
    def __init__(self, wide, orders, totals, sends, lands, gathers, send_sems, recv_sems):
        me, self.plane = lax.axis_index("wide"), lax.axis_index("tensor")
        self.bits = bits_of(me, wide)
        self.partners = [me + (1 - 2 * bit) * (1 << k) for k, bit in enumerate(self.bits)]
        self.steps = len(self.bits)
        self.orders, self.totals, self.sends, self.lands, self.gathers = orders, totals, sends, lands, gathers
        self.send_sems, self.recv_sems = send_sems, recv_sems

    def piece(self, i, step):
        rows = self.gathers[i].shape[0]
        base = 0
        for s in range(step):
            base = base + self.bits[self.orders[i][s]] * (rows >> (s + 1))
        length = rows >> (step + 1)
        bit = self.bits[self.orders[i][step]]
        return pl.multiple_of(base + bit * length, 16), pl.multiple_of(base + (1 - bit) * length, 16), length

    def staged(self, i, step):
        rows = self.gathers[i].shape[0]
        return rows - (rows >> step)

    def transfer(self, i, k):
        step = k if k < self.steps else 2 * self.steps - 1 - k
        kept, _, length = self.piece(i, step)
        if k < self.steps:
            at = self.staged(i, step)
            source, target = self.sends[i].at[pl.ds(at, length)], self.lands[i].at[pl.ds(at, length)]
        else:
            source = target = self.gathers[i].at[pl.ds(kept, length)]
        return pltpu.make_async_remote_copy(
            source, target, self.send_sems.at[i, k], self.recv_sems.at[i, k],
            device_id=(self.partners[self.orders[i][step]], self.plane), device_id_type=MESH,
        )

    def begin(self, i, k):
        if k < self.steps:
            _, other, length = self.piece(i, k)
            at = self.staged(i, k)
            self.sends[i][at : at + length, :] = self.totals[i][pl.ds(other, length), :].astype(BF16)
        self.transfer(i, k).start()

    def advance(self, i, k):
        self.transfer(i, k).wait()
        if k < self.steps:
            kept, _, length = self.piece(i, k)
            at = self.staged(i, k)
            value = self.totals[i][pl.ds(kept, length), :] + self.lands[i][at : at + length, :].astype(F32)
            if k + 1 < self.steps:
                self.totals[i][pl.ds(kept, length), :] = value
            else:
                self.gathers[i][pl.ds(kept, length), :] = value.astype(BF16)
        if k + 1 < 2 * self.steps:
            self.begin(i, k + 1)


def greet(wide):
    me, plane = lax.axis_index("wide"), lax.axis_index("tensor")
    barrier = pltpu.get_barrier_semaphore()

    def hail(d, carry):
        pl.semaphore_signal(barrier, inc=1, device_id=(lax.rem(me + d, wide), plane), device_id_type=MESH)
        return carry

    lax.fori_loop(1, wide, hail, 0)
    pl.semaphore_signal(barrier, inc=1, device_id=(me, 1 - plane), device_id_type=MESH)
    pl.semaphore_wait(barrier, wide)


def put_row(small, at, row):
    for c in range(row.shape[1] // 128):
        small[at + c : at + c + 1, :] = row[:, 128 * c : 128 * (c + 1)]
    return at + row.shape[1] // 128


def get_row(small, at, width):
    return jnp.concatenate([small[at + c : at + c + 1, :] for c in range(width // 128)], axis=1)


def image_back(heads, qkv, context_grad):
    width = heads * HEAD_DIM
    scale = HEAD_DIM**-0.5
    parts = [[], [], []]
    for head in range(heads):
        h = head * HEAD_DIM
        query = qkv[:, h : h + HEAD_DIM]
        keys = qkv[:, width + h : width + h + HEAD_DIM]
        values = qkv[:, 2 * width + h : 2 * width + h + HEAD_DIM]
        upstream = context_grad[:, h : h + HEAD_DIM]
        probs = softmax_rows(dot_rows(query, keys), scale)
        prob_grad = dot_rows(upstream, values)
        inward = jnp.sum(probs * prob_grad, axis=-1, keepdims=True)
        score_grad = (probs * (prob_grad - inward)).astype(BF16)
        parts[0].append(dot(score_grad, keys) * scale)
        parts[1].append(dot_columns(score_grad, query) * scale)
        parts[2].append(dot_columns(probs.astype(BF16), upstream))
    return jnp.concatenate(parts[0] + parts[1] + parts[2], axis=1).astype(BF16)


def column_dots(left, right, put, tile=256):
    def body(i, carry):
        at = pl.multiple_of(i * tile, tile)
        put(at, tile, dot_columns(left[:, pl.ds(at, tile)], right[...]))
        return carry

    lax.fori_loop(0, left.shape[1] // tile, body, 0)


def image_forward(heads, qkv):
    width = heads * HEAD_DIM
    parts = []
    for head in range(heads):
        h = head * HEAD_DIM
        probs = softmax_rows(
            dot_rows(qkv[:, h : h + HEAD_DIM], qkv[:, width + h : width + h + HEAD_DIM]), HEAD_DIM**-0.5
        )
        parts.append(dot(probs.astype(BF16), qkv[:, 2 * width + h : 2 * width + h + HEAD_DIM]))
    return jnp.concatenate(parts, axis=1).astype(BF16)


def token_hits(choices, slots):
    slot = lax.broadcasted_iota(jnp.int32, (choices.shape[0], slots), 1)
    return [slot == choices[:, j : j + 1] for j in range(2)]


def slot_hits(first, count, targets):
    slot = first + lax.broadcasted_iota(jnp.int32, (count, targets.shape[1]), 0)
    return ((slot == targets[0:1, :]) | (slot == targets[1:2, :])).astype(BF16)


def slot_targets(choice_ids, ranks, capacity, room):
    count = choice_ids.shape[1]
    order_keys = jnp.concatenate([ranks, ranks + count])
    flat_ids = choice_ids.reshape(2 * count)
    earlier = (order_keys[None, :] < order_keys[:, None]) & (flat_ids[None, :] == flat_ids[:, None])
    position = jnp.sum(earlier.astype(jnp.int32), axis=1).reshape(2, count)
    kept = position < capacity
    targets = jnp.where(kept, choice_ids * room + position, -1)
    marks = jnp.where(kept, choice_ids, -1)
    places = jnp.where(kept, position, -1)
    return targets, jnp.concatenate([targets, marks, places]).T


def forward(
    wide, room, group, heads, rows,
    tokens, cotangent, targets, choices, pre_gain, pre_shift, weight_qkv, qv_bias, projection, proj_bias,
    mid_gain, mid_shift, hidden, hidden_bias, output, output_bias, moe_gain, moe_shift, router,
    qkv_out, context_out, first_out, second_out, lowered_out, route_out, gates_out, table_out, upstream_out,
    placed, projection_peer, context_peer, partial_own, partial_peer, sems,
):
    me, plane = lax.axis_index("wide"), lax.axis_index("tensor")
    chunks, groups = tokens.shape[0] // rows, wide // group
    mine = lax.div(me, group)
    block = group * room
    width = heads * HEAD_DIM
    row_at, context_at, partial_at, last_at = 0, wide, wide + chunks, wide + 2 * chunks
    greet(wide)

    def rows_of(index):
        return pl.ds(pl.multiple_of(index * room, 16), room)

    def chunk_of(index):
        return pl.ds(pl.multiple_of(index * rows, 16), rows)

    def move(source, target, base, sent, landed, device):
        return pltpu.make_async_remote_copy(
            source, target, sems.at[0, base + sent], sems.at[1, base + landed], device_id=device, device_id_type=MESH
        )

    def across(source, target, base, index):
        there = chunk_of(index)
        return move(source.at[there], target.at[there], base, index, index, (me, 1 - plane))

    def row_copy(other, sender):
        return move(placed.at[rows_of(other)], upstream_out.at[rows_of(sender)], row_at, other, sender, (other, plane))

    weights = move(projection, projection_peer, last_at, 0, 0, (me, 1 - plane))
    weights.start()
    table_out[...] = jnp.zeros_like(table_out)

    def attend_chunk(c):
        there = chunk_of(c)
        normed, _ = normalized(tokens[there, :].astype(F32))
        lowered = (normed * pre_gain[...] + pre_shift[...]).astype(BF16)
        parts = [dot(lowered, weight_qkv[s]) for s in range(3)]
        parts = [parts[0] + qv_bias[0:1, :], parts[1], parts[2] + qv_bias[1:2, :]]
        qkv = jnp.concatenate(parts, axis=1).astype(BF16)
        qkv_out[there, :] = qkv
        contexts = [
            image_forward(heads, qkv[image * PATCHES : (image + 1) * PATCHES]) for image in range(rows // PATCHES)
        ]
        context_out[there, :] = jnp.concatenate(contexts, axis=0)
        across(context_out, context_peer, context_at, c).start()

    def place_group(k):
        q = lax.rem(mine + k, groups)
        hits = slot_hits(q * block, block, targets)
        here = pl.ds(pl.multiple_of(q * block, 16), block)
        placed[here, :] = dot(hits, cotangent[...].astype(BF16)).astype(BF16)
        for j in range(group):
            e = q * group + j

            @pl.when(e != me)
            def _(e=e):
                row_copy(e, me).start()

            @pl.when(e == me)
            def _(e=e):
                upstream_out[rows_of(e), :] = placed[rows_of(e), :]

    def feed_chunk(c):
        there = chunk_of(c)
        across(context_out, context_peer, context_at, c).wait()
        branch = dot(context_out[there, :], projection[...]) + dot(context_peer[there, :], projection_peer[...])
        first = tokens[there, :].astype(F32) + branch + proj_bias[...]
        first_out[there, :] = first
        normed, _ = normalized(first)
        lowered = (normed * mid_gain[...] + mid_shift[...]).astype(BF16)
        activated = gelu(dot(lowered, hidden[...]) + hidden_bias[...]).astype(BF16)
        partial_own[there, :] = dot(activated, output[...]).astype(BF16)
        across(partial_own, partial_peer, partial_at, c).start()

    def route_chunk(c):
        there = chunk_of(c)
        across(partial_own, partial_peer, partial_at, c).wait()
        partial = partial_own[there, :].astype(F32) + partial_peer[there, :].astype(F32)
        second = first_out[there, :] + partial + output_bias[...]
        second_out[there, :] = second
        normed, _ = normalized(second)
        normed = normed * moe_gain[...] + moe_shift[...]
        lowered_out[there, :] = normed.astype(BF16)
        logits = lax.dot_general(
            normed, router[...], (((1,), (1,)), ((), ())), precision=HIGHEST, preferred_element_type=F32
        )
        grown = jnp.exp(logits - jnp.max(logits, axis=-1, keepdims=True))
        route = grown / jnp.sum(grown, axis=-1, keepdims=True)
        route_out[there, :] = route
        number = lax.broadcasted_iota(jnp.int32, route.shape, 1)
        picks = choices[there, :]
        chosen = [jnp.where(number == picks[:, 2 + j : 3 + j], route, 0.0) for j in range(2)]
        gates_out[there, :] = jnp.concatenate([jnp.sum(part, axis=1, keepdims=True) for part in chosen], axis=1)
        for part, spot in zip(chosen, spots(picks[:, 4:6])):
            table_out[...] += dot_columns(part, spot, HIGHEST)

    def turn(c, carry):
        @pl.when(c < chunks)
        def _():
            attend_chunk(c)

        @pl.when(c < groups)
        def _():
            place_group(c)

        @pl.when(c == 1)
        def _():
            weights.wait()

        @pl.when((c >= 1) & (c <= chunks))
        def _():
            feed_chunk(c - 1)

        @pl.when(c >= 2)
        def _():
            route_chunk(c - 2)

        return carry

    lax.fori_loop(0, chunks + 2, turn, 0)

    def take_rows(d, carry):
        other = lax.rem(me + d, wide)
        row_copy(other, other).wait_recv()
        row_copy(other, me).wait_send()
        return carry

    lax.fori_loop(1, wide, take_rows, 0)


def experts(
    wide, room, group,
    lowered, targets, table, upstream, weight_in, bias_in, weight_out, bias_out,
    own_home, peer_home, gate_home, result_out, in_grad, out_grad, in_bias_grad, out_bias_grad,
    placed, arrived, act, inner_grad, slot_grad, grad_kept, grad_sent, grad_landed, result_kept, result_sent,
    result_landed, grad_back, gate_sent, gate_arrived, gate_back, gate_own, gate_peer, sems,
):
    me, plane = lax.axis_index("wide"), lax.axis_index("tensor")
    groups = wide // group
    mine = lax.div(me, group)
    half = own_home.shape[1]
    block = group * room
    row_at, gate_at, home_at, back_at = 0, wide, 2 * wide, 3 * wide
    grad_at, result_at, share_at, table_at = 4 * wide, 4 * wide + groups, 4 * wide + 2 * groups, 4 * wide + 3 * groups

    greet(wide)

    def rows_of(index):
        return pl.ds(pl.multiple_of(index * room, 16), room)

    def rows_of_group(index):
        return pl.ds(pl.multiple_of(index * block, 16), block)

    def move(source, target, base, sent, landed, device):
        return pltpu.make_async_remote_copy(
            source, target, sems.at[0, base + sent], sems.at[1, base + landed], device_id=device, device_id_type=MESH
        )

    def row_copy(other, sender):
        return move(placed.at[rows_of(other)], arrived.at[rows_of(sender)], row_at, other, sender, (other, plane))

    def gate_copy(other, sender):
        return move(gate_sent.at[other], gate_arrived.at[sender], gate_at, other, sender, (other, plane))

    def home_copy(other, sender):
        return move(grad_back.at[rows_of(other)], own_home.at[rows_of(sender)], home_at, other, sender, (other, plane))

    def back_copy(other, sender):
        return move(gate_back.at[other], gate_own.at[sender], back_at, other, sender, (other, plane))

    def across(source, target, base, index):
        there = rows_of_group(index)
        return move(source.at[there], target.at[there], base, index, index, (me, 1 - plane))

    for e in range(wide):
        gate_sent[e] = jnp.broadcast_to(table[e : e + 1, :], gate_sent.shape[1:])
    in_bias_grad[...] = jnp.zeros_like(in_bias_grad)
    out_bias_grad[...] = jnp.zeros_like(out_bias_grad)

    def place_group(k, carry):
        q = lax.rem(mine + k, groups)
        slot = q * block + lax.broadcasted_iota(jnp.int32, (block, targets.shape[1]), 0)
        hits = ((slot == targets[0:1, :]) | (slot == targets[1:2, :])).astype(BF16)
        placed[rows_of_group(q), :] = dot(hits, lowered[...]).astype(BF16)
        for j in range(group):
            e = q * group + j

            @pl.when(e != me)
            def _(e=e):
                row_copy(e, me).start()
                gate_copy(e, me).start()

            @pl.when(e == me)
            def _(e=e):
                arrived[rows_of(e), :] = placed[rows_of(e), :]
                gate_arrived[e] = gate_sent[e]

        return carry

    lax.fori_loop(0, groups, place_group, 0)
    diagonal = lax.broadcasted_iota(jnp.int32, (room, 128), 0) == lax.broadcasted_iota(jnp.int32, (room, 128), 1)
    first_plane = plane == 0

    def give_back(p):
        across(grad_sent, grad_landed, grad_at, p).wait()
        there = rows_of_group(p)
        grad_back[there, :] = (grad_kept[there, :] + grad_landed[there, :].astype(F32)).astype(BF16)
        for j in range(group):
            w = p * group + j

            @pl.when(w != me)
            def _(w=w):
                home_copy(w, me).start()

            @pl.when(w == me)
            def _(w=w):
                own_home[rows_of(w), :] = grad_back[rows_of(w), :]

    def expert_group(k, carry):
        p = lax.rem(mine + groups - k, groups)
        there = rows_of_group(p)
        columns = []
        for j in range(group):
            w = p * group + j

            @pl.when(w != me)
            def _(w=w):
                row_copy(w, w).wait_recv()
                gate_copy(w, w).wait_recv()

            columns.append(jnp.sum(jnp.where(diagonal, gate_arrived[w][0:1, :], 0.0), axis=1, keepdims=True))
        gates = jnp.concatenate(columns, axis=0)
        inner = dot(arrived[there, :], weight_in[...]) + bias_in[...]
        acted, slope = gelu_parts(inner)
        acted = acted.astype(BF16)
        act[there, :] = acted
        result = dot(acted, weight_out[...])
        raised = upstream[there, :].astype(F32)
        slot = (raised * gates).astype(BF16)
        slot_grad[there, :] = slot
        out_bias_grad[0:1, :] += jnp.sum(slot.astype(F32), axis=0, keepdims=True)
        inward = (dot_rows(slot, weight_out[...]) * slope).astype(BF16)
        inner_grad[there, :] = inward
        in_bias_grad[0:1, :] += jnp.sum(inward.astype(F32), axis=0, keepdims=True)
        grad = dot_rows(inward, weight_in[...])
        low, high = grad[:, :half], grad[:, half:]
        grad_sent[there, :] = jnp.where(first_plane, high, low).astype(BF16)
        across(grad_sent, grad_landed, grad_at, p).start()
        grad_kept[there, :] = jnp.where(first_plane, low, high)
        biased = result + bias_out[...]
        low, high = biased[:, :half], biased[:, half:]
        result_kept[there, :] = jnp.where(first_plane, low, high)
        low, high = result[:, :half], result[:, half:]
        result_sent[there, :] = jnp.where(first_plane, high, low).astype(BF16)
        across(result_sent, result_landed, result_at, p).start()
        slopes = jnp.sum(raised * jnp.where(first_plane, biased, result), axis=1, keepdims=True)
        for j in range(group):
            w = p * group + j
            row = jnp.sum(
                jnp.where(diagonal, slopes[j * room : (j + 1) * room], 0.0), axis=0, keepdims=True
            )
            gate_back[w] = jnp.broadcast_to(row, gate_back.shape[1:])

            @pl.when(w != me)
            def _(w=w):
                back_copy(w, me).start()

            @pl.when(w == me)
            def _(w=w):
                gate_own[w] = gate_back[w]

        @pl.when(k > 0)
        def _():
            give_back(lax.rem(mine + groups - k + 1, groups))

        return carry

    lax.fori_loop(0, groups, expert_group, 0)
    give_back(lax.rem(mine + 1, groups))

    tile = act.shape[1] // groups

    def share_group(k, carry):
        at = pl.multiple_of(k * tile, 128)
        out_grad[pl.ds(at, tile), :] = dot_columns(act[:, pl.ds(at, tile)], slot_grad[...]).astype(BF16)
        q = lax.rem(mine + k, groups)
        for j in range(group):
            e = q * group + j

            @pl.when(e != me)
            def _(e=e):
                home_copy(e, e).wait_recv()

        across(own_home, peer_home, share_at, q).start()
        return carry

    lax.fori_loop(0, groups, share_group, 0)

    def take_gates(d, carry):
        back_copy(lax.rem(me + d, wide), lax.rem(me + d, wide)).wait_recv()
        return carry

    lax.fori_loop(1, wide, take_gates, 0)
    tables = move(gate_own, gate_peer, table_at, 0, 0, (me, 1 - plane))
    tables.start()

    def put(at, tile, value):
        in_grad[pl.ds(at, tile), :] = value.astype(BF16)

    column_dots(arrived, inner_grad, put)

    def take_result(p, carry):
        across(result_sent, result_landed, result_at, p).wait()
        there = rows_of_group(p)
        result_out[there, :] = (result_kept[there, :] + result_landed[there, :].astype(F32)).astype(BF16)
        return carry

    lax.fori_loop(0, groups, take_result, 0)

    def end_sends(d, carry):
        other = lax.rem(me + d, wide)
        row_copy(other, me).wait_send()
        gate_copy(other, me).wait_send()
        home_copy(other, me).wait_send()
        back_copy(other, me).wait_send()
        return carry

    lax.fori_loop(1, wide, end_sends, 0)
    tables.wait()
    for e in range(wide):
        gate_home[e : e + 1, :] = gate_own[e][0:1, :] + gate_peer[e][0:1, :]

    def end_share(q, carry):
        across(own_home, peer_home, share_at, q).wait()
        return carry

    lax.fori_loop(0, groups, end_share, 0)


def backward(
    wide, room, heads, layout, orders, rows,
    second, cotangent, route, choices, gates, moe_gain, moe_shift, router, gate_grads, row_own, row_peer, result,
    first, tokens, qkv, context, mid_gain, mid_shift, pre_gain, pre_shift, hidden, hidden_bias, output, projection,
    weight_qkv,
    block_out, grad_out, hidden_out, output_out, qkv_out, proj_out, *rest,
):
    vectors_out, rest = rest[: len(layout)], rest[len(layout) :]
    (lowered_mid, act, inner_grad, mid_own, mid_peer, branch, qkv_grad, lowered_pre, pre_peer, result_own, result_peer,
     moe_sums, router_sums, mid_sums, hidden_sums, qkv_sums, pre_sums, small_sums) = rest[:18]
    hidden_total, output_total, qkv_total, proj_total, small = rest[18:23]
    sends, lands = rest[23:29], rest[29:35]
    mid_sems, pre_sems, result_sems, send_sems, recv_sems = rest[35:]
    me, plane = lax.axis_index("wide"), lax.axis_index("tensor")
    chunks = tokens.shape[0] // rows
    model = tokens.shape[1]
    width = heads * HEAD_DIM
    split = qkv_total.shape[0] // 2
    totals = (
        hidden_total, output_total, qkv_total.at[pl.ds(0, split)], qkv_total.at[pl.ds(split, split)], proj_total, small
    )
    gathers = (
        hidden_out, output_out, qkv_out.at[pl.ds(0, split)], qkv_out.at[pl.ds(split, split)], proj_out, small_sums
    )
    greet(wide)
    sums = Sums(wide, orders, totals, sends, lands, gathers, send_sems, recv_sems)

    def rows_of(index):
        return pl.ds(pl.multiple_of(index * room, 16), room)

    def result_copy(other, sender):
        return pltpu.make_async_remote_copy(
            result.at[rows_of(other)], result_own.at[rows_of(sender)], result_sems.at[0, other],
            result_sems.at[1, sender], device_id=(other, plane), device_id_type=MESH,
        )

    def send_result(d, carry):
        result_copy(lax.rem(me + d, wide), me).start()
        return carry

    lax.fori_loop(1, wide, send_result, 0)
    result_own[rows_of(me), :] = result[rows_of(me), :]

    def across(own, peer, sems, chunk):
        at = pl.multiple_of(chunk * rows, rows)
        return pltpu.make_async_remote_copy(
            own.at[pl.ds(at, rows)], peer.at[pl.ds(at, rows)], sems.at[0, chunk], sems.at[1, chunk],
            device_id=(me, 1 - plane), device_id_type=MESH,
        )

    for vector in (moe_sums, router_sums, mid_sums, hidden_sums, qkv_sums, pre_sums):
        vector[...] = jnp.zeros_like(vector)
    first_plane = plane == 0

    def ordered(own, peer):
        return jnp.concatenate([jnp.where(first_plane, own, peer), jnp.where(first_plane, peer, own)], axis=1)

    def settle(here):
        picks = choices[here, :]
        hits = token_hits(picks, row_own.shape[0])
        table = (hits[0] | hits[1]).astype(BF16)
        moe_grad = ordered(dot(table, row_own[...]), dot(table, row_peer[...]))
        chances = route[here, :]
        number = lax.broadcasted_iota(jnp.int32, chances.shape, 1)
        route_grad = jnp.zeros_like(chances)
        for j, spot in enumerate(spots(picks[:, 4:6])):
            at_place = lax.dot_general(
                spot, gate_grads[...], (((1,), (1,)), ((), ())), precision=HIGHEST, preferred_element_type=F32
            )
            route_grad = route_grad + jnp.where(number == picks[:, 2 + j : 3 + j], at_place, 0.0)
        logit_grad = chances * (route_grad - jnp.sum(chances * route_grad, axis=1, keepdims=True))
        normed, scale = normalized(second[here, :])
        router_sums[...] += dot_columns(logit_grad, normed * moe_gain[...] + moe_shift[...], HIGHEST)
        moe_grad = moe_grad + jnp.dot(logit_grad, router[...], precision=HIGHEST, preferred_element_type=F32)
        grad = cotangent[here, :] + norm_back(normed, scale, moe_gain[...], moe_grad)
        grad_out[here, :] = grad
        branch[here, :] = grad.astype(BF16)
        moe_sums[0:1, :] += jnp.sum(moe_grad * normed, axis=0, keepdims=True)
        moe_sums[1:2, :] += jnp.sum(moe_grad, axis=0, keepdims=True)
        moe_sums[2:3, :] += jnp.sum(grad, axis=0, keepdims=True)

    def feed_chunk(chunk, carry):
        here = pl.ds(pl.multiple_of(chunk * rows, rows), rows)
        settle(here)
        normed, _ = normalized(first[here, :])
        lowered = (normed * mid_gain[...] + mid_shift[...]).astype(BF16)
        lowered_mid[here, :] = lowered
        acted, slope = gelu_parts(dot(lowered, hidden[...]) + hidden_bias[...])
        act[here, :] = acted.astype(BF16)
        inward = (dot_rows(branch[here, :], output[...]) * slope).astype(BF16)
        inner_grad[here, :] = inward
        hidden_sums[0:1, :] += jnp.sum(inward.astype(F32), axis=0, keepdims=True)
        mid_own[here, :] = dot_rows(inward, hidden[...]).astype(BF16)
        across(mid_own, mid_peer, mid_sems, chunk).start()
        return carry

    lax.fori_loop(0, chunks, feed_chunk, 0)

    def put_in(total):
        def put(at, tile, value):
            total[pl.ds(at, tile), :] = value

        return put

    column_dots(lowered_mid, inner_grad, put_in(hidden_total))
    sums.begin(0, 0)
    column_dots(act, branch, put_in(output_total))
    sums.begin(1, 0)

    def attend_chunk(chunk, carry):
        here = pl.ds(pl.multiple_of(chunk * rows, rows), rows)
        across(mid_own, mid_peer, mid_sems, chunk).wait()
        mid_grad = mid_own[here, :].astype(F32) + mid_peer[here, :].astype(F32)
        normed, scale = normalized(first[here, :])
        first_grad = grad_out[here, :] + norm_back(normed, scale, mid_gain[...], mid_grad)
        grad_out[here, :] = first_grad
        lowered_grad = first_grad.astype(BF16)
        branch[here, :] = lowered_grad
        mid_sums[0:1, :] += jnp.sum(mid_grad * normed, axis=0, keepdims=True)
        mid_sums[1:2, :] += jnp.sum(mid_grad, axis=0, keepdims=True)
        mid_sums[2:3, :] += jnp.sum(first_grad, axis=0, keepdims=True)
        normed, _ = normalized(tokens[here, :].astype(F32))
        lowered_pre[here, :] = (normed * pre_gain[...] + pre_shift[...]).astype(BF16)
        context_grad = dot_rows(lowered_grad, projection[...]).astype(BF16)
        for image in range(rows // PATCHES):
            at = pl.multiple_of(chunk * rows + image * PATCHES, PATCHES)
            block = qkv[pl.ds(at, PATCHES), :]
            grad = image_back(heads, block, context_grad[image * PATCHES : (image + 1) * PATCHES])
            qkv_grad[pl.ds(at, PATCHES), :] = grad
            pre = sum(dot_rows(grad[:, s * width : (s + 1) * width], weight_qkv[s]) for s in range(3))
            mid_own[pl.ds(at, PATCHES), :] = pre.astype(BF16)
            qkv_sums[0:1, :] += jnp.sum(grad.astype(F32), axis=0, keepdims=True)
            for k in range(sums.steps):

                @pl.when(chunk == k)
                def _(i=image, k=k):
                    if i < 2:
                        sums.advance(i, k)

        across(mid_own, pre_peer, pre_sems, chunk).start()
        return carry

    lax.fori_loop(0, chunks, attend_chunk, 0)

    def take_result(d, carry):
        other = lax.rem(me + d, wide)
        result_copy(other, other).wait_recv()
        result_copy(other, me).wait_send()
        return carry

    lax.fori_loop(1, wide, take_result, 0)
    share = pltpu.make_async_remote_copy(
        result_own, result_peer, result_sems.at[0, wide], result_sems.at[1, wide],
        device_id=(me, 1 - plane), device_id_type=MESH,
    )
    share.start()
    column_dots(context, branch, put_in(proj_total))
    sums.begin(4, 0)

    def put_thirds(at, tile, value):
        for s in range(3):
            there = pl.ds(pl.multiple_of(s * model + at, 16), tile)
            qkv_total[there, :] = value[:, s * width : (s + 1) * width]

    column_dots(lowered_pre, qkv_grad, put_thirds)
    sums.begin(2, 0)
    sums.begin(3, 0)

    def finish_chunk(chunk, carry):
        here = pl.ds(pl.multiple_of(chunk * rows, rows), rows)
        across(mid_own, pre_peer, pre_sems, chunk).wait()
        upstream = mid_own[here, :].astype(F32) + pre_peer[here, :].astype(F32)
        normed, scale = normalized(tokens[here, :].astype(F32))
        grad_out[here, :] += norm_back(normed, scale, pre_gain[...], upstream)
        pre_sums[0:1, :] += jnp.sum(upstream * normed, axis=0, keepdims=True)
        pre_sums[1:2, :] += jnp.sum(upstream, axis=0, keepdims=True)
        return carry

    lax.fori_loop(0, chunks, finish_chunk, 0)
    small[...] = jnp.zeros_like(small)
    at = 0
    for vector, picked in zip((pre_sums, mid_sums, moe_sums, hidden_sums, qkv_sums, router_sums), layout):
        for r in picked:
            at = put_row(small, at, vector[r : r + 1, :])
    sums.begin(5, 0)

    def blend(chunk, carry):
        here = pl.ds(pl.multiple_of(chunk * rows, rows), rows)
        mixture = second[here, :]
        for j, hit in enumerate(token_hits(choices[here, :], result_own.shape[0])):
            table = hit.astype(BF16)
            picked = ordered(dot(table, result_own[...]), dot(table, result_peer[...]))
            mixture = mixture + gates[here, j : j + 1] * picked
        block_out[here, :] = mixture.astype(BF16)
        return carry

    for k in range(2 * sums.steps):
        if k < sums.steps:
            for i in (0, 1):
                sums.advance(i, sums.steps + k)
        for i in (4, 2, 3, 5):
            sums.advance(i, k)
        if k == sums.steps - 1:
            share.wait()
        if k >= sums.steps - 1:
            first_chunk = (k - sums.steps + 1) * chunks // (sums.steps + 1)
            lax.fori_loop(first_chunk, (k - sums.steps + 2) * chunks // (sums.steps + 1), blend, 0)
    at = 0
    for out, picked in zip(vectors_out, layout):
        for i in range(len(picked)):
            out[i : i + 1, :] = get_row(small_sums, at, out.shape[1]).astype(F32)
            at += out.shape[1] // 128


def widen(pairs, layout, *refs):
    ins, outs = refs[: pairs + len(layout)], refs[pairs + len(layout) :]
    for source, out in zip(ins[:pairs], outs[:pairs]):
        out[...] = source[...].astype(out.dtype)
    outs = iter(outs[pairs:])
    for source, picked in zip(ins[pairs:], layout):
        for r in picked:
            out = next(outs)
            out[...] = source[r : r + out.shape[0], : out.shape[1]]


def shards(
    wide,
    tokens_in, pre_gain, pre_shift, qkv_weight, qv_bias, proj_weight, proj_bias, mid_gain, mid_shift,
    hidden_weight, hidden_bias, output_weight, output_bias, moe_gain, moe_shift, router_weight,
    expert_in, expert_in_bias, expert_out, expert_out_bias, expert_ids, priority, cotangent,
):
    tokens, model = tokens_in.shape
    width = qkv_weight.shape[2]
    heads = width // HEAD_DIM
    hidden = hidden_weight.shape[1]
    count = router_weight.shape[1]
    capacity = tokens // count
    room = -(-capacity // 16) * 16
    slots = count * room
    half = model // 2
    lanes = 3 * width
    rows = 2 * PATCHES
    chunks = tokens // rows
    group = 4
    steps = wide.bit_length() - 1

    def row(vector):
        return vector.reshape(1, -1)

    def remote(kernel, name, identity, ins, outs, scratch):
        return pl.pallas_call(
            kernel,
            out_shape=[jax.ShapeDtypeStruct(shape, dtype) for shape, dtype in outs],
            in_specs=[pl.BlockSpec(memory_space=pltpu.VMEM)] * len(ins),
            out_specs=[pl.BlockSpec(memory_space=pltpu.VMEM)] * len(outs),
            scratch_shapes=scratch,
            compiler_params=pltpu.CompilerParams(
                vmem_limit_bytes=VMEM_BYTES, collective_id=identity, has_side_effects=True
            ),
            name=name,
        )(*ins)

    def room_for(local):
        return [pltpu.VMEM(shape, dtype) for shape, dtype in local]

    pre_gain, pre_shift, proj_bias = row(pre_gain), row(pre_shift), row(proj_bias)
    mid_gain, mid_shift, hidden_bias = row(mid_gain), row(mid_shift), row(hidden_bias)
    output_bias, moe_gain, moe_shift = row(output_bias), row(moe_gain), row(moe_shift)
    weight_qkv = qkv_weight.transpose(1, 0, 2)
    router = router_weight.T
    targets, choices = slot_targets(expert_ids.T, priority[0], capacity, room)

    qkv, context, first, second, lowered, route, gates, table, upstream = remote(
        functools.partial(forward, wide, room, group, heads, rows), "forward", 1,
        [tokens_in, cotangent, targets, choices, pre_gain, pre_shift, weight_qkv, qv_bias, proj_weight, proj_bias,
         mid_gain, mid_shift, hidden_weight, hidden_bias, output_weight, output_bias, moe_gain, moe_shift, router],
        [((tokens, lanes), BF16), ((tokens, width), BF16), ((tokens, model), F32), ((tokens, model), F32),
         ((tokens, model), BF16), ((tokens, count), F32), ((tokens, 2), F32), ((count, 128), F32), ((slots, model), BF16)],
        room_for([((slots, model), BF16), ((width, model), BF16), ((tokens, width), BF16), ((tokens, model), BF16),
                  ((tokens, model), BF16)]) + [pltpu.SemaphoreType.DMA((2, wide + 2 * chunks + 1))],
    )

    tables = [((count, 8, 128), F32)] * 5
    row_own, row_peer, gate_grads, result, in_grad, out_grad, in_bias, out_bias = remote(
        functools.partial(experts, wide, room, group), "experts", 2,
        [lowered, targets, table, upstream, expert_in[0], expert_in_bias, expert_out[0], expert_out_bias],
        [((slots, half), BF16), ((slots, half), BF16), ((count, 128), F32), ((slots, half), BF16),
         ((model, hidden), BF16), ((hidden, model), BF16), ((8, hidden), F32), ((8, model), F32)],
        room_for([((slots, model), BF16), ((slots, model), BF16), ((slots, hidden), BF16), ((slots, hidden), BF16),
                  ((slots, model), BF16), ((slots, half), F32), ((slots, half), BF16), ((slots, half), BF16),
                  ((slots, half), F32), ((slots, half), BF16), ((slots, half), BF16), ((slots, half), BF16)] + tables)
        + [pltpu.SemaphoreType.DMA((2, 4 * wide + 3 * (wide // group) + 1))],
    )

    layout = [(0, 1), (0, 1, 2), (0, 1, 2), (0,), (0,), tuple(range(count))]
    vectors = [((8, model), F32), ((8, model), F32), ((8, model), F32), ((8, hidden), F32), ((8, lanes), F32), ((count, model), F32)]
    near, far = tuple(range(steps)), (0,) + tuple(range(2, steps)) + (1,)
    summed = [(model, hidden), (hidden, model), (3 * model // 2, width), (3 * model // 2, width), (width, model), (16 * wide, 128)]
    block_out, grad, hidden_g, output_g, qkv_g, proj_g, *sums = remote(
        functools.partial(backward, wide, room, heads, layout, (near, far, near, far, near, far), rows), "backward", 3,
        [second, cotangent, route, choices, gates, moe_gain, moe_shift, router, gate_grads, row_own, row_peer, result,
         first, tokens_in, qkv, context, mid_gain, mid_shift, pre_gain, pre_shift, hidden_weight, hidden_bias,
         output_weight, proj_weight, weight_qkv],
        [((tokens, model), BF16), ((tokens, model), F32), ((model, hidden), BF16), ((hidden, model), BF16),
         ((3 * model, width), BF16), ((width, model), BF16)] + vectors,
        room_for([((tokens, model), BF16), ((tokens, hidden), BF16), ((tokens, hidden), BF16), ((tokens, model), BF16),
                  ((tokens, model), BF16), ((tokens, model), BF16), ((tokens, lanes), BF16), ((tokens, model), BF16),
                  ((tokens, model), BF16), ((slots, half), BF16), ((slots, half), BF16), ((8, model), F32),
                  ((count, model), F32), ((8, model), F32), ((8, hidden), F32), ((8, lanes), F32), ((8, model), F32),
                  (summed[-1], BF16), (summed[0], F32), (summed[1], F32), ((3 * model, width), F32), (summed[4], F32),
                  (summed[5], F32)] + [(shape, BF16) for shape in summed] * 2)
        + [pltpu.SemaphoreType.DMA((2, chunks))] * 2 + [pltpu.SemaphoreType.DMA((2, wide + 1))]
        + [pltpu.SemaphoreType.DMA((len(summed), 2 * steps))] * 2,
    )

    pairs = [
        (block_out, BF16), (grad, F32), (hidden_g, F32), (output_g, F32), (qkv_g.reshape(3, model, width), F32),
        (proj_g, F32), (in_grad, F32), (out_grad, F32),
    ]
    singles = [(0, 1), (0, 1, 2), (0, 1, 2), (0,), (0,), (0,), (0,), (0,)]
    sources = list(sums) + [in_bias, out_bias]
    sizes = [(1, model)] * 8 + [(1, hidden), (1, lanes), (count, model), (1, hidden), (1, model)]
    parts = 4

    def spec(shape):
        if len(shape) == 3:
            return pl.BlockSpec((shape[0], shape[1] // parts, shape[2]), lambda i: (0, i, 0))
        return pl.BlockSpec((shape[0] // parts, shape[1]), lambda i: (i, 0))

    def whole(shape):
        return pl.BlockSpec(shape, lambda i: (0, 0))

    outs = pl.pallas_call(
        functools.partial(widen, len(pairs), singles),
        grid=(parts,),
        in_specs=[spec(source.shape) for source, _ in pairs] + [whole(source.shape) for source in sources],
        out_specs=[spec(source.shape) for source, _ in pairs] + [whole(size) for size in sizes],
        out_shape=[jax.ShapeDtypeStruct(source.shape, dtype) for source, dtype in pairs]
        + [jax.ShapeDtypeStruct(size, F32) for size in sizes],
        compiler_params=pltpu.CompilerParams(vmem_limit_bytes=VMEM_BYTES),
        name="widen",
    )(*[source for source, _ in pairs], *sources)
    block_out, grad, hidden_g, output_g, qkv_g, proj_g, in_grad, out_grad = outs[:8]
    pre_gain_g, pre_shift_g, mid_gain_g, mid_shift_g, proj_bias_g, moe_gain_g, moe_shift_g, output_bias_g = (
        vector.reshape(model) for vector in outs[8:16]
    )
    hidden_bias_g, qkv_bias_g, router_g, in_bias_g, out_bias_g = outs[16:]
    return (
        block_out, grad, pre_gain_g, pre_shift_g, qkv_g.transpose(1, 0, 2),
        jnp.concatenate([qkv_bias_g[:, :width], qkv_bias_g[:, 2 * width :]]), proj_g, proj_bias_g, mid_gain_g,
        mid_shift_g, hidden_g, hidden_bias_g.reshape(hidden), output_g, output_bias_g, moe_gain_g, moe_shift_g,
        router_g.T, in_grad[None], in_bias_g, out_grad[None], out_bias_g,
    )


def layer_norm(values, gain, shift):
    centered = values - jnp.mean(values, axis=-1, keepdims=True)
    variance = jnp.mean(centered * centered, axis=-1, keepdims=True)
    return centered * lax.rsqrt(variance + 1e-06) * gain + shift


def norm_grad(values, gain, shift, upstream):
    _, pullback = jax.vjp(layer_norm, values, gain, shift)
    return pullback(upstream)


def gelu_grad(inner, upstream):
    _, pullback = jax.vjp(jax.nn.gelu, inner)
    return pullback(upstream)[0]


def slot_tables(choice_ids, ranks, capacity, experts):
    count = choice_ids.shape[0]
    order_keys = jnp.concatenate([ranks, ranks + count])
    flat_ids = jnp.concatenate([choice_ids[:, 0], choice_ids[:, 1]])
    earlier = (order_keys[None, :] < order_keys[:, None]) & (flat_ids[None, :] == flat_ids[:, None])
    position = jnp.sum(earlier.astype(jnp.int32), axis=1)
    kept = position < capacity
    position = position.reshape(2, count)
    kept = kept.reshape(2, count)
    columns = jnp.arange(experts * capacity, dtype=jnp.int32)
    target = choice_ids.T * capacity + position
    tables = (target[:, :, None] == columns[None, None, :]) & kept[:, :, None]
    return (tables, kept)


def plain(
    tokens_in,
    pre_gain,
    pre_shift,
    qkv_weight,
    qv_bias,
    proj_weight,
    proj_bias,
    mid_gain,
    mid_shift,
    hidden_weight,
    hidden_bias,
    output_weight,
    output_bias,
    moe_gain,
    moe_shift,
    router_weight,
    expert_in,
    expert_in_bias,
    expert_out,
    expert_out_bias,
    expert_ids,
    priority,
    cotangent,
):
    tokens = tokens_in.shape[0]
    model_width = tokens_in.shape[1]
    local_heads = qkv_weight.shape[2] // HEAD_DIM
    images = tokens // PATCHES
    experts = router_weight.shape[1]
    capacity = tokens // experts
    score_scale = float(HEAD_DIM) ** (-0.5)
    highest = lax.Precision.HIGHEST
    residual = tokens_in.astype(jnp.float32)
    normed_pre = layer_norm(residual, pre_gain, pre_shift)
    lowered_pre = normed_pre.astype(jnp.bfloat16)
    blank = jnp.zeros_like(qv_bias[0])
    qkv_shift = jnp.stack([qv_bias[0], blank, qv_bias[1]])
    qkv = (
        jnp.einsum("td,dsk->tsk", lowered_pre, qkv_weight, preferred_element_type=jnp.float32)
        + qkv_shift
    ).astype(jnp.bfloat16)
    grid = qkv.reshape(images, PATCHES, 3, local_heads, HEAD_DIM)
    query, keys, values = (grid[:, :, 0], grid[:, :, 1], grid[:, :, 2])
    scores = (
        jnp.einsum("bqhd,bkhd->bhqk", query, keys, preferred_element_type=jnp.float32) * score_scale
    )
    log_total = jax.nn.logsumexp(scores, axis=-1, keepdims=True)
    weights = jnp.exp(scores - log_total).astype(jnp.bfloat16)
    context = jnp.einsum("bhqk,bkhd->bqhd", weights, values, preferred_element_type=jnp.float32)
    context = context.astype(jnp.bfloat16).reshape(tokens, local_heads * HEAD_DIM)
    branch = lax.psum(jnp.dot(context, proj_weight, preferred_element_type=jnp.float32), "tensor")
    first = residual + branch + proj_bias
    normed_mid = layer_norm(first, mid_gain, mid_shift)
    lowered_mid = normed_mid.astype(jnp.bfloat16)
    inner = jnp.dot(lowered_mid, hidden_weight, preferred_element_type=jnp.float32) + hidden_bias
    activated = jax.nn.gelu(inner).astype(jnp.bfloat16)
    partial_out = jnp.dot(activated, output_weight, preferred_element_type=jnp.float32)
    second = first + lax.psum(partial_out, "tensor") + output_bias
    normed_moe = layer_norm(second, moe_gain, moe_shift)
    lowered_moe = normed_moe.astype(jnp.bfloat16)
    route = jax.nn.softmax(jnp.dot(normed_moe, router_weight, precision=highest), axis=-1)
    tables, kept = slot_tables(expert_ids, priority[0], capacity, experts)
    tables = tables.astype(jnp.bfloat16)
    dispatch = tables[0] + tables[1]
    buffers = jnp.einsum("tk,td->kd", dispatch, lowered_moe, preferred_element_type=jnp.float32)
    buffers = buffers.astype(jnp.bfloat16).reshape(experts, capacity, model_width)
    arrived = lax.all_to_all(buffers, "wide", split_axis=0, concat_axis=1, tiled=True)
    expert_inner = (
        jnp.einsum("erd,edf->erf", arrived, expert_in, preferred_element_type=jnp.float32)
        + expert_in_bias[:, None, :]
    )
    expert_act = jax.nn.gelu(expert_inner).astype(jnp.bfloat16)
    expert_partial = jnp.einsum(
        "erf,efd->erd", expert_act, expert_out, preferred_element_type=jnp.float32
    )
    expert_result = (
        lax.psum(expert_partial.astype(jnp.bfloat16), "tensor").astype(jnp.float32)
        + expert_out_bias[:, None, :]
    ).astype(jnp.bfloat16)
    returned = lax.all_to_all(
        expert_result, "wide", split_axis=1, concat_axis=0, tiled=True
    ).reshape(experts * capacity, model_width)
    picked = jnp.einsum("jtk,kd->jtd", tables, returned, preferred_element_type=jnp.float32)
    expert_range = jnp.arange(experts, dtype=jnp.int32)
    chosen = (expert_ids.T[:, :, None] == expert_range[None, None, :]).astype(jnp.float32) * kept[
        :, :, None
    ].astype(jnp.float32)
    gates = jnp.sum(chosen * route[None], axis=-1)
    mixture = jnp.sum(gates[:, :, None] * picked, axis=0)
    block_out = (second + mixture).astype(jnp.bfloat16)
    gate_grad = jnp.sum(picked * cotangent[None], axis=-1)
    weighted = (gates[:, :, None] * cotangent[None]).astype(jnp.bfloat16)
    slot_grad = jnp.einsum("jtk,jtd->kd", tables, weighted, preferred_element_type=jnp.float32)
    slot_grad = slot_grad.astype(jnp.bfloat16).reshape(experts, capacity, model_width)
    result_grad = lax.all_to_all(slot_grad, "wide", split_axis=0, concat_axis=1, tiled=True)
    expert_out_bias_grad = jnp.sum(result_grad.astype(jnp.float32), axis=1)
    expert_out_grad = jnp.einsum(
        "erf,erd->efd", expert_act, result_grad, preferred_element_type=jnp.float32
    )
    act_grad = jnp.einsum(
        "erd,efd->erf", result_grad, expert_out, preferred_element_type=jnp.float32
    )
    expert_inner_grad = gelu_grad(expert_inner, act_grad).astype(jnp.bfloat16)
    expert_in_bias_grad = jnp.sum(expert_inner_grad.astype(jnp.float32), axis=1)
    expert_in_grad = jnp.einsum(
        "erd,erf->edf", arrived, expert_inner_grad, preferred_element_type=jnp.float32
    )
    arrived_partial = jnp.einsum(
        "erf,edf->erd", expert_inner_grad, expert_in, preferred_element_type=jnp.float32
    )
    arrived_grad = lax.psum(arrived_partial.astype(jnp.bfloat16), "tensor")
    buffer_grad = lax.all_to_all(
        arrived_grad, "wide", split_axis=1, concat_axis=0, tiled=True
    ).reshape(experts * capacity, model_width)
    moe_input_grad = jnp.dot(dispatch, buffer_grad, preferred_element_type=jnp.float32)
    route_grad = jnp.sum(gate_grad[:, :, None] * chosen, axis=0)
    logit_grad = route * (route_grad - jnp.sum(route * route_grad, axis=-1, keepdims=True))
    router_grad = jnp.einsum("td,te->de", normed_moe, logit_grad, precision=highest)
    moe_input_grad = moe_input_grad + jnp.einsum(
        "te,de->td", logit_grad, router_weight, precision=highest
    )
    second_part, moe_gain_grad, moe_shift_grad = norm_grad(
        second, moe_gain, moe_shift, moe_input_grad
    )
    second_grad = cotangent + second_part
    lowered_second = second_grad.astype(jnp.bfloat16)
    output_bias_grad = jnp.sum(second_grad, axis=0)
    output_weight_grad = jnp.einsum(
        "tf,td->fd", activated, lowered_second, preferred_element_type=jnp.float32
    )
    activated_grad = jnp.einsum(
        "td,fd->tf", lowered_second, output_weight, preferred_element_type=jnp.float32
    )
    inner_grad = gelu_grad(inner, activated_grad).astype(jnp.bfloat16)
    hidden_bias_grad = jnp.sum(inner_grad.astype(jnp.float32), axis=0)
    hidden_weight_grad = jnp.einsum(
        "td,tf->df", lowered_mid, inner_grad, preferred_element_type=jnp.float32
    )
    mid_partial = jnp.einsum(
        "tf,df->td", inner_grad, hidden_weight, preferred_element_type=jnp.float32
    )
    mid_grad = lax.psum(mid_partial, "tensor")
    first_part, mid_gain_grad, mid_shift_grad = norm_grad(first, mid_gain, mid_shift, mid_grad)
    first_grad = second_grad + first_part
    proj_bias_grad = jnp.sum(first_grad, axis=0)
    branch_grad = first_grad.astype(jnp.bfloat16)
    proj_weight_grad = jnp.einsum(
        "tk,td->kd", context, branch_grad, preferred_element_type=jnp.float32
    )
    context_grad = jnp.einsum(
        "td,kd->tk", branch_grad, proj_weight, preferred_element_type=jnp.float32
    )
    context_grad = context_grad.astype(jnp.bfloat16).reshape(images, PATCHES, local_heads, HEAD_DIM)
    scores = (
        jnp.einsum("bqhd,bkhd->bhqk", query, keys, preferred_element_type=jnp.float32) * score_scale
    )
    probs = jnp.exp(scores - log_total)
    weights = probs.astype(jnp.bfloat16)
    value_grad = jnp.einsum(
        "bhqk,bqhd->bkhd", weights, context_grad, preferred_element_type=jnp.float32
    )
    prob_grad = jnp.einsum(
        "bqhd,bkhd->bhqk", context_grad, values, preferred_element_type=jnp.float32
    )
    score_grad = (probs * (prob_grad - jnp.sum(probs * prob_grad, axis=-1, keepdims=True))).astype(
        jnp.bfloat16
    )
    query_grad = (
        jnp.einsum("bhqk,bkhd->bqhd", score_grad, keys, preferred_element_type=jnp.float32)
        * score_scale
    )
    key_grad = (
        jnp.einsum("bhqk,bqhd->bkhd", score_grad, query, preferred_element_type=jnp.float32)
        * score_scale
    )
    qkv_grad = jnp.stack([query_grad, key_grad, value_grad], axis=2).astype(jnp.bfloat16)
    qkv_grad = qkv_grad.reshape(tokens, 3, local_heads * HEAD_DIM)
    qkv_sums = jnp.sum(qkv_grad.astype(jnp.float32), axis=0)
    qv_bias_grad = jnp.stack([qkv_sums[0], qkv_sums[2]])
    qkv_weight_grad = jnp.einsum(
        "td,tsk->dsk", lowered_pre, qkv_grad, preferred_element_type=jnp.float32
    )
    pre_partial = jnp.einsum(
        "tsk,dsk->td", qkv_grad, qkv_weight, preferred_element_type=jnp.float32
    )
    pre_grad = lax.psum(pre_partial.astype(jnp.bfloat16), "tensor").astype(jnp.float32)
    input_part, pre_gain_grad, pre_shift_grad = norm_grad(residual, pre_gain, pre_shift, pre_grad)
    tokens_grad = first_grad + input_part
    shared = (
        lax.psum(pre_gain_grad.astype(jnp.bfloat16), "wide").astype(jnp.float32),
        lax.psum(pre_shift_grad.astype(jnp.bfloat16), "wide").astype(jnp.float32),
        lax.psum(qkv_weight_grad.astype(jnp.bfloat16), "wide").astype(jnp.float32),
        lax.psum(qv_bias_grad.astype(jnp.bfloat16), "wide").astype(jnp.float32),
        lax.psum(proj_weight_grad.astype(jnp.bfloat16), "wide").astype(jnp.float32),
        lax.psum(proj_bias_grad.astype(jnp.bfloat16), "wide").astype(jnp.float32),
        lax.psum(mid_gain_grad.astype(jnp.bfloat16), "wide").astype(jnp.float32),
        lax.psum(mid_shift_grad.astype(jnp.bfloat16), "wide").astype(jnp.float32),
        lax.psum(hidden_weight_grad.astype(jnp.bfloat16), "wide").astype(jnp.float32),
        lax.psum(hidden_bias_grad.astype(jnp.bfloat16), "wide").astype(jnp.float32),
        lax.psum(output_weight_grad.astype(jnp.bfloat16), "wide").astype(jnp.float32),
        lax.psum(output_bias_grad.astype(jnp.bfloat16), "wide").astype(jnp.float32),
        lax.psum(moe_gain_grad.astype(jnp.bfloat16), "wide").astype(jnp.float32),
        lax.psum(moe_shift_grad.astype(jnp.bfloat16), "wide").astype(jnp.float32),
        lax.psum(router_grad.astype(jnp.bfloat16), "wide").astype(jnp.float32),
    )
    return (
        (block_out, tokens_grad)
        + tuple(shared)
        + (expert_in_grad, expert_in_bias_grad, expert_out_grad, expert_out_bias_grad)
    )


def solution(mesh):
    body = functools.partial(shards, mesh.shape["wide"]) if mesh.shape["tensor"] == 2 else plain
    return jax.shard_map(
        body,
        mesh=mesh,
        in_specs=(
            P("wide", None), P(), P(), P(None, None, "tensor"), P(None, "tensor"), P("tensor", None), P(), P(), P(),
            P(None, "tensor"), P("tensor"), P("tensor", None), P(), P(), P(), P(),
            P("wide", None, "tensor"), P("wide", "tensor"), P("wide", "tensor", None), P("wide", None),
            P("wide", None), P("wide", None), P("wide", None),
        ),
        out_specs=(
            P("wide", None), P("wide", None), P(), P(), P(None, None, "tensor"), P(None, "tensor"), P("tensor", None),
            P(), P(), P(), P(None, "tensor"), P("tensor"), P("tensor", None), P(), P(), P(), P(),
            P("wide", None, "tensor"), P("wide", "tensor"), P("wide", "tensor", None), P("wide", None),
        ),
        check_vma=False,
    )
```

```python
import functools

import jax
import jax.numpy as jnp
from jax import lax
from jax.experimental import pallas as pl
from jax.experimental.pallas import tpu as pltpu
from jax.sharding import PartitionSpec as P

HEAD_DIM = 64
PATCHES = 144
BF16 = jnp.bfloat16
F32 = jnp.float32
HIGHEST = lax.Precision.HIGHEST
MESH = pl.DeviceIdType.MESH
VMEM_BYTES = 60 * 1024 * 1024


def dot(left, right):
    return jnp.dot(left, right, preferred_element_type=F32)


def dot_rows(left, right):
    return lax.dot_general(left, right, (((1,), (1,)), ((), ())), preferred_element_type=F32)


def dot_columns(left, right, precision=None):
    return lax.dot_general(
        left, right, (((0,), (0,)), ((), ())), precision=precision, preferred_element_type=F32
    )


def normalized(values):
    centered = values - jnp.mean(values, axis=-1, keepdims=True)
    variance = jnp.mean(centered * centered, axis=-1, keepdims=True)
    scale = lax.rsqrt(variance + 1e-06)
    return centered * scale, scale


def norm_back(rows, scale, gain, upstream):
    scaled = upstream * gain
    inward = jnp.mean(scaled, axis=-1, keepdims=True)
    along = jnp.mean(scaled * rows, axis=-1, keepdims=True)
    return scale * (scaled - inward - rows * along)


def gelu_parts(inner):
    square = inner * inner
    bend = jnp.tanh(0.7978845608028654 * inner * (1.0 + 0.044715 * square))
    half = 0.5 * (1.0 + bend)
    slope = half + (0.5 * 0.7978845608028654) * inner * (1.0 - bend * bend) * (
        1.0 + 0.134145 * square
    )
    return inner * half, slope


def gelu(inner):
    return inner * (0.5 * (1.0 + jnp.tanh(0.7978845608028654 * inner * (1.0 + 0.044715 * inner * inner))))


def softmax_rows(scores, scale):
    peak = jnp.max(scores, axis=-1, keepdims=True)
    weights = jnp.exp((scores - peak) * scale)
    return weights * (1.0 / jnp.sum(weights, axis=-1, keepdims=True))


def spots(places):
    lane = lax.broadcasted_iota(jnp.int32, (places.shape[0], 128), 1)
    return [(lane == places[:, j : j + 1]).astype(F32) for j in range(2)]


def bits_of(index, wide):
    return [lax.rem(lax.div(index, 1 << k), 2) for k in range(wide.bit_length() - 1)]


class Sums:
    def __init__(self, wide, orders, totals, sends, lands, gathers, send_sems, recv_sems):
        me, self.plane = lax.axis_index("wide"), lax.axis_index("tensor")
        self.bits = bits_of(me, wide)
        self.partners = [me + (1 - 2 * bit) * (1 << k) for k, bit in enumerate(self.bits)]
        self.steps = len(self.bits)
        self.orders, self.totals, self.sends, self.lands, self.gathers = orders, totals, sends, lands, gathers
        self.send_sems, self.recv_sems = send_sems, recv_sems

    def piece(self, i, step):
        rows = self.gathers[i].shape[0]
        base = 0
        for s in range(step):
            base = base + self.bits[self.orders[i][s]] * (rows >> (s + 1))
        length = rows >> (step + 1)
        bit = self.bits[self.orders[i][step]]
        return pl.multiple_of(base + bit * length, 16), pl.multiple_of(base + (1 - bit) * length, 16), length

    def staged(self, i, step):
        rows = self.gathers[i].shape[0]
        return rows - (rows >> step)

    def transfer(self, i, k):
        step = k if k < self.steps else 2 * self.steps - 1 - k
        kept, _, length = self.piece(i, step)
        if k < self.steps:
            at = self.staged(i, step)
            source, target = self.sends[i].at[pl.ds(at, length)], self.lands[i].at[pl.ds(at, length)]
        else:
            source = target = self.gathers[i].at[pl.ds(kept, length)]
        return pltpu.make_async_remote_copy(
            source, target, self.send_sems.at[i, k], self.recv_sems.at[i, k],
            device_id=(self.partners[self.orders[i][step]], self.plane), device_id_type=MESH,
        )

    def begin(self, i, k):
        if k < self.steps:
            _, other, length = self.piece(i, k)
            at = self.staged(i, k)
            self.sends[i][at : at + length, :] = self.totals[i][pl.ds(other, length), :].astype(BF16)
        self.transfer(i, k).start()

    def advance(self, i, k):
        self.transfer(i, k).wait()
        if k < self.steps:
            kept, _, length = self.piece(i, k)
            at = self.staged(i, k)
            value = self.totals[i][pl.ds(kept, length), :] + self.lands[i][at : at + length, :].astype(F32)
            if k + 1 < self.steps:
                self.totals[i][pl.ds(kept, length), :] = value
            else:
                self.gathers[i][pl.ds(kept, length), :] = value.astype(BF16)
        if k + 1 < 2 * self.steps:
            self.begin(i, k + 1)


def greet(wide):
    me, plane = lax.axis_index("wide"), lax.axis_index("tensor")
    barrier = pltpu.get_barrier_semaphore()

    def hail(d, carry):
        pl.semaphore_signal(barrier, inc=1, device_id=(lax.rem(me + d, wide), plane), device_id_type=MESH)
        return carry

    lax.fori_loop(1, wide, hail, 0)
    pl.semaphore_signal(barrier, inc=1, device_id=(me, 1 - plane), device_id_type=MESH)
    pl.semaphore_wait(barrier, wide)


def put_row(small, at, row):
    for c in range(row.shape[1] // 128):
        small[at + c : at + c + 1, :] = row[:, 128 * c : 128 * (c + 1)]
    return at + row.shape[1] // 128


def get_row(small, at, width):
    return jnp.concatenate([small[at + c : at + c + 1, :] for c in range(width // 128)], axis=1)


def image_back(heads, qkv, context_grad):
    width = heads * HEAD_DIM
    scale = HEAD_DIM**-0.5
    parts = [[], [], []]
    for head in range(heads):
        h = head * HEAD_DIM
        query = qkv[:, h : h + HEAD_DIM]
        keys = qkv[:, width + h : width + h + HEAD_DIM]
        values = qkv[:, 2 * width + h : 2 * width + h + HEAD_DIM]
        upstream = context_grad[:, h : h + HEAD_DIM]
        probs = softmax_rows(dot_rows(query, keys), scale)
        prob_grad = dot_rows(upstream, values)
        inward = jnp.sum(probs * prob_grad, axis=-1, keepdims=True)
        score_grad = (probs * (prob_grad - inward)).astype(BF16)
        parts[0].append(dot(score_grad, keys) * scale)
        parts[1].append(dot_columns(score_grad, query) * scale)
        parts[2].append(dot_columns(probs.astype(BF16), upstream))
    return jnp.concatenate(parts[0] + parts[1] + parts[2], axis=1).astype(BF16)


def column_dots(left, right, put, tile=256):
    def body(i, carry):
        at = pl.multiple_of(i * tile, tile)
        put(at, tile, dot_columns(left[:, pl.ds(at, tile)], right[...]))
        return carry

    lax.fori_loop(0, left.shape[1] // tile, body, 0)


def image_forward(heads, qkv):
    width = heads * HEAD_DIM
    parts = []
    for head in range(heads):
        h = head * HEAD_DIM
        probs = softmax_rows(
            dot_rows(qkv[:, h : h + HEAD_DIM], qkv[:, width + h : width + h + HEAD_DIM]), HEAD_DIM**-0.5
        )
        parts.append(dot(probs.astype(BF16), qkv[:, 2 * width + h : 2 * width + h + HEAD_DIM]))
    return jnp.concatenate(parts, axis=1).astype(BF16)


def token_hits(choices, slots):
    slot = lax.broadcasted_iota(jnp.int32, (choices.shape[0], slots), 1)
    return [slot == choices[:, j : j + 1] for j in range(2)]


def slot_hits(first, count, targets):
    slot = first + lax.broadcasted_iota(jnp.int32, (count, targets.shape[1]), 0)
    return ((slot == targets[0:1, :]) | (slot == targets[1:2, :])).astype(BF16)


def slot_targets(choice_ids, ranks, capacity, room):
    count = choice_ids.shape[1]
    order_keys = jnp.concatenate([ranks, ranks + count])
    flat_ids = choice_ids.reshape(2 * count)
    earlier = (order_keys[None, :] < order_keys[:, None]) & (flat_ids[None, :] == flat_ids[:, None])
    position = jnp.sum(earlier.astype(jnp.int32), axis=1).reshape(2, count)
    kept = position < capacity
    targets = jnp.where(kept, choice_ids * room + position, -1)
    marks = jnp.where(kept, choice_ids, -1)
    places = jnp.where(kept, position, -1)
    return targets, jnp.concatenate([targets, marks, places]).T


def forward(
    wide, room, group, heads, rows,
    tokens, cotangent, targets, choices, pre_gain, pre_shift, weight_qkv, qv_bias, projection, proj_bias,
    mid_gain, mid_shift, hidden, hidden_bias, output, output_bias, moe_gain, moe_shift, router,
    qkv_out, context_out, first_out, second_out, lowered_out, route_out, gates_out, table_out, upstream_out,
    placed, projection_peer, context_peer, partial_own, partial_peer, sems,
):
    me, plane = lax.axis_index("wide"), lax.axis_index("tensor")
    chunks, groups = tokens.shape[0] // rows, wide // group
    mine = lax.div(me, group)
    block = group * room
    width = heads * HEAD_DIM
    row_at, context_at, partial_at, last_at = 0, wide, wide + chunks, wide + 2 * chunks
    greet(wide)

    def rows_of(index):
        return pl.ds(pl.multiple_of(index * room, 16), room)

    def chunk_of(index):
        return pl.ds(pl.multiple_of(index * rows, 16), rows)

    def move(source, target, base, sent, landed, device):
        return pltpu.make_async_remote_copy(
            source, target, sems.at[0, base + sent], sems.at[1, base + landed], device_id=device, device_id_type=MESH
        )

    def across(source, target, base, index):
        there = chunk_of(index)
        return move(source.at[there], target.at[there], base, index, index, (me, 1 - plane))

    def row_copy(other, sender):
        return move(placed.at[rows_of(other)], upstream_out.at[rows_of(sender)], row_at, other, sender, (other, plane))

    weights = move(projection, projection_peer, last_at, 0, 0, (me, 1 - plane))
    weights.start()
    table_out[...] = jnp.zeros_like(table_out)

    def attend_chunk(c):
        there = chunk_of(c)
        normed, _ = normalized(tokens[there, :].astype(F32))
        lowered = (normed * pre_gain[...] + pre_shift[...]).astype(BF16)
        parts = [dot(lowered, weight_qkv[s]) for s in range(3)]
        parts = [parts[0] + qv_bias[0:1, :], parts[1], parts[2] + qv_bias[1:2, :]]
        qkv = jnp.concatenate(parts, axis=1).astype(BF16)
        qkv_out[there, :] = qkv
        contexts = [
            image_forward(heads, qkv[image * PATCHES : (image + 1) * PATCHES]) for image in range(rows // PATCHES)
        ]
        context_out[there, :] = jnp.concatenate(contexts, axis=0)
        across(context_out, context_peer, context_at, c).start()

    def place_group(k):
        q = lax.rem(mine + k, groups)
        hits = slot_hits(q * block, block, targets)
        here = pl.ds(pl.multiple_of(q * block, 16), block)
        placed[here, :] = dot(hits, cotangent[...].astype(BF16)).astype(BF16)
        for j in range(group):
            e = q * group + j

            @pl.when(e != me)
            def _(e=e):
                row_copy(e, me).start()

            @pl.when(e == me)
            def _(e=e):
                upstream_out[rows_of(e), :] = placed[rows_of(e), :]

    def feed_chunk(c):
        there = chunk_of(c)
        across(context_out, context_peer, context_at, c).wait()
        branch = dot(context_out[there, :], projection[...]) + dot(context_peer[there, :], projection_peer[...])
        first = tokens[there, :].astype(F32) + branch + proj_bias[...]
        first_out[there, :] = first
        normed, _ = normalized(first)
        lowered = (normed * mid_gain[...] + mid_shift[...]).astype(BF16)
        activated = gelu(dot(lowered, hidden[...]) + hidden_bias[...]).astype(BF16)
        partial_own[there, :] = dot(activated, output[...]).astype(BF16)
        across(partial_own, partial_peer, partial_at, c).start()

    def route_chunk(c):
        there = chunk_of(c)
        across(partial_own, partial_peer, partial_at, c).wait()
        partial = partial_own[there, :].astype(F32) + partial_peer[there, :].astype(F32)
        second = first_out[there, :] + partial + output_bias[...]
        second_out[there, :] = second
        normed, _ = normalized(second)
        normed = normed * moe_gain[...] + moe_shift[...]
        lowered_out[there, :] = normed.astype(BF16)
        logits = lax.dot_general(
            normed, router[...], (((1,), (1,)), ((), ())), precision=HIGHEST, preferred_element_type=F32
        )
        grown = jnp.exp(logits - jnp.max(logits, axis=-1, keepdims=True))
        route = grown / jnp.sum(grown, axis=-1, keepdims=True)
        route_out[there, :] = route
        number = lax.broadcasted_iota(jnp.int32, route.shape, 1)
        picks = choices[there, :]
        chosen = [jnp.where(number == picks[:, 2 + j : 3 + j], route, 0.0) for j in range(2)]
        gates_out[there, :] = jnp.concatenate([jnp.sum(part, axis=1, keepdims=True) for part in chosen], axis=1)
        for part, spot in zip(chosen, spots(picks[:, 4:6])):
            table_out[...] += dot_columns(part, spot, HIGHEST)

    def turn(c, carry):
        @pl.when(c < chunks)
        def _():
            attend_chunk(c)

        @pl.when(c < groups)
        def _():
            place_group(c)

        @pl.when(c == 1)
        def _():
            weights.wait()

        @pl.when((c >= 1) & (c <= chunks))
        def _():
            feed_chunk(c - 1)

        @pl.when(c >= 2)
        def _():
            route_chunk(c - 2)

        return carry

    lax.fori_loop(0, chunks + 2, turn, 0)

    def take_rows(d, carry):
        other = lax.rem(me + d, wide)
        row_copy(other, other).wait_recv()
        row_copy(other, me).wait_send()
        return carry

    lax.fori_loop(1, wide, take_rows, 0)


def experts(
    wide, room, group,
    lowered, targets, table, upstream, weight_in, bias_in, weight_out, bias_out,
    own_home, peer_home, gate_home, result_out, in_grad, out_grad, in_bias_grad, out_bias_grad,
    columns, placed, rows_own, rows_peer, act, inner_grad, slot_grad, grad_kept, grad_sent, grad_landed,
    grad_back, gate_sent, gate_arrived, gate_back, gate_own, gate_peer, sems,
):
    me, plane = lax.axis_index("wide"), lax.axis_index("tensor")
    groups = wide // group
    mine = lax.div(me, group)
    half = own_home.shape[1]
    block = group * room
    row_at, gate_at, home_at, back_at = 0, wide, 2 * wide, 3 * wide
    grad_at, share_at, join_at, table_at = 4 * wide, 4 * wide + groups, 4 * wide + 2 * groups, 4 * wide + 3 * groups
    greet(wide)

    def rows_of(index):
        return pl.ds(pl.multiple_of(index * room, 16), room)

    def rows_of_group(index):
        return pl.ds(pl.multiple_of(index * block, 16), block)

    def move(source, target, base, sent, landed, device):
        return pltpu.make_async_remote_copy(
            source, target, sems.at[0, base + sent], sems.at[1, base + landed], device_id=device, device_id_type=MESH
        )

    def row_copy(other, sender):
        return move(placed.at[rows_of(other)], rows_own.at[rows_of(sender)], row_at, other, sender, (other, plane))

    def gate_copy(other, sender):
        return move(gate_sent.at[other], gate_arrived.at[sender], gate_at, other, sender, (other, plane))

    def home_copy(other, sender):
        return move(grad_back.at[rows_of(other)], own_home.at[rows_of(sender)], home_at, other, sender, (other, plane))

    def back_copy(other, sender):
        return move(gate_back.at[other], gate_own.at[sender], back_at, other, sender, (other, plane))

    def across(source, target, base, index):
        there = rows_of_group(index)
        return move(source.at[there], target.at[there], base, index, index, (me, 1 - plane))

    first_plane = plane == 0
    columns[...] = jnp.where(first_plane, lowered[:, :half], lowered[:, half:])
    own_half = pl.ds(pl.multiple_of(plane * half, 16), half)
    peer_half = pl.ds(pl.multiple_of((1 - plane) * half, 16), half)
    for e in range(wide):
        gate_sent[e] = jnp.broadcast_to(table[e : e + 1, :], gate_sent.shape[1:])
    in_bias_grad[...] = jnp.zeros_like(in_bias_grad)
    out_bias_grad[...] = jnp.zeros_like(out_bias_grad)

    def place_group(k, carry):
        q = lax.rem(mine + k, groups)
        placed[rows_of_group(q), :] = dot(slot_hits(q * block, block, targets), columns[...]).astype(BF16)
        for j in range(group):
            e = q * group + j

            @pl.when(e != me)
            def _(e=e):
                row_copy(e, me).start()
                gate_copy(e, me).start()

            @pl.when(e == me)
            def _(e=e):
                rows_own[rows_of(e), :] = placed[rows_of(e), :]
                gate_arrived[e] = gate_sent[e]

        return carry

    lax.fori_loop(0, groups, place_group, 0)
    diagonal = lax.broadcasted_iota(jnp.int32, (room, 128), 0) == lax.broadcasted_iota(jnp.int32, (room, 128), 1)

    def join_group(p):
        for j in range(group):
            w = p * group + j

            @pl.when(w != me)
            def _(w=w):
                row_copy(w, w).wait_recv()
                gate_copy(w, w).wait_recv()

        across(rows_own, rows_peer, join_at, p).start()

    def expert_group(p):
        there = rows_of_group(p)
        across(rows_own, rows_peer, join_at, p).wait()
        gates = jnp.concatenate(
            [
                jnp.sum(jnp.where(diagonal, gate_arrived[p * group + j][0:1, :], 0.0), axis=1, keepdims=True)
                for j in range(group)
            ],
            axis=0,
        )
        inner = dot(rows_own[there, :], weight_in[own_half, :]) + dot(rows_peer[there, :], weight_in[peer_half, :])
        acted, slope = gelu_parts(inner + bias_in[...])
        acted = acted.astype(BF16)
        act[there, :] = acted
        raised = upstream[there, :].astype(F32)
        slot = (raised * gates).astype(BF16)
        slot_grad[there, :] = slot
        inward = (dot_rows(slot, weight_out[...]) * slope).astype(BF16)
        inner_grad[there, :] = inward
        grad_sent[there, :] = dot_rows(inward, weight_in[peer_half, :]).astype(BF16)
        across(grad_sent, grad_landed, grad_at, p).start()
        grad_kept[there, :] = dot_rows(inward, weight_in[own_half, :])
        result = dot(acted, weight_out[...]) + bias_out[...] * jnp.where(first_plane, 1.0, 0.0)
        result_out[there, :] = result.astype(BF16)
        out_bias_grad[0:1, :] += jnp.sum(slot.astype(F32), axis=0, keepdims=True)
        in_bias_grad[0:1, :] += jnp.sum(inward.astype(F32), axis=0, keepdims=True)
        slopes = jnp.sum(raised * result, axis=1, keepdims=True)
        for j in range(group):
            w = p * group + j
            row = jnp.sum(
                jnp.where(diagonal, slopes[j * room : (j + 1) * room], 0.0), axis=0, keepdims=True
            )
            gate_back[w] = jnp.broadcast_to(row, gate_back.shape[1:])

            @pl.when(w != me)
            def _(w=w):
                back_copy(w, me).start()

            @pl.when(w == me)
            def _(w=w):
                gate_own[w] = gate_back[w]

    def give_back(p):
        across(grad_sent, grad_landed, grad_at, p).wait()
        there = rows_of_group(p)
        grad_back[there, :] = (grad_kept[there, :] + grad_landed[there, :].astype(F32)).astype(BF16)
        for j in range(group):
            w = p * group + j

            @pl.when(w != me)
            def _(w=w):
                home_copy(w, me).start()

            @pl.when(w == me)
            def _(w=w):
                own_home[rows_of(w), :] = grad_back[rows_of(w), :]

    def turn(k, carry):
        @pl.when(k < groups)
        def _():
            join_group(lax.rem(mine + groups - k, groups))

        @pl.when((k >= 1) & (k <= groups))
        def _():
            expert_group(lax.rem(mine + groups - k + 1, groups))

        @pl.when(k >= 2)
        def _():
            give_back(lax.rem(mine + groups - k + 2, groups))

        return carry

    lax.fori_loop(0, groups + 2, turn, 0)
    tile = act.shape[1] // groups

    def share_group(k, carry):
        at = pl.multiple_of(k * tile, 128)
        out_grad[pl.ds(at, tile), :] = dot_columns(act[:, pl.ds(at, tile)], slot_grad[...]).astype(BF16)
        q = lax.rem(mine + k, groups)
        for j in range(group):
            e = q * group + j

            @pl.when(e != me)
            def _(e=e):
                home_copy(e, e).wait_recv()

        across(own_home, peer_home, share_at, q).start()
        return carry

    lax.fori_loop(0, groups, share_group, 0)

    def take_gates(d, carry):
        other = lax.rem(me + d, wide)
        back_copy(other, other).wait_recv()
        return carry

    lax.fori_loop(1, wide, take_gates, 0)
    tables = move(gate_own, gate_peer, table_at, 0, 0, (me, 1 - plane))
    tables.start()
    in_grad[own_half, :] = dot_columns(rows_own[...], inner_grad[...]).astype(BF16)
    in_grad[peer_half, :] = dot_columns(rows_peer[...], inner_grad[...]).astype(BF16)

    def end_sends(d, carry):
        other = lax.rem(me + d, wide)
        row_copy(other, me).wait_send()
        gate_copy(other, me).wait_send()
        home_copy(other, me).wait_send()
        back_copy(other, me).wait_send()
        return carry

    lax.fori_loop(1, wide, end_sends, 0)
    tables.wait()
    for e in range(wide):
        gate_home[e : e + 1, :] = gate_own[e][0:1, :] + gate_peer[e][0:1, :]

    def end_share(q, carry):
        across(own_home, peer_home, share_at, q).wait()
        return carry

    lax.fori_loop(0, groups, end_share, 0)


def backward(
    wide, room, heads, layout, orders, rows,
    second, cotangent, route, choices, gates, moe_gain, moe_shift, router, gate_grads, row_own, row_peer, result,
    first, tokens, qkv, context, mid_gain, mid_shift, pre_gain, pre_shift, hidden, hidden_bias, output, projection,
    weight_qkv,
    block_out, grad_out, hidden_out, output_out, qkv_out, proj_out, *rest,
):
    vectors_out, pre_out, rest = rest[: len(layout)], rest[len(layout)], rest[len(layout) + 1 :]
    (lowered_mid, act, inner_grad, mid_own, mid_peer, branch, qkv_grad, lowered_pre, pre_peer, result_own, blend_peer,
     pre_tile, pre_tiles, pre_total, pre_other, moe_sums, router_sums, mid_sums, hidden_sums, qkv_sums, pre_sums, small_sums) = rest[:22]
    hidden_total, output_total, qkv_total, proj_total, small = rest[22:27]
    sends, lands = rest[27:33], rest[33:39]
    mid_sems, pre_sems, blend_sems, result_sems, send_sems, recv_sems = rest[39:]
    blend_own = lowered_mid
    me, plane = lax.axis_index("wide"), lax.axis_index("tensor")
    chunks = tokens.shape[0] // rows
    model = tokens.shape[1]
    width = heads * HEAD_DIM
    split = qkv_total.shape[0] // 2
    totals = (
        hidden_total, output_total, qkv_total.at[pl.ds(0, split)], qkv_total.at[pl.ds(split, split)], proj_total, small
    )
    gathers = (
        hidden_out, output_out, qkv_out.at[pl.ds(0, split)], qkv_out.at[pl.ds(split, split)], proj_out, small_sums
    )
    greet(wide)
    sums = Sums(wide, orders, totals, sends, lands, gathers, send_sems, recv_sems)

    def rows_of(index):
        return pl.ds(pl.multiple_of(index * room, 16), room)

    def result_copy(other, sender):
        return pltpu.make_async_remote_copy(
            result.at[rows_of(other)], result_own.at[rows_of(sender)], result_sems.at[0, other],
            result_sems.at[1, sender], device_id=(other, plane), device_id_type=MESH,
        )

    def send_result(d, carry):
        result_copy(lax.rem(me + d, wide), me).start()
        return carry

    lax.fori_loop(1, wide, send_result, 0)
    result_own[rows_of(me), :] = result[rows_of(me), :]

    def across(own, peer, sems, chunk):
        at = pl.multiple_of(chunk * rows, rows)
        return pltpu.make_async_remote_copy(
            own.at[pl.ds(at, rows)], peer.at[pl.ds(at, rows)], sems.at[0, chunk], sems.at[1, chunk],
            device_id=(me, 1 - plane), device_id_type=MESH,
        )

    for vector in (moe_sums, router_sums, mid_sums, hidden_sums, qkv_sums, pre_sums):
        vector[...] = jnp.zeros_like(vector)
    first_plane = plane == 0

    def ordered(own, peer):
        return jnp.concatenate([jnp.where(first_plane, own, peer), jnp.where(first_plane, peer, own)], axis=1)

    def settle(here):
        picks = choices[here, :]
        hits = token_hits(picks, row_own.shape[0])
        table = (hits[0] | hits[1]).astype(BF16)
        moe_grad = ordered(dot(table, row_own[...]), dot(table, row_peer[...]))
        chances = route[here, :]
        number = lax.broadcasted_iota(jnp.int32, chances.shape, 1)
        route_grad = jnp.zeros_like(chances)
        for j, spot in enumerate(spots(picks[:, 4:6])):
            at_place = lax.dot_general(
                spot, gate_grads[...], (((1,), (1,)), ((), ())), precision=HIGHEST, preferred_element_type=F32
            )
            route_grad = route_grad + jnp.where(number == picks[:, 2 + j : 3 + j], at_place, 0.0)
        logit_grad = chances * (route_grad - jnp.sum(chances * route_grad, axis=1, keepdims=True))
        normed, scale = normalized(second[here, :])
        router_sums[...] += dot_columns(logit_grad, normed * moe_gain[...] + moe_shift[...], HIGHEST)
        moe_grad = moe_grad + jnp.dot(logit_grad, router[...], precision=HIGHEST, preferred_element_type=F32)
        grad = cotangent[here, :] + norm_back(normed, scale, moe_gain[...], moe_grad)
        grad_out[here, :] = grad
        branch[here, :] = grad.astype(BF16)
        moe_sums[0:1, :] += jnp.sum(moe_grad * normed, axis=0, keepdims=True)
        moe_sums[1:2, :] += jnp.sum(moe_grad, axis=0, keepdims=True)
        moe_sums[2:3, :] += jnp.sum(grad, axis=0, keepdims=True)

    def feed_chunk(chunk, carry):
        here = pl.ds(pl.multiple_of(chunk * rows, rows), rows)
        settle(here)
        normed, _ = normalized(first[here, :])
        lowered = (normed * mid_gain[...] + mid_shift[...]).astype(BF16)
        lowered_mid[here, :] = lowered
        acted, slope = gelu_parts(dot(lowered, hidden[...]) + hidden_bias[...])
        act[here, :] = acted.astype(BF16)
        inward = (dot_rows(branch[here, :], output[...]) * slope).astype(BF16)
        inner_grad[here, :] = inward
        hidden_sums[0:1, :] += jnp.sum(inward.astype(F32), axis=0, keepdims=True)
        mid_own[here, :] = dot_rows(inward, hidden[...]).astype(BF16)
        across(mid_own, mid_peer, mid_sems, chunk).start()
        return carry

    lax.fori_loop(0, chunks, feed_chunk, 0)

    def put_in(total):
        def put(at, tile, value):
            total[pl.ds(at, tile), :] = value

        return put

    column_dots(lowered_mid, inner_grad, put_in(hidden_total))
    sums.begin(0, 0)
    column_dots(act, branch, put_in(output_total))
    sums.begin(1, 0)

    def attend_chunk(chunk, carry):
        here = pl.ds(pl.multiple_of(chunk * rows, rows), rows)
        across(mid_own, mid_peer, mid_sems, chunk).wait()
        mid_grad = mid_own[here, :].astype(F32) + mid_peer[here, :].astype(F32)
        normed, scale = normalized(first[here, :])
        first_grad = grad_out[here, :] + norm_back(normed, scale, mid_gain[...], mid_grad)
        grad_out[here, :] = first_grad
        lowered_grad = first_grad.astype(BF16)
        branch[here, :] = lowered_grad
        mid_sums[0:1, :] += jnp.sum(mid_grad * normed, axis=0, keepdims=True)
        mid_sums[1:2, :] += jnp.sum(mid_grad, axis=0, keepdims=True)
        mid_sums[2:3, :] += jnp.sum(first_grad, axis=0, keepdims=True)
        normed, _ = normalized(tokens[here, :].astype(F32))
        lowered_pre[here, :] = (normed * pre_gain[...] + pre_shift[...]).astype(BF16)
        context_grad = dot_rows(lowered_grad, projection[...]).astype(BF16)
        for image in range(rows // PATCHES):
            at = pl.multiple_of(chunk * rows + image * PATCHES, PATCHES)
            block = qkv[pl.ds(at, PATCHES), :]
            grad = image_back(heads, block, context_grad[image * PATCHES : (image + 1) * PATCHES])
            qkv_grad[pl.ds(at, PATCHES), :] = grad
            pre = sum(dot_rows(grad[:, s * width : (s + 1) * width], weight_qkv[s]) for s in range(3))
            pre = pre.astype(BF16)
            mid_own[pl.ds(at, PATCHES), :] = pre
            pre = pre.astype(F32)
            pre_sums[0:1, :] += jnp.sum(pre * normed[image * PATCHES : (image + 1) * PATCHES], axis=0, keepdims=True)
            pre_sums[1:2, :] += jnp.sum(pre, axis=0, keepdims=True)
            qkv_sums[0:1, :] += jnp.sum(grad.astype(F32), axis=0, keepdims=True)
            for k in range(sums.steps):

                @pl.when(chunk == k)
                def _(i=image, k=k):
                    if i < 2:
                        sums.advance(i, k)

        across(mid_own, pre_peer, pre_sems, chunk).start()
        return carry

    lax.fori_loop(0, chunks, attend_chunk, 0)

    small[...] = jnp.zeros_like(small)
    at = 0
    for vector, picked in zip((mid_sums, moe_sums, hidden_sums, qkv_sums, router_sums), layout):
        for r in picked:
            at = put_row(small, at, vector[r : r + 1, :])
    sums.begin(5, 0)
    put_row(pre_tile, put_row(pre_tile, 0, pre_sums[0:1, :]), pre_sums[1:2, :])

    def pre_copy(other, sender):
        return pltpu.make_async_remote_copy(
            pre_tile, pre_tiles.at[sender], result_sems.at[0, wide + other], result_sems.at[1, wide + sender],
            device_id=(other, plane), device_id_type=MESH,
        )

    def send_pre(d, carry):
        pre_copy(lax.rem(me + d, wide), me).start()
        return carry

    lax.fori_loop(1, wide, send_pre, 0)
    pre_tiles[me] = pre_tile[...]
    column_dots(context, branch, put_in(proj_total))
    sums.begin(4, 0)

    def put_thirds(at, tile, value):
        for s in range(3):
            there = pl.ds(pl.multiple_of(s * model + at, 16), tile)
            qkv_total[there, :] = value[:, s * width : (s + 1) * width]

    column_dots(lowered_pre, qkv_grad, put_thirds)
    sums.begin(2, 0)
    sums.begin(3, 0)

    def finish_chunk(chunk, carry):
        here = pl.ds(pl.multiple_of(chunk * rows, rows), rows)
        across(mid_own, pre_peer, pre_sems, chunk).wait()
        upstream = mid_own[here, :].astype(F32) + pre_peer[here, :].astype(F32)
        normed, scale = normalized(tokens[here, :].astype(F32))
        grad_out[here, :] += norm_back(normed, scale, pre_gain[...], upstream)
        return carry

    def take_result(d, carry):
        other = lax.rem(me + d, wide)
        result_copy(other, other).wait_recv()
        result_copy(other, me).wait_send()
        return carry

    lax.fori_loop(1, wide, take_result, 0)

    def blend(chunk, carry):
        here = pl.ds(pl.multiple_of(chunk * rows, rows), rows)
        hits = token_hits(choices[here, :], result_own.shape[0])
        table = jnp.where(hits[0], gates[here, 0:1], jnp.where(hits[1], gates[here, 1:2], 0.0)).astype(BF16)
        blend_own[here, :] = dot(table, result_own[...]).astype(BF16)
        across(blend_own, blend_peer, blend_sems, chunk).start()
        return carry

    def blend_end(chunk, carry):
        here = pl.ds(pl.multiple_of(chunk * rows, rows), rows)
        across(blend_own, blend_peer, blend_sems, chunk).wait()
        mixture = blend_own[here, :].astype(F32) + blend_peer[here, :].astype(F32)
        block_out[here, :] = (second[here, :] + mixture).astype(BF16)
        return carry

    def take_pre(d, carry):
        other = lax.rem(me + d, wide)
        pre_copy(other, other).wait_recv()
        pre_copy(other, me).wait_send()
        return carry

    pre_share = pltpu.make_async_remote_copy(
        pre_total, pre_other, result_sems.at[0, 2 * wide], result_sems.at[1, 2 * wide],
        device_id=(me, 1 - plane), device_id_type=MESH,
    )
    for k in range(2 * sums.steps):
        if k < sums.steps:
            for i in (0, 1):
                sums.advance(i, sums.steps + k)
        for i in (5, 4, 2, 3):
            sums.advance(i, k)
        if k < sums.steps:
            lax.fori_loop(k * chunks // sums.steps, (k + 1) * chunks // sums.steps, blend, 0)
            lax.fori_loop(k * chunks // sums.steps, (k + 1) * chunks // sums.steps, finish_chunk, 0)
        else:
            first_chunk = (k - sums.steps) * chunks // sums.steps
            lax.fori_loop(first_chunk, (k - sums.steps + 1) * chunks // sums.steps, blend_end, 0)
        if k == sums.steps - 1:
            lax.fori_loop(1, wide, take_pre, 0)
            pre_total[...] = sum(pre_tiles[w] for w in range(wide))
            pre_share.start()
    pre_share.wait()
    pre_tile[...] = pre_total[...] + pre_other[...]
    pre_out[0:1, :] = get_row(pre_tile, 0, model)
    pre_out[1:2, :] = get_row(pre_tile, model // 128, model)
    at = 0
    for out, picked in zip(vectors_out, layout):
        for i in range(len(picked)):
            out[i : i + 1, :] = get_row(small_sums, at, out.shape[1]).astype(F32)
            at += out.shape[1] // 128


def widen(pairs, layout, *refs):
    ins, outs = refs[: pairs + len(layout)], refs[pairs + len(layout) :]
    for source, out in zip(ins[:pairs], outs[:pairs]):
        out[...] = source[...].astype(out.dtype)
    outs = iter(outs[pairs:])
    for source, picked in zip(ins[pairs:], layout):
        for r in picked:
            out = next(outs)
            out[...] = source[r : r + out.shape[0], : out.shape[1]]


def shards(
    wide,
    tokens_in, pre_gain, pre_shift, qkv_weight, qv_bias, proj_weight, proj_bias, mid_gain, mid_shift,
    hidden_weight, hidden_bias, output_weight, output_bias, moe_gain, moe_shift, router_weight,
    expert_in, expert_in_bias, expert_out, expert_out_bias, expert_ids, priority, cotangent,
):
    tokens, model = tokens_in.shape
    width = qkv_weight.shape[2]
    heads = width // HEAD_DIM
    hidden = hidden_weight.shape[1]
    count = router_weight.shape[1]
    capacity = tokens // count
    room = -(-capacity // 16) * 16
    slots = count * room
    half = model // 2
    lanes = 3 * width
    rows = 2 * PATCHES
    chunks = tokens // rows
    group = 4
    steps = wide.bit_length() - 1

    def row(vector):
        return vector.reshape(1, -1)

    def remote(kernel, name, identity, ins, outs, scratch):
        return pl.pallas_call(
            kernel,
            out_shape=[jax.ShapeDtypeStruct(shape, dtype) for shape, dtype in outs],
            in_specs=[pl.BlockSpec(memory_space=pltpu.VMEM)] * len(ins),
            out_specs=[pl.BlockSpec(memory_space=pltpu.VMEM)] * len(outs),
            scratch_shapes=scratch,
            compiler_params=pltpu.CompilerParams(
                vmem_limit_bytes=VMEM_BYTES, collective_id=identity, has_side_effects=True
            ),
            name=name,
        )(*ins)

    def room_for(local):
        return [pltpu.VMEM(shape, dtype) for shape, dtype in local]

    pre_gain, pre_shift, proj_bias = row(pre_gain), row(pre_shift), row(proj_bias)
    mid_gain, mid_shift, hidden_bias = row(mid_gain), row(mid_shift), row(hidden_bias)
    output_bias, moe_gain, moe_shift = row(output_bias), row(moe_gain), row(moe_shift)
    weight_qkv = qkv_weight.transpose(1, 0, 2)
    router = router_weight.T
    targets, choices = slot_targets(expert_ids.T, priority[0], capacity, room)

    qkv, context, first, second, lowered, route, gates, table, upstream = remote(
        functools.partial(forward, wide, room, group, heads, rows), "forward", 1,
        [tokens_in, cotangent, targets, choices, pre_gain, pre_shift, weight_qkv, qv_bias, proj_weight, proj_bias,
         mid_gain, mid_shift, hidden_weight, hidden_bias, output_weight, output_bias, moe_gain, moe_shift, router],
        [((tokens, lanes), BF16), ((tokens, width), BF16), ((tokens, model), F32), ((tokens, model), F32),
         ((tokens, model), BF16), ((tokens, count), F32), ((tokens, 2), F32), ((count, 128), F32), ((slots, model), BF16)],
        room_for([((slots, model), BF16), ((width, model), BF16), ((tokens, width), BF16), ((tokens, model), BF16),
                  ((tokens, model), BF16)]) + [pltpu.SemaphoreType.DMA((2, wide + 2 * chunks + 1))],
    )

    tables = [((count, 8, 128), F32)] * 5
    row_own, row_peer, gate_grads, result, in_grad, out_grad, in_bias, out_bias = remote(
        functools.partial(experts, wide, room, group), "experts", 2,
        [lowered, targets, table, upstream, expert_in[0], expert_in_bias, expert_out[0], expert_out_bias],
        [((slots, half), BF16), ((slots, half), BF16), ((count, 128), F32), ((slots, model), BF16),
         ((model, hidden), BF16), ((hidden, model), BF16), ((8, hidden), F32), ((8, model), F32)],
        room_for([((tokens, half), BF16), ((slots, half), BF16), ((slots, half), BF16), ((slots, half), BF16),
                  ((slots, hidden), BF16), ((slots, hidden), BF16), ((slots, model), BF16), ((slots, half), F32),
                  ((slots, half), BF16), ((slots, half), BF16), ((slots, half), BF16)] + tables)
        + [pltpu.SemaphoreType.DMA((2, 4 * wide + 3 * (wide // group) + 1))],
    )

    layout = [(0, 1, 2), (0, 1, 2), (0,), (0,), tuple(range(count))]
    vectors = [((8, model), F32), ((8, model), F32), ((8, hidden), F32), ((8, lanes), F32), ((count, model), F32)]
    near, far = tuple(range(steps)), (0,) + tuple(range(2, steps)) + (1,)
    summed = [(model, hidden), (hidden, model), (3 * model // 2, width), (3 * model // 2, width), (width, model), (16 * wide, 128)]
    block_out, grad, hidden_g, output_g, qkv_g, proj_g, *sums = remote(
        functools.partial(backward, wide, room, heads, layout, (near, far, near, far, near, far), rows), "backward", 3,
        [second, cotangent, route, choices, gates, moe_gain, moe_shift, router, gate_grads, row_own, row_peer, result,
         first, tokens_in, qkv, context, mid_gain, mid_shift, pre_gain, pre_shift, hidden_weight, hidden_bias,
         output_weight, proj_weight, weight_qkv],
        [((tokens, model), BF16), ((tokens, model), F32), ((model, hidden), BF16), ((hidden, model), BF16),
         ((3 * model, width), BF16), ((width, model), BF16)] + vectors + [((8, model), F32)],
        room_for([((tokens, model), BF16), ((tokens, hidden), BF16), ((tokens, hidden), BF16), ((tokens, model), BF16),
                  ((tokens, model), BF16), ((tokens, model), BF16), ((tokens, lanes), BF16), ((tokens, model), BF16),
                  ((tokens, model), BF16), ((slots, model), BF16), ((tokens, model), BF16),
                  ((2 * model // 128, 128), F32), ((wide, 2 * model // 128, 128), F32), ((2 * model // 128, 128), F32),
                  ((2 * model // 128, 128), F32), ((8, model), F32), ((count, model), F32), ((8, model), F32), ((8, hidden), F32), ((8, lanes), F32), ((8, model), F32),
                  (summed[-1], BF16), (summed[0], F32), (summed[1], F32), ((3 * model, width), F32), (summed[4], F32),
                  (summed[5], F32)] + [(shape, BF16) for shape in summed] * 2)
        + [pltpu.SemaphoreType.DMA((2, chunks))] * 3 + [pltpu.SemaphoreType.DMA((2, 2 * wide + 1))]
        + [pltpu.SemaphoreType.DMA((len(summed), 2 * steps))] * 2,
    )

    pairs = [
        (block_out, BF16), (grad, F32), (hidden_g, F32), (output_g, F32), (qkv_g.reshape(3, model, width), F32),
        (proj_g, F32), (in_grad, F32), (out_grad, F32),
    ]
    singles = [(0, 1), (0, 1, 2), (0, 1, 2), (0,), (0,), (0,), (0,), (0,)]
    sources = [sums[-1]] + list(sums[:-1]) + [in_bias, out_bias]
    sizes = [(1, model)] * 8 + [(1, hidden), (1, lanes), (count, model), (1, hidden), (1, model)]
    parts = 4

    def spec(shape):
        if len(shape) == 3:
            return pl.BlockSpec((shape[0], shape[1] // parts, shape[2]), lambda i: (0, i, 0))
        return pl.BlockSpec((shape[0] // parts, shape[1]), lambda i: (i, 0))

    def whole(shape):
        return pl.BlockSpec(shape, lambda i: (0, 0))

    outs = pl.pallas_call(
        functools.partial(widen, len(pairs), singles),
        grid=(parts,),
        in_specs=[spec(source.shape) for source, _ in pairs] + [whole(source.shape) for source in sources],
        out_specs=[spec(source.shape) for source, _ in pairs] + [whole(size) for size in sizes],
        out_shape=[jax.ShapeDtypeStruct(source.shape, dtype) for source, dtype in pairs]
        + [jax.ShapeDtypeStruct(size, F32) for size in sizes],
        compiler_params=pltpu.CompilerParams(vmem_limit_bytes=VMEM_BYTES),
        name="widen",
    )(*[source for source, _ in pairs], *sources)
    block_out, grad, hidden_g, output_g, qkv_g, proj_g, in_grad, out_grad = outs[:8]
    pre_gain_g, pre_shift_g, mid_gain_g, mid_shift_g, proj_bias_g, moe_gain_g, moe_shift_g, output_bias_g = (
        vector.reshape(model) for vector in outs[8:16]
    )
    hidden_bias_g, qkv_bias_g, router_g, in_bias_g, out_bias_g = outs[16:]
    return (
        block_out, grad, pre_gain_g, pre_shift_g, qkv_g.transpose(1, 0, 2),
        jnp.concatenate([qkv_bias_g[:, :width], qkv_bias_g[:, 2 * width :]]), proj_g, proj_bias_g, mid_gain_g,
        mid_shift_g, hidden_g, hidden_bias_g.reshape(hidden), output_g, output_bias_g, moe_gain_g, moe_shift_g,
        router_g.T, in_grad[None], in_bias_g, out_grad[None], out_bias_g,
    )


def layer_norm(values, gain, shift):
    centered = values - jnp.mean(values, axis=-1, keepdims=True)
    variance = jnp.mean(centered * centered, axis=-1, keepdims=True)
    return centered * lax.rsqrt(variance + 1e-06) * gain + shift


def norm_grad(values, gain, shift, upstream):
    _, pullback = jax.vjp(layer_norm, values, gain, shift)
    return pullback(upstream)


def gelu_grad(inner, upstream):
    _, pullback = jax.vjp(jax.nn.gelu, inner)
    return pullback(upstream)[0]


def slot_tables(choice_ids, ranks, capacity, experts):
    count = choice_ids.shape[0]
    order_keys = jnp.concatenate([ranks, ranks + count])
    flat_ids = jnp.concatenate([choice_ids[:, 0], choice_ids[:, 1]])
    earlier = (order_keys[None, :] < order_keys[:, None]) & (flat_ids[None, :] == flat_ids[:, None])
    position = jnp.sum(earlier.astype(jnp.int32), axis=1)
    kept = position < capacity
    position = position.reshape(2, count)
    kept = kept.reshape(2, count)
    columns = jnp.arange(experts * capacity, dtype=jnp.int32)
    target = choice_ids.T * capacity + position
    tables = (target[:, :, None] == columns[None, None, :]) & kept[:, :, None]
    return (tables, kept)


def plain(
    tokens_in,
    pre_gain,
    pre_shift,
    qkv_weight,
    qv_bias,
    proj_weight,
    proj_bias,
    mid_gain,
    mid_shift,
    hidden_weight,
    hidden_bias,
    output_weight,
    output_bias,
    moe_gain,
    moe_shift,
    router_weight,
    expert_in,
    expert_in_bias,
    expert_out,
    expert_out_bias,
    expert_ids,
    priority,
    cotangent,
):
    tokens = tokens_in.shape[0]
    model_width = tokens_in.shape[1]
    local_heads = qkv_weight.shape[2] // HEAD_DIM
    images = tokens // PATCHES
    experts = router_weight.shape[1]
    capacity = tokens // experts
    score_scale = float(HEAD_DIM) ** (-0.5)
    highest = lax.Precision.HIGHEST
    residual = tokens_in.astype(jnp.float32)
    normed_pre = layer_norm(residual, pre_gain, pre_shift)
    lowered_pre = normed_pre.astype(jnp.bfloat16)
    blank = jnp.zeros_like(qv_bias[0])
    qkv_shift = jnp.stack([qv_bias[0], blank, qv_bias[1]])
    qkv = (
        jnp.einsum("td,dsk->tsk", lowered_pre, qkv_weight, preferred_element_type=jnp.float32)
        + qkv_shift
    ).astype(jnp.bfloat16)
    grid = qkv.reshape(images, PATCHES, 3, local_heads, HEAD_DIM)
    query, keys, values = (grid[:, :, 0], grid[:, :, 1], grid[:, :, 2])
    scores = (
        jnp.einsum("bqhd,bkhd->bhqk", query, keys, preferred_element_type=jnp.float32) * score_scale
    )
    log_total = jax.nn.logsumexp(scores, axis=-1, keepdims=True)
    weights = jnp.exp(scores - log_total).astype(jnp.bfloat16)
    context = jnp.einsum("bhqk,bkhd->bqhd", weights, values, preferred_element_type=jnp.float32)
    context = context.astype(jnp.bfloat16).reshape(tokens, local_heads * HEAD_DIM)
    branch = lax.psum(jnp.dot(context, proj_weight, preferred_element_type=jnp.float32), "tensor")
    first = residual + branch + proj_bias
    normed_mid = layer_norm(first, mid_gain, mid_shift)
    lowered_mid = normed_mid.astype(jnp.bfloat16)
    inner = jnp.dot(lowered_mid, hidden_weight, preferred_element_type=jnp.float32) + hidden_bias
    activated = jax.nn.gelu(inner).astype(jnp.bfloat16)
    partial_out = jnp.dot(activated, output_weight, preferred_element_type=jnp.float32)
    second = first + lax.psum(partial_out, "tensor") + output_bias
    normed_moe = layer_norm(second, moe_gain, moe_shift)
    lowered_moe = normed_moe.astype(jnp.bfloat16)
    route = jax.nn.softmax(jnp.dot(normed_moe, router_weight, precision=highest), axis=-1)
    tables, kept = slot_tables(expert_ids, priority[0], capacity, experts)
    tables = tables.astype(jnp.bfloat16)
    dispatch = tables[0] + tables[1]
    buffers = jnp.einsum("tk,td->kd", dispatch, lowered_moe, preferred_element_type=jnp.float32)
    buffers = buffers.astype(jnp.bfloat16).reshape(experts, capacity, model_width)
    arrived = lax.all_to_all(buffers, "wide", split_axis=0, concat_axis=1, tiled=True)
    expert_inner = (
        jnp.einsum("erd,edf->erf", arrived, expert_in, preferred_element_type=jnp.float32)
        + expert_in_bias[:, None, :]
    )
    expert_act = jax.nn.gelu(expert_inner).astype(jnp.bfloat16)
    expert_partial = jnp.einsum(
        "erf,efd->erd", expert_act, expert_out, preferred_element_type=jnp.float32
    )
    expert_result = (
        lax.psum(expert_partial.astype(jnp.bfloat16), "tensor").astype(jnp.float32)
        + expert_out_bias[:, None, :]
    ).astype(jnp.bfloat16)
    returned = lax.all_to_all(
        expert_result, "wide", split_axis=1, concat_axis=0, tiled=True
    ).reshape(experts * capacity, model_width)
    picked = jnp.einsum("jtk,kd->jtd", tables, returned, preferred_element_type=jnp.float32)
    expert_range = jnp.arange(experts, dtype=jnp.int32)
    chosen = (expert_ids.T[:, :, None] == expert_range[None, None, :]).astype(jnp.float32) * kept[
        :, :, None
    ].astype(jnp.float32)
    gates = jnp.sum(chosen * route[None], axis=-1)
    mixture = jnp.sum(gates[:, :, None] * picked, axis=0)
    block_out = (second + mixture).astype(jnp.bfloat16)
    gate_grad = jnp.sum(picked * cotangent[None], axis=-1)
    weighted = (gates[:, :, None] * cotangent[None]).astype(jnp.bfloat16)
    slot_grad = jnp.einsum("jtk,jtd->kd", tables, weighted, preferred_element_type=jnp.float32)
    slot_grad = slot_grad.astype(jnp.bfloat16).reshape(experts, capacity, model_width)
    result_grad = lax.all_to_all(slot_grad, "wide", split_axis=0, concat_axis=1, tiled=True)
    expert_out_bias_grad = jnp.sum(result_grad.astype(jnp.float32), axis=1)
    expert_out_grad = jnp.einsum(
        "erf,erd->efd", expert_act, result_grad, preferred_element_type=jnp.float32
    )
    act_grad = jnp.einsum(
        "erd,efd->erf", result_grad, expert_out, preferred_element_type=jnp.float32
    )
    expert_inner_grad = gelu_grad(expert_inner, act_grad).astype(jnp.bfloat16)
    expert_in_bias_grad = jnp.sum(expert_inner_grad.astype(jnp.float32), axis=1)
    expert_in_grad = jnp.einsum(
        "erd,erf->edf", arrived, expert_inner_grad, preferred_element_type=jnp.float32
    )
    arrived_partial = jnp.einsum(
        "erf,edf->erd", expert_inner_grad, expert_in, preferred_element_type=jnp.float32
    )
    arrived_grad = lax.psum(arrived_partial.astype(jnp.bfloat16), "tensor")
    buffer_grad = lax.all_to_all(
        arrived_grad, "wide", split_axis=1, concat_axis=0, tiled=True
    ).reshape(experts * capacity, model_width)
    moe_input_grad = jnp.dot(dispatch, buffer_grad, preferred_element_type=jnp.float32)
    route_grad = jnp.sum(gate_grad[:, :, None] * chosen, axis=0)
    logit_grad = route * (route_grad - jnp.sum(route * route_grad, axis=-1, keepdims=True))
    router_grad = jnp.einsum("td,te->de", normed_moe, logit_grad, precision=highest)
    moe_input_grad = moe_input_grad + jnp.einsum(
        "te,de->td", logit_grad, router_weight, precision=highest
    )
    second_part, moe_gain_grad, moe_shift_grad = norm_grad(
        second, moe_gain, moe_shift, moe_input_grad
    )
    second_grad = cotangent + second_part
    lowered_second = second_grad.astype(jnp.bfloat16)
    output_bias_grad = jnp.sum(second_grad, axis=0)
    output_weight_grad = jnp.einsum(
        "tf,td->fd", activated, lowered_second, preferred_element_type=jnp.float32
    )
    activated_grad = jnp.einsum(
        "td,fd->tf", lowered_second, output_weight, preferred_element_type=jnp.float32
    )
    inner_grad = gelu_grad(inner, activated_grad).astype(jnp.bfloat16)
    hidden_bias_grad = jnp.sum(inner_grad.astype(jnp.float32), axis=0)
    hidden_weight_grad = jnp.einsum(
        "td,tf->df", lowered_mid, inner_grad, preferred_element_type=jnp.float32
    )
    mid_partial = jnp.einsum(
        "tf,df->td", inner_grad, hidden_weight, preferred_element_type=jnp.float32
    )
    mid_grad = lax.psum(mid_partial, "tensor")
    first_part, mid_gain_grad, mid_shift_grad = norm_grad(first, mid_gain, mid_shift, mid_grad)
    first_grad = second_grad + first_part
    proj_bias_grad = jnp.sum(first_grad, axis=0)
    branch_grad = first_grad.astype(jnp.bfloat16)
    proj_weight_grad = jnp.einsum(
        "tk,td->kd", context, branch_grad, preferred_element_type=jnp.float32
    )
    context_grad = jnp.einsum(
        "td,kd->tk", branch_grad, proj_weight, preferred_element_type=jnp.float32
    )
    context_grad = context_grad.astype(jnp.bfloat16).reshape(images, PATCHES, local_heads, HEAD_DIM)
    scores = (
        jnp.einsum("bqhd,bkhd->bhqk", query, keys, preferred_element_type=jnp.float32) * score_scale
    )
    probs = jnp.exp(scores - log_total)
    weights = probs.astype(jnp.bfloat16)
    value_grad = jnp.einsum(
        "bhqk,bqhd->bkhd", weights, context_grad, preferred_element_type=jnp.float32
    )
    prob_grad = jnp.einsum(
        "bqhd,bkhd->bhqk", context_grad, values, preferred_element_type=jnp.float32
    )
    score_grad = (probs * (prob_grad - jnp.sum(probs * prob_grad, axis=-1, keepdims=True))).astype(
        jnp.bfloat16
    )
    query_grad = (
        jnp.einsum("bhqk,bkhd->bqhd", score_grad, keys, preferred_element_type=jnp.float32)
        * score_scale
    )
    key_grad = (
        jnp.einsum("bhqk,bqhd->bkhd", score_grad, query, preferred_element_type=jnp.float32)
        * score_scale
    )
    qkv_grad = jnp.stack([query_grad, key_grad, value_grad], axis=2).astype(jnp.bfloat16)
    qkv_grad = qkv_grad.reshape(tokens, 3, local_heads * HEAD_DIM)
    qkv_sums = jnp.sum(qkv_grad.astype(jnp.float32), axis=0)
    qv_bias_grad = jnp.stack([qkv_sums[0], qkv_sums[2]])
    qkv_weight_grad = jnp.einsum(
        "td,tsk->dsk", lowered_pre, qkv_grad, preferred_element_type=jnp.float32
    )
    pre_partial = jnp.einsum(
        "tsk,dsk->td", qkv_grad, qkv_weight, preferred_element_type=jnp.float32
    )
    pre_grad = lax.psum(pre_partial.astype(jnp.bfloat16), "tensor").astype(jnp.float32)
    input_part, pre_gain_grad, pre_shift_grad = norm_grad(residual, pre_gain, pre_shift, pre_grad)
    tokens_grad = first_grad + input_part
    shared = (
        lax.psum(pre_gain_grad.astype(jnp.bfloat16), "wide").astype(jnp.float32),
        lax.psum(pre_shift_grad.astype(jnp.bfloat16), "wide").astype(jnp.float32),
        lax.psum(qkv_weight_grad.astype(jnp.bfloat16), "wide").astype(jnp.float32),
        lax.psum(qv_bias_grad.astype(jnp.bfloat16), "wide").astype(jnp.float32),
        lax.psum(proj_weight_grad.astype(jnp.bfloat16), "wide").astype(jnp.float32),
        lax.psum(proj_bias_grad.astype(jnp.bfloat16), "wide").astype(jnp.float32),
        lax.psum(mid_gain_grad.astype(jnp.bfloat16), "wide").astype(jnp.float32),
        lax.psum(mid_shift_grad.astype(jnp.bfloat16), "wide").astype(jnp.float32),
        lax.psum(hidden_weight_grad.astype(jnp.bfloat16), "wide").astype(jnp.float32),
        lax.psum(hidden_bias_grad.astype(jnp.bfloat16), "wide").astype(jnp.float32),
        lax.psum(output_weight_grad.astype(jnp.bfloat16), "wide").astype(jnp.float32),
        lax.psum(output_bias_grad.astype(jnp.bfloat16), "wide").astype(jnp.float32),
        lax.psum(moe_gain_grad.astype(jnp.bfloat16), "wide").astype(jnp.float32),
        lax.psum(moe_shift_grad.astype(jnp.bfloat16), "wide").astype(jnp.float32),
        lax.psum(router_grad.astype(jnp.bfloat16), "wide").astype(jnp.float32),
    )
    return (
        (block_out, tokens_grad)
        + tuple(shared)
        + (expert_in_grad, expert_in_bias_grad, expert_out_grad, expert_out_bias_grad)
    )


def solution(mesh):
    body = functools.partial(shards, mesh.shape["wide"]) if mesh.shape["tensor"] == 2 else plain
    return jax.shard_map(
        body,
        mesh=mesh,
        in_specs=(
            P("wide", None), P(), P(), P(None, None, "tensor"), P(None, "tensor"), P("tensor", None), P(), P(), P(),
            P(None, "tensor"), P("tensor"), P("tensor", None), P(), P(), P(), P(),
            P("wide", None, "tensor"), P("wide", "tensor"), P("wide", "tensor", None), P("wide", None),
            P("wide", None), P("wide", None), P("wide", None),
        ),
        out_specs=(
            P("wide", None), P("wide", None), P(), P(), P(None, None, "tensor"), P(None, "tensor"), P("tensor", None),
            P(), P(), P(), P(None, "tensor"), P("tensor"), P("tensor", None), P(), P(), P(), P(),
            P("wide", None, "tensor"), P("wide", "tensor"), P("wide", "tensor", None), P("wide", None),
        ),
        check_vma=False,
    )
```

```python
import functools

import jax
import jax.numpy as jnp
from jax import lax
from jax.experimental import pallas as pl
from jax.experimental.pallas import tpu as pltpu
from jax.sharding import PartitionSpec as P

HEAD_DIM = 64
PATCHES = 144
BF16 = jnp.bfloat16
F32 = jnp.float32
HIGHEST = lax.Precision.HIGHEST
MESH = pl.DeviceIdType.MESH
VMEM_BYTES = 60 * 1024 * 1024


def dot(left, right):
    return jnp.dot(left, right, preferred_element_type=F32)


def dot_rows(left, right):
    return lax.dot_general(left, right, (((1,), (1,)), ((), ())), preferred_element_type=F32)


def dot_columns(left, right, precision=None):
    return lax.dot_general(
        left, right, (((0,), (0,)), ((), ())), precision=precision, preferred_element_type=F32
    )


def normalized(values):
    centered = values - jnp.mean(values, axis=-1, keepdims=True)
    variance = jnp.mean(centered * centered, axis=-1, keepdims=True)
    scale = lax.rsqrt(variance + 1e-06)
    return centered * scale, scale


def norm_back(rows, scale, gain, upstream):
    scaled = upstream * gain
    inward = jnp.mean(scaled, axis=-1, keepdims=True)
    along = jnp.mean(scaled * rows, axis=-1, keepdims=True)
    return scale * (scaled - inward - rows * along)


def gelu_parts(inner):
    square = inner * inner
    bend = jnp.tanh(0.7978845608028654 * inner * (1.0 + 0.044715 * square))
    half = 0.5 * (1.0 + bend)
    slope = half + (0.5 * 0.7978845608028654) * inner * (1.0 - bend * bend) * (
        1.0 + 0.134145 * square
    )
    return inner * half, slope


def gelu(inner):
    return inner * (0.5 * (1.0 + jnp.tanh(0.7978845608028654 * inner * (1.0 + 0.044715 * inner * inner))))


def softmax_rows(scores, scale):
    peak = jnp.max(scores, axis=-1, keepdims=True)
    weights = jnp.exp((scores - peak) * scale)
    return weights * (1.0 / jnp.sum(weights, axis=-1, keepdims=True))


def spots(places):
    lane = lax.broadcasted_iota(jnp.int32, (places.shape[0], 128), 1)
    return [(lane == places[:, j : j + 1]).astype(F32) for j in range(2)]


def bits_of(index, wide):
    return [lax.rem(lax.div(index, 1 << k), 2) for k in range(wide.bit_length() - 1)]


class Sums:
    def __init__(self, wide, orders, totals, sends, lands, gathers, send_sems, recv_sems):
        me, self.plane = lax.axis_index("wide"), lax.axis_index("tensor")
        self.bits = bits_of(me, wide)
        self.partners = [me + (1 - 2 * bit) * (1 << k) for k, bit in enumerate(self.bits)]
        self.steps = len(self.bits)
        self.orders, self.totals, self.sends, self.lands, self.gathers = orders, totals, sends, lands, gathers
        self.send_sems, self.recv_sems = send_sems, recv_sems

    def piece(self, i, step):
        rows = self.gathers[i].shape[0]
        base = 0
        for s in range(step):
            base = base + self.bits[self.orders[i][s]] * (rows >> (s + 1))
        length = rows >> (step + 1)
        bit = self.bits[self.orders[i][step]]
        return pl.multiple_of(base + bit * length, 16), pl.multiple_of(base + (1 - bit) * length, 16), length

    def staged(self, i, step):
        rows = self.gathers[i].shape[0]
        return rows - (rows >> step)

    def transfer(self, i, k):
        step = k if k < self.steps else 2 * self.steps - 1 - k
        kept, _, length = self.piece(i, step)
        if k < self.steps:
            at = self.staged(i, step)
            source, target = self.sends[i].at[pl.ds(at, length)], self.lands[i].at[pl.ds(at, length)]
        else:
            source = target = self.gathers[i].at[pl.ds(kept, length)]
        return pltpu.make_async_remote_copy(
            source, target, self.send_sems.at[i, k], self.recv_sems.at[i, k],
            device_id=(self.partners[self.orders[i][step]], self.plane), device_id_type=MESH,
        )

    def begin(self, i, k):
        if k < self.steps:
            _, other, length = self.piece(i, k)
            at = self.staged(i, k)
            self.sends[i][at : at + length, :] = self.totals[i][pl.ds(other, length), :].astype(BF16)
        self.transfer(i, k).start()

    def advance(self, i, k):
        self.transfer(i, k).wait()
        if k < self.steps:
            kept, _, length = self.piece(i, k)
            at = self.staged(i, k)
            value = self.totals[i][pl.ds(kept, length), :] + self.lands[i][at : at + length, :].astype(F32)
            if k + 1 < self.steps:
                self.totals[i][pl.ds(kept, length), :] = value
            else:
                self.gathers[i][pl.ds(kept, length), :] = value.astype(BF16)
        if k + 1 < 2 * self.steps:
            self.begin(i, k + 1)


def greet(wide):
    me, plane = lax.axis_index("wide"), lax.axis_index("tensor")
    barrier = pltpu.get_barrier_semaphore()

    def hail(d, carry):
        pl.semaphore_signal(barrier, inc=1, device_id=(lax.rem(me + d, wide), plane), device_id_type=MESH)
        return carry

    lax.fori_loop(1, wide, hail, 0)
    pl.semaphore_signal(barrier, inc=1, device_id=(me, 1 - plane), device_id_type=MESH)
    pl.semaphore_wait(barrier, wide)


def put_row(small, at, row):
    for c in range(row.shape[1] // 128):
        small[at + c : at + c + 1, :] = row[:, 128 * c : 128 * (c + 1)]
    return at + row.shape[1] // 128


def get_row(small, at, width):
    return jnp.concatenate([small[at + c : at + c + 1, :] for c in range(width // 128)], axis=1)


def image_back(heads, qkv, context_grad):
    width = heads * HEAD_DIM
    scale = HEAD_DIM**-0.5
    parts = [[], [], []]
    for head in range(heads):
        h = head * HEAD_DIM
        query = qkv[:, h : h + HEAD_DIM]
        keys = qkv[:, width + h : width + h + HEAD_DIM]
        values = qkv[:, 2 * width + h : 2 * width + h + HEAD_DIM]
        upstream = context_grad[:, h : h + HEAD_DIM]
        probs = softmax_rows(dot_rows(query, keys), scale)
        prob_grad = dot_rows(upstream, values)
        inward = jnp.sum(probs * prob_grad, axis=-1, keepdims=True)
        score_grad = (probs * (prob_grad - inward)).astype(BF16)
        parts[0].append(dot(score_grad, keys) * scale)
        parts[1].append(dot_columns(score_grad, query) * scale)
        parts[2].append(dot_columns(probs.astype(BF16), upstream))
    return jnp.concatenate(parts[0] + parts[1] + parts[2], axis=1).astype(BF16)


def column_dots(left, right, put, tile=256):
    def body(i, carry):
        at = pl.multiple_of(i * tile, tile)
        put(at, tile, dot_columns(left[:, pl.ds(at, tile)], right[...]))
        return carry

    lax.fori_loop(0, left.shape[1] // tile, body, 0)


def image_forward(heads, qkv):
    width = heads * HEAD_DIM
    parts = []
    for head in range(heads):
        h = head * HEAD_DIM
        probs = softmax_rows(
            dot_rows(qkv[:, h : h + HEAD_DIM], qkv[:, width + h : width + h + HEAD_DIM]), HEAD_DIM**-0.5
        )
        parts.append(dot(probs.astype(BF16), qkv[:, 2 * width + h : 2 * width + h + HEAD_DIM]))
    return jnp.concatenate(parts, axis=1).astype(BF16)


def token_hits(choices, slots):
    slot = lax.broadcasted_iota(jnp.int32, (choices.shape[0], slots), 1)
    return [slot == choices[:, j : j + 1] for j in range(2)]


def slot_hits(first, count, targets):
    slot = first + lax.broadcasted_iota(jnp.int32, (count, targets.shape[1]), 0)
    return ((slot == targets[0:1, :]) | (slot == targets[1:2, :])).astype(BF16)


def count_slots(ids, priority, experts, capacity, room):
    tokens = ids.shape[1]
    wide_rows = jnp.concatenate([ids, priority, jnp.zeros((5, tokens), jnp.int32)], axis=0)
    eye = lax.broadcasted_iota(jnp.int32, (8, 8), 0) == lax.broadcasted_iota(jnp.int32, (8, 8), 1)
    turned = dot_columns(wide_rows.astype(F32), eye.astype(F32), HIGHEST).astype(jnp.int32)
    rank, ranks = turned[:, 2:3], priority

    def fold(numbers, own, before, axis):
        later = [jnp.where(numbers == own[0], before, 0.0), jnp.where(numbers == own[1] + experts, before, 0.0)]
        return [jnp.sum(part, axis=axis, keepdims=True) for part in later]

    def finish(own, counts, firsts):
        counts = [counts[0], counts[1] + firsts]
        places = [count.astype(jnp.int32) for count in counts]
        kept = [place < capacity for place in places]
        return (
            [jnp.where(keep, choice * room + place, -1) for keep, choice, place in zip(kept, own, places)],
            [jnp.where(keep, choice, -1) for keep, choice in zip(kept, own)],
            [jnp.where(keep, place, -1) for keep, place in zip(kept, places)],
        )

    number = lax.broadcasted_iota(jnp.int32, (2 * experts, tokens), 0)
    by_row = [ids[0:1, :], ids[1:2, :]]
    held = ((number == by_row[0]) | (number == by_row[1] + experts)).astype(BF16)
    before = dot(held, (rank < ranks).astype(BF16))
    first_counts = jnp.sum(held.astype(F32), axis=1, keepdims=True)
    firsts = jnp.sum(jnp.where(number == by_row[1], first_counts, 0.0), axis=0, keepdims=True)
    targets, _, _ = finish(by_row, fold(number, by_row, before, 0), firsts)

    number = lax.broadcasted_iota(jnp.int32, (tokens, 2 * experts), 1)
    by_token = [turned[:, 0:1], turned[:, 1:2]]
    held_by_token = ((number == by_token[0]) | (number == by_token[1] + experts)).astype(BF16)
    before = dot((ranks < rank).astype(BF16), held_by_token)
    first_counts = jnp.sum(held_by_token.astype(F32), axis=0, keepdims=True)
    firsts = jnp.sum(jnp.where(number == by_token[1], first_counts, 0.0), axis=1, keepdims=True)
    groups = finish(by_token, fold(number, by_token, before, 1), firsts)
    choices = jnp.concatenate([part for group in groups for part in group], axis=1)
    return jnp.concatenate(targets, axis=0), choices


def front(
    wide, room, group, heads, rows, experts,
    tokens_h, cotangent_h, weight_qkv_h, projection_h, hidden_h, output_h, weight_in_h, weight_out_h,
    ids, priority, pre_gain, pre_shift, qv_bias, proj_bias, mid_gain, mid_shift, hidden_bias, output_bias,
    moe_gain, moe_shift, router, bias_in, bias_out,
    qkv_h, context_h, first_h, second_h, info_h, result_h, in_grad_h, out_grad_h, own_home, peer_home,
    gate_home, in_bias_grad, out_bias_grad,
    tokens, cotangent, weight_qkv, projection, hidden, output, weight_in, weight_out,
    qkv, context, first, second, info, result, in_grad, out_grad,
    targets, table, raised_placed, upstream, projection_peer, context_peer, partial_own, partial_peer,
    columns, placed, rows_own, rows_peer, act, inner_grad, slot_grad, grad_kept, grad_sent, grad_landed,
    grad_back, gate_sent, gate_arrived, gate_back, gate_own, gate_peer,
    sems, load_sems, chunk_sems, store_sems, group_sems,
):
    me, plane = lax.axis_index("wide"), lax.axis_index("tensor")
    chunks, groups = tokens.shape[0] // rows, wide // group
    mine = lax.div(me, group)
    block = group * room
    width = heads * HEAD_DIM
    half = columns.shape[1]
    capacity = tokens.shape[0] // experts
    row_at, gate_at, home_at, back_at, up_at = 0, wide, 2 * wide, 3 * wide, 4 * wide
    grad_at, share_at, join_at = 5 * wide, 5 * wide + groups, 5 * wide + 2 * groups
    context_at = 5 * wide + 3 * groups
    partial_at, last_at = context_at + chunks, context_at + 2 * chunks

    def rows_of(index):
        return pl.ds(pl.multiple_of(index * room, 16), room)

    def rows_of_group(index):
        return pl.ds(pl.multiple_of(index * block, 16), block)

    def chunk_of(index):
        return pl.ds(pl.multiple_of(index * rows, 16), rows)

    def load_tokens(c):
        return pltpu.make_async_copy(tokens_h.at[chunk_of(c)], tokens.at[chunk_of(c)], chunk_sems.at[c])

    def start_tokens(c, carry):
        load_tokens(c).start()
        return carry

    loads = [
        pltpu.make_async_copy(source, target, load_sems.at[i])
        for i, (source, target) in enumerate(
            [(weight_qkv_h, weight_qkv), (projection_h, projection), (hidden_h, hidden), (output_h, output),
             (cotangent_h, cotangent), (weight_in_h, weight_in), (weight_out_h, weight_out)]
        )
    ]
    loads[0].start()
    lax.fori_loop(0, chunks, start_tokens, 0)
    for load in loads[1:]:
        load.start()

    def store(kind, source, target, c):
        return pltpu.make_async_copy(source.at[chunk_of(c)], target.at[chunk_of(c)], store_sems.at[kind, c])

    stores = [(qkv, qkv_h), (context, context_h), (first, first_h), (second, second_h), (info, info_h)]
    greet(wide)

    def move(source, target, base, sent, landed, device):
        return pltpu.make_async_remote_copy(
            source, target, sems.at[0, base + sent], sems.at[1, base + landed], device_id=device, device_id_type=MESH
        )

    def across_chunk(source, target, base, index):
        there = chunk_of(index)
        return move(source.at[there], target.at[there], base, index, index, (me, 1 - plane))

    def up_copy(other, sender):
        return move(raised_placed.at[rows_of(other)], upstream.at[rows_of(sender)], up_at, other, sender, (other, plane))

    weights = move(projection_h, projection_peer, last_at, 0, 0, (me, 1 - plane))
    weights.start()
    first_plane = plane == 0
    table[...] = jnp.zeros_like(table)
    in_bias_grad[...] = jnp.zeros_like(in_bias_grad)
    out_bias_grad[...] = jnp.zeros_like(out_bias_grad)

    def attend_chunk(c):
        there = chunk_of(c)
        load_tokens(c).wait()
        normed, _ = normalized(tokens[there, :].astype(F32))
        lowered = (normed * pre_gain[...] + pre_shift[...]).astype(BF16)
        parts = [dot(lowered, weight_qkv[s]) for s in range(3)]
        parts = [parts[0] + qv_bias[0:1, :], parts[1], parts[2] + qv_bias[1:2, :]]
        value = jnp.concatenate(parts, axis=1).astype(BF16)
        qkv[there, :] = value
        contexts = [
            image_forward(heads, value[image * PATCHES : (image + 1) * PATCHES]) for image in range(rows // PATCHES)
        ]
        context[there, :] = jnp.concatenate(contexts, axis=0)
        across_chunk(context, context_peer, context_at, c).start()
        store(0, qkv, qkv_h, c).start()
        store(1, context, context_h, c).start()

    def find_slots():
        by_row, choices = count_slots(ids[...], priority[...], experts, capacity, room)
        targets[0:2, :] = by_row
        info[:, experts : experts + 6] = choices.astype(F32)

    def raise_group(k):
        q = lax.rem(mine + k, groups)
        hits = slot_hits(q * block, block, targets)
        raised_placed[rows_of_group(q), :] = dot(hits, cotangent[...].astype(BF16)).astype(BF16)
        for j in range(group):
            e = q * group + j

            @pl.when(e != me)
            def _(e=e):
                up_copy(e, me).start()

            @pl.when(e == me)
            def _(e=e):
                upstream[rows_of(e), :] = raised_placed[rows_of(e), :]

    def feed_chunk(c):
        there = chunk_of(c)
        across_chunk(context, context_peer, context_at, c).wait()
        branch = dot(context[there, :], projection[...]) + dot(context_peer[there, :], projection_peer[...])
        value = tokens[there, :].astype(F32) + branch + proj_bias[...]
        first[there, :] = value
        normed, _ = normalized(value)
        lowered = (normed * mid_gain[...] + mid_shift[...]).astype(BF16)
        activated = gelu(dot(lowered, hidden[...]) + hidden_bias[...]).astype(BF16)
        partial_own[there, :] = dot(activated, output[...]).astype(BF16)
        across_chunk(partial_own, partial_peer, partial_at, c).start()
        store(2, first, first_h, c).start()

    def route_chunk(c):
        there = chunk_of(c)
        across_chunk(partial_own, partial_peer, partial_at, c).wait()
        partial = partial_own[there, :].astype(F32) + partial_peer[there, :].astype(F32)
        value = first[there, :] + partial + output_bias[...]
        second[there, :] = value
        normed, _ = normalized(value)
        normed = normed * moe_gain[...] + moe_shift[...]
        columns[there, :] = jnp.where(first_plane, normed[:, :half], normed[:, half:]).astype(BF16)
        logits = lax.dot_general(
            normed, router[...], (((1,), (1,)), ((), ())), precision=HIGHEST, preferred_element_type=F32
        )
        grown = jnp.exp(logits - jnp.max(logits, axis=-1, keepdims=True))
        route = grown / jnp.sum(grown, axis=-1, keepdims=True)
        info[there, 0:experts] = route
        number = lax.broadcasted_iota(jnp.int32, route.shape, 1)
        picks = info[there, experts : experts + 6].astype(jnp.int32)
        for j, spot in enumerate(spots(picks[:, 4:6])):
            table[...] += dot_columns(jnp.where(number == picks[:, 2 + j : 3 + j], route, 0.0), spot, HIGHEST)
        store(3, second, second_h, c).start()
        store(4, info, info_h, c).start()

    def turn(c, carry):
        @pl.when(c < chunks)
        def _():
            attend_chunk(c)

        @pl.when(c == 0)
        def _():
            loads[4].wait()
            find_slots()

        @pl.when(c < groups)
        def _():
            raise_group(c)

        @pl.when(c == 1)
        def _():
            weights.wait()
            for load in loads[1:4]:
                load.wait()

        @pl.when((c >= 1) & (c <= chunks))
        def _():
            feed_chunk(c - 1)

        @pl.when(c >= 2)
        def _():
            route_chunk(c - 2)

        return carry

    info[...] = jnp.zeros_like(info)
    loads[0].wait()
    lax.fori_loop(0, chunks + 2, turn, 0)

    def row_copy(other, sender):
        return move(placed.at[rows_of(other)], rows_own.at[rows_of(sender)], row_at, other, sender, (other, plane))

    def gate_copy(other, sender):
        return move(gate_sent.at[other], gate_arrived.at[sender], gate_at, other, sender, (other, plane))

    def home_copy(other, sender):
        return move(grad_back.at[rows_of(other)], own_home.at[rows_of(sender)], home_at, other, sender, (other, plane))

    def back_copy(other, sender):
        return move(gate_back.at[other], gate_own.at[sender], back_at, other, sender, (other, plane))

    def across(source, target, base, index):
        there = rows_of_group(index)
        return move(source.at[there], target.at[there], base, index, index, (me, 1 - plane))

    own_half = pl.ds(pl.multiple_of(plane * half, 16), half)
    peer_half = pl.ds(pl.multiple_of((1 - plane) * half, 16), half)
    for e in range(wide):
        gate_sent[e] = jnp.broadcast_to(table[e : e + 1, :], gate_sent.shape[1:])

    def place_group(k, carry):
        q = lax.rem(mine + k, groups)
        placed[rows_of_group(q), :] = dot(slot_hits(q * block, block, targets), columns[...]).astype(BF16)
        for j in range(group):
            e = q * group + j

            @pl.when(e != me)
            def _(e=e):
                row_copy(e, me).start()
                gate_copy(e, me).start()

            @pl.when(e == me)
            def _(e=e):
                rows_own[rows_of(e), :] = placed[rows_of(e), :]
                gate_arrived[e] = gate_sent[e]

        return carry

    lax.fori_loop(0, groups, place_group, 0)
    loads[5].wait()
    loads[6].wait()
    diagonal = lax.broadcasted_iota(jnp.int32, (room, 128), 0) == lax.broadcasted_iota(jnp.int32, (room, 128), 1)

    def store_result(p):
        there = rows_of_group(p)
        return pltpu.make_async_copy(result.at[there], result_h.at[there], group_sems.at[p])

    def join_group(p):
        for j in range(group):
            w = p * group + j

            @pl.when(w != me)
            def _(w=w):
                row_copy(w, w).wait_recv()
                gate_copy(w, w).wait_recv()

        across(rows_own, rows_peer, join_at, p).start()
        for j in range(group):
            w = p * group + j

            @pl.when(w != me)
            def _(w=w):
                up_copy(w, w).wait_recv()

    def expert_group(p):
        there = rows_of_group(p)
        across(rows_own, rows_peer, join_at, p).wait()
        gates = jnp.concatenate(
            [
                jnp.sum(jnp.where(diagonal, gate_arrived[p * group + j][0:1, :], 0.0), axis=1, keepdims=True)
                for j in range(group)
            ],
            axis=0,
        )
        inner = dot(rows_own[there, :], weight_in[own_half, :]) + dot(rows_peer[there, :], weight_in[peer_half, :])
        acted, slope = gelu_parts(inner + bias_in[...])
        acted = acted.astype(BF16)
        act[there, :] = acted
        raised = upstream[there, :].astype(F32)
        slot = (raised * gates).astype(BF16)
        slot_grad[there, :] = slot
        inward = (dot_rows(slot, weight_out[...]) * slope).astype(BF16)
        inner_grad[there, :] = inward
        grad_sent[there, :] = dot_rows(inward, weight_in[peer_half, :]).astype(BF16)
        across(grad_sent, grad_landed, grad_at, p).start()
        grad_kept[there, :] = dot_rows(inward, weight_in[own_half, :])
        value = dot(acted, weight_out[...]) + bias_out[...] * jnp.where(first_plane, 1.0, 0.0)
        result[there, :] = value.astype(BF16)
        store_result(p).start()
        out_bias_grad[0:1, :] += jnp.sum(slot.astype(F32), axis=0, keepdims=True)
        in_bias_grad[0:1, :] += jnp.sum(inward.astype(F32), axis=0, keepdims=True)
        slopes = jnp.sum(raised * value, axis=1, keepdims=True)
        for j in range(group):
            w = p * group + j
            row = jnp.sum(
                jnp.where(diagonal, slopes[j * room : (j + 1) * room], 0.0), axis=0, keepdims=True
            )
            gate_back[w] = jnp.broadcast_to(row, gate_back.shape[1:])

            @pl.when(w != me)
            def _(w=w):
                back_copy(w, me).start()

            @pl.when(w == me)
            def _(w=w):
                gate_own[w] = gate_back[w]

    own_rows = pltpu.make_async_copy(grad_back.at[rows_of(me)], own_home.at[rows_of(me)], group_sems.at[groups])

    def give_back(p):
        across(grad_sent, grad_landed, grad_at, p).wait()
        there = rows_of_group(p)
        grad_back[there, :] = (grad_kept[there, :] + grad_landed[there, :].astype(F32)).astype(BF16)
        for j in range(group):
            w = p * group + j

            @pl.when(w != me)
            def _(w=w):
                home_copy(w, me).start()

            @pl.when(w == me)
            def _(w=w):
                own_rows.start()

    def expert_turn(k, carry):
        @pl.when(k < groups)
        def _():
            join_group(lax.rem(mine + groups - k, groups))

        @pl.when((k >= 1) & (k <= groups))
        def _():
            expert_group(lax.rem(mine + groups - k + 1, groups))

        @pl.when(k >= 2)
        def _():
            give_back(lax.rem(mine + groups - k + 2, groups))

        return carry

    lax.fori_loop(0, groups + 2, expert_turn, 0)
    own_rows.wait()
    tile = act.shape[1] // groups

    def share_group(k, carry):
        at = pl.multiple_of(k * tile, 128)
        out_grad[pl.ds(at, tile), :] = dot_columns(act[:, pl.ds(at, tile)], slot_grad[...]).astype(BF16)
        q = lax.rem(mine + k, groups)
        for j in range(group):
            e = q * group + j

            @pl.when(e != me)
            def _(e=e):
                home_copy(e, e).wait_recv()

        across(own_home, peer_home, share_at, q).start()
        return carry

    lax.fori_loop(0, groups, share_group, 0)
    out_store = pltpu.make_async_copy(out_grad, out_grad_h, load_sems.at[7])
    out_store.start()

    def take_gates(d, carry):
        other = lax.rem(me + d, wide)
        back_copy(other, other).wait_recv()
        return carry

    lax.fori_loop(1, wide, take_gates, 0)
    tables = move(gate_own, gate_peer, last_at, 1, 1, (me, 1 - plane))
    tables.start()
    in_grad[own_half, :] = dot_columns(rows_own[...], inner_grad[...]).astype(BF16)
    in_grad[peer_half, :] = dot_columns(rows_peer[...], inner_grad[...]).astype(BF16)
    in_store = pltpu.make_async_copy(in_grad, in_grad_h, load_sems.at[8])
    in_store.start()

    def end_sends(d, carry):
        other = lax.rem(me + d, wide)
        up_copy(other, me).wait_send()
        row_copy(other, me).wait_send()
        gate_copy(other, me).wait_send()
        home_copy(other, me).wait_send()
        back_copy(other, me).wait_send()
        return carry

    lax.fori_loop(1, wide, end_sends, 0)

    def end_stores(c, carry):
        for kind, (source, target) in enumerate(stores):
            store(kind, source, target, c).wait()
        return carry

    lax.fori_loop(0, chunks, end_stores, 0)
    tables.wait()
    for e in range(wide):
        gate_home[e : e + 1, :] = gate_own[e][0:1, :] + gate_peer[e][0:1, :]

    def end_groups(q, carry):
        store_result(q).wait()
        across(own_home, peer_home, share_at, q).wait()
        return carry

    lax.fori_loop(0, groups, end_groups, 0)
    out_store.wait()
    in_store.wait()


def backward(
    wide, room, heads, layout, orders, rows,
    second_h, cotangent_h, info_h, first_h, tokens_h, qkv_h, context_h, hidden_h, output_h, projection_h, weight_qkv_h,
    row_own_h, row_peer_h, result,
    moe_gain, moe_shift, router, gate_grads, mid_gain, mid_shift, pre_gain, pre_shift, hidden_bias,
    block_h, grad_h, hidden_out_h, output_out_h, qkv_out_h, proj_out_h, *rest,
):
    vectors_out, pre_out, rest = rest[: len(layout)], rest[len(layout)], rest[len(layout) + 1 :]
    (second, cotangent, info, first, tokens, qkv, context, hidden, output, projection, weight_qkv, row_own, row_peer,
     block_out, grad_out, hidden_out, output_out, qkv_out, proj_out), rest = rest[:19], rest[19:]
    load_sems, chunk_sems, store_sems, rest = rest[-3], rest[-2], rest[-1], rest[:-3]
    (lowered_mid, act, inner_grad, mid_own, mid_peer, branch, qkv_grad, lowered_pre, pre_peer, result_own, blend_peer,
     pre_tile, pre_tiles, pre_total, pre_other, moe_sums, router_sums, mid_sums, hidden_sums, qkv_sums, pre_sums, small_sums) = rest[:22]
    hidden_total, output_total, qkv_total, proj_total, small = rest[22:27]
    sends, lands = rest[27:33], rest[33:39]
    mid_sems, pre_sems, blend_sems, result_sems, send_sems, recv_sems = rest[39:]
    blend_own = lowered_mid
    me, plane = lax.axis_index("wide"), lax.axis_index("tensor")
    chunks = tokens.shape[0] // rows
    model = tokens.shape[1]
    width = heads * HEAD_DIM
    split = qkv_total.shape[0] // 2
    totals = (
        hidden_total, output_total, qkv_total.at[pl.ds(0, split)], qkv_total.at[pl.ds(split, split)], proj_total, small
    )
    gathers = (
        hidden_out, output_out, qkv_out.at[pl.ds(0, split)], qkv_out.at[pl.ds(split, split)], proj_out, small_sums
    )

    def chunk_of(index):
        return pl.ds(pl.multiple_of(index * rows, 16), rows)

    early = [(info_h, info), (second_h, second), (cotangent_h, cotangent), (first_h, first)]
    late = [(tokens_h, tokens), (qkv_h, qkv)]

    def load(kind, pair, c):
        return pltpu.make_async_copy(pair[0].at[chunk_of(c)], pair[1].at[chunk_of(c)], chunk_sems.at[kind, c])

    def start_early(c, carry):
        for kind, pair in enumerate(early):
            load(kind, pair, c).start()
        return carry

    def start_late(c, carry):
        for kind, pair in enumerate(late):
            load(len(early) + kind, pair, c).start()
        return carry

    loads = [
        pltpu.make_async_copy(source, target, load_sems.at[i])
        for i, (source, target) in enumerate(
            [(row_own_h, row_own), (row_peer_h, row_peer), (hidden_h, hidden), (output_h, output),
             (projection_h, projection), (weight_qkv_h, weight_qkv), (context_h, context)]
        )
    ]
    for part in loads[:2]:
        part.start()
    start_early(0, 0)
    for part in loads[2:4]:
        part.start()
    lax.fori_loop(1, chunks, start_early, 0)
    for part in loads[4:]:
        part.start()
    lax.fori_loop(0, chunks, start_late, 0)
    whole_stores = [
        pltpu.make_async_copy(source, target, load_sems.at[len(loads) + i])
        for i, (source, target) in enumerate(
            [(hidden_out, hidden_out_h), (output_out, output_out_h), (qkv_out, qkv_out_h), (proj_out, proj_out_h)]
        )
    ]

    def store(kind, source, target, c):
        return pltpu.make_async_copy(source.at[chunk_of(c)], target.at[chunk_of(c)], store_sems.at[kind, c])

    greet(wide)
    sums = Sums(wide, orders, totals, sends, lands, gathers, send_sems, recv_sems)

    def rows_of(index):
        return pl.ds(pl.multiple_of(index * room, 16), room)

    def result_copy(other, sender):
        return pltpu.make_async_remote_copy(
            result.at[rows_of(other)], result_own.at[rows_of(sender)], result_sems.at[0, other],
            result_sems.at[1, sender], device_id=(other, plane), device_id_type=MESH,
        )

    def send_result(d, carry):
        result_copy(lax.rem(me + d, wide), me).start()
        return carry

    lax.fori_loop(1, wide, send_result, 0)
    own_rows = pltpu.make_async_copy(
        result.at[rows_of(me)], result_own.at[rows_of(me)], load_sems.at[len(loads) + len(whole_stores)]
    )
    own_rows.start()

    def across(own, peer, sems, chunk):
        at = pl.multiple_of(chunk * rows, rows)
        return pltpu.make_async_remote_copy(
            own.at[pl.ds(at, rows)], peer.at[pl.ds(at, rows)], sems.at[0, chunk], sems.at[1, chunk],
            device_id=(me, 1 - plane), device_id_type=MESH,
        )

    for vector in (moe_sums, router_sums, mid_sums, hidden_sums, qkv_sums, pre_sums):
        vector[...] = jnp.zeros_like(vector)
    first_plane = plane == 0

    def ordered(own, peer):
        return jnp.concatenate([jnp.where(first_plane, own, peer), jnp.where(first_plane, peer, own)], axis=1)

    def settle(here):
        experts = router.shape[0]
        picks = info[here, experts : experts + 6].astype(jnp.int32)
        hits = token_hits(picks, row_own.shape[0])
        table = (hits[0] | hits[1]).astype(BF16)
        moe_grad = ordered(dot(table, row_own[...]), dot(table, row_peer[...]))
        chances = info[here, 0:experts]
        number = lax.broadcasted_iota(jnp.int32, chances.shape, 1)
        route_grad = jnp.zeros_like(chances)
        for j, spot in enumerate(spots(picks[:, 4:6])):
            at_place = lax.dot_general(
                spot, gate_grads[...], (((1,), (1,)), ((), ())), precision=HIGHEST, preferred_element_type=F32
            )
            route_grad = route_grad + jnp.where(number == picks[:, 2 + j : 3 + j], at_place, 0.0)
        logit_grad = chances * (route_grad - jnp.sum(chances * route_grad, axis=1, keepdims=True))
        normed, scale = normalized(second[here, :])
        router_sums[...] += dot_columns(logit_grad, normed * moe_gain[...] + moe_shift[...], HIGHEST)
        moe_grad = moe_grad + jnp.dot(logit_grad, router[...], precision=HIGHEST, preferred_element_type=F32)
        grad = cotangent[here, :] + norm_back(normed, scale, moe_gain[...], moe_grad)
        grad_out[here, :] = grad
        branch[here, :] = grad.astype(BF16)
        moe_sums[0:1, :] += jnp.sum(moe_grad * normed, axis=0, keepdims=True)
        moe_sums[1:2, :] += jnp.sum(moe_grad, axis=0, keepdims=True)
        moe_sums[2:3, :] += jnp.sum(grad, axis=0, keepdims=True)

    def feed_chunk(chunk, carry):
        here = chunk_of(chunk)
        for kind, pair in enumerate(early):
            load(kind, pair, chunk).wait()
        settle(here)

        @pl.when(chunk == 0)
        def _():
            loads[2].wait()
            loads[3].wait()

        normed, _ = normalized(first[here, :])
        lowered = (normed * mid_gain[...] + mid_shift[...]).astype(BF16)
        lowered_mid[here, :] = lowered
        acted, slope = gelu_parts(dot(lowered, hidden[...]) + hidden_bias[...])
        act[here, :] = acted.astype(BF16)
        inward = (dot_rows(branch[here, :], output[...]) * slope).astype(BF16)
        inner_grad[here, :] = inward
        hidden_sums[0:1, :] += jnp.sum(inward.astype(F32), axis=0, keepdims=True)
        mid_own[here, :] = dot_rows(inward, hidden[...]).astype(BF16)
        across(mid_own, mid_peer, mid_sems, chunk).start()
        return carry

    loads[0].wait()
    loads[1].wait()
    lax.fori_loop(0, chunks, feed_chunk, 0)

    def put_in(total):
        def put(at, tile, value):
            total[pl.ds(at, tile), :] = value

        return put

    column_dots(lowered_mid, inner_grad, put_in(hidden_total))
    sums.begin(0, 0)
    column_dots(act, branch, put_in(output_total))
    sums.begin(1, 0)

    def attend_chunk(chunk, carry):
        here = pl.ds(pl.multiple_of(chunk * rows, rows), rows)
        for kind, pair in enumerate(late):
            load(len(early) + kind, pair, chunk).wait()
        across(mid_own, mid_peer, mid_sems, chunk).wait()
        mid_grad = mid_own[here, :].astype(F32) + mid_peer[here, :].astype(F32)
        normed, scale = normalized(first[here, :])
        first_grad = grad_out[here, :] + norm_back(normed, scale, mid_gain[...], mid_grad)
        grad_out[here, :] = first_grad
        lowered_grad = first_grad.astype(BF16)
        branch[here, :] = lowered_grad
        mid_sums[0:1, :] += jnp.sum(mid_grad * normed, axis=0, keepdims=True)
        mid_sums[1:2, :] += jnp.sum(mid_grad, axis=0, keepdims=True)
        mid_sums[2:3, :] += jnp.sum(first_grad, axis=0, keepdims=True)
        normed, _ = normalized(tokens[here, :].astype(F32))
        lowered_pre[here, :] = (normed * pre_gain[...] + pre_shift[...]).astype(BF16)
        context_grad = dot_rows(lowered_grad, projection[...]).astype(BF16)
        for image in range(rows // PATCHES):
            at = pl.multiple_of(chunk * rows + image * PATCHES, PATCHES)
            block = qkv[pl.ds(at, PATCHES), :]
            grad = image_back(heads, block, context_grad[image * PATCHES : (image + 1) * PATCHES])
            qkv_grad[pl.ds(at, PATCHES), :] = grad
            pre = sum(dot_rows(grad[:, s * width : (s + 1) * width], weight_qkv[s]) for s in range(3))
            pre = pre.astype(BF16)
            mid_own[pl.ds(at, PATCHES), :] = pre
            pre = pre.astype(F32)
            pre_sums[0:1, :] += jnp.sum(pre * normed[image * PATCHES : (image + 1) * PATCHES], axis=0, keepdims=True)
            pre_sums[1:2, :] += jnp.sum(pre, axis=0, keepdims=True)
            qkv_sums[0:1, :] += jnp.sum(grad.astype(F32), axis=0, keepdims=True)
            for k in range(sums.steps):

                @pl.when(chunk == k)
                def _(i=image, k=k):
                    if i < 2:
                        sums.advance(i, k)

        across(mid_own, pre_peer, pre_sems, chunk).start()
        return carry

    loads[4].wait()
    loads[5].wait()
    lax.fori_loop(0, chunks, attend_chunk, 0)
    loads[6].wait()

    small[...] = jnp.zeros_like(small)
    at = 0
    for vector, picked in zip((mid_sums, moe_sums, hidden_sums, qkv_sums, router_sums), layout):
        for r in picked:
            at = put_row(small, at, vector[r : r + 1, :])
    sums.begin(5, 0)
    put_row(pre_tile, put_row(pre_tile, 0, pre_sums[0:1, :]), pre_sums[1:2, :])

    def pre_copy(other, sender):
        return pltpu.make_async_remote_copy(
            pre_tile, pre_tiles.at[sender], result_sems.at[0, wide + other], result_sems.at[1, wide + sender],
            device_id=(other, plane), device_id_type=MESH,
        )

    def send_pre(d, carry):
        pre_copy(lax.rem(me + d, wide), me).start()
        return carry

    lax.fori_loop(1, wide, send_pre, 0)
    pre_tiles[me] = pre_tile[...]
    column_dots(context, branch, put_in(proj_total))
    sums.begin(4, 0)

    def put_thirds(at, tile, value):
        for s in range(3):
            there = pl.ds(pl.multiple_of(s * model + at, 16), tile)
            qkv_total[there, :] = value[:, s * width : (s + 1) * width]

    column_dots(lowered_pre, qkv_grad, put_thirds)
    sums.begin(2, 0)
    sums.begin(3, 0)

    def finish_chunk(chunk, carry):
        here = pl.ds(pl.multiple_of(chunk * rows, rows), rows)
        across(mid_own, pre_peer, pre_sems, chunk).wait()
        upstream = mid_own[here, :].astype(F32) + pre_peer[here, :].astype(F32)
        normed, scale = normalized(tokens[here, :].astype(F32))
        grad_out[here, :] += norm_back(normed, scale, pre_gain[...], upstream)
        store(0, grad_out, grad_h, chunk).start()
        return carry

    def take_result(d, carry):
        other = lax.rem(me + d, wide)
        result_copy(other, other).wait_recv()
        result_copy(other, me).wait_send()
        return carry

    lax.fori_loop(1, wide, take_result, 0)
    own_rows.wait()

    def blend(chunk, carry):
        here = pl.ds(pl.multiple_of(chunk * rows, rows), rows)
        experts = router.shape[0]
        picks, chances = info[here, experts : experts + 6].astype(jnp.int32), info[here, 0:experts]
        number = lax.broadcasted_iota(jnp.int32, chances.shape, 1)
        gates = [
            jnp.sum(jnp.where(number == picks[:, 2 + j : 3 + j], chances, 0.0), axis=1, keepdims=True)
            for j in range(2)
        ]
        hits = token_hits(picks, result_own.shape[0])
        table = jnp.where(hits[0], gates[0], jnp.where(hits[1], gates[1], 0.0)).astype(BF16)
        blend_own[here, :] = dot(table, result_own[...]).astype(BF16)
        across(blend_own, blend_peer, blend_sems, chunk).start()
        return carry

    def blend_end(chunk, carry):
        here = pl.ds(pl.multiple_of(chunk * rows, rows), rows)
        across(blend_own, blend_peer, blend_sems, chunk).wait()
        mixture = blend_own[here, :].astype(F32) + blend_peer[here, :].astype(F32)
        block_out[here, :] = (second[here, :] + mixture).astype(BF16)
        store(1, block_out, block_h, chunk).start()
        return carry

    def take_pre(d, carry):
        other = lax.rem(me + d, wide)
        pre_copy(other, other).wait_recv()
        pre_copy(other, me).wait_send()
        return carry

    pre_share = pltpu.make_async_remote_copy(
        pre_total, pre_other, result_sems.at[0, 2 * wide], result_sems.at[1, 2 * wide],
        device_id=(me, 1 - plane), device_id_type=MESH,
    )
    for k in range(2 * sums.steps):
        if k < sums.steps:
            for i in (0, 1):
                sums.advance(i, sums.steps + k)
        for i in (5, 4, 2, 3):
            sums.advance(i, k)
        if k < sums.steps:
            lax.fori_loop(k * chunks // sums.steps, (k + 1) * chunks // sums.steps, blend, 0)
            lax.fori_loop(k * chunks // sums.steps, (k + 1) * chunks // sums.steps, finish_chunk, 0)
        else:
            first_chunk = (k - sums.steps) * chunks // sums.steps
            lax.fori_loop(first_chunk, (k - sums.steps + 1) * chunks // sums.steps, blend_end, 0)
        if k == sums.steps - 1:
            for part in whole_stores[:2]:
                part.start()
            lax.fori_loop(1, wide, take_pre, 0)
            pre_total[...] = sum(pre_tiles[w] for w in range(wide))
            pre_share.start()
    for part in whole_stores[2:]:
        part.start()
    pre_share.wait()
    pre_tile[...] = pre_total[...] + pre_other[...]
    pre_out[0:1, :] = get_row(pre_tile, 0, model)
    pre_out[1:2, :] = get_row(pre_tile, model // 128, model)
    at = 0
    for out, picked in zip(vectors_out, layout):
        for i in range(len(picked)):
            out[i : i + 1, :] = get_row(small_sums, at, out.shape[1]).astype(F32)
            at += out.shape[1] // 128

    def end_stores(c, carry):
        store(0, grad_out, grad_h, c).wait()
        store(1, block_out, block_h, c).wait()
        return carry

    lax.fori_loop(0, chunks, end_stores, 0)
    for part in whole_stores:
        part.wait()


def widen(pairs, layout, *refs):
    ins, outs = refs[: pairs + len(layout)], refs[pairs + len(layout) :]
    for source, out in zip(ins[:pairs], outs[:pairs]):
        out[...] = source[...].astype(out.dtype)
    outs = iter(outs[pairs:])
    for source, picked in zip(ins[pairs:], layout):
        for r in picked:
            out = next(outs)
            out[...] = source[r : r + out.shape[0], : out.shape[1]]


def shards(
    wide,
    tokens_in, pre_gain, pre_shift, qkv_weight, qv_bias, proj_weight, proj_bias, mid_gain, mid_shift,
    hidden_weight, hidden_bias, output_weight, output_bias, moe_gain, moe_shift, router_weight,
    expert_in, expert_in_bias, expert_out, expert_out_bias, expert_ids, priority, cotangent,
):
    tokens, model = tokens_in.shape
    width = qkv_weight.shape[2]
    heads = width // HEAD_DIM
    hidden = hidden_weight.shape[1]
    count = router_weight.shape[1]
    capacity = tokens // count
    room = -(-capacity // 16) * 16
    slots = count * room
    half = model // 2
    lanes = 3 * width
    rows = 2 * PATCHES
    chunks = tokens // rows
    group = 4
    steps = wide.bit_length() - 1

    def row(vector):
        return vector.reshape(1, -1)

    def remote(kernel, name, identity, far_ins, ins, far_outs, outs, scratch):
        far, near = pl.BlockSpec(memory_space=pl.ANY), pl.BlockSpec(memory_space=pltpu.VMEM)
        return pl.pallas_call(
            kernel,
            out_shape=[jax.ShapeDtypeStruct(shape, dtype) for shape, dtype in far_outs + outs],
            in_specs=[far] * len(far_ins) + [near] * len(ins),
            out_specs=[far] * len(far_outs) + [near] * len(outs),
            scratch_shapes=scratch,
            compiler_params=pltpu.CompilerParams(
                vmem_limit_bytes=VMEM_BYTES, collective_id=identity, has_side_effects=True
            ),
            name=name,
        )(*far_ins, *ins)

    def room_for(local):
        return [pltpu.VMEM(shape, dtype) for shape, dtype in local]

    pre_gain, pre_shift, proj_bias = row(pre_gain), row(pre_shift), row(proj_bias)
    mid_gain, mid_shift, hidden_bias = row(mid_gain), row(mid_shift), row(hidden_bias)
    output_bias, moe_gain, moe_shift = row(output_bias), row(moe_gain), row(moe_shift)
    weight_qkv = qkv_weight.transpose(1, 0, 2)
    router = router_weight.T
    groups = wide // group
    kept = [
        ((tokens, lanes), BF16), ((tokens, width), BF16), ((tokens, model), F32), ((tokens, model), F32),
        ((tokens, 128), F32), ((slots, model), BF16), ((model, hidden), BF16), ((hidden, model), BF16),
    ]
    homes = [((slots, half), BF16), ((slots, half), BF16)]
    fetched = [tokens_in, cotangent, weight_qkv, proj_weight, hidden_weight, output_weight, expert_in[0], expert_out[0]]
    tables = [((count, 8, 128), F32)] * 5
    qkv, context, first, second, info, result, in_grad, out_grad, row_own, row_peer, gate_grads, in_bias, out_bias = remote(
        functools.partial(front, wide, room, group, heads, rows, count), "front", 1,
        fetched,
        [expert_ids.T, priority, pre_gain, pre_shift, qv_bias, proj_bias, mid_gain, mid_shift, hidden_bias, output_bias,
         moe_gain, moe_shift, router, expert_in_bias, expert_out_bias],
        kept + homes,
        [((count, 128), F32), ((8, hidden), F32), ((8, model), F32)],
        room_for([(array.shape, array.dtype) for array in fetched] + kept
                 + [((8, tokens), jnp.int32), ((count, 128), F32), ((slots, model), BF16), ((slots, model), BF16),
                    ((width, model), BF16), ((tokens, width), BF16), ((tokens, model), BF16), ((tokens, model), BF16),
                    ((tokens, half), BF16), ((slots, half), BF16), ((slots, half), BF16), ((slots, half), BF16),
                    ((slots, hidden), BF16), ((slots, hidden), BF16), ((slots, model), BF16), ((slots, half), F32),
                    ((slots, half), BF16), ((slots, half), BF16), ((slots, half), BF16)] + tables)
        + [pltpu.SemaphoreType.DMA((2, 5 * wide + 3 * groups + 2 * chunks + 2)), pltpu.SemaphoreType.DMA((9,)),
           pltpu.SemaphoreType.DMA((chunks,)), pltpu.SemaphoreType.DMA((5, chunks)), pltpu.SemaphoreType.DMA((groups + 1,))],
    )

    layout = [(0, 1, 2), (0, 1, 2), (0,), (0,), tuple(range(count))]
    vectors = [((8, model), F32), ((8, model), F32), ((8, hidden), F32), ((8, lanes), F32), ((count, model), F32)]
    near, far = tuple(range(steps)), (0,) + tuple(range(2, steps)) + (1,)
    summed = [(model, hidden), (hidden, model), (3 * model // 2, width), (3 * model // 2, width), (width, model), (16 * wide, 128)]
    fetched = [second, cotangent, info, first, tokens_in, qkv, context, hidden_weight, output_weight, proj_weight, weight_qkv, row_own, row_peer]
    given = [
        ((tokens, model), BF16), ((tokens, model), F32), ((model, hidden), BF16), ((hidden, model), BF16),
        ((3 * model, width), BF16), ((width, model), BF16),
    ]
    tile = (2 * model // 128, 128)
    block_out, grad, hidden_g, output_g, qkv_g, proj_g, *sums = remote(
        functools.partial(backward, wide, room, heads, layout, (near, far, near, far, near, far), rows), "backward", 2,
        fetched + [result],
        [moe_gain, moe_shift, router, gate_grads, mid_gain, mid_shift, pre_gain, pre_shift, hidden_bias],
        given, vectors + [((8, model), F32)],
        room_for([(array.shape, array.dtype) for array in fetched] + given
                 + [((tokens, model), BF16), ((tokens, hidden), BF16), ((tokens, hidden), BF16), ((tokens, model), BF16),
                    ((tokens, model), BF16), ((tokens, model), BF16), ((tokens, lanes), BF16), ((tokens, model), BF16),
                    ((tokens, model), BF16), ((slots, model), BF16), ((tokens, model), BF16),
                    (tile, F32), ((wide,) + tile, F32), (tile, F32), (tile, F32), ((8, model), F32), ((count, model), F32),
                    ((8, model), F32), ((8, hidden), F32), ((8, lanes), F32), ((8, model), F32), (summed[-1], BF16),
                    (summed[0], F32), (summed[1], F32), ((3 * model, width), F32), (summed[4], F32), (summed[5], F32)]
                 + [(shape, BF16) for shape in summed] * 2)
        + [pltpu.SemaphoreType.DMA((2, chunks))] * 3 + [pltpu.SemaphoreType.DMA((2, 2 * wide + 1))]
        + [pltpu.SemaphoreType.DMA((len(summed), 2 * steps))] * 2
        + [pltpu.SemaphoreType.DMA((12,)), pltpu.SemaphoreType.DMA((6, chunks)), pltpu.SemaphoreType.DMA((2, chunks))],
    )

    pairs = [
        (block_out, BF16), (grad, F32), (hidden_g, F32), (output_g, F32), (qkv_g.reshape(3, model, width), F32),
        (proj_g, F32), (in_grad, F32), (out_grad, F32),
    ]
    singles = [(0, 1), (0, 1, 2), (0, 1, 2), (0,), (0,), (0,), (0,), (0,)]
    sources = [sums[-1]] + list(sums[:-1]) + [in_bias, out_bias]
    sizes = [(1, model)] * 8 + [(1, hidden), (1, lanes), (count, model), (1, hidden), (1, model)]
    parts = 4

    def spec(shape):
        if len(shape) == 3:
            return pl.BlockSpec((shape[0], shape[1] // parts, shape[2]), lambda i: (0, i, 0))
        return pl.BlockSpec((shape[0] // parts, shape[1]), lambda i: (i, 0))

    def whole(shape):
        return pl.BlockSpec(shape, lambda i: (0, 0))

    outs = pl.pallas_call(
        functools.partial(widen, len(pairs), singles),
        grid=(parts,),
        in_specs=[spec(source.shape) for source, _ in pairs] + [whole(source.shape) for source in sources],
        out_specs=[spec(source.shape) for source, _ in pairs] + [whole(size) for size in sizes],
        out_shape=[jax.ShapeDtypeStruct(source.shape, dtype) for source, dtype in pairs]
        + [jax.ShapeDtypeStruct(size, F32) for size in sizes],
        compiler_params=pltpu.CompilerParams(vmem_limit_bytes=VMEM_BYTES),
        name="widen",
    )(*[source for source, _ in pairs], *sources)
    block_out, grad, hidden_g, output_g, qkv_g, proj_g, in_grad, out_grad = outs[:8]
    pre_gain_g, pre_shift_g, mid_gain_g, mid_shift_g, proj_bias_g, moe_gain_g, moe_shift_g, output_bias_g = (
        vector.reshape(model) for vector in outs[8:16]
    )
    hidden_bias_g, qkv_bias_g, router_g, in_bias_g, out_bias_g = outs[16:]
    return (
        block_out, grad, pre_gain_g, pre_shift_g, qkv_g.transpose(1, 0, 2),
        jnp.concatenate([qkv_bias_g[:, :width], qkv_bias_g[:, 2 * width :]]), proj_g, proj_bias_g, mid_gain_g,
        mid_shift_g, hidden_g, hidden_bias_g.reshape(hidden), output_g, output_bias_g, moe_gain_g, moe_shift_g,
        router_g.T, in_grad[None], in_bias_g, out_grad[None], out_bias_g,
    )


def layer_norm(values, gain, shift):
    centered = values - jnp.mean(values, axis=-1, keepdims=True)
    variance = jnp.mean(centered * centered, axis=-1, keepdims=True)
    return centered * lax.rsqrt(variance + 1e-06) * gain + shift


def norm_grad(values, gain, shift, upstream):
    _, pullback = jax.vjp(layer_norm, values, gain, shift)
    return pullback(upstream)


def gelu_grad(inner, upstream):
    _, pullback = jax.vjp(jax.nn.gelu, inner)
    return pullback(upstream)[0]


def slot_tables(choice_ids, ranks, capacity, experts):
    count = choice_ids.shape[0]
    order_keys = jnp.concatenate([ranks, ranks + count])
    flat_ids = jnp.concatenate([choice_ids[:, 0], choice_ids[:, 1]])
    earlier = (order_keys[None, :] < order_keys[:, None]) & (flat_ids[None, :] == flat_ids[:, None])
    position = jnp.sum(earlier.astype(jnp.int32), axis=1)
    kept = position < capacity
    position = position.reshape(2, count)
    kept = kept.reshape(2, count)
    columns = jnp.arange(experts * capacity, dtype=jnp.int32)
    target = choice_ids.T * capacity + position
    tables = (target[:, :, None] == columns[None, None, :]) & kept[:, :, None]
    return (tables, kept)


def plain(
    tokens_in,
    pre_gain,
    pre_shift,
    qkv_weight,
    qv_bias,
    proj_weight,
    proj_bias,
    mid_gain,
    mid_shift,
    hidden_weight,
    hidden_bias,
    output_weight,
    output_bias,
    moe_gain,
    moe_shift,
    router_weight,
    expert_in,
    expert_in_bias,
    expert_out,
    expert_out_bias,
    expert_ids,
    priority,
    cotangent,
):
    tokens = tokens_in.shape[0]
    model_width = tokens_in.shape[1]
    local_heads = qkv_weight.shape[2] // HEAD_DIM
    images = tokens // PATCHES
    experts = router_weight.shape[1]
    capacity = tokens // experts
    score_scale = float(HEAD_DIM) ** (-0.5)
    highest = lax.Precision.HIGHEST
    residual = tokens_in.astype(jnp.float32)
    normed_pre = layer_norm(residual, pre_gain, pre_shift)
    lowered_pre = normed_pre.astype(jnp.bfloat16)
    blank = jnp.zeros_like(qv_bias[0])
    qkv_shift = jnp.stack([qv_bias[0], blank, qv_bias[1]])
    qkv = (
        jnp.einsum("td,dsk->tsk", lowered_pre, qkv_weight, preferred_element_type=jnp.float32)
        + qkv_shift
    ).astype(jnp.bfloat16)
    grid = qkv.reshape(images, PATCHES, 3, local_heads, HEAD_DIM)
    query, keys, values = (grid[:, :, 0], grid[:, :, 1], grid[:, :, 2])
    scores = (
        jnp.einsum("bqhd,bkhd->bhqk", query, keys, preferred_element_type=jnp.float32) * score_scale
    )
    log_total = jax.nn.logsumexp(scores, axis=-1, keepdims=True)
    weights = jnp.exp(scores - log_total).astype(jnp.bfloat16)
    context = jnp.einsum("bhqk,bkhd->bqhd", weights, values, preferred_element_type=jnp.float32)
    context = context.astype(jnp.bfloat16).reshape(tokens, local_heads * HEAD_DIM)
    branch = lax.psum(jnp.dot(context, proj_weight, preferred_element_type=jnp.float32), "tensor")
    first = residual + branch + proj_bias
    normed_mid = layer_norm(first, mid_gain, mid_shift)
    lowered_mid = normed_mid.astype(jnp.bfloat16)
    inner = jnp.dot(lowered_mid, hidden_weight, preferred_element_type=jnp.float32) + hidden_bias
    activated = jax.nn.gelu(inner).astype(jnp.bfloat16)
    partial_out = jnp.dot(activated, output_weight, preferred_element_type=jnp.float32)
    second = first + lax.psum(partial_out, "tensor") + output_bias
    normed_moe = layer_norm(second, moe_gain, moe_shift)
    lowered_moe = normed_moe.astype(jnp.bfloat16)
    route = jax.nn.softmax(jnp.dot(normed_moe, router_weight, precision=highest), axis=-1)
    tables, kept = slot_tables(expert_ids, priority[0], capacity, experts)
    tables = tables.astype(jnp.bfloat16)
    dispatch = tables[0] + tables[1]
    buffers = jnp.einsum("tk,td->kd", dispatch, lowered_moe, preferred_element_type=jnp.float32)
    buffers = buffers.astype(jnp.bfloat16).reshape(experts, capacity, model_width)
    arrived = lax.all_to_all(buffers, "wide", split_axis=0, concat_axis=1, tiled=True)
    expert_inner = (
        jnp.einsum("erd,edf->erf", arrived, expert_in, preferred_element_type=jnp.float32)
        + expert_in_bias[:, None, :]
    )
    expert_act = jax.nn.gelu(expert_inner).astype(jnp.bfloat16)
    expert_partial = jnp.einsum(
        "erf,efd->erd", expert_act, expert_out, preferred_element_type=jnp.float32
    )
    expert_result = (
        lax.psum(expert_partial.astype(jnp.bfloat16), "tensor").astype(jnp.float32)
        + expert_out_bias[:, None, :]
    ).astype(jnp.bfloat16)
    returned = lax.all_to_all(
        expert_result, "wide", split_axis=1, concat_axis=0, tiled=True
    ).reshape(experts * capacity, model_width)
    picked = jnp.einsum("jtk,kd->jtd", tables, returned, preferred_element_type=jnp.float32)
    expert_range = jnp.arange(experts, dtype=jnp.int32)
    chosen = (expert_ids.T[:, :, None] == expert_range[None, None, :]).astype(jnp.float32) * kept[
        :, :, None
    ].astype(jnp.float32)
    gates = jnp.sum(chosen * route[None], axis=-1)
    mixture = jnp.sum(gates[:, :, None] * picked, axis=0)
    block_out = (second + mixture).astype(jnp.bfloat16)
    gate_grad = jnp.sum(picked * cotangent[None], axis=-1)
    weighted = (gates[:, :, None] * cotangent[None]).astype(jnp.bfloat16)
    slot_grad = jnp.einsum("jtk,jtd->kd", tables, weighted, preferred_element_type=jnp.float32)
    slot_grad = slot_grad.astype(jnp.bfloat16).reshape(experts, capacity, model_width)
    result_grad = lax.all_to_all(slot_grad, "wide", split_axis=0, concat_axis=1, tiled=True)
    expert_out_bias_grad = jnp.sum(result_grad.astype(jnp.float32), axis=1)
    expert_out_grad = jnp.einsum(
        "erf,erd->efd", expert_act, result_grad, preferred_element_type=jnp.float32
    )
    act_grad = jnp.einsum(
        "erd,efd->erf", result_grad, expert_out, preferred_element_type=jnp.float32
    )
    expert_inner_grad = gelu_grad(expert_inner, act_grad).astype(jnp.bfloat16)
    expert_in_bias_grad = jnp.sum(expert_inner_grad.astype(jnp.float32), axis=1)
    expert_in_grad = jnp.einsum(
        "erd,erf->edf", arrived, expert_inner_grad, preferred_element_type=jnp.float32
    )
    arrived_partial = jnp.einsum(
        "erf,edf->erd", expert_inner_grad, expert_in, preferred_element_type=jnp.float32
    )
    arrived_grad = lax.psum(arrived_partial.astype(jnp.bfloat16), "tensor")
    buffer_grad = lax.all_to_all(
        arrived_grad, "wide", split_axis=1, concat_axis=0, tiled=True
    ).reshape(experts * capacity, model_width)
    moe_input_grad = jnp.dot(dispatch, buffer_grad, preferred_element_type=jnp.float32)
    route_grad = jnp.sum(gate_grad[:, :, None] * chosen, axis=0)
    logit_grad = route * (route_grad - jnp.sum(route * route_grad, axis=-1, keepdims=True))
    router_grad = jnp.einsum("td,te->de", normed_moe, logit_grad, precision=highest)
    moe_input_grad = moe_input_grad + jnp.einsum(
        "te,de->td", logit_grad, router_weight, precision=highest
    )
    second_part, moe_gain_grad, moe_shift_grad = norm_grad(
        second, moe_gain, moe_shift, moe_input_grad
    )
    second_grad = cotangent + second_part
    lowered_second = second_grad.astype(jnp.bfloat16)
    output_bias_grad = jnp.sum(second_grad, axis=0)
    output_weight_grad = jnp.einsum(
        "tf,td->fd", activated, lowered_second, preferred_element_type=jnp.float32
    )
    activated_grad = jnp.einsum(
        "td,fd->tf", lowered_second, output_weight, preferred_element_type=jnp.float32
    )
    inner_grad = gelu_grad(inner, activated_grad).astype(jnp.bfloat16)
    hidden_bias_grad = jnp.sum(inner_grad.astype(jnp.float32), axis=0)
    hidden_weight_grad = jnp.einsum(
        "td,tf->df", lowered_mid, inner_grad, preferred_element_type=jnp.float32
    )
    mid_partial = jnp.einsum(
        "tf,df->td", inner_grad, hidden_weight, preferred_element_type=jnp.float32
    )
    mid_grad = lax.psum(mid_partial, "tensor")
    first_part, mid_gain_grad, mid_shift_grad = norm_grad(first, mid_gain, mid_shift, mid_grad)
    first_grad = second_grad + first_part
    proj_bias_grad = jnp.sum(first_grad, axis=0)
    branch_grad = first_grad.astype(jnp.bfloat16)
    proj_weight_grad = jnp.einsum(
        "tk,td->kd", context, branch_grad, preferred_element_type=jnp.float32
    )
    context_grad = jnp.einsum(
        "td,kd->tk", branch_grad, proj_weight, preferred_element_type=jnp.float32
    )
    context_grad = context_grad.astype(jnp.bfloat16).reshape(images, PATCHES, local_heads, HEAD_DIM)
    scores = (
        jnp.einsum("bqhd,bkhd->bhqk", query, keys, preferred_element_type=jnp.float32) * score_scale
    )
    probs = jnp.exp(scores - log_total)
    weights = probs.astype(jnp.bfloat16)
    value_grad = jnp.einsum(
        "bhqk,bqhd->bkhd", weights, context_grad, preferred_element_type=jnp.float32
    )
    prob_grad = jnp.einsum(
        "bqhd,bkhd->bhqk", context_grad, values, preferred_element_type=jnp.float32
    )
    score_grad = (probs * (prob_grad - jnp.sum(probs * prob_grad, axis=-1, keepdims=True))).astype(
        jnp.bfloat16
    )
    query_grad = (
        jnp.einsum("bhqk,bkhd->bqhd", score_grad, keys, preferred_element_type=jnp.float32)
        * score_scale
    )
    key_grad = (
        jnp.einsum("bhqk,bqhd->bkhd", score_grad, query, preferred_element_type=jnp.float32)
        * score_scale
    )
    qkv_grad = jnp.stack([query_grad, key_grad, value_grad], axis=2).astype(jnp.bfloat16)
    qkv_grad = qkv_grad.reshape(tokens, 3, local_heads * HEAD_DIM)
    qkv_sums = jnp.sum(qkv_grad.astype(jnp.float32), axis=0)
    qv_bias_grad = jnp.stack([qkv_sums[0], qkv_sums[2]])
    qkv_weight_grad = jnp.einsum(
        "td,tsk->dsk", lowered_pre, qkv_grad, preferred_element_type=jnp.float32
    )
    pre_partial = jnp.einsum(
        "tsk,dsk->td", qkv_grad, qkv_weight, preferred_element_type=jnp.float32
    )
    pre_grad = lax.psum(pre_partial.astype(jnp.bfloat16), "tensor").astype(jnp.float32)
    input_part, pre_gain_grad, pre_shift_grad = norm_grad(residual, pre_gain, pre_shift, pre_grad)
    tokens_grad = first_grad + input_part
    shared = (
        lax.psum(pre_gain_grad.astype(jnp.bfloat16), "wide").astype(jnp.float32),
        lax.psum(pre_shift_grad.astype(jnp.bfloat16), "wide").astype(jnp.float32),
        lax.psum(qkv_weight_grad.astype(jnp.bfloat16), "wide").astype(jnp.float32),
        lax.psum(qv_bias_grad.astype(jnp.bfloat16), "wide").astype(jnp.float32),
        lax.psum(proj_weight_grad.astype(jnp.bfloat16), "wide").astype(jnp.float32),
        lax.psum(proj_bias_grad.astype(jnp.bfloat16), "wide").astype(jnp.float32),
        lax.psum(mid_gain_grad.astype(jnp.bfloat16), "wide").astype(jnp.float32),
        lax.psum(mid_shift_grad.astype(jnp.bfloat16), "wide").astype(jnp.float32),
        lax.psum(hidden_weight_grad.astype(jnp.bfloat16), "wide").astype(jnp.float32),
        lax.psum(hidden_bias_grad.astype(jnp.bfloat16), "wide").astype(jnp.float32),
        lax.psum(output_weight_grad.astype(jnp.bfloat16), "wide").astype(jnp.float32),
        lax.psum(output_bias_grad.astype(jnp.bfloat16), "wide").astype(jnp.float32),
        lax.psum(moe_gain_grad.astype(jnp.bfloat16), "wide").astype(jnp.float32),
        lax.psum(moe_shift_grad.astype(jnp.bfloat16), "wide").astype(jnp.float32),
        lax.psum(router_grad.astype(jnp.bfloat16), "wide").astype(jnp.float32),
    )
    return (
        (block_out, tokens_grad)
        + tuple(shared)
        + (expert_in_grad, expert_in_bias_grad, expert_out_grad, expert_out_bias_grad)
    )


def solution(mesh):
    body = functools.partial(shards, mesh.shape["wide"]) if mesh.shape["tensor"] == 2 else plain
    return jax.shard_map(
        body,
        mesh=mesh,
        in_specs=(
            P("wide", None), P(), P(), P(None, None, "tensor"), P(None, "tensor"), P("tensor", None), P(), P(), P(),
            P(None, "tensor"), P("tensor"), P("tensor", None), P(), P(), P(), P(),
            P("wide", None, "tensor"), P("wide", "tensor"), P("wide", "tensor", None), P("wide", None),
            P("wide", None), P("wide", None), P("wide", None),
        ),
        out_specs=(
            P("wide", None), P("wide", None), P(), P(), P(None, None, "tensor"), P(None, "tensor"), P("tensor", None),
            P(), P(), P(), P(None, "tensor"), P("tensor"), P("tensor", None), P(), P(), P(), P(),
            P("wide", None, "tensor"), P("wide", "tensor"), P("wide", "tensor", None), P("wide", None),
        ),
        check_vma=False,
    )
```

```python
import functools

import jax
import jax.numpy as jnp
from jax import lax
from jax.experimental import pallas as pl
from jax.experimental.pallas import tpu as pltpu
from jax.sharding import PartitionSpec as P

HEAD_DIM = 64
PATCHES = 144
BF16 = jnp.bfloat16
F32 = jnp.float32
HIGHEST = lax.Precision.HIGHEST
MESH = pl.DeviceIdType.MESH
VMEM_BYTES = 60 * 1024 * 1024


def dot(left, right):
    return jnp.dot(left, right, preferred_element_type=F32)


def dot_rows(left, right):
    return lax.dot_general(left, right, (((1,), (1,)), ((), ())), preferred_element_type=F32)


def dot_columns(left, right, precision=None):
    return lax.dot_general(
        left, right, (((0,), (0,)), ((), ())), precision=precision, preferred_element_type=F32
    )


def normalized(values):
    centered = values - jnp.mean(values, axis=-1, keepdims=True)
    variance = jnp.mean(centered * centered, axis=-1, keepdims=True)
    scale = lax.rsqrt(variance + 1e-06)
    return centered * scale, scale


def norm_back(rows, scale, gain, upstream):
    scaled = upstream * gain
    inward = jnp.mean(scaled, axis=-1, keepdims=True)
    along = jnp.mean(scaled * rows, axis=-1, keepdims=True)
    return scale * (scaled - inward - rows * along)


def gelu_parts(inner):
    square = inner * inner
    bend = jnp.tanh(0.7978845608028654 * inner * (1.0 + 0.044715 * square))
    half = 0.5 * (1.0 + bend)
    slope = half + (0.5 * 0.7978845608028654) * inner * (1.0 - bend * bend) * (
        1.0 + 0.134145 * square
    )
    return inner * half, slope


def gelu(inner):
    return inner * (0.5 * (1.0 + jnp.tanh(0.7978845608028654 * inner * (1.0 + 0.044715 * inner * inner))))


def softmax_rows(scores, scale):
    peak = jnp.max(scores, axis=-1, keepdims=True)
    weights = jnp.exp((scores - peak) * scale)
    return weights * (1.0 / jnp.sum(weights, axis=-1, keepdims=True))


def spots(places):
    lane = lax.broadcasted_iota(jnp.int32, (places.shape[0], 128), 1)
    return [(lane == places[:, j : j + 1]).astype(F32) for j in range(2)]


def bits_of(index, wide):
    return [lax.rem(lax.div(index, 1 << k), 2) for k in range(wide.bit_length() - 1)]


class Sums:
    def __init__(self, wide, orders, totals, sends, lands, gathers, send_sems, recv_sems):
        me, self.plane = lax.axis_index("wide"), lax.axis_index("tensor")
        self.bits = bits_of(me, wide)
        self.partners = [me + (1 - 2 * bit) * (1 << k) for k, bit in enumerate(self.bits)]
        self.steps = len(self.bits)
        self.orders, self.totals, self.sends, self.lands, self.gathers = orders, totals, sends, lands, gathers
        self.send_sems, self.recv_sems = send_sems, recv_sems

    def piece(self, i, step):
        rows = self.gathers[i].shape[0]
        base = 0
        for s in range(step):
            base = base + self.bits[self.orders[i][s]] * (rows >> (s + 1))
        length = rows >> (step + 1)
        bit = self.bits[self.orders[i][step]]
        return pl.multiple_of(base + bit * length, 16), pl.multiple_of(base + (1 - bit) * length, 16), length

    def staged(self, i, step):
        rows = self.gathers[i].shape[0]
        return rows - (rows >> step)

    def transfer(self, i, k):
        step = k if k < self.steps else 2 * self.steps - 1 - k
        kept, _, length = self.piece(i, step)
        if k < self.steps:
            at = self.staged(i, step)
            source, target = self.sends[i].at[pl.ds(at, length)], self.lands[i].at[pl.ds(at, length)]
        else:
            source = target = self.gathers[i].at[pl.ds(kept, length)]
        return pltpu.make_async_remote_copy(
            source, target, self.send_sems.at[i, k], self.recv_sems.at[i, k],
            device_id=(self.partners[self.orders[i][step]], self.plane), device_id_type=MESH,
        )

    def begin(self, i, k):
        if k < self.steps:
            _, other, length = self.piece(i, k)
            at = self.staged(i, k)
            self.sends[i][at : at + length, :] = self.totals[i][pl.ds(other, length), :].astype(BF16)
        self.transfer(i, k).start()

    def advance(self, i, k):
        self.transfer(i, k).wait()
        if k < self.steps:
            kept, _, length = self.piece(i, k)
            at = self.staged(i, k)
            value = self.totals[i][pl.ds(kept, length), :] + self.lands[i][at : at + length, :].astype(F32)
            if k + 1 < self.steps:
                self.totals[i][pl.ds(kept, length), :] = value
            else:
                self.gathers[i][pl.ds(kept, length), :] = value.astype(BF16)
        if k + 1 < 2 * self.steps:
            self.begin(i, k + 1)


def greet(wide):
    me, plane = lax.axis_index("wide"), lax.axis_index("tensor")
    barrier = pltpu.get_barrier_semaphore()

    def hail(d, carry):
        pl.semaphore_signal(barrier, inc=1, device_id=(lax.rem(me + d, wide), plane), device_id_type=MESH)
        return carry

    lax.fori_loop(1, wide, hail, 0)
    pl.semaphore_signal(barrier, inc=1, device_id=(me, 1 - plane), device_id_type=MESH)
    pl.semaphore_wait(barrier, wide)


def put_row(small, at, row):
    for c in range(row.shape[1] // 128):
        small[at + c : at + c + 1, :] = row[:, 128 * c : 128 * (c + 1)]
    return at + row.shape[1] // 128


def get_row(small, at, width):
    return jnp.concatenate([small[at + c : at + c + 1, :] for c in range(width // 128)], axis=1)


def image_back(heads, qkv, context_grad):
    width = heads * HEAD_DIM
    scale = HEAD_DIM**-0.5
    parts = [[], [], []]
    for head in range(heads):
        h = head * HEAD_DIM
        query = qkv[:, h : h + HEAD_DIM]
        keys = qkv[:, width + h : width + h + HEAD_DIM]
        values = qkv[:, 2 * width + h : 2 * width + h + HEAD_DIM]
        upstream = context_grad[:, h : h + HEAD_DIM]
        scores = dot_rows(keys, query)
        weights = jnp.exp((scores - jnp.max(scores, axis=0, keepdims=True)) * scale)
        probs = weights * (1.0 / jnp.sum(weights, axis=0, keepdims=True))
        prob_grad = dot_rows(values, upstream)
        inward = jnp.sum(probs * prob_grad, axis=0, keepdims=True)
        score_grad = (probs * (prob_grad - inward)).astype(BF16)
        parts[0].append(dot_columns(score_grad, keys) * scale)
        parts[1].append(dot(score_grad, query) * scale)
        parts[2].append(dot(probs.astype(BF16), upstream))
    return jnp.concatenate(parts[0] + parts[1] + parts[2], axis=1).astype(BF16)


def column_dots(left, right, put, tile=256):
    def body(i, carry):
        at = pl.multiple_of(i * tile, tile)
        put(at, tile, dot_columns(left[:, pl.ds(at, tile)], right[...]))
        return carry

    lax.fori_loop(0, left.shape[1] // tile, body, 0)


def image_forward(heads, qkv):
    width = heads * HEAD_DIM
    parts = []
    for head in range(heads):
        h = head * HEAD_DIM
        probs = softmax_rows(
            dot_rows(qkv[:, h : h + HEAD_DIM], qkv[:, width + h : width + h + HEAD_DIM]), HEAD_DIM**-0.5
        )
        parts.append(dot(probs.astype(BF16), qkv[:, 2 * width + h : 2 * width + h + HEAD_DIM]))
    return jnp.concatenate(parts, axis=1).astype(BF16)


def token_hits(choices, slots):
    slot = lax.broadcasted_iota(jnp.int32, (choices.shape[0], slots), 1)
    return [slot == choices[:, j : j + 1] for j in range(2)]


def slot_hits(first, count, targets):
    slot = first + lax.broadcasted_iota(jnp.int32, (count, targets.shape[1]), 0)
    return ((slot == targets[0:1, :]) | (slot == targets[1:2, :])).astype(BF16)


def count_slots(ids, priority, experts, capacity, room):
    tokens = ids.shape[1]
    wide_rows = jnp.concatenate([ids, priority, jnp.zeros((5, tokens), jnp.int32)], axis=0)
    eye = lax.broadcasted_iota(jnp.int32, (8, 8), 0) == lax.broadcasted_iota(jnp.int32, (8, 8), 1)
    turned = dot_columns(wide_rows.astype(F32), eye.astype(F32), HIGHEST).astype(jnp.int32)
    rank, ranks = turned[:, 2:3], priority

    def fold(numbers, own, before, axis):
        later = [jnp.where(numbers == own[0], before, 0.0), jnp.where(numbers == own[1] + experts, before, 0.0)]
        return [jnp.sum(part, axis=axis, keepdims=True) for part in later]

    def finish(own, counts, firsts):
        counts = [counts[0], counts[1] + firsts]
        places = [count.astype(jnp.int32) for count in counts]
        kept = [place < capacity for place in places]
        return (
            [jnp.where(keep, choice * room + place, -1) for keep, choice, place in zip(kept, own, places)],
            [jnp.where(keep, choice, -1) for keep, choice in zip(kept, own)],
            [jnp.where(keep, place, -1) for keep, place in zip(kept, places)],
        )

    number = lax.broadcasted_iota(jnp.int32, (2 * experts, tokens), 0)
    by_row = [ids[0:1, :], ids[1:2, :]]
    held = ((number == by_row[0]) | (number == by_row[1] + experts)).astype(BF16)
    before = dot(held, (rank < ranks).astype(BF16))
    first_counts = jnp.sum(held.astype(F32), axis=1, keepdims=True)
    firsts = jnp.sum(jnp.where(number == by_row[1], first_counts, 0.0), axis=0, keepdims=True)
    targets, _, _ = finish(by_row, fold(number, by_row, before, 0), firsts)

    number = lax.broadcasted_iota(jnp.int32, (tokens, 2 * experts), 1)
    by_token = [turned[:, 0:1], turned[:, 1:2]]
    held_by_token = ((number == by_token[0]) | (number == by_token[1] + experts)).astype(BF16)
    before = dot((ranks < rank).astype(BF16), held_by_token)
    first_counts = jnp.sum(held_by_token.astype(F32), axis=0, keepdims=True)
    firsts = jnp.sum(jnp.where(number == by_token[1], first_counts, 0.0), axis=1, keepdims=True)
    groups = finish(by_token, fold(number, by_token, before, 1), firsts)
    choices = jnp.concatenate([part for group in groups for part in group], axis=1)
    return jnp.concatenate(targets, axis=0), choices


def front(
    wide, room, group, heads, rows, experts,
    tokens_h, cotangent_h, weight_qkv_h, projection_h, hidden_h, output_h, weight_in_h, weight_out_h,
    ids, priority, pre_gain, pre_shift, qv_bias, proj_bias, mid_gain, mid_shift, hidden_bias, output_bias,
    moe_gain, moe_shift, router, bias_in, bias_out,
    qkv_h, context_h, first_h, second_h, info_h, result_h, in_grad_h, out_grad_h, own_home, peer_home,
    gate_home, in_bias_grad, out_bias_grad,
    tokens, cotangent, weight_qkv, projection, hidden, output, weight_in, weight_out,
    qkv, context, first, second, info, result, in_grad, out_grad,
    targets, table, raised_placed, upstream, projection_peer, context_peer, partial_own, partial_peer,
    columns, other_columns, placed, other_placed, rows_own, rows_peer, act, inner_grad, slot_grad, grad_kept, grad_sent, grad_landed,
    grad_back, gate_sent, gate_arrived, gate_back, gate_own, gate_peer,
    sems, load_sems, chunk_sems, store_sems, group_sems,
):
    me, plane = lax.axis_index("wide"), lax.axis_index("tensor")
    chunks, groups = tokens.shape[0] // rows, wide // group
    mine = lax.div(me, group)
    block = group * room
    width = heads * HEAD_DIM
    half = columns.shape[1]
    capacity = tokens.shape[0] // experts
    row_at, gate_at, home_at, back_at, up_at = 0, wide, 2 * wide, 3 * wide, 4 * wide
    grad_at, share_at, join_at = 5 * wide, 5 * wide + groups, 5 * wide + 2 * groups
    context_at = 5 * wide + 3 * groups
    partial_at, last_at = context_at + chunks, context_at + 2 * chunks
    other_at = last_at + 2

    def rows_of(index):
        return pl.ds(pl.multiple_of(index * room, 16), room)

    def rows_of_group(index):
        return pl.ds(pl.multiple_of(index * block, 16), block)

    def chunk_of(index):
        return pl.ds(pl.multiple_of(index * rows, 16), rows)

    def load_tokens(c):
        return pltpu.make_async_copy(tokens_h.at[chunk_of(c)], tokens.at[chunk_of(c)], chunk_sems.at[c])

    def start_tokens(c, carry):
        load_tokens(c).start()
        return carry

    loads = [
        pltpu.make_async_copy(source, target, load_sems.at[i])
        for i, (source, target) in enumerate(
            [(weight_qkv_h, weight_qkv), (projection_h, projection), (hidden_h, hidden), (output_h, output),
             (cotangent_h, cotangent), (weight_in_h, weight_in), (weight_out_h, weight_out)]
        )
    ]
    loads[0].start()
    lax.fori_loop(0, chunks, start_tokens, 0)
    for load in loads[1:]:
        load.start()

    def store(kind, source, target, c):
        return pltpu.make_async_copy(source.at[chunk_of(c)], target.at[chunk_of(c)], store_sems.at[kind, c])

    stores = [(qkv, qkv_h), (context, context_h), (first, first_h), (second, second_h), (info, info_h)]
    greet(wide)

    def move(source, target, base, sent, landed, device):
        return pltpu.make_async_remote_copy(
            source, target, sems.at[0, base + sent], sems.at[1, base + landed], device_id=device, device_id_type=MESH
        )

    def across_chunk(source, target, base, index):
        there = chunk_of(index)
        return move(source.at[there], target.at[there], base, index, index, (me, 1 - plane))

    def up_copy(other, sender):
        return move(raised_placed.at[rows_of(other)], upstream.at[rows_of(sender)], up_at, other, sender, (other, plane))

    weights = move(projection_h, projection_peer, last_at, 0, 0, (me, 1 - plane))
    weights.start()
    first_plane = plane == 0
    table[...] = jnp.zeros_like(table)
    in_bias_grad[...] = jnp.zeros_like(in_bias_grad)
    out_bias_grad[...] = jnp.zeros_like(out_bias_grad)

    def attend_chunk(c):
        there = chunk_of(c)
        load_tokens(c).wait()
        normed, _ = normalized(tokens[there, :].astype(F32))
        lowered = (normed * pre_gain[...] + pre_shift[...]).astype(BF16)
        parts = [dot(lowered, weight_qkv[s]) for s in range(3)]
        parts = [parts[0] + qv_bias[0:1, :], parts[1], parts[2] + qv_bias[1:2, :]]
        value = jnp.concatenate(parts, axis=1).astype(BF16)
        qkv[there, :] = value
        contexts = [
            image_forward(heads, value[image * PATCHES : (image + 1) * PATCHES]) for image in range(rows // PATCHES)
        ]
        context[there, :] = jnp.concatenate(contexts, axis=0)
        across_chunk(context, context_peer, context_at, c).start()
        store(0, qkv, qkv_h, c).start()
        store(1, context, context_h, c).start()

    def find_slots():
        by_row, choices = count_slots(ids[...], priority[...], experts, capacity, room)
        targets[0:2, :] = by_row
        info[:, experts : experts + 6] = choices.astype(F32)

    def raise_group(k):
        q = lax.rem(mine + k, groups)
        hits = slot_hits(q * block, block, targets)
        raised_placed[rows_of_group(q), :] = dot(hits, cotangent[...].astype(BF16)).astype(BF16)
        for j in range(group):
            e = q * group + j

            @pl.when(e != me)
            def _(e=e):
                up_copy(e, me).start()

            @pl.when(e == me)
            def _(e=e):
                upstream[rows_of(e), :] = raised_placed[rows_of(e), :]

    def feed_chunk(c):
        there = chunk_of(c)
        across_chunk(context, context_peer, context_at, c).wait()
        branch = dot(context[there, :], projection[...]) + dot(context_peer[there, :], projection_peer[...])
        value = tokens[there, :].astype(F32) + branch + proj_bias[...]
        first[there, :] = value
        normed, _ = normalized(value)
        lowered = (normed * mid_gain[...] + mid_shift[...]).astype(BF16)
        activated = gelu(dot(lowered, hidden[...]) + hidden_bias[...]).astype(BF16)
        partial_own[there, :] = dot(activated, output[...]).astype(BF16)
        across_chunk(partial_own, partial_peer, partial_at, c).start()
        store(2, first, first_h, c).start()

    def route_chunk(c):
        there = chunk_of(c)
        across_chunk(partial_own, partial_peer, partial_at, c).wait()
        partial = partial_own[there, :].astype(F32) + partial_peer[there, :].astype(F32)
        value = first[there, :] + partial + output_bias[...]
        second[there, :] = value
        normed, _ = normalized(value)
        normed = normed * moe_gain[...] + moe_shift[...]
        columns[there, :] = jnp.where(first_plane, normed[:, :half], normed[:, half:]).astype(BF16)
        other_columns[there, :] = jnp.where(first_plane, normed[:, half:], normed[:, :half]).astype(BF16)
        logits = lax.dot_general(
            normed, router[...], (((1,), (1,)), ((), ())), precision=HIGHEST, preferred_element_type=F32
        )
        grown = jnp.exp(logits - jnp.max(logits, axis=-1, keepdims=True))
        route = grown / jnp.sum(grown, axis=-1, keepdims=True)
        info[there, 0:experts] = route
        number = lax.broadcasted_iota(jnp.int32, route.shape, 1)
        picks = info[there, experts : experts + 6].astype(jnp.int32)
        for j, spot in enumerate(spots(picks[:, 4:6])):
            table[...] += dot_columns(jnp.where(number == picks[:, 2 + j : 3 + j], route, 0.0), spot, HIGHEST)
        store(3, second, second_h, c).start()
        store(4, info, info_h, c).start()

    def turn(c, carry):
        @pl.when(c < chunks)
        def _():
            attend_chunk(c)

        @pl.when(c == 0)
        def _():
            loads[4].wait()
            find_slots()

        @pl.when(c < groups)
        def _():
            raise_group(c)

        @pl.when(c == 1)
        def _():
            weights.wait()
            for load in loads[1:4]:
                load.wait()

        @pl.when((c >= 1) & (c <= chunks))
        def _():
            feed_chunk(c - 1)

        @pl.when(c >= 2)
        def _():
            route_chunk(c - 2)

        return carry

    info[...] = jnp.zeros_like(info)
    loads[0].wait()
    lax.fori_loop(0, chunks + 2, turn, 0)

    def row_copy(other, sender):
        return move(placed.at[rows_of(other)], rows_own.at[rows_of(sender)], row_at, other, sender, (other, plane))

    def other_copy(other, sender):
        return move(other_placed.at[rows_of(other)], rows_peer.at[rows_of(sender)], other_at, other, sender, (other, plane))

    def turned(k, sign):
        pairs = groups // 2
        pair = lax.rem(lax.div(mine, 2) + sign * lax.div(k, 2) + pairs, pairs)
        return 2 * pair + lax.rem(mine + k, 2), k < 2

    def gate_copy(other, sender):
        return move(gate_sent.at[other], gate_arrived.at[sender], gate_at, other, sender, (other, plane))

    def home_copy(other, sender):
        return move(grad_back.at[rows_of(other)], own_home.at[rows_of(sender)], home_at, other, sender, (other, plane))

    def back_copy(other, sender):
        return move(gate_back.at[other], gate_own.at[sender], back_at, other, sender, (other, plane))

    def across(source, target, base, index):
        there = rows_of_group(index)
        return move(source.at[there], target.at[there], base, index, index, (me, 1 - plane))

    own_half = pl.ds(pl.multiple_of(plane * half, 16), half)
    peer_half = pl.ds(pl.multiple_of((1 - plane) * half, 16), half)
    for e in range(wide):
        gate_sent[e] = jnp.broadcast_to(table[e : e + 1, :], gate_sent.shape[1:])

    def place_group(k, carry):
        q, near = turned(k, 1)
        hits = slot_hits(q * block, block, targets)
        placed[rows_of_group(q), :] = dot(hits, columns[...]).astype(BF16)

        @pl.when(near)
        def _():
            other_placed[rows_of_group(q), :] = dot(hits, other_columns[...]).astype(BF16)

        for j in range(group):
            e = q * group + j

            @pl.when(e != me)
            def _(e=e):
                row_copy(e, me).start()
                gate_copy(e, me).start()

            @pl.when((e != me) & near)
            def _(e=e):
                other_copy(e, me).start()

            @pl.when(e == me)
            def _(e=e):
                rows_own[rows_of(e), :] = placed[rows_of(e), :]
                rows_peer[rows_of(e), :] = other_placed[rows_of(e), :]
                gate_arrived[e] = gate_sent[e]

        return carry

    lax.fori_loop(0, groups, place_group, 0)
    loads[5].wait()
    loads[6].wait()
    diagonal = lax.broadcasted_iota(jnp.int32, (room, 128), 0) == lax.broadcasted_iota(jnp.int32, (room, 128), 1)

    def store_result(p):
        there = rows_of_group(p)
        return pltpu.make_async_copy(result.at[there], result_h.at[there], group_sems.at[p])

    def join_group(k):
        p, near = turned(k, -1)
        for j in range(group):
            w = p * group + j

            @pl.when(w != me)
            def _(w=w):
                row_copy(w, w).wait_recv()
                gate_copy(w, w).wait_recv()

        @pl.when(jnp.logical_not(near))
        def _():
            across(rows_own, rows_peer, join_at, p).start()

        for j in range(group):
            w = p * group + j

            @pl.when((w != me) & near)
            def _(w=w):
                other_copy(w, w).wait_recv()

            @pl.when(w != me)
            def _(w=w):
                up_copy(w, w).wait_recv()

    def expert_group(k):
        p, near = turned(k, -1)
        there = rows_of_group(p)

        @pl.when(jnp.logical_not(near))
        def _():
            across(rows_own, rows_peer, join_at, p).wait()

        gates = jnp.concatenate(
            [
                jnp.sum(jnp.where(diagonal, gate_arrived[p * group + j][0:1, :], 0.0), axis=1, keepdims=True)
                for j in range(group)
            ],
            axis=0,
        )
        inner = dot(rows_own[there, :], weight_in[own_half, :]) + dot(rows_peer[there, :], weight_in[peer_half, :])
        acted, slope = gelu_parts(inner + bias_in[...])
        acted = acted.astype(BF16)
        act[there, :] = acted
        raised = upstream[there, :].astype(F32)
        slot = (raised * gates).astype(BF16)
        slot_grad[there, :] = slot
        inward = (dot_rows(slot, weight_out[...]) * slope).astype(BF16)
        inner_grad[there, :] = inward
        grad_sent[there, :] = dot_rows(inward, weight_in[peer_half, :]).astype(BF16)
        across(grad_sent, grad_landed, grad_at, p).start()
        grad_kept[there, :] = dot_rows(inward, weight_in[own_half, :])
        value = dot(acted, weight_out[...]) + bias_out[...] * jnp.where(first_plane, 1.0, 0.0)
        result[there, :] = value.astype(BF16)
        store_result(p).start()
        out_bias_grad[0:1, :] += jnp.sum(slot.astype(F32), axis=0, keepdims=True)
        in_bias_grad[0:1, :] += jnp.sum(inward.astype(F32), axis=0, keepdims=True)
        slopes = jnp.sum(raised * value, axis=1, keepdims=True)
        for j in range(group):
            w = p * group + j
            row = jnp.sum(
                jnp.where(diagonal, slopes[j * room : (j + 1) * room], 0.0), axis=0, keepdims=True
            )
            gate_back[w] = jnp.broadcast_to(row, gate_back.shape[1:])

            @pl.when(w != me)
            def _(w=w):
                back_copy(w, me).start()

            @pl.when(w == me)
            def _(w=w):
                gate_own[w] = gate_back[w]

    own_rows = pltpu.make_async_copy(grad_back.at[rows_of(me)], own_home.at[rows_of(me)], group_sems.at[groups])

    def give_back(k):
        p, _ = turned(k, -1)
        across(grad_sent, grad_landed, grad_at, p).wait()
        there = rows_of_group(p)
        grad_back[there, :] = (grad_kept[there, :] + grad_landed[there, :].astype(F32)).astype(BF16)
        for j in range(group):
            w = p * group + j

            @pl.when(w != me)
            def _(w=w):
                home_copy(w, me).start()

            @pl.when(w == me)
            def _(w=w):
                own_rows.start()

    def expert_turn(s, carry):
        @pl.when(s < groups)
        def _():
            join_group(s)

        @pl.when(s < 2)
        def _():
            expert_group(s)

        @pl.when((s >= 3) & (s <= groups))
        def _():
            expert_group(s - 1)

        @pl.when((s >= 1) & (s <= 2))
        def _():
            give_back(s - 1)

        @pl.when(s >= 4)
        def _():
            give_back(s - 2)

        return carry

    lax.fori_loop(0, groups + 2, expert_turn, 0)
    own_rows.wait()
    tile = act.shape[1] // groups

    def share_group(k, carry):
        at = pl.multiple_of(k * tile, 128)
        out_grad[pl.ds(at, tile), :] = dot_columns(act[:, pl.ds(at, tile)], slot_grad[...]).astype(BF16)
        q, _ = turned(k, 1)
        for j in range(group):
            e = q * group + j

            @pl.when(e != me)
            def _(e=e):
                home_copy(e, e).wait_recv()

        across(own_home, peer_home, share_at, q).start()
        return carry

    lax.fori_loop(0, groups, share_group, 0)
    out_store = pltpu.make_async_copy(out_grad, out_grad_h, load_sems.at[7])
    out_store.start()

    def take_gates(d, carry):
        other = lax.rem(me + d, wide)
        back_copy(other, other).wait_recv()
        return carry

    lax.fori_loop(1, wide, take_gates, 0)
    tables = move(gate_own, gate_peer, last_at, 1, 1, (me, 1 - plane))
    tables.start()
    in_grad[own_half, :] = dot_columns(rows_own[...], inner_grad[...]).astype(BF16)
    in_grad[peer_half, :] = dot_columns(rows_peer[...], inner_grad[...]).astype(BF16)
    in_store = pltpu.make_async_copy(in_grad, in_grad_h, load_sems.at[8])
    in_store.start()

    def end_sends(d, carry):
        other = lax.rem(me + d, wide)
        up_copy(other, me).wait_send()
        row_copy(other, me).wait_send()
        gate_copy(other, me).wait_send()
        home_copy(other, me).wait_send()
        back_copy(other, me).wait_send()
        return carry

    lax.fori_loop(1, wide, end_sends, 0)

    def end_others(k, carry):
        q, _ = turned(k, 1)
        for j in range(group):
            e = q * group + j

            @pl.when(e != me)
            def _(e=e):
                other_copy(e, me).wait_send()

        return carry

    lax.fori_loop(0, 2, end_others, 0)

    def end_stores(c, carry):
        for kind, (source, target) in enumerate(stores):
            store(kind, source, target, c).wait()
        return carry

    lax.fori_loop(0, chunks, end_stores, 0)
    tables.wait()
    for e in range(wide):
        gate_home[e : e + 1, :] = gate_own[e][0:1, :] + gate_peer[e][0:1, :]

    def end_groups(q, carry):
        store_result(q).wait()
        across(own_home, peer_home, share_at, q).wait()
        return carry

    lax.fori_loop(0, groups, end_groups, 0)
    out_store.wait()
    in_store.wait()


def backward(
    wide, room, heads, layout, orders, rows,
    second_h, cotangent_h, info_h, first_h, tokens_h, qkv_h, context_h, hidden_h, output_h, projection_h, weight_qkv_h,
    row_own_h, row_peer_h, result,
    moe_gain, moe_shift, router, gate_grads, mid_gain, mid_shift, pre_gain, pre_shift, hidden_bias,
    block_h, grad_h, hidden_out_h, output_out_h, qkv_out_h, proj_out_h, *rest,
):
    vectors_out, pre_out, rest = rest[: len(layout)], rest[len(layout)], rest[len(layout) + 1 :]
    (second, cotangent, info, first, tokens, qkv, context, hidden, output, projection, weight_qkv, row_own, row_peer,
     block_out, grad_out, hidden_out, output_out, qkv_out, proj_out), rest = rest[:19], rest[19:]
    load_sems, chunk_sems, store_sems, rest = rest[-3], rest[-2], rest[-1], rest[:-3]
    (lowered_mid, act, inner_grad, mid_own, mid_peer, branch, qkv_grad, lowered_pre, pre_peer, result_own, blend_peer,
     pre_tile, pre_tiles, pre_total, pre_other, moe_sums, router_sums, mid_sums, hidden_sums, qkv_sums, pre_sums, small_sums) = rest[:22]
    hidden_total, output_total, qkv_total, proj_total, small = rest[22:27]
    sends, lands = rest[27:33], rest[33:39]
    mid_sems, pre_sems, blend_sems, result_sems, send_sems, recv_sems = rest[39:]
    blend_own = lowered_mid
    me, plane = lax.axis_index("wide"), lax.axis_index("tensor")
    chunks = tokens.shape[0] // rows
    model = tokens.shape[1]
    width = heads * HEAD_DIM
    split = qkv_total.shape[0] // 2
    totals = (
        hidden_total, output_total, qkv_total.at[pl.ds(0, split)], qkv_total.at[pl.ds(split, split)], proj_total, small
    )
    gathers = (
        hidden_out, output_out, qkv_out.at[pl.ds(0, split)], qkv_out.at[pl.ds(split, split)], proj_out, small_sums
    )

    def chunk_of(index):
        return pl.ds(pl.multiple_of(index * rows, 16), rows)

    early = [(info_h, info), (second_h, second), (cotangent_h, cotangent), (first_h, first)]
    late = [(tokens_h, tokens), (qkv_h, qkv)]

    def load(kind, pair, c):
        return pltpu.make_async_copy(pair[0].at[chunk_of(c)], pair[1].at[chunk_of(c)], chunk_sems.at[kind, c])

    def start_early(c, carry):
        for kind, pair in enumerate(early):
            load(kind, pair, c).start()
        return carry

    def start_late(c, carry):
        for kind, pair in enumerate(late):
            load(len(early) + kind, pair, c).start()
        return carry

    loads = [
        pltpu.make_async_copy(source, target, load_sems.at[i])
        for i, (source, target) in enumerate(
            [(row_own_h, row_own), (row_peer_h, row_peer), (hidden_h, hidden), (output_h, output),
             (projection_h, projection), (weight_qkv_h, weight_qkv), (context_h, context)]
        )
    ]
    for part in loads[:2]:
        part.start()
    start_early(0, 0)
    for part in loads[2:4]:
        part.start()
    lax.fori_loop(1, chunks, start_early, 0)
    for part in loads[4:]:
        part.start()
    lax.fori_loop(0, chunks, start_late, 0)
    whole_stores = [
        pltpu.make_async_copy(source, target, load_sems.at[len(loads) + i])
        for i, (source, target) in enumerate(
            [(hidden_out, hidden_out_h), (output_out, output_out_h), (qkv_out, qkv_out_h), (proj_out, proj_out_h)]
        )
    ]

    def store(kind, source, target, c):
        return pltpu.make_async_copy(source.at[chunk_of(c)], target.at[chunk_of(c)], store_sems.at[kind, c])

    greet(wide)
    sums = Sums(wide, orders, totals, sends, lands, gathers, send_sems, recv_sems)

    def rows_of(index):
        return pl.ds(pl.multiple_of(index * room, 16), room)

    def result_copy(other, sender):
        return pltpu.make_async_remote_copy(
            result.at[rows_of(other)], result_own.at[rows_of(sender)], result_sems.at[0, other],
            result_sems.at[1, sender], device_id=(other, plane), device_id_type=MESH,
        )

    def send_result(d, carry):
        result_copy(lax.rem(me + d, wide), me).start()
        return carry

    lax.fori_loop(1, wide, send_result, 0)
    own_rows = pltpu.make_async_copy(
        result.at[rows_of(me)], result_own.at[rows_of(me)], load_sems.at[len(loads) + len(whole_stores)]
    )
    own_rows.start()

    def across(own, peer, sems, chunk):
        at = pl.multiple_of(chunk * rows, rows)
        return pltpu.make_async_remote_copy(
            own.at[pl.ds(at, rows)], peer.at[pl.ds(at, rows)], sems.at[0, chunk], sems.at[1, chunk],
            device_id=(me, 1 - plane), device_id_type=MESH,
        )

    for vector in (moe_sums, router_sums, mid_sums, hidden_sums, qkv_sums, pre_sums):
        vector[...] = jnp.zeros_like(vector)
    first_plane = plane == 0

    def ordered(own, peer):
        return jnp.concatenate([jnp.where(first_plane, own, peer), jnp.where(first_plane, peer, own)], axis=1)

    def settle(here):
        experts = router.shape[0]
        picks = info[here, experts : experts + 6].astype(jnp.int32)
        hits = token_hits(picks, row_own.shape[0])
        table = (hits[0] | hits[1]).astype(BF16)
        moe_grad = ordered(dot(table, row_own[...]), dot(table, row_peer[...]))
        chances = info[here, 0:experts]
        number = lax.broadcasted_iota(jnp.int32, chances.shape, 1)
        route_grad = jnp.zeros_like(chances)
        for j, spot in enumerate(spots(picks[:, 4:6])):
            at_place = dot_rows(spot.astype(BF16), gate_grads[...].astype(BF16))
            route_grad = route_grad + jnp.where(number == picks[:, 2 + j : 3 + j], at_place, 0.0)
        logit_grad = chances * (route_grad - jnp.sum(chances * route_grad, axis=1, keepdims=True))
        normed, scale = normalized(second[here, :])
        logit_grad = logit_grad.astype(BF16)
        router_sums[...] += dot_columns(logit_grad, (normed * moe_gain[...] + moe_shift[...]).astype(BF16))
        moe_grad = moe_grad + dot(logit_grad, router[...].astype(BF16))
        grad = cotangent[here, :] + norm_back(normed, scale, moe_gain[...], moe_grad)
        grad_out[here, :] = grad
        branch[here, :] = grad.astype(BF16)
        moe_sums[0:1, :] += jnp.sum(moe_grad * normed, axis=0, keepdims=True)
        moe_sums[1:2, :] += jnp.sum(moe_grad, axis=0, keepdims=True)
        moe_sums[2:3, :] += jnp.sum(grad, axis=0, keepdims=True)

    def feed_chunk(chunk, carry):
        here = chunk_of(chunk)
        for kind, pair in enumerate(early):
            load(kind, pair, chunk).wait()
        settle(here)

        @pl.when(chunk == 0)
        def _():
            loads[2].wait()
            loads[3].wait()

        normed, _ = normalized(first[here, :])
        lowered = (normed * mid_gain[...] + mid_shift[...]).astype(BF16)
        lowered_mid[here, :] = lowered
        acted, slope = gelu_parts(dot(lowered, hidden[...]) + hidden_bias[...])
        act[here, :] = acted.astype(BF16)
        inward = (dot_rows(branch[here, :], output[...]) * slope).astype(BF16)
        inner_grad[here, :] = inward
        hidden_sums[0:1, :] += jnp.sum(inward.astype(F32), axis=0, keepdims=True)
        mid_own[here, :] = dot_rows(inward, hidden[...]).astype(BF16)
        across(mid_own, mid_peer, mid_sems, chunk).start()
        return carry

    loads[0].wait()
    loads[1].wait()
    lax.fori_loop(0, chunks, feed_chunk, 0)

    def put_in(total):
        def put(at, tile, value):
            total[pl.ds(at, tile), :] = value

        return put

    column_dots(lowered_mid, inner_grad, put_in(hidden_total))
    sums.begin(0, 0)
    column_dots(act, branch, put_in(output_total))
    sums.begin(1, 0)

    images = rows // PATCHES
    taken = ((3, 7), (3, 7))

    def attend_chunk(chunk, carry):
        here = pl.ds(pl.multiple_of(chunk * rows, rows), rows)
        for kind, pair in enumerate(late):
            load(len(early) + kind, pair, chunk).wait()
        across(mid_own, mid_peer, mid_sems, chunk).wait()
        mid_grad = mid_own[here, :].astype(F32) + mid_peer[here, :].astype(F32)
        normed, scale = normalized(first[here, :])
        first_grad = grad_out[here, :] + norm_back(normed, scale, mid_gain[...], mid_grad)
        grad_out[here, :] = first_grad
        lowered_grad = first_grad.astype(BF16)
        branch[here, :] = lowered_grad
        mid_sums[0:1, :] += jnp.sum(mid_grad * normed, axis=0, keepdims=True)
        mid_sums[1:2, :] += jnp.sum(mid_grad, axis=0, keepdims=True)
        mid_sums[2:3, :] += jnp.sum(first_grad, axis=0, keepdims=True)
        normed, _ = normalized(tokens[here, :].astype(F32))
        lowered_pre[here, :] = (normed * pre_gain[...] + pre_shift[...]).astype(BF16)
        context_grad = dot_rows(lowered_grad, projection[...]).astype(BF16)
        for image in range(rows // PATCHES):
            at = pl.multiple_of(chunk * rows + image * PATCHES, PATCHES)
            block = qkv[pl.ds(at, PATCHES), :]
            grad = image_back(heads, block, context_grad[image * PATCHES : (image + 1) * PATCHES])
            qkv_grad[pl.ds(at, PATCHES), :] = grad
            pre = sum(dot_rows(grad[:, s * width : (s + 1) * width], weight_qkv[s]) for s in range(3))
            pre = pre.astype(BF16)
            mid_own[pl.ds(at, PATCHES), :] = pre
            pre = pre.astype(F32)
            pre_sums[0:1, :] += jnp.sum(pre * normed[image * PATCHES : (image + 1) * PATCHES], axis=0, keepdims=True)
            pre_sums[1:2, :] += jnp.sum(pre, axis=0, keepdims=True)
            qkv_sums[0:1, :] += jnp.sum(grad.astype(F32), axis=0, keepdims=True)
            for i, steps in enumerate(taken):
                for k, boundary in enumerate(steps):
                    if boundary % images == image:

                        @pl.when(chunk == boundary // images)
                        def _(i=i, k=k):
                            sums.advance(i, k)

        across(mid_own, pre_peer, pre_sems, chunk).start()
        return carry

    loads[4].wait()
    loads[5].wait()
    lax.fori_loop(0, chunks, attend_chunk, 0)
    loads[6].wait()

    put_row(pre_tile, put_row(pre_tile, 0, pre_sums[0:1, :]), pre_sums[1:2, :])

    def pre_copy(other, sender):
        return pltpu.make_async_remote_copy(
            pre_tile, pre_tiles.at[sender], result_sems.at[0, wide + other], result_sems.at[1, wide + sender],
            device_id=(other, plane), device_id_type=MESH,
        )

    def send_pre(d, carry):
        pre_copy(lax.rem(me + d, wide), me).start()
        return carry

    lax.fori_loop(1, wide, send_pre, 0)
    pre_tiles[me] = pre_tile[...]

    def put_thirds(at, tile, value):
        for s in range(3):
            there = pl.ds(pl.multiple_of(s * model + at, 16), tile)
            qkv_total[there, :] = value[:, s * width : (s + 1) * width]

    column_dots(lowered_pre, qkv_grad, put_thirds)
    sums.begin(2, 0)
    sums.begin(3, 0)
    column_dots(context, branch, put_in(proj_total))
    sums.begin(4, 0)
    small[...] = jnp.zeros_like(small)
    at = 0
    for vector, picked in zip((mid_sums, moe_sums, hidden_sums, qkv_sums, router_sums), layout):
        for r in picked:
            at = put_row(small, at, vector[r : r + 1, :])
    sums.begin(5, 0)

    def finish_chunk(chunk, carry):
        here = pl.ds(pl.multiple_of(chunk * rows, rows), rows)
        across(mid_own, pre_peer, pre_sems, chunk).wait()
        upstream = mid_own[here, :].astype(F32) + pre_peer[here, :].astype(F32)
        normed, scale = normalized(tokens[here, :].astype(F32))
        grad_out[here, :] += norm_back(normed, scale, pre_gain[...], upstream)
        store(0, grad_out, grad_h, chunk).start()
        return carry

    def take_result(d, carry):
        other = lax.rem(me + d, wide)
        result_copy(other, other).wait_recv()
        result_copy(other, me).wait_send()
        return carry

    lax.fori_loop(1, wide, take_result, 0)
    own_rows.wait()

    def blend(chunk, carry):
        here = pl.ds(pl.multiple_of(chunk * rows, rows), rows)
        experts = router.shape[0]
        picks, chances = info[here, experts : experts + 6].astype(jnp.int32), info[here, 0:experts]
        number = lax.broadcasted_iota(jnp.int32, chances.shape, 1)
        gates = [
            jnp.sum(jnp.where(number == picks[:, 2 + j : 3 + j], chances, 0.0), axis=1, keepdims=True)
            for j in range(2)
        ]
        hits = token_hits(picks, result_own.shape[0])
        table = jnp.where(hits[0], gates[0], jnp.where(hits[1], gates[1], 0.0)).astype(BF16)
        blend_own[here, :] = dot(table, result_own[...]).astype(BF16)
        across(blend_own, blend_peer, blend_sems, chunk).start()
        return carry

    def blend_end(chunk, carry):
        here = pl.ds(pl.multiple_of(chunk * rows, rows), rows)
        across(blend_own, blend_peer, blend_sems, chunk).wait()
        mixture = blend_own[here, :].astype(F32) + blend_peer[here, :].astype(F32)
        block_out[here, :] = (second[here, :] + mixture).astype(BF16)
        store(1, block_out, block_h, chunk).start()
        return carry

    def take_pre(d, carry):
        other = lax.rem(me + d, wide)
        pre_copy(other, other).wait_recv()
        pre_copy(other, me).wait_send()
        return carry

    pre_share = pltpu.make_async_remote_copy(
        pre_total, pre_other, result_sems.at[0, 2 * wide], result_sems.at[1, 2 * wide],
        device_id=(me, 1 - plane), device_id_type=MESH,
    )
    ends = (1, 3, 5, 7)
    for k in range(2 * sums.steps):
        for i in (0, 1):
            if len(taken[i]) + k < 2 * sums.steps:
                sums.advance(i, len(taken[i]) + k)
        for i in (5, 4, 2, 3):
            sums.advance(i, k)
        if k < chunks:
            blend(k, 0)
        if k in ends:
            finish_chunk(ends.index(k), 0)
        if k == sums.steps - 1:
            lax.fori_loop(1, wide, take_pre, 0)
            pre_total[...] = sum(pre_tiles[w] for w in range(wide))
            pre_share.start()
    for part in whole_stores:
        part.start()
    lax.fori_loop(0, chunks, blend_end, 0)
    pre_share.wait()
    pre_tile[...] = pre_total[...] + pre_other[...]
    pre_out[0:1, :] = get_row(pre_tile, 0, model)
    pre_out[1:2, :] = get_row(pre_tile, model // 128, model)
    at = 0
    for out, picked in zip(vectors_out, layout):
        for i in range(len(picked)):
            out[i : i + 1, :] = get_row(small_sums, at, out.shape[1]).astype(F32)
            at += out.shape[1] // 128

    def end_stores(c, carry):
        store(0, grad_out, grad_h, c).wait()
        store(1, block_out, block_h, c).wait()
        return carry

    lax.fori_loop(0, chunks, end_stores, 0)
    for part in whole_stores:
        part.wait()


def widen(pairs, layout, *refs):
    ins, outs = refs[: pairs + len(layout)], refs[pairs + len(layout) :]
    for source, out in zip(ins[:pairs], outs[:pairs]):
        out[...] = source[...].astype(out.dtype)
    outs = iter(outs[pairs:])
    for source, picked in zip(ins[pairs:], layout):
        for r in picked:
            out = next(outs)
            if out.shape[0] == 2:
                out[0:1, :] = source[0:1, : out.shape[1]]
                out[1:2, :] = source[0:1, 2 * out.shape[1] :]
            else:
                out[...] = source[r : r + out.shape[0], : out.shape[1]]


def shards(
    wide,
    tokens_in, pre_gain, pre_shift, qkv_weight, qv_bias, proj_weight, proj_bias, mid_gain, mid_shift,
    hidden_weight, hidden_bias, output_weight, output_bias, moe_gain, moe_shift, router_weight,
    expert_in, expert_in_bias, expert_out, expert_out_bias, expert_ids, priority, cotangent,
):
    tokens, model = tokens_in.shape
    width = qkv_weight.shape[2]
    heads = width // HEAD_DIM
    hidden = hidden_weight.shape[1]
    count = router_weight.shape[1]
    capacity = tokens // count
    room = -(-capacity // 16) * 16
    slots = count * room
    half = model // 2
    lanes = 3 * width
    rows = 2 * PATCHES
    chunks = tokens // rows
    group = 4
    steps = wide.bit_length() - 1

    def row(vector):
        return vector.reshape(1, -1)

    def remote(kernel, name, identity, far_ins, ins, far_outs, outs, scratch):
        far, near = pl.BlockSpec(memory_space=pl.ANY), pl.BlockSpec(memory_space=pltpu.VMEM)
        return pl.pallas_call(
            kernel,
            out_shape=[jax.ShapeDtypeStruct(shape, dtype) for shape, dtype in far_outs + outs],
            in_specs=[far] * len(far_ins) + [near] * len(ins),
            out_specs=[far] * len(far_outs) + [near] * len(outs),
            scratch_shapes=scratch,
            compiler_params=pltpu.CompilerParams(
                vmem_limit_bytes=VMEM_BYTES, collective_id=identity, has_side_effects=True
            ),
            name=name,
        )(*far_ins, *ins)

    def room_for(local):
        return [pltpu.VMEM(shape, dtype) for shape, dtype in local]

    pre_gain, pre_shift, proj_bias = row(pre_gain), row(pre_shift), row(proj_bias)
    mid_gain, mid_shift, hidden_bias = row(mid_gain), row(mid_shift), row(hidden_bias)
    output_bias, moe_gain, moe_shift = row(output_bias), row(moe_gain), row(moe_shift)
    weight_qkv = qkv_weight.transpose(1, 0, 2)
    router = router_weight.T
    groups = wide // group
    kept = [
        ((tokens, lanes), BF16), ((tokens, width), BF16), ((tokens, model), F32), ((tokens, model), F32),
        ((tokens, 128), F32), ((slots, model), BF16), ((model, hidden), BF16), ((hidden, model), BF16),
    ]
    homes = [((slots, half), BF16), ((slots, half), BF16)]
    fetched = [tokens_in, cotangent, weight_qkv, proj_weight, hidden_weight, output_weight, expert_in[0], expert_out[0]]
    tables = [((count, 8, 128), F32)] * 5
    qkv, context, first, second, info, result, in_grad, out_grad, row_own, row_peer, gate_grads, in_bias, out_bias = remote(
        functools.partial(front, wide, room, group, heads, rows, count), "front", 1,
        fetched,
        [expert_ids.T, priority, pre_gain, pre_shift, qv_bias, proj_bias, mid_gain, mid_shift, hidden_bias, output_bias,
         moe_gain, moe_shift, router, expert_in_bias, expert_out_bias],
        kept + homes,
        [((count, 128), F32), ((8, hidden), F32), ((8, model), F32)],
        room_for([(array.shape, array.dtype) for array in fetched] + kept
                 + [((8, tokens), jnp.int32), ((count, 128), F32), ((slots, model), BF16), ((slots, model), BF16),
                    ((width, model), BF16), ((tokens, width), BF16), ((tokens, model), BF16), ((tokens, model), BF16),
                    ((tokens, half), BF16), ((tokens, half), BF16), ((slots, half), BF16), ((slots, half), BF16),
                    ((slots, half), BF16), ((slots, half), BF16),
                    ((slots, hidden), BF16), ((slots, hidden), BF16), ((slots, model), BF16), ((slots, half), F32),
                    ((slots, half), BF16), ((slots, half), BF16), ((slots, half), BF16)] + tables)
        + [pltpu.SemaphoreType.DMA((2, 6 * wide + 3 * groups + 2 * chunks + 2)), pltpu.SemaphoreType.DMA((9,)),
           pltpu.SemaphoreType.DMA((chunks,)), pltpu.SemaphoreType.DMA((5, chunks)), pltpu.SemaphoreType.DMA((groups + 1,))],
    )

    layout = [(0, 1, 2), (0, 1, 2), (0,), (0,), tuple(range(count))]
    vectors = [((8, model), F32), ((8, model), F32), ((8, hidden), F32), ((8, lanes), F32), ((count, model), F32)]
    near, far = tuple(range(steps)), (0,) + tuple(range(2, steps)) + (1,)
    summed = [(model, hidden), (hidden, model), (3 * model // 2, width), (3 * model // 2, width), (width, model), (16 * wide, 128)]
    fetched = [second, cotangent, info, first, tokens_in, qkv, context, hidden_weight, output_weight, proj_weight, weight_qkv, row_own, row_peer]
    given = [
        ((tokens, model), BF16), ((tokens, model), F32), ((model, hidden), BF16), ((hidden, model), BF16),
        ((3 * model, width), BF16), ((width, model), BF16),
    ]
    tile = (2 * model // 128, 128)
    block_out, grad, hidden_g, output_g, qkv_g, proj_g, *sums = remote(
        functools.partial(backward, wide, room, heads, layout, (near, far, near, far, near, far), rows), "backward", 2,
        fetched + [result],
        [moe_gain, moe_shift, router, gate_grads, mid_gain, mid_shift, pre_gain, pre_shift, hidden_bias],
        given, vectors + [((8, model), F32)],
        room_for([(array.shape, array.dtype) for array in fetched] + given
                 + [((tokens, model), BF16), ((tokens, hidden), BF16), ((tokens, hidden), BF16), ((tokens, model), BF16),
                    ((tokens, model), BF16), ((tokens, model), BF16), ((tokens, lanes), BF16), ((tokens, model), BF16),
                    ((tokens, model), BF16), ((slots, model), BF16), ((tokens, model), BF16),
                    (tile, F32), ((wide,) + tile, F32), (tile, F32), (tile, F32), ((8, model), F32), ((count, model), F32),
                    ((8, model), F32), ((8, hidden), F32), ((8, lanes), F32), ((8, model), F32), (summed[-1], BF16),
                    (summed[0], F32), (summed[1], F32), ((3 * model, width), F32), (summed[4], F32), (summed[5], F32)]
                 + [(shape, BF16) for shape in summed] * 2)
        + [pltpu.SemaphoreType.DMA((2, chunks))] * 3 + [pltpu.SemaphoreType.DMA((2, 2 * wide + 1))]
        + [pltpu.SemaphoreType.DMA((len(summed), 2 * steps))] * 2
        + [pltpu.SemaphoreType.DMA((12,)), pltpu.SemaphoreType.DMA((6, chunks)), pltpu.SemaphoreType.DMA((2, chunks))],
    )

    pairs = [
        (block_out, BF16), (grad, F32), (hidden_g, F32), (output_g, F32), (qkv_g.reshape(3, model, width), F32),
        (proj_g, F32), (in_grad, F32), (out_grad, F32),
    ]
    singles = [(0, 1), (0, 1, 2), (0, 1, 2), (0,), (0,), (0,), (0,), (0,)]
    sources = [sums[-1]] + list(sums[:-1]) + [in_bias, out_bias]
    sizes = [(1, model)] * 8 + [(1, hidden), (2, width), (count, model), (1, hidden), (1, model)]
    parts = 2

    def spec(shape):
        if len(shape) == 3:
            return pl.BlockSpec((shape[0], shape[1] // parts, shape[2]), lambda i: (0, i, 0))
        return pl.BlockSpec((shape[0] // parts, shape[1]), lambda i: (i, 0))

    def whole(shape):
        return pl.BlockSpec(shape, lambda i: (0, 0))

    outs = pl.pallas_call(
        functools.partial(widen, len(pairs), singles),
        grid=(parts,),
        in_specs=[spec(source.shape) for source, _ in pairs] + [whole(source.shape) for source in sources],
        out_specs=[spec(source.shape) for source, _ in pairs] + [whole(size) for size in sizes],
        out_shape=[jax.ShapeDtypeStruct(source.shape, dtype) for source, dtype in pairs]
        + [jax.ShapeDtypeStruct(size, F32) for size in sizes],
        compiler_params=pltpu.CompilerParams(vmem_limit_bytes=VMEM_BYTES),
        name="widen",
    )(*[source for source, _ in pairs], *sources)
    block_out, grad, hidden_g, output_g, qkv_g, proj_g, in_grad, out_grad = outs[:8]
    pre_gain_g, pre_shift_g, mid_gain_g, mid_shift_g, proj_bias_g, moe_gain_g, moe_shift_g, output_bias_g = (
        vector.reshape(model) for vector in outs[8:16]
    )
    hidden_bias_g, qkv_bias_g, router_g, in_bias_g, out_bias_g = outs[16:]
    return (
        block_out, grad, pre_gain_g, pre_shift_g, qkv_g.transpose(1, 0, 2),
        qkv_bias_g, proj_g, proj_bias_g, mid_gain_g,
        mid_shift_g, hidden_g, hidden_bias_g.reshape(hidden), output_g, output_bias_g, moe_gain_g, moe_shift_g,
        router_g.T, in_grad[None], in_bias_g, out_grad[None], out_bias_g,
    )


def layer_norm(values, gain, shift):
    centered = values - jnp.mean(values, axis=-1, keepdims=True)
    variance = jnp.mean(centered * centered, axis=-1, keepdims=True)
    return centered * lax.rsqrt(variance + 1e-06) * gain + shift


def norm_grad(values, gain, shift, upstream):
    _, pullback = jax.vjp(layer_norm, values, gain, shift)
    return pullback(upstream)


def gelu_grad(inner, upstream):
    _, pullback = jax.vjp(jax.nn.gelu, inner)
    return pullback(upstream)[0]


def slot_tables(choice_ids, ranks, capacity, experts):
    count = choice_ids.shape[0]
    order_keys = jnp.concatenate([ranks, ranks + count])
    flat_ids = jnp.concatenate([choice_ids[:, 0], choice_ids[:, 1]])
    earlier = (order_keys[None, :] < order_keys[:, None]) & (flat_ids[None, :] == flat_ids[:, None])
    position = jnp.sum(earlier.astype(jnp.int32), axis=1)
    kept = position < capacity
    position = position.reshape(2, count)
    kept = kept.reshape(2, count)
    columns = jnp.arange(experts * capacity, dtype=jnp.int32)
    target = choice_ids.T * capacity + position
    tables = (target[:, :, None] == columns[None, None, :]) & kept[:, :, None]
    return (tables, kept)


def plain(
    tokens_in,
    pre_gain,
    pre_shift,
    qkv_weight,
    qv_bias,
    proj_weight,
    proj_bias,
    mid_gain,
    mid_shift,
    hidden_weight,
    hidden_bias,
    output_weight,
    output_bias,
    moe_gain,
    moe_shift,
    router_weight,
    expert_in,
    expert_in_bias,
    expert_out,
    expert_out_bias,
    expert_ids,
    priority,
    cotangent,
):
    tokens = tokens_in.shape[0]
    model_width = tokens_in.shape[1]
    local_heads = qkv_weight.shape[2] // HEAD_DIM
    images = tokens // PATCHES
    experts = router_weight.shape[1]
    capacity = tokens // experts
    score_scale = float(HEAD_DIM) ** (-0.5)
    highest = lax.Precision.HIGHEST
    residual = tokens_in.astype(jnp.float32)
    normed_pre = layer_norm(residual, pre_gain, pre_shift)
    lowered_pre = normed_pre.astype(jnp.bfloat16)
    blank = jnp.zeros_like(qv_bias[0])
    qkv_shift = jnp.stack([qv_bias[0], blank, qv_bias[1]])
    qkv = (
        jnp.einsum("td,dsk->tsk", lowered_pre, qkv_weight, preferred_element_type=jnp.float32)
        + qkv_shift
    ).astype(jnp.bfloat16)
    grid = qkv.reshape(images, PATCHES, 3, local_heads, HEAD_DIM)
    query, keys, values = (grid[:, :, 0], grid[:, :, 1], grid[:, :, 2])
    scores = (
        jnp.einsum("bqhd,bkhd->bhqk", query, keys, preferred_element_type=jnp.float32) * score_scale
    )
    log_total = jax.nn.logsumexp(scores, axis=-1, keepdims=True)
    weights = jnp.exp(scores - log_total).astype(jnp.bfloat16)
    context = jnp.einsum("bhqk,bkhd->bqhd", weights, values, preferred_element_type=jnp.float32)
    context = context.astype(jnp.bfloat16).reshape(tokens, local_heads * HEAD_DIM)
    branch = lax.psum(jnp.dot(context, proj_weight, preferred_element_type=jnp.float32), "tensor")
    first = residual + branch + proj_bias
    normed_mid = layer_norm(first, mid_gain, mid_shift)
    lowered_mid = normed_mid.astype(jnp.bfloat16)
    inner = jnp.dot(lowered_mid, hidden_weight, preferred_element_type=jnp.float32) + hidden_bias
    activated = jax.nn.gelu(inner).astype(jnp.bfloat16)
    partial_out = jnp.dot(activated, output_weight, preferred_element_type=jnp.float32)
    second = first + lax.psum(partial_out, "tensor") + output_bias
    normed_moe = layer_norm(second, moe_gain, moe_shift)
    lowered_moe = normed_moe.astype(jnp.bfloat16)
    route = jax.nn.softmax(jnp.dot(normed_moe, router_weight, precision=highest), axis=-1)
    tables, kept = slot_tables(expert_ids, priority[0], capacity, experts)
    tables = tables.astype(jnp.bfloat16)
    dispatch = tables[0] + tables[1]
    buffers = jnp.einsum("tk,td->kd", dispatch, lowered_moe, preferred_element_type=jnp.float32)
    buffers = buffers.astype(jnp.bfloat16).reshape(experts, capacity, model_width)
    arrived = lax.all_to_all(buffers, "wide", split_axis=0, concat_axis=1, tiled=True)
    expert_inner = (
        jnp.einsum("erd,edf->erf", arrived, expert_in, preferred_element_type=jnp.float32)
        + expert_in_bias[:, None, :]
    )
    expert_act = jax.nn.gelu(expert_inner).astype(jnp.bfloat16)
    expert_partial = jnp.einsum(
        "erf,efd->erd", expert_act, expert_out, preferred_element_type=jnp.float32
    )
    expert_result = (
        lax.psum(expert_partial.astype(jnp.bfloat16), "tensor").astype(jnp.float32)
        + expert_out_bias[:, None, :]
    ).astype(jnp.bfloat16)
    returned = lax.all_to_all(
        expert_result, "wide", split_axis=1, concat_axis=0, tiled=True
    ).reshape(experts * capacity, model_width)
    picked = jnp.einsum("jtk,kd->jtd", tables, returned, preferred_element_type=jnp.float32)
    expert_range = jnp.arange(experts, dtype=jnp.int32)
    chosen = (expert_ids.T[:, :, None] == expert_range[None, None, :]).astype(jnp.float32) * kept[
        :, :, None
    ].astype(jnp.float32)
    gates = jnp.sum(chosen * route[None], axis=-1)
    mixture = jnp.sum(gates[:, :, None] * picked, axis=0)
    block_out = (second + mixture).astype(jnp.bfloat16)
    gate_grad = jnp.sum(picked * cotangent[None], axis=-1)
    weighted = (gates[:, :, None] * cotangent[None]).astype(jnp.bfloat16)
    slot_grad = jnp.einsum("jtk,jtd->kd", tables, weighted, preferred_element_type=jnp.float32)
    slot_grad = slot_grad.astype(jnp.bfloat16).reshape(experts, capacity, model_width)
    result_grad = lax.all_to_all(slot_grad, "wide", split_axis=0, concat_axis=1, tiled=True)
    expert_out_bias_grad = jnp.sum(result_grad.astype(jnp.float32), axis=1)
    expert_out_grad = jnp.einsum(
        "erf,erd->efd", expert_act, result_grad, preferred_element_type=jnp.float32
    )
    act_grad = jnp.einsum(
        "erd,efd->erf", result_grad, expert_out, preferred_element_type=jnp.float32
    )
    expert_inner_grad = gelu_grad(expert_inner, act_grad).astype(jnp.bfloat16)
    expert_in_bias_grad = jnp.sum(expert_inner_grad.astype(jnp.float32), axis=1)
    expert_in_grad = jnp.einsum(
        "erd,erf->edf", arrived, expert_inner_grad, preferred_element_type=jnp.float32
    )
    arrived_partial = jnp.einsum(
        "erf,edf->erd", expert_inner_grad, expert_in, preferred_element_type=jnp.float32
    )
    arrived_grad = lax.psum(arrived_partial.astype(jnp.bfloat16), "tensor")
    buffer_grad = lax.all_to_all(
        arrived_grad, "wide", split_axis=1, concat_axis=0, tiled=True
    ).reshape(experts * capacity, model_width)
    moe_input_grad = jnp.dot(dispatch, buffer_grad, preferred_element_type=jnp.float32)
    route_grad = jnp.sum(gate_grad[:, :, None] * chosen, axis=0)
    logit_grad = route * (route_grad - jnp.sum(route * route_grad, axis=-1, keepdims=True))
    router_grad = jnp.einsum("td,te->de", normed_moe, logit_grad, precision=highest)
    moe_input_grad = moe_input_grad + jnp.einsum(
        "te,de->td", logit_grad, router_weight, precision=highest
    )
    second_part, moe_gain_grad, moe_shift_grad = norm_grad(
        second, moe_gain, moe_shift, moe_input_grad
    )
    second_grad = cotangent + second_part
    lowered_second = second_grad.astype(jnp.bfloat16)
    output_bias_grad = jnp.sum(second_grad, axis=0)
    output_weight_grad = jnp.einsum(
        "tf,td->fd", activated, lowered_second, preferred_element_type=jnp.float32
    )
    activated_grad = jnp.einsum(
        "td,fd->tf", lowered_second, output_weight, preferred_element_type=jnp.float32
    )
    inner_grad = gelu_grad(inner, activated_grad).astype(jnp.bfloat16)
    hidden_bias_grad = jnp.sum(inner_grad.astype(jnp.float32), axis=0)
    hidden_weight_grad = jnp.einsum(
        "td,tf->df", lowered_mid, inner_grad, preferred_element_type=jnp.float32
    )
    mid_partial = jnp.einsum(
        "tf,df->td", inner_grad, hidden_weight, preferred_element_type=jnp.float32
    )
    mid_grad = lax.psum(mid_partial, "tensor")
    first_part, mid_gain_grad, mid_shift_grad = norm_grad(first, mid_gain, mid_shift, mid_grad)
    first_grad = second_grad + first_part
    proj_bias_grad = jnp.sum(first_grad, axis=0)
    branch_grad = first_grad.astype(jnp.bfloat16)
    proj_weight_grad = jnp.einsum(
        "tk,td->kd", context, branch_grad, preferred_element_type=jnp.float32
    )
    context_grad = jnp.einsum(
        "td,kd->tk", branch_grad, proj_weight, preferred_element_type=jnp.float32
    )
    context_grad = context_grad.astype(jnp.bfloat16).reshape(images, PATCHES, local_heads, HEAD_DIM)
    scores = (
        jnp.einsum("bqhd,bkhd->bhqk", query, keys, preferred_element_type=jnp.float32) * score_scale
    )
    probs = jnp.exp(scores - log_total)
    weights = probs.astype(jnp.bfloat16)
    value_grad = jnp.einsum(
        "bhqk,bqhd->bkhd", weights, context_grad, preferred_element_type=jnp.float32
    )
    prob_grad = jnp.einsum(
        "bqhd,bkhd->bhqk", context_grad, values, preferred_element_type=jnp.float32
    )
    score_grad = (probs * (prob_grad - jnp.sum(probs * prob_grad, axis=-1, keepdims=True))).astype(
        jnp.bfloat16
    )
    query_grad = (
        jnp.einsum("bhqk,bkhd->bqhd", score_grad, keys, preferred_element_type=jnp.float32)
        * score_scale
    )
    key_grad = (
        jnp.einsum("bhqk,bqhd->bkhd", score_grad, query, preferred_element_type=jnp.float32)
        * score_scale
    )
    qkv_grad = jnp.stack([query_grad, key_grad, value_grad], axis=2).astype(jnp.bfloat16)
    qkv_grad = qkv_grad.reshape(tokens, 3, local_heads * HEAD_DIM)
    qkv_sums = jnp.sum(qkv_grad.astype(jnp.float32), axis=0)
    qv_bias_grad = jnp.stack([qkv_sums[0], qkv_sums[2]])
    qkv_weight_grad = jnp.einsum(
        "td,tsk->dsk", lowered_pre, qkv_grad, preferred_element_type=jnp.float32
    )
    pre_partial = jnp.einsum(
        "tsk,dsk->td", qkv_grad, qkv_weight, preferred_element_type=jnp.float32
    )
    pre_grad = lax.psum(pre_partial.astype(jnp.bfloat16), "tensor").astype(jnp.float32)
    input_part, pre_gain_grad, pre_shift_grad = norm_grad(residual, pre_gain, pre_shift, pre_grad)
    tokens_grad = first_grad + input_part
    shared = (
        lax.psum(pre_gain_grad.astype(jnp.bfloat16), "wide").astype(jnp.float32),
        lax.psum(pre_shift_grad.astype(jnp.bfloat16), "wide").astype(jnp.float32),
        lax.psum(qkv_weight_grad.astype(jnp.bfloat16), "wide").astype(jnp.float32),
        lax.psum(qv_bias_grad.astype(jnp.bfloat16), "wide").astype(jnp.float32),
        lax.psum(proj_weight_grad.astype(jnp.bfloat16), "wide").astype(jnp.float32),
        lax.psum(proj_bias_grad.astype(jnp.bfloat16), "wide").astype(jnp.float32),
        lax.psum(mid_gain_grad.astype(jnp.bfloat16), "wide").astype(jnp.float32),
        lax.psum(mid_shift_grad.astype(jnp.bfloat16), "wide").astype(jnp.float32),
        lax.psum(hidden_weight_grad.astype(jnp.bfloat16), "wide").astype(jnp.float32),
        lax.psum(hidden_bias_grad.astype(jnp.bfloat16), "wide").astype(jnp.float32),
        lax.psum(output_weight_grad.astype(jnp.bfloat16), "wide").astype(jnp.float32),
        lax.psum(output_bias_grad.astype(jnp.bfloat16), "wide").astype(jnp.float32),
        lax.psum(moe_gain_grad.astype(jnp.bfloat16), "wide").astype(jnp.float32),
        lax.psum(moe_shift_grad.astype(jnp.bfloat16), "wide").astype(jnp.float32),
        lax.psum(router_grad.astype(jnp.bfloat16), "wide").astype(jnp.float32),
    )
    return (
        (block_out, tokens_grad)
        + tuple(shared)
        + (expert_in_grad, expert_in_bias_grad, expert_out_grad, expert_out_bias_grad)
    )


def solution(mesh):
    body = functools.partial(shards, mesh.shape["wide"]) if mesh.shape["tensor"] == 2 else plain
    return jax.shard_map(
        body,
        mesh=mesh,
        in_specs=(
            P("wide", None), P(), P(), P(None, None, "tensor"), P(None, "tensor"), P("tensor", None), P(), P(), P(),
            P(None, "tensor"), P("tensor"), P("tensor", None), P(), P(), P(), P(),
            P("wide", None, "tensor"), P("wide", "tensor"), P("wide", "tensor", None), P("wide", None),
            P("wide", None), P("wide", None), P("wide", None),
        ),
        out_specs=(
            P("wide", None), P("wide", None), P(), P(), P(None, None, "tensor"), P(None, "tensor"), P("tensor", None),
            P(), P(), P(), P(None, "tensor"), P("tensor"), P("tensor", None), P(), P(), P(), P(),
            P("wide", None, "tensor"), P("wide", "tensor"), P("wide", "tensor", None), P("wide", None),
        ),
        check_vma=False,
    )
```

```python
import functools

import jax
import jax.numpy as jnp
from jax import lax
from jax.experimental import pallas as pl
from jax.experimental.pallas import tpu as pltpu
from jax.sharding import PartitionSpec as P

HEAD_DIM = 64
PATCHES = 144
BF16 = jnp.bfloat16
F32 = jnp.float32
HIGHEST = lax.Precision.HIGHEST
MESH = pl.DeviceIdType.MESH
VMEM_BYTES = 60 * 1024 * 1024


def dot(left, right):
    return jnp.dot(left, right, preferred_element_type=F32)


def dot_rows(left, right):
    return lax.dot_general(left, right, (((1,), (1,)), ((), ())), preferred_element_type=F32)


def dot_columns(left, right, precision=None):
    return lax.dot_general(
        left, right, (((0,), (0,)), ((), ())), precision=precision, preferred_element_type=F32
    )


def normalized(values):
    centered = values - jnp.mean(values, axis=-1, keepdims=True)
    variance = jnp.mean(centered * centered, axis=-1, keepdims=True)
    scale = lax.rsqrt(variance + 1e-06)
    return centered * scale, scale


def norm_back(rows, scale, gain, upstream):
    scaled = upstream * gain
    inward = jnp.mean(scaled, axis=-1, keepdims=True)
    along = jnp.mean(scaled * rows, axis=-1, keepdims=True)
    return scale * (scaled - inward - rows * along)


def gelu_parts(inner):
    square = inner * inner
    bend = jnp.tanh(0.7978845608028654 * inner * (1.0 + 0.044715 * square))
    half = 0.5 * (1.0 + bend)
    slope = half + (0.5 * 0.7978845608028654) * inner * (1.0 - bend * bend) * (
        1.0 + 0.134145 * square
    )
    return inner * half, slope


def gelu(inner):
    return inner * (0.5 * (1.0 + jnp.tanh(0.7978845608028654 * inner * (1.0 + 0.044715 * inner * inner))))


def softmax_rows(scores, scale):
    peak = jnp.max(scores, axis=-1, keepdims=True)
    weights = jnp.exp((scores - peak) * scale)
    return weights * (1.0 / jnp.sum(weights, axis=-1, keepdims=True))


def spots(places):
    lane = lax.broadcasted_iota(jnp.int32, (places.shape[0], 128), 1)
    return [(lane == places[:, j : j + 1]).astype(F32) for j in range(2)]


def bits_of(index, wide):
    return [lax.rem(lax.div(index, 1 << k), 2) for k in range(wide.bit_length() - 1)]


class Sums:
    def __init__(self, wide, orders, totals, sends, lands, gathers, send_sems, recv_sems):
        me, self.plane = lax.axis_index("wide"), lax.axis_index("tensor")
        self.bits = bits_of(me, wide)
        self.partners = [me + (1 - 2 * bit) * (1 << k) for k, bit in enumerate(self.bits)]
        self.steps = len(self.bits)
        self.orders, self.totals, self.sends, self.lands, self.gathers = orders, totals, sends, lands, gathers
        self.send_sems, self.recv_sems = send_sems, recv_sems

    def piece(self, i, step):
        rows = self.gathers[i].shape[0]
        base = 0
        for s in range(step):
            base = base + self.bits[self.orders[i][s]] * (rows >> (s + 1))
        length = rows >> (step + 1)
        bit = self.bits[self.orders[i][step]]
        return pl.multiple_of(base + bit * length, 16), pl.multiple_of(base + (1 - bit) * length, 16), length

    def staged(self, i, step):
        rows = self.gathers[i].shape[0]
        return rows - (rows >> step)

    def transfer(self, i, k):
        step = k if k < self.steps else 2 * self.steps - 1 - k
        kept, _, length = self.piece(i, step)
        if k < self.steps:
            at = self.staged(i, step)
            source, target = self.sends[i].at[pl.ds(at, length)], self.lands[i].at[pl.ds(at, length)]
        else:
            source = target = self.gathers[i].at[pl.ds(kept, length)]
        return pltpu.make_async_remote_copy(
            source, target, self.send_sems.at[i, k], self.recv_sems.at[i, k],
            device_id=(self.partners[self.orders[i][step]], self.plane), device_id_type=MESH,
        )

    def begin(self, i, k):
        if k < self.steps:
            _, other, length = self.piece(i, k)
            at = self.staged(i, k)
            self.sends[i][at : at + length, :] = self.totals[i][pl.ds(other, length), :].astype(BF16)
        self.transfer(i, k).start()

    def advance(self, i, k):
        self.transfer(i, k).wait()
        if k < self.steps:
            kept, _, length = self.piece(i, k)
            at = self.staged(i, k)
            value = self.totals[i][pl.ds(kept, length), :] + self.lands[i][at : at + length, :].astype(F32)
            if k + 1 < self.steps:
                self.totals[i][pl.ds(kept, length), :] = value
            else:
                self.gathers[i][pl.ds(kept, length), :] = value.astype(BF16)
        if k + 1 < 2 * self.steps:
            self.begin(i, k + 1)


def greet(wide):
    me, plane = lax.axis_index("wide"), lax.axis_index("tensor")
    barrier = pltpu.get_barrier_semaphore()

    def hail(d, carry):
        pl.semaphore_signal(barrier, inc=1, device_id=(lax.rem(me + d, wide), plane), device_id_type=MESH)
        return carry

    lax.fori_loop(1, wide, hail, 0)
    pl.semaphore_signal(barrier, inc=1, device_id=(me, 1 - plane), device_id_type=MESH)
    pl.semaphore_wait(barrier, wide)


def put_row(small, at, row):
    for c in range(row.shape[1] // 128):
        small[at + c : at + c + 1, :] = row[:, 128 * c : 128 * (c + 1)]
    return at + row.shape[1] // 128


def get_row(small, at, width):
    return jnp.concatenate([small[at + c : at + c + 1, :] for c in range(width // 128)], axis=1)


def image_back(heads, qkv, context_grad):
    width = heads * HEAD_DIM
    scale = HEAD_DIM**-0.5
    parts = [[], [], []]
    for head in range(heads):
        h = head * HEAD_DIM
        query = qkv[:, h : h + HEAD_DIM]
        keys = qkv[:, width + h : width + h + HEAD_DIM]
        values = qkv[:, 2 * width + h : 2 * width + h + HEAD_DIM]
        upstream = context_grad[:, h : h + HEAD_DIM]
        scores = dot_rows(keys, query)
        weights = jnp.exp((scores - jnp.max(scores, axis=0, keepdims=True)) * scale)
        probs = weights * (1.0 / jnp.sum(weights, axis=0, keepdims=True))
        prob_grad = dot_rows(values, upstream)
        inward = jnp.sum(probs * prob_grad, axis=0, keepdims=True)
        score_grad = (probs * (prob_grad - inward)).astype(BF16)
        parts[0].append(dot_columns(score_grad, keys) * scale)
        parts[1].append(dot(score_grad, query) * scale)
        parts[2].append(dot(probs.astype(BF16), upstream))
    return jnp.concatenate(parts[0] + parts[1] + parts[2], axis=1).astype(BF16)


def column_dots(left, right, put, tile=256):
    def body(i, carry):
        at = pl.multiple_of(i * tile, tile)
        put(at, tile, dot_columns(left[:, pl.ds(at, tile)], right[...]))
        return carry

    lax.fori_loop(0, left.shape[1] // tile, body, 0)


def image_forward(heads, qkv):
    width = heads * HEAD_DIM
    parts = []
    for head in range(heads):
        h = head * HEAD_DIM
        probs = softmax_rows(
            dot_rows(qkv[:, h : h + HEAD_DIM], qkv[:, width + h : width + h + HEAD_DIM]), HEAD_DIM**-0.5
        )
        parts.append(dot(probs.astype(BF16), qkv[:, 2 * width + h : 2 * width + h + HEAD_DIM]))
    return jnp.concatenate(parts, axis=1).astype(BF16)


def token_hits(choices, slots):
    slot = lax.broadcasted_iota(jnp.int32, (choices.shape[0], slots), 1)
    return [slot == choices[:, j : j + 1] for j in range(2)]


def slot_hits(first, count, targets):
    slot = first + lax.broadcasted_iota(jnp.int32, (count, targets.shape[1]), 0)
    return ((slot == targets[0:1, :]) | (slot == targets[1:2, :])).astype(BF16)


def count_slots(ids, priority, experts, capacity, room):
    tokens = ids.shape[1]
    wide_rows = jnp.concatenate([ids, priority, jnp.zeros((5, tokens), jnp.int32)], axis=0)
    eye = lax.broadcasted_iota(jnp.int32, (8, 8), 0) == lax.broadcasted_iota(jnp.int32, (8, 8), 1)
    turned = dot_columns(wide_rows.astype(F32), eye.astype(F32), HIGHEST).astype(jnp.int32)
    rank, ranks = turned[:, 2:3], priority

    def fold(numbers, own, before, axis):
        later = [jnp.where(numbers == own[0], before, 0.0), jnp.where(numbers == own[1] + experts, before, 0.0)]
        return [jnp.sum(part, axis=axis, keepdims=True) for part in later]

    def finish(own, counts, firsts):
        counts = [counts[0], counts[1] + firsts]
        places = [count.astype(jnp.int32) for count in counts]
        kept = [place < capacity for place in places]
        return (
            [jnp.where(keep, choice * room + place, -1) for keep, choice, place in zip(kept, own, places)],
            [jnp.where(keep, choice, -1) for keep, choice in zip(kept, own)],
            [jnp.where(keep, place, -1) for keep, place in zip(kept, places)],
        )

    number = lax.broadcasted_iota(jnp.int32, (2 * experts, tokens), 0)
    by_row = [ids[0:1, :], ids[1:2, :]]
    held = ((number == by_row[0]) | (number == by_row[1] + experts)).astype(BF16)
    before = dot(held, (rank < ranks).astype(BF16))
    first_counts = jnp.sum(held.astype(F32), axis=1, keepdims=True)
    firsts = jnp.sum(jnp.where(number == by_row[1], first_counts, 0.0), axis=0, keepdims=True)
    targets, _, _ = finish(by_row, fold(number, by_row, before, 0), firsts)

    number = lax.broadcasted_iota(jnp.int32, (tokens, 2 * experts), 1)
    by_token = [turned[:, 0:1], turned[:, 1:2]]
    held_by_token = ((number == by_token[0]) | (number == by_token[1] + experts)).astype(BF16)
    before = dot((ranks < rank).astype(BF16), held_by_token)
    first_counts = jnp.sum(held_by_token.astype(F32), axis=0, keepdims=True)
    firsts = jnp.sum(jnp.where(number == by_token[1], first_counts, 0.0), axis=1, keepdims=True)
    groups = finish(by_token, fold(number, by_token, before, 1), firsts)
    choices = jnp.concatenate([part for group in groups for part in group], axis=1)
    return jnp.concatenate(targets, axis=0), choices


def front(
    wide, room, group, heads, rows, experts,
    tokens_h, cotangent_h, weight_qkv_h, projection_h, hidden_h, output_h, weight_in_h, weight_out_h,
    ids, priority, pre_gain, pre_shift, qv_bias, proj_bias, mid_gain, mid_shift, hidden_bias, output_bias,
    moe_gain, moe_shift, router, bias_in, bias_out,
    qkv_h, context_h, first_h, second_h, info_h, result_h, in_grad_h, out_grad_h, fed_h, slope_h, lowered_h, own_home, peer_home,
    gate_home, in_bias_grad, out_bias_grad,
    tokens, cotangent, weight_qkv, projection, hidden, output, weight_in, weight_out,
    qkv, context, first, second, info, result, in_grad, out_grad, fed, slopes_kept, lowered_mid,
    targets, table, raised_placed, upstream, projection_peer, context_peer, partial_own, partial_peer,
    columns, other_columns, placed, other_placed, rows_own, rows_peer, act, inner_grad, slot_grad, grad_kept, grad_sent, grad_landed,
    grad_back, gate_sent, gate_arrived, gate_back, gate_own, gate_peer,
    sems, load_sems, chunk_sems, store_sems, group_sems,
):
    me, plane = lax.axis_index("wide"), lax.axis_index("tensor")
    chunks, groups = tokens.shape[0] // rows, wide // group
    mine = lax.div(me, group)
    block = group * room
    width = heads * HEAD_DIM
    half = columns.shape[1]
    capacity = tokens.shape[0] // experts
    row_at, gate_at, home_at, back_at, up_at = 0, wide, 2 * wide, 3 * wide, 4 * wide
    grad_at, share_at, join_at = 5 * wide, 5 * wide + groups, 5 * wide + 2 * groups
    context_at = 5 * wide + 3 * groups
    partial_at, last_at = context_at + chunks, context_at + 2 * chunks
    other_at = last_at + 2

    def rows_of(index):
        return pl.ds(pl.multiple_of(index * room, 16), room)

    def rows_of_group(index):
        return pl.ds(pl.multiple_of(index * block, 16), block)

    def chunk_of(index):
        return pl.ds(pl.multiple_of(index * rows, 16), rows)

    def load_tokens(c):
        return pltpu.make_async_copy(tokens_h.at[chunk_of(c)], tokens.at[chunk_of(c)], chunk_sems.at[c])

    def start_tokens(c, carry):
        load_tokens(c).start()
        return carry

    loads = [
        pltpu.make_async_copy(source, target, load_sems.at[i])
        for i, (source, target) in enumerate(
            [(weight_qkv_h, weight_qkv), (projection_h, projection), (hidden_h, hidden), (output_h, output),
             (cotangent_h, cotangent), (weight_in_h, weight_in), (weight_out_h, weight_out)]
        )
    ]
    loads[0].start()
    lax.fori_loop(0, chunks, start_tokens, 0)
    for load in loads[1:]:
        load.start()

    def store(kind, source, target, c):
        return pltpu.make_async_copy(source.at[chunk_of(c)], target.at[chunk_of(c)], store_sems.at[kind, c])

    stores = [(qkv, qkv_h), (context, context_h), (first, first_h), (second, second_h), (info, info_h), (fed, fed_h), (slopes_kept, slope_h),
              (lowered_mid, lowered_h)]
    greet(wide)

    def move(source, target, base, sent, landed, device):
        return pltpu.make_async_remote_copy(
            source, target, sems.at[0, base + sent], sems.at[1, base + landed], device_id=device, device_id_type=MESH
        )

    def across_chunk(source, target, base, index):
        there = chunk_of(index)
        return move(source.at[there], target.at[there], base, index, index, (me, 1 - plane))

    def up_copy(other, sender):
        return move(raised_placed.at[rows_of(other)], upstream.at[rows_of(sender)], up_at, other, sender, (other, plane))

    weights = move(projection_h, projection_peer, last_at, 0, 0, (me, 1 - plane))
    weights.start()
    first_plane = plane == 0
    table[...] = jnp.zeros_like(table)
    in_bias_grad[...] = jnp.zeros_like(in_bias_grad)
    out_bias_grad[...] = jnp.zeros_like(out_bias_grad)

    def attend_chunk(c):
        there = chunk_of(c)
        load_tokens(c).wait()
        normed, _ = normalized(tokens[there, :].astype(F32))
        lowered = (normed * pre_gain[...] + pre_shift[...]).astype(BF16)
        parts = [dot(lowered, weight_qkv[s]) for s in range(3)]
        parts = [parts[0] + qv_bias[0:1, :], parts[1], parts[2] + qv_bias[1:2, :]]
        value = jnp.concatenate(parts, axis=1).astype(BF16)
        qkv[there, :] = value
        contexts = [
            image_forward(heads, value[image * PATCHES : (image + 1) * PATCHES]) for image in range(rows // PATCHES)
        ]
        context[there, :] = jnp.concatenate(contexts, axis=0)
        across_chunk(context, context_peer, context_at, c).start()
        store(0, qkv, qkv_h, c).start()
        store(1, context, context_h, c).start()

    def find_slots():
        by_row, choices = count_slots(ids[...], priority[...], experts, capacity, room)
        targets[0:2, :] = by_row
        info[:, experts : experts + 6] = choices.astype(F32)

    def raise_group(k):
        q = lax.rem(mine + k, groups)
        hits = slot_hits(q * block, block, targets)
        raised_placed[rows_of_group(q), :] = dot(hits, cotangent[...].astype(BF16)).astype(BF16)
        for j in range(group):
            e = q * group + j

            @pl.when(e != me)
            def _(e=e):
                up_copy(e, me).start()

            @pl.when(e == me)
            def _(e=e):
                upstream[rows_of(e), :] = raised_placed[rows_of(e), :]

    def feed_chunk(c):
        there = chunk_of(c)
        across_chunk(context, context_peer, context_at, c).wait()
        branch = dot(context[there, :], projection[...]) + dot(context_peer[there, :], projection_peer[...])
        value = tokens[there, :].astype(F32) + branch + proj_bias[...]
        first[there, :] = value
        normed, _ = normalized(value)
        lowered = (normed * mid_gain[...] + mid_shift[...]).astype(BF16)
        activated, slope = gelu_parts(dot(lowered, hidden[...]) + hidden_bias[...])
        activated = activated.astype(BF16)
        partial_own[there, :] = dot(activated, output[...]).astype(BF16)
        across_chunk(partial_own, partial_peer, partial_at, c).start()
        fed[there, :] = activated
        slopes_kept[there, :] = slope.astype(BF16)
        lowered_mid[there, :] = lowered
        for kind in (5, 6, 7):
            store(kind, *stores[kind], c).start()
        store(2, first, first_h, c).start()

    def route_chunk(c):
        there = chunk_of(c)
        across_chunk(partial_own, partial_peer, partial_at, c).wait()
        partial = partial_own[there, :].astype(F32) + partial_peer[there, :].astype(F32)
        value = first[there, :] + partial + output_bias[...]
        second[there, :] = value
        normed, _ = normalized(value)
        normed = normed * moe_gain[...] + moe_shift[...]
        columns[there, :] = jnp.where(first_plane, normed[:, :half], normed[:, half:]).astype(BF16)
        other_columns[there, :] = jnp.where(first_plane, normed[:, half:], normed[:, :half]).astype(BF16)
        logits = lax.dot_general(
            normed, router[...], (((1,), (1,)), ((), ())), precision=HIGHEST, preferred_element_type=F32
        )
        grown = jnp.exp(logits - jnp.max(logits, axis=-1, keepdims=True))
        route = grown / jnp.sum(grown, axis=-1, keepdims=True)
        info[there, 0:experts] = route
        number = lax.broadcasted_iota(jnp.int32, route.shape, 1)
        picks = info[there, experts : experts + 6].astype(jnp.int32)
        for j, spot in enumerate(spots(picks[:, 4:6])):
            table[...] += dot_columns(jnp.where(number == picks[:, 2 + j : 3 + j], route, 0.0), spot, HIGHEST)
        store(3, second, second_h, c).start()
        store(4, info, info_h, c).start()

    def turn(c, carry):
        @pl.when(c < chunks)
        def _():
            attend_chunk(c)

        @pl.when(c == 0)
        def _():
            loads[4].wait()
            find_slots()

        @pl.when(c < chunks)
        def _():
            for part in range(groups // chunks):
                raise_group(c * (groups // chunks) + part)

        @pl.when(c == 1)
        def _():
            weights.wait()
            for load in loads[1:4]:
                load.wait()

        @pl.when((c >= 1) & (c <= chunks))
        def _():
            feed_chunk(c - 1)

        @pl.when(c >= 2)
        def _():
            route_chunk(c - 2)

        return carry

    info[...] = jnp.zeros_like(info)
    loads[0].wait()
    lax.fori_loop(0, chunks + 2, turn, 0)

    def row_copy(other, sender):
        return move(placed.at[rows_of(other)], rows_own.at[rows_of(sender)], row_at, other, sender, (other, plane))

    def other_copy(other, sender):
        return move(other_placed.at[rows_of(other)], rows_peer.at[rows_of(sender)], other_at, other, sender, (other, plane))

    near_groups = groups // 2
    sides = groups // 4

    def turned(k, sign):
        turn, side = lax.div(k, sides), lax.rem(mine + k, sides)
        place = lax.div(mine, sides)
        pair = lax.rem(lax.div(place, 2) + sign * lax.div(turn, 2) + 2, 2)
        return sides * (2 * pair + lax.rem(place + turn, 2)) + side, k < near_groups

    def gate_copy(other, sender):
        return move(gate_sent.at[other], gate_arrived.at[sender], gate_at, other, sender, (other, plane))

    def home_copy(other, sender):
        return move(grad_back.at[rows_of(other)], own_home.at[rows_of(sender)], home_at, other, sender, (other, plane))

    def back_copy(other, sender):
        return move(gate_back.at[other], gate_own.at[sender], back_at, other, sender, (other, plane))

    def across(source, target, base, index):
        there = rows_of_group(index)
        return move(source.at[there], target.at[there], base, index, index, (me, 1 - plane))

    own_half = pl.ds(pl.multiple_of(plane * half, 16), half)
    peer_half = pl.ds(pl.multiple_of((1 - plane) * half, 16), half)
    for e in range(wide):
        gate_sent[e] = jnp.broadcast_to(table[e : e + 1, :], gate_sent.shape[1:])

    def place_group(k, carry):
        q, near = turned(k, 1)
        hits = slot_hits(q * block, block, targets)
        placed[rows_of_group(q), :] = dot(hits, columns[...]).astype(BF16)

        @pl.when(near)
        def _():
            other_placed[rows_of_group(q), :] = dot(hits, other_columns[...]).astype(BF16)

        for j in range(group):
            e = q * group + j

            @pl.when(e != me)
            def _(e=e):
                row_copy(e, me).start()
                gate_copy(e, me).start()

            @pl.when((e != me) & near)
            def _(e=e):
                other_copy(e, me).start()

            @pl.when(e == me)
            def _(e=e):
                rows_own[rows_of(e), :] = placed[rows_of(e), :]
                rows_peer[rows_of(e), :] = other_placed[rows_of(e), :]
                gate_arrived[e] = gate_sent[e]

        return carry

    lax.fori_loop(0, groups, place_group, 0)
    loads[5].wait()
    loads[6].wait()
    diagonal = lax.broadcasted_iota(jnp.int32, (room, 128), 0) == lax.broadcasted_iota(jnp.int32, (room, 128), 1)

    def store_result(p):
        there = rows_of_group(p)
        return pltpu.make_async_copy(result.at[there], result_h.at[there], group_sems.at[p])

    def join_group(k):
        p, near = turned(k, -1)
        for j in range(group):
            w = p * group + j

            @pl.when(w != me)
            def _(w=w):
                row_copy(w, w).wait_recv()
                gate_copy(w, w).wait_recv()

        @pl.when(jnp.logical_not(near))
        def _():
            across(rows_own, rows_peer, join_at, p).start()

        for j in range(group):
            w = p * group + j

            @pl.when((w != me) & near)
            def _(w=w):
                other_copy(w, w).wait_recv()

            @pl.when(w != me)
            def _(w=w):
                up_copy(w, w).wait_recv()

    def expert_group(k):
        p, near = turned(k, -1)
        there = rows_of_group(p)

        @pl.when(jnp.logical_not(near))
        def _():
            across(rows_own, rows_peer, join_at, p).wait()

        gates = jnp.concatenate(
            [
                jnp.sum(jnp.where(diagonal, gate_arrived[p * group + j][0:1, :], 0.0), axis=1, keepdims=True)
                for j in range(group)
            ],
            axis=0,
        )
        inner = dot(rows_own[there, :], weight_in[own_half, :]) + dot(rows_peer[there, :], weight_in[peer_half, :])
        acted, slope = gelu_parts(inner + bias_in[...])
        acted = acted.astype(BF16)
        act[there, :] = acted
        raised = upstream[there, :].astype(F32)
        slot = (raised * gates).astype(BF16)
        slot_grad[there, :] = slot
        inward = (dot_rows(slot, weight_out[...]) * slope).astype(BF16)
        inner_grad[there, :] = inward
        grad_sent[there, :] = dot_rows(inward, weight_in[peer_half, :]).astype(BF16)
        across(grad_sent, grad_landed, grad_at, p).start()
        grad_kept[there, :] = dot_rows(inward, weight_in[own_half, :])

    def result_group(k, carry):
        p, _ = turned(k, -1)
        there = rows_of_group(p)
        value = dot(act[there, :], weight_out[...]) + bias_out[...] * jnp.where(first_plane, 1.0, 0.0)
        result[there, :] = value.astype(BF16)
        store_result(p).start()
        out_bias_grad[0:1, :] += jnp.sum(slot_grad[there, :].astype(F32), axis=0, keepdims=True)
        in_bias_grad[0:1, :] += jnp.sum(inner_grad[there, :].astype(F32), axis=0, keepdims=True)
        slopes = jnp.sum(upstream[there, :].astype(F32) * value, axis=1, keepdims=True)
        for j in range(group):
            w = p * group + j
            row = jnp.sum(
                jnp.where(diagonal, slopes[j * room : (j + 1) * room], 0.0), axis=0, keepdims=True
            )
            gate_back[w] = jnp.broadcast_to(row, gate_back.shape[1:])

            @pl.when(w != me)
            def _(w=w):
                back_copy(w, me).start()

            @pl.when(w == me)
            def _(w=w):
                gate_own[w] = gate_back[w]

        return carry

    own_rows = pltpu.make_async_copy(grad_back.at[rows_of(me)], own_home.at[rows_of(me)], group_sems.at[groups])

    def give_back(k):
        p, _ = turned(k, -1)
        across(grad_sent, grad_landed, grad_at, p).wait()
        there = rows_of_group(p)
        grad_back[there, :] = (grad_kept[there, :] + grad_landed[there, :].astype(F32)).astype(BF16)
        for j in range(group):
            w = p * group + j

            @pl.when(w != me)
            def _(w=w):
                home_copy(w, me).start()

            @pl.when(w == me)
            def _(w=w):
                own_rows.start()

    def share_group(k, carry):
        q, _ = turned(k, 1)
        for j in range(group):
            e = q * group + j

            @pl.when(e != me)
            def _(e=e):
                home_copy(e, e).wait_recv()

            @pl.when(e == me)
            def _():
                own_rows.wait()

        across(own_home, peer_home, share_at, q).start()
        return carry

    def expert_turn(s, carry):
        @pl.when(s < groups)
        def _():
            join_group(s)

        @pl.when(s < near_groups)
        def _():
            expert_group(s)

        @pl.when((s > near_groups) & (s <= groups))
        def _():
            expert_group(s - 1)

        @pl.when((s >= 1) & (s <= near_groups))
        def _():
            give_back(s - 1)

        @pl.when(s >= near_groups + 2)
        def _():
            give_back(s - 2)
            share_group(s - near_groups - 2, 0)

        return carry

    lax.fori_loop(0, groups + 2, expert_turn, 0)
    lax.fori_loop(0, groups, result_group, 0)
    lax.fori_loop(near_groups, groups, share_group, 0)

    def put_out(at, tile, value):
        out_grad[pl.ds(at, tile), :] = value.astype(BF16)

    column_dots(act, slot_grad, put_out)
    out_store = pltpu.make_async_copy(out_grad, out_grad_h, load_sems.at[7])
    out_store.start()

    def take_gates(d, carry):
        other = lax.rem(me + d, wide)
        back_copy(other, other).wait_recv()
        return carry

    lax.fori_loop(1, wide, take_gates, 0)
    tables = move(gate_own, gate_peer, last_at, 1, 1, (me, 1 - plane))
    tables.start()
    in_grad[own_half, :] = dot_columns(rows_own[...], inner_grad[...]).astype(BF16)
    in_grad[peer_half, :] = dot_columns(rows_peer[...], inner_grad[...]).astype(BF16)
    in_store = pltpu.make_async_copy(in_grad, in_grad_h, load_sems.at[8])
    in_store.start()

    def end_sends(d, carry):
        other = lax.rem(me + d, wide)
        up_copy(other, me).wait_send()
        row_copy(other, me).wait_send()
        gate_copy(other, me).wait_send()
        home_copy(other, me).wait_send()
        back_copy(other, me).wait_send()
        return carry

    lax.fori_loop(1, wide, end_sends, 0)

    def end_others(k, carry):
        q, _ = turned(k, 1)
        for j in range(group):
            e = q * group + j

            @pl.when(e != me)
            def _(e=e):
                other_copy(e, me).wait_send()

        return carry

    lax.fori_loop(0, near_groups, end_others, 0)

    def end_stores(c, carry):
        for kind, (source, target) in enumerate(stores):
            store(kind, source, target, c).wait()
        return carry

    lax.fori_loop(0, chunks, end_stores, 0)
    tables.wait()
    for e in range(wide):
        gate_home[e : e + 1, :] = gate_own[e][0:1, :] + gate_peer[e][0:1, :]

    def end_groups(q, carry):
        store_result(q).wait()
        across(own_home, peer_home, share_at, q).wait()
        return carry

    lax.fori_loop(0, groups, end_groups, 0)
    out_store.wait()
    in_store.wait()


def backward(
    wide, room, heads, layout, orders, rows,
    second_h, cotangent_h, info_h, first_h, tokens_h, qkv_h, context_h, hidden_h, output_h, projection_h, weight_qkv_h,
    row_own_h, row_peer_h, act_h, slope_h, lowered_h, result,
    moe_gain, moe_shift, router, gate_grads, mid_gain, pre_gain, pre_shift,
    block_h, grad_h, hidden_out_h, output_out_h, qkv_out_h, proj_out_h, *rest,
):
    vectors_out, pre_out, rest = rest[: len(layout)], rest[len(layout)], rest[len(layout) + 1 :]
    (second, cotangent, info, first, tokens, qkv, context, hidden, output, projection, weight_qkv, row_own, row_peer,
     act, slopes, lowered_mid, block_out, grad_out, hidden_out, output_out, qkv_out, proj_out), rest = rest[:22], rest[22:]
    load_sems, chunk_sems, store_sems, rest = rest[-3], rest[-2], rest[-1], rest[:-3]
    (inner_grad, mid_own, mid_peer, branch, qkv_grad, lowered_pre, pre_peer, result_own, blend_peer,
     pre_tile, pre_tiles, pre_total, pre_other, moe_sums, router_sums, mid_sums, hidden_sums, qkv_sums, pre_sums, small_sums) = rest[:20]
    hidden_total, output_total, qkv_total, proj_total, small = rest[20:25]
    sends, lands = rest[25:31], rest[31:37]
    mid_sems, pre_sems, blend_sems, result_sems, send_sems, recv_sems = rest[37:]
    blend_own = lowered_mid
    me, plane = lax.axis_index("wide"), lax.axis_index("tensor")
    chunks = tokens.shape[0] // rows
    model = tokens.shape[1]
    width = heads * HEAD_DIM
    split = qkv_total.shape[0] // 2
    totals = (
        hidden_total, output_total, qkv_total.at[pl.ds(0, split)], qkv_total.at[pl.ds(split, split)], proj_total, small
    )
    gathers = (
        hidden_out, output_out, qkv_out.at[pl.ds(0, split)], qkv_out.at[pl.ds(split, split)], proj_out, small_sums
    )

    def chunk_of(index):
        return pl.ds(pl.multiple_of(index * rows, 16), rows)

    early = [(info_h, info), (second_h, second), (cotangent_h, cotangent), (slope_h, slopes)]
    late = [(tokens_h, tokens), (qkv_h, qkv), (first_h, first)]
    middle = [(lowered_h, lowered_mid), (act_h, act)]

    def load(kind, pair, c):
        return pltpu.make_async_copy(pair[0].at[chunk_of(c)], pair[1].at[chunk_of(c)], chunk_sems.at[kind, c])

    def start_early(c, carry):
        for kind, pair in enumerate(early):
            load(kind, pair, c).start()
        return carry

    def start_late(c, carry):
        for kind, pair in enumerate(late):
            load(len(early) + kind, pair, c).start()
        return carry

    middle_loads = [
        pltpu.make_async_copy(source, target, load_sems.at[12 + i]) for i, (source, target) in enumerate(middle)
    ]
    loads = [
        pltpu.make_async_copy(source, target, load_sems.at[i])
        for i, (source, target) in enumerate(
            [(row_own_h, row_own), (row_peer_h, row_peer), (hidden_h, hidden), (output_h, output),
             (projection_h, projection), (weight_qkv_h, weight_qkv), (context_h, context)]
        )
    ]
    for part in loads[:2]:
        part.start()
    start_early(0, 0)
    for part in loads[2:4]:
        part.start()
    lax.fori_loop(1, chunks, start_early, 0)
    for part in loads[4:]:
        part.start()
    for part in middle_loads:
        part.start()
    lax.fori_loop(0, chunks, start_late, 0)
    whole_stores = [
        pltpu.make_async_copy(source, target, load_sems.at[len(loads) + i])
        for i, (source, target) in enumerate(
            [(hidden_out, hidden_out_h), (output_out, output_out_h), (qkv_out, qkv_out_h), (proj_out, proj_out_h)]
        )
    ]

    def store(kind, source, target, c):
        return pltpu.make_async_copy(source.at[chunk_of(c)], target.at[chunk_of(c)], store_sems.at[kind, c])

    greet(wide)
    sums = Sums(wide, orders, totals, sends, lands, gathers, send_sems, recv_sems)

    def rows_of(index):
        return pl.ds(pl.multiple_of(index * room, 16), room)

    def result_copy(other, sender):
        return pltpu.make_async_remote_copy(
            result.at[rows_of(other)], result_own.at[rows_of(sender)], result_sems.at[0, other],
            result_sems.at[1, sender], device_id=(other, plane), device_id_type=MESH,
        )

    def send_result(d, carry):
        result_copy(lax.rem(me + d, wide), me).start()
        return carry

    lax.fori_loop(1, wide, send_result, 0)
    own_rows = pltpu.make_async_copy(
        result.at[rows_of(me)], result_own.at[rows_of(me)], load_sems.at[len(loads) + len(whole_stores)]
    )
    own_rows.start()

    def across(own, peer, sems, chunk):
        at = pl.multiple_of(chunk * rows, rows)
        return pltpu.make_async_remote_copy(
            own.at[pl.ds(at, rows)], peer.at[pl.ds(at, rows)], sems.at[0, chunk], sems.at[1, chunk],
            device_id=(me, 1 - plane), device_id_type=MESH,
        )

    for vector in (moe_sums, router_sums, mid_sums, hidden_sums, qkv_sums, pre_sums):
        vector[...] = jnp.zeros_like(vector)
    first_plane = plane == 0

    def ordered(own, peer):
        return jnp.concatenate([jnp.where(first_plane, own, peer), jnp.where(first_plane, peer, own)], axis=1)

    def settle(here):
        experts = router.shape[0]
        picks = info[here, experts : experts + 6].astype(jnp.int32)
        hits = token_hits(picks, row_own.shape[0])
        table = (hits[0] | hits[1]).astype(BF16)
        moe_grad = ordered(dot(table, row_own[...]), dot(table, row_peer[...]))
        chances = info[here, 0:experts]
        number = lax.broadcasted_iota(jnp.int32, chances.shape, 1)
        route_grad = jnp.zeros_like(chances)
        for j, spot in enumerate(spots(picks[:, 4:6])):
            at_place = dot_rows(spot.astype(BF16), gate_grads[...].astype(BF16))
            route_grad = route_grad + jnp.where(number == picks[:, 2 + j : 3 + j], at_place, 0.0)
        logit_grad = chances * (route_grad - jnp.sum(chances * route_grad, axis=1, keepdims=True))
        normed, scale = normalized(second[here, :])
        logit_grad = logit_grad.astype(BF16)
        router_sums[...] += dot_columns(logit_grad, (normed * moe_gain[...] + moe_shift[...]).astype(BF16))
        moe_grad = moe_grad + dot(logit_grad, router[...].astype(BF16))
        grad = cotangent[here, :] + norm_back(normed, scale, moe_gain[...], moe_grad)
        grad_out[here, :] = grad
        branch[here, :] = grad.astype(BF16)
        moe_sums[0:1, :] += jnp.sum(moe_grad * normed, axis=0, keepdims=True)
        moe_sums[1:2, :] += jnp.sum(moe_grad, axis=0, keepdims=True)
        moe_sums[2:3, :] += jnp.sum(grad, axis=0, keepdims=True)

    def feed_chunk(chunk, carry):
        here = chunk_of(chunk)
        for kind, pair in enumerate(early):
            load(kind, pair, chunk).wait()
        settle(here)

        @pl.when(chunk == 0)
        def _():
            loads[2].wait()
            loads[3].wait()

        inward = (dot_rows(branch[here, :], output[...]) * slopes[here, :].astype(F32)).astype(BF16)
        inner_grad[here, :] = inward
        hidden_sums[0:1, :] += jnp.sum(inward.astype(F32), axis=0, keepdims=True)
        mid_own[here, :] = dot_rows(inward, hidden[...]).astype(BF16)
        across(mid_own, mid_peer, mid_sems, chunk).start()
        return carry

    loads[0].wait()
    loads[1].wait()
    lax.fori_loop(0, chunks, feed_chunk, 0)

    def put_in(total):
        def put(at, tile, value):
            total[pl.ds(at, tile), :] = value

        return put

    for part in middle_loads:
        part.wait()
    column_dots(lowered_mid, inner_grad, put_in(hidden_total))
    sums.begin(0, 0)
    column_dots(act, branch, put_in(output_total))
    sums.begin(1, 0)

    images = rows // PATCHES
    taken = ((3, 7), (3, 7))

    def attend_chunk(chunk, carry):
        here = pl.ds(pl.multiple_of(chunk * rows, rows), rows)
        for kind, pair in enumerate(late):
            load(len(early) + kind, pair, chunk).wait()
        across(mid_own, mid_peer, mid_sems, chunk).wait()
        mid_grad = mid_own[here, :].astype(F32) + mid_peer[here, :].astype(F32)
        normed, scale = normalized(first[here, :])
        first_grad = grad_out[here, :] + norm_back(normed, scale, mid_gain[...], mid_grad)
        grad_out[here, :] = first_grad
        lowered_grad = first_grad.astype(BF16)
        branch[here, :] = lowered_grad
        mid_sums[0:1, :] += jnp.sum(mid_grad * normed, axis=0, keepdims=True)
        mid_sums[1:2, :] += jnp.sum(mid_grad, axis=0, keepdims=True)
        mid_sums[2:3, :] += jnp.sum(first_grad, axis=0, keepdims=True)
        normed, _ = normalized(tokens[here, :].astype(F32))
        lowered_pre[here, :] = (normed * pre_gain[...] + pre_shift[...]).astype(BF16)
        context_grad = dot_rows(lowered_grad, projection[...]).astype(BF16)
        for image in range(rows // PATCHES):
            at = pl.multiple_of(chunk * rows + image * PATCHES, PATCHES)
            block = qkv[pl.ds(at, PATCHES), :]
            grad = image_back(heads, block, context_grad[image * PATCHES : (image + 1) * PATCHES])
            qkv_grad[pl.ds(at, PATCHES), :] = grad
            pre = sum(dot_rows(grad[:, s * width : (s + 1) * width], weight_qkv[s]) for s in range(3))
            pre = pre.astype(BF16)
            mid_own[pl.ds(at, PATCHES), :] = pre
            pre = pre.astype(F32)
            pre_sums[0:1, :] += jnp.sum(pre * normed[image * PATCHES : (image + 1) * PATCHES], axis=0, keepdims=True)
            pre_sums[1:2, :] += jnp.sum(pre, axis=0, keepdims=True)
            qkv_sums[0:1, :] += jnp.sum(grad.astype(F32), axis=0, keepdims=True)
            for i, steps in enumerate(taken):
                for k, boundary in enumerate(steps):
                    if boundary % images == image:

                        @pl.when(chunk == boundary // images)
                        def _(i=i, k=k):
                            sums.advance(i, k)

        across(mid_own, pre_peer, pre_sems, chunk).start()
        return carry

    loads[4].wait()
    loads[5].wait()
    lax.fori_loop(0, chunks, attend_chunk, 0)
    loads[6].wait()

    put_row(pre_tile, put_row(pre_tile, 0, pre_sums[0:1, :]), pre_sums[1:2, :])

    def pre_copy(other, sender):
        return pltpu.make_async_remote_copy(
            pre_tile, pre_tiles.at[sender], result_sems.at[0, wide + other], result_sems.at[1, wide + sender],
            device_id=(other, plane), device_id_type=MESH,
        )

    def send_pre(d, carry):
        pre_copy(lax.rem(me + d, wide), me).start()
        return carry

    lax.fori_loop(1, wide, send_pre, 0)
    pre_tiles[me] = pre_tile[...]

    def put_thirds(at, tile, value):
        for s in range(3):
            there = pl.ds(pl.multiple_of(s * model + at, 16), tile)
            qkv_total[there, :] = value[:, s * width : (s + 1) * width]

    column_dots(lowered_pre, qkv_grad, put_thirds)
    sums.begin(2, 0)
    sums.begin(3, 0)
    column_dots(context, branch, put_in(proj_total))
    sums.begin(4, 0)
    small[...] = jnp.zeros_like(small)
    at = 0
    for vector, picked in zip((mid_sums, moe_sums, hidden_sums, qkv_sums, router_sums), layout):
        for r in picked:
            at = put_row(small, at, vector[r : r + 1, :])
    sums.begin(5, 0)

    def finish_chunk(chunk, carry):
        here = pl.ds(pl.multiple_of(chunk * rows, rows), rows)
        across(mid_own, pre_peer, pre_sems, chunk).wait()
        upstream = mid_own[here, :].astype(F32) + pre_peer[here, :].astype(F32)
        normed, scale = normalized(tokens[here, :].astype(F32))
        grad_out[here, :] += norm_back(normed, scale, pre_gain[...], upstream)
        store(0, grad_out, grad_h, chunk).start()
        return carry

    def take_result(d, carry):
        other = lax.rem(me + d, wide)
        result_copy(other, other).wait_recv()
        result_copy(other, me).wait_send()
        return carry

    lax.fori_loop(1, wide, take_result, 0)
    own_rows.wait()

    def blend(chunk, carry):
        here = pl.ds(pl.multiple_of(chunk * rows, rows), rows)
        experts = router.shape[0]
        picks, chances = info[here, experts : experts + 6].astype(jnp.int32), info[here, 0:experts]
        number = lax.broadcasted_iota(jnp.int32, chances.shape, 1)
        gates = [
            jnp.sum(jnp.where(number == picks[:, 2 + j : 3 + j], chances, 0.0), axis=1, keepdims=True)
            for j in range(2)
        ]
        hits = token_hits(picks, result_own.shape[0])
        table = jnp.where(hits[0], gates[0], jnp.where(hits[1], gates[1], 0.0)).astype(BF16)
        blend_own[here, :] = dot(table, result_own[...]).astype(BF16)
        across(blend_own, blend_peer, blend_sems, chunk).start()
        return carry

    def blend_end(chunk, carry):
        here = pl.ds(pl.multiple_of(chunk * rows, rows), rows)
        across(blend_own, blend_peer, blend_sems, chunk).wait()
        mixture = blend_own[here, :].astype(F32) + blend_peer[here, :].astype(F32)
        block_out[here, :] = (second[here, :] + mixture).astype(BF16)
        store(1, block_out, block_h, chunk).start()
        return carry

    def take_pre(d, carry):
        other = lax.rem(me + d, wide)
        pre_copy(other, other).wait_recv()
        pre_copy(other, me).wait_send()
        return carry

    pre_share = pltpu.make_async_remote_copy(
        pre_total, pre_other, result_sems.at[0, 2 * wide], result_sems.at[1, 2 * wide],
        device_id=(me, 1 - plane), device_id_type=MESH,
    )
    ends = (1, 3, 5, 7)
    for k in range(2 * sums.steps):
        for i in (0, 1):
            if len(taken[i]) + k < 2 * sums.steps:
                sums.advance(i, len(taken[i]) + k)
        for i in (5, 4, 2, 3):
            sums.advance(i, k)
        if k < chunks:
            blend(k, 0)
        if k in ends:
            finish_chunk(ends.index(k), 0)
        if k == sums.steps - 1:
            lax.fori_loop(1, wide, take_pre, 0)
            pre_total[...] = sum(pre_tiles[w] for w in range(wide))
            pre_share.start()
    for part in whole_stores:
        part.start()
    lax.fori_loop(0, chunks, blend_end, 0)
    pre_share.wait()
    pre_tile[...] = pre_total[...] + pre_other[...]
    pre_out[0:1, :] = get_row(pre_tile, 0, model)
    pre_out[1:2, :] = get_row(pre_tile, model // 128, model)
    at = 0
    for out, picked in zip(vectors_out, layout):
        for i in range(len(picked)):
            out[i : i + 1, :] = get_row(small_sums, at, out.shape[1]).astype(F32)
            at += out.shape[1] // 128

    def end_stores(c, carry):
        store(0, grad_out, grad_h, c).wait()
        store(1, block_out, block_h, c).wait()
        return carry

    lax.fori_loop(0, chunks, end_stores, 0)
    for part in whole_stores:
        part.wait()


def widen(pairs, layout, *refs):
    ins, outs = refs[: pairs + len(layout)], refs[pairs + len(layout) :]
    for source, out in zip(ins[:pairs], outs[:pairs]):
        out[...] = source[...].astype(out.dtype)
    outs = iter(outs[pairs:])
    for source, picked in zip(ins[pairs:], layout):
        for r in picked:
            out = next(outs)
            if out.shape[0] == 2:
                out[0:1, :] = source[0:1, : out.shape[1]]
                out[1:2, :] = source[0:1, 2 * out.shape[1] :]
            else:
                out[...] = source[r : r + out.shape[0], : out.shape[1]]


def shards(
    wide,
    tokens_in, pre_gain, pre_shift, qkv_weight, qv_bias, proj_weight, proj_bias, mid_gain, mid_shift,
    hidden_weight, hidden_bias, output_weight, output_bias, moe_gain, moe_shift, router_weight,
    expert_in, expert_in_bias, expert_out, expert_out_bias, expert_ids, priority, cotangent,
):
    tokens, model = tokens_in.shape
    width = qkv_weight.shape[2]
    heads = width // HEAD_DIM
    hidden = hidden_weight.shape[1]
    count = router_weight.shape[1]
    capacity = tokens // count
    room = -(-capacity // 16) * 16
    slots = count * room
    half = model // 2
    lanes = 3 * width
    rows = 2 * PATCHES
    chunks = tokens // rows
    group = 2
    steps = wide.bit_length() - 1

    def row(vector):
        return vector.reshape(1, -1)

    def remote(kernel, name, identity, far_ins, ins, far_outs, outs, scratch):
        far, near = pl.BlockSpec(memory_space=pl.ANY), pl.BlockSpec(memory_space=pltpu.VMEM)
        return pl.pallas_call(
            kernel,
            out_shape=[jax.ShapeDtypeStruct(shape, dtype) for shape, dtype in far_outs + outs],
            in_specs=[far] * len(far_ins) + [near] * len(ins),
            out_specs=[far] * len(far_outs) + [near] * len(outs),
            scratch_shapes=scratch,
            compiler_params=pltpu.CompilerParams(
                vmem_limit_bytes=VMEM_BYTES, collective_id=identity, has_side_effects=True
            ),
            name=name,
        )(*far_ins, *ins)

    def room_for(local):
        return [pltpu.VMEM(shape, dtype) for shape, dtype in local]

    pre_gain, pre_shift, proj_bias = row(pre_gain), row(pre_shift), row(proj_bias)
    mid_gain, mid_shift, hidden_bias = row(mid_gain), row(mid_shift), row(hidden_bias)
    output_bias, moe_gain, moe_shift = row(output_bias), row(moe_gain), row(moe_shift)
    weight_qkv = qkv_weight.transpose(1, 0, 2)
    router = router_weight.T
    groups = wide // group
    kept = [
        ((tokens, lanes), BF16), ((tokens, width), BF16), ((tokens, model), F32), ((tokens, model), F32),
        ((tokens, 128), F32), ((slots, model), BF16), ((model, hidden), BF16), ((hidden, model), BF16),
        ((tokens, hidden), BF16), ((tokens, hidden), BF16), ((tokens, model), BF16),
    ]
    homes = [((slots, half), BF16), ((slots, half), BF16)]
    fetched = [tokens_in, cotangent, weight_qkv, proj_weight, hidden_weight, output_weight, expert_in[0], expert_out[0]]
    tables = [((count, 8, 128), F32)] * 5
    (qkv, context, first, second, info, result, in_grad, out_grad, fed, slopes, lowered, row_own, row_peer, gate_grads,
     in_bias, out_bias) = remote(
        functools.partial(front, wide, room, group, heads, rows, count), "front", 1,
        fetched,
        [expert_ids.T, priority, pre_gain, pre_shift, qv_bias, proj_bias, mid_gain, mid_shift, hidden_bias, output_bias,
         moe_gain, moe_shift, router, expert_in_bias, expert_out_bias],
        kept + homes,
        [((count, 128), F32), ((8, hidden), F32), ((8, model), F32)],
        room_for([(array.shape, array.dtype) for array in fetched] + kept
                 + [((8, tokens), jnp.int32), ((count, 128), F32), ((slots, model), BF16), ((slots, model), BF16),
                    ((width, model), BF16), ((tokens, width), BF16), ((tokens, model), BF16), ((tokens, model), BF16),
                    ((tokens, half), BF16), ((tokens, half), BF16), ((slots, half), BF16), ((slots, half), BF16),
                    ((slots, half), BF16), ((slots, half), BF16),
                    ((slots, hidden), BF16), ((slots, hidden), BF16), ((slots, model), BF16), ((slots, half), F32),
                    ((slots, half), BF16), ((slots, half), BF16), ((slots, half), BF16)] + tables)
        + [pltpu.SemaphoreType.DMA((2, 6 * wide + 3 * groups + 2 * chunks + 2)), pltpu.SemaphoreType.DMA((9,)),
           pltpu.SemaphoreType.DMA((chunks,)), pltpu.SemaphoreType.DMA((8, chunks)), pltpu.SemaphoreType.DMA((groups + 1,))],
    )

    layout = [(0, 1, 2), (0, 1, 2), (0,), (0,), tuple(range(count))]
    vectors = [((8, model), F32), ((8, model), F32), ((8, hidden), F32), ((8, lanes), F32), ((count, model), F32)]
    near, far = tuple(range(steps)), (0,) + tuple(range(2, steps)) + (1,)
    summed = [(model, hidden), (hidden, model), (3 * model // 2, width), (3 * model // 2, width), (width, model), (16 * wide, 128)]
    fetched = [second, cotangent, info, first, tokens_in, qkv, context, hidden_weight, output_weight, proj_weight, weight_qkv, row_own, row_peer,
               fed, slopes, lowered]
    given = [
        ((tokens, model), BF16), ((tokens, model), F32), ((model, hidden), BF16), ((hidden, model), BF16),
        ((3 * model, width), BF16), ((width, model), BF16),
    ]
    tile = (2 * model // 128, 128)
    block_out, grad, hidden_g, output_g, qkv_g, proj_g, *sums = remote(
        functools.partial(backward, wide, room, heads, layout, (near, far, near, far, near, far), rows), "backward", 2,
        fetched + [result],
        [moe_gain, moe_shift, router, gate_grads, mid_gain, pre_gain, pre_shift],
        given, vectors + [((8, model), F32)],
        room_for([(array.shape, array.dtype) for array in fetched] + given
                 + [((tokens, hidden), BF16), ((tokens, model), BF16),
                    ((tokens, model), BF16), ((tokens, model), BF16), ((tokens, lanes), BF16), ((tokens, model), BF16),
                    ((tokens, model), BF16), ((slots, model), BF16), ((tokens, model), BF16),
                    (tile, F32), ((wide,) + tile, F32), (tile, F32), (tile, F32), ((8, model), F32), ((count, model), F32),
                    ((8, model), F32), ((8, hidden), F32), ((8, lanes), F32), ((8, model), F32), (summed[-1], BF16),
                    (summed[0], F32), (summed[1], F32), ((3 * model, width), F32), (summed[4], F32), (summed[5], F32)]
                 + [(shape, BF16) for shape in summed] * 2)
        + [pltpu.SemaphoreType.DMA((2, chunks))] * 3 + [pltpu.SemaphoreType.DMA((2, 2 * wide + 1))]
        + [pltpu.SemaphoreType.DMA((len(summed), 2 * steps))] * 2
        + [pltpu.SemaphoreType.DMA((14,)), pltpu.SemaphoreType.DMA((7, chunks)), pltpu.SemaphoreType.DMA((2, chunks))],
    )

    pairs = [
        (block_out, BF16), (grad, F32), (hidden_g, F32), (output_g, F32), (qkv_g.reshape(3, model, width), F32),
        (proj_g, F32), (in_grad, F32), (out_grad, F32),
    ]
    singles = [(0, 1), (0, 1, 2), (0, 1, 2), (0,), (0,), (0,), (0,), (0,)]
    sources = [sums[-1]] + list(sums[:-1]) + [in_bias, out_bias]
    sizes = [(1, model)] * 8 + [(1, hidden), (2, width), (count, model), (1, hidden), (1, model)]
    parts = 2

    def spec(shape):
        if len(shape) == 3:
            return pl.BlockSpec((shape[0], shape[1] // parts, shape[2]), lambda i: (0, i, 0))
        return pl.BlockSpec((shape[0] // parts, shape[1]), lambda i: (i, 0))

    def whole(shape):
        return pl.BlockSpec(shape, lambda i: (0, 0))

    outs = pl.pallas_call(
        functools.partial(widen, len(pairs), singles),
        grid=(parts,),
        in_specs=[spec(source.shape) for source, _ in pairs] + [whole(source.shape) for source in sources],
        out_specs=[spec(source.shape) for source, _ in pairs] + [whole(size) for size in sizes],
        out_shape=[jax.ShapeDtypeStruct(source.shape, dtype) for source, dtype in pairs]
        + [jax.ShapeDtypeStruct(size, F32) for size in sizes],
        compiler_params=pltpu.CompilerParams(vmem_limit_bytes=VMEM_BYTES),
        name="widen",
    )(*[source for source, _ in pairs], *sources)
    block_out, grad, hidden_g, output_g, qkv_g, proj_g, in_grad, out_grad = outs[:8]
    pre_gain_g, pre_shift_g, mid_gain_g, mid_shift_g, proj_bias_g, moe_gain_g, moe_shift_g, output_bias_g = (
        vector.reshape(model) for vector in outs[8:16]
    )
    hidden_bias_g, qkv_bias_g, router_g, in_bias_g, out_bias_g = outs[16:]
    return (
        block_out, grad, pre_gain_g, pre_shift_g, qkv_g.transpose(1, 0, 2),
        qkv_bias_g, proj_g, proj_bias_g, mid_gain_g,
        mid_shift_g, hidden_g, hidden_bias_g.reshape(hidden), output_g, output_bias_g, moe_gain_g, moe_shift_g,
        router_g.T, in_grad[None], in_bias_g, out_grad[None], out_bias_g,
    )


def layer_norm(values, gain, shift):
    centered = values - jnp.mean(values, axis=-1, keepdims=True)
    variance = jnp.mean(centered * centered, axis=-1, keepdims=True)
    return centered * lax.rsqrt(variance + 1e-06) * gain + shift


def norm_grad(values, gain, shift, upstream):
    _, pullback = jax.vjp(layer_norm, values, gain, shift)
    return pullback(upstream)


def gelu_grad(inner, upstream):
    _, pullback = jax.vjp(jax.nn.gelu, inner)
    return pullback(upstream)[0]


def slot_tables(choice_ids, ranks, capacity, experts):
    count = choice_ids.shape[0]
    order_keys = jnp.concatenate([ranks, ranks + count])
    flat_ids = jnp.concatenate([choice_ids[:, 0], choice_ids[:, 1]])
    earlier = (order_keys[None, :] < order_keys[:, None]) & (flat_ids[None, :] == flat_ids[:, None])
    position = jnp.sum(earlier.astype(jnp.int32), axis=1)
    kept = position < capacity
    position = position.reshape(2, count)
    kept = kept.reshape(2, count)
    columns = jnp.arange(experts * capacity, dtype=jnp.int32)
    target = choice_ids.T * capacity + position
    tables = (target[:, :, None] == columns[None, None, :]) & kept[:, :, None]
    return (tables, kept)


def plain(
    tokens_in,
    pre_gain,
    pre_shift,
    qkv_weight,
    qv_bias,
    proj_weight,
    proj_bias,
    mid_gain,
    mid_shift,
    hidden_weight,
    hidden_bias,
    output_weight,
    output_bias,
    moe_gain,
    moe_shift,
    router_weight,
    expert_in,
    expert_in_bias,
    expert_out,
    expert_out_bias,
    expert_ids,
    priority,
    cotangent,
):
    tokens = tokens_in.shape[0]
    model_width = tokens_in.shape[1]
    local_heads = qkv_weight.shape[2] // HEAD_DIM
    images = tokens // PATCHES
    experts = router_weight.shape[1]
    capacity = tokens // experts
    score_scale = float(HEAD_DIM) ** (-0.5)
    highest = lax.Precision.HIGHEST
    residual = tokens_in.astype(jnp.float32)
    normed_pre = layer_norm(residual, pre_gain, pre_shift)
    lowered_pre = normed_pre.astype(jnp.bfloat16)
    blank = jnp.zeros_like(qv_bias[0])
    qkv_shift = jnp.stack([qv_bias[0], blank, qv_bias[1]])
    qkv = (
        jnp.einsum("td,dsk->tsk", lowered_pre, qkv_weight, preferred_element_type=jnp.float32)
        + qkv_shift
    ).astype(jnp.bfloat16)
    grid = qkv.reshape(images, PATCHES, 3, local_heads, HEAD_DIM)
    query, keys, values = (grid[:, :, 0], grid[:, :, 1], grid[:, :, 2])
    scores = (
        jnp.einsum("bqhd,bkhd->bhqk", query, keys, preferred_element_type=jnp.float32) * score_scale
    )
    log_total = jax.nn.logsumexp(scores, axis=-1, keepdims=True)
    weights = jnp.exp(scores - log_total).astype(jnp.bfloat16)
    context = jnp.einsum("bhqk,bkhd->bqhd", weights, values, preferred_element_type=jnp.float32)
    context = context.astype(jnp.bfloat16).reshape(tokens, local_heads * HEAD_DIM)
    branch = lax.psum(jnp.dot(context, proj_weight, preferred_element_type=jnp.float32), "tensor")
    first = residual + branch + proj_bias
    normed_mid = layer_norm(first, mid_gain, mid_shift)
    lowered_mid = normed_mid.astype(jnp.bfloat16)
    inner = jnp.dot(lowered_mid, hidden_weight, preferred_element_type=jnp.float32) + hidden_bias
    activated = jax.nn.gelu(inner).astype(jnp.bfloat16)
    partial_out = jnp.dot(activated, output_weight, preferred_element_type=jnp.float32)
    second = first + lax.psum(partial_out, "tensor") + output_bias
    normed_moe = layer_norm(second, moe_gain, moe_shift)
    lowered_moe = normed_moe.astype(jnp.bfloat16)
    route = jax.nn.softmax(jnp.dot(normed_moe, router_weight, precision=highest), axis=-1)
    tables, kept = slot_tables(expert_ids, priority[0], capacity, experts)
    tables = tables.astype(jnp.bfloat16)
    dispatch = tables[0] + tables[1]
    buffers = jnp.einsum("tk,td->kd", dispatch, lowered_moe, preferred_element_type=jnp.float32)
    buffers = buffers.astype(jnp.bfloat16).reshape(experts, capacity, model_width)
    arrived = lax.all_to_all(buffers, "wide", split_axis=0, concat_axis=1, tiled=True)
    expert_inner = (
        jnp.einsum("erd,edf->erf", arrived, expert_in, preferred_element_type=jnp.float32)
        + expert_in_bias[:, None, :]
    )
    expert_act = jax.nn.gelu(expert_inner).astype(jnp.bfloat16)
    expert_partial = jnp.einsum(
        "erf,efd->erd", expert_act, expert_out, preferred_element_type=jnp.float32
    )
    expert_result = (
        lax.psum(expert_partial.astype(jnp.bfloat16), "tensor").astype(jnp.float32)
        + expert_out_bias[:, None, :]
    ).astype(jnp.bfloat16)
    returned = lax.all_to_all(
        expert_result, "wide", split_axis=1, concat_axis=0, tiled=True
    ).reshape(experts * capacity, model_width)
    picked = jnp.einsum("jtk,kd->jtd", tables, returned, preferred_element_type=jnp.float32)
    expert_range = jnp.arange(experts, dtype=jnp.int32)
    chosen = (expert_ids.T[:, :, None] == expert_range[None, None, :]).astype(jnp.float32) * kept[
        :, :, None
    ].astype(jnp.float32)
    gates = jnp.sum(chosen * route[None], axis=-1)
    mixture = jnp.sum(gates[:, :, None] * picked, axis=0)
    block_out = (second + mixture).astype(jnp.bfloat16)
    gate_grad = jnp.sum(picked * cotangent[None], axis=-1)
    weighted = (gates[:, :, None] * cotangent[None]).astype(jnp.bfloat16)
    slot_grad = jnp.einsum("jtk,jtd->kd", tables, weighted, preferred_element_type=jnp.float32)
    slot_grad = slot_grad.astype(jnp.bfloat16).reshape(experts, capacity, model_width)
    result_grad = lax.all_to_all(slot_grad, "wide", split_axis=0, concat_axis=1, tiled=True)
    expert_out_bias_grad = jnp.sum(result_grad.astype(jnp.float32), axis=1)
    expert_out_grad = jnp.einsum(
        "erf,erd->efd", expert_act, result_grad, preferred_element_type=jnp.float32
    )
    act_grad = jnp.einsum(
        "erd,efd->erf", result_grad, expert_out, preferred_element_type=jnp.float32
    )
    expert_inner_grad = gelu_grad(expert_inner, act_grad).astype(jnp.bfloat16)
    expert_in_bias_grad = jnp.sum(expert_inner_grad.astype(jnp.float32), axis=1)
    expert_in_grad = jnp.einsum(
        "erd,erf->edf", arrived, expert_inner_grad, preferred_element_type=jnp.float32
    )
    arrived_partial = jnp.einsum(
        "erf,edf->erd", expert_inner_grad, expert_in, preferred_element_type=jnp.float32
    )
    arrived_grad = lax.psum(arrived_partial.astype(jnp.bfloat16), "tensor")
    buffer_grad = lax.all_to_all(
        arrived_grad, "wide", split_axis=1, concat_axis=0, tiled=True
    ).reshape(experts * capacity, model_width)
    moe_input_grad = jnp.dot(dispatch, buffer_grad, preferred_element_type=jnp.float32)
    route_grad = jnp.sum(gate_grad[:, :, None] * chosen, axis=0)
    logit_grad = route * (route_grad - jnp.sum(route * route_grad, axis=-1, keepdims=True))
    router_grad = jnp.einsum("td,te->de", normed_moe, logit_grad, precision=highest)
    moe_input_grad = moe_input_grad + jnp.einsum(
        "te,de->td", logit_grad, router_weight, precision=highest
    )
    second_part, moe_gain_grad, moe_shift_grad = norm_grad(
        second, moe_gain, moe_shift, moe_input_grad
    )
    second_grad = cotangent + second_part
    lowered_second = second_grad.astype(jnp.bfloat16)
    output_bias_grad = jnp.sum(second_grad, axis=0)
    output_weight_grad = jnp.einsum(
        "tf,td->fd", activated, lowered_second, preferred_element_type=jnp.float32
    )
    activated_grad = jnp.einsum(
        "td,fd->tf", lowered_second, output_weight, preferred_element_type=jnp.float32
    )
    inner_grad = gelu_grad(inner, activated_grad).astype(jnp.bfloat16)
    hidden_bias_grad = jnp.sum(inner_grad.astype(jnp.float32), axis=0)
    hidden_weight_grad = jnp.einsum(
        "td,tf->df", lowered_mid, inner_grad, preferred_element_type=jnp.float32
    )
    mid_partial = jnp.einsum(
        "tf,df->td", inner_grad, hidden_weight, preferred_element_type=jnp.float32
    )
    mid_grad = lax.psum(mid_partial, "tensor")
    first_part, mid_gain_grad, mid_shift_grad = norm_grad(first, mid_gain, mid_shift, mid_grad)
    first_grad = second_grad + first_part
    proj_bias_grad = jnp.sum(first_grad, axis=0)
    branch_grad = first_grad.astype(jnp.bfloat16)
    proj_weight_grad = jnp.einsum(
        "tk,td->kd", context, branch_grad, preferred_element_type=jnp.float32
    )
    context_grad = jnp.einsum(
        "td,kd->tk", branch_grad, proj_weight, preferred_element_type=jnp.float32
    )
    context_grad = context_grad.astype(jnp.bfloat16).reshape(images, PATCHES, local_heads, HEAD_DIM)
    scores = (
        jnp.einsum("bqhd,bkhd->bhqk", query, keys, preferred_element_type=jnp.float32) * score_scale
    )
    probs = jnp.exp(scores - log_total)
    weights = probs.astype(jnp.bfloat16)
    value_grad = jnp.einsum(
        "bhqk,bqhd->bkhd", weights, context_grad, preferred_element_type=jnp.float32
    )
    prob_grad = jnp.einsum(
        "bqhd,bkhd->bhqk", context_grad, values, preferred_element_type=jnp.float32
    )
    score_grad = (probs * (prob_grad - jnp.sum(probs * prob_grad, axis=-1, keepdims=True))).astype(
        jnp.bfloat16
    )
    query_grad = (
        jnp.einsum("bhqk,bkhd->bqhd", score_grad, keys, preferred_element_type=jnp.float32)
        * score_scale
    )
    key_grad = (
        jnp.einsum("bhqk,bqhd->bkhd", score_grad, query, preferred_element_type=jnp.float32)
        * score_scale
    )
    qkv_grad = jnp.stack([query_grad, key_grad, value_grad], axis=2).astype(jnp.bfloat16)
    qkv_grad = qkv_grad.reshape(tokens, 3, local_heads * HEAD_DIM)
    qkv_sums = jnp.sum(qkv_grad.astype(jnp.float32), axis=0)
    qv_bias_grad = jnp.stack([qkv_sums[0], qkv_sums[2]])
    qkv_weight_grad = jnp.einsum(
        "td,tsk->dsk", lowered_pre, qkv_grad, preferred_element_type=jnp.float32
    )
    pre_partial = jnp.einsum(
        "tsk,dsk->td", qkv_grad, qkv_weight, preferred_element_type=jnp.float32
    )
    pre_grad = lax.psum(pre_partial.astype(jnp.bfloat16), "tensor").astype(jnp.float32)
    input_part, pre_gain_grad, pre_shift_grad = norm_grad(residual, pre_gain, pre_shift, pre_grad)
    tokens_grad = first_grad + input_part
    shared = (
        lax.psum(pre_gain_grad.astype(jnp.bfloat16), "wide").astype(jnp.float32),
        lax.psum(pre_shift_grad.astype(jnp.bfloat16), "wide").astype(jnp.float32),
        lax.psum(qkv_weight_grad.astype(jnp.bfloat16), "wide").astype(jnp.float32),
        lax.psum(qv_bias_grad.astype(jnp.bfloat16), "wide").astype(jnp.float32),
        lax.psum(proj_weight_grad.astype(jnp.bfloat16), "wide").astype(jnp.float32),
        lax.psum(proj_bias_grad.astype(jnp.bfloat16), "wide").astype(jnp.float32),
        lax.psum(mid_gain_grad.astype(jnp.bfloat16), "wide").astype(jnp.float32),
        lax.psum(mid_shift_grad.astype(jnp.bfloat16), "wide").astype(jnp.float32),
        lax.psum(hidden_weight_grad.astype(jnp.bfloat16), "wide").astype(jnp.float32),
        lax.psum(hidden_bias_grad.astype(jnp.bfloat16), "wide").astype(jnp.float32),
        lax.psum(output_weight_grad.astype(jnp.bfloat16), "wide").astype(jnp.float32),
        lax.psum(output_bias_grad.astype(jnp.bfloat16), "wide").astype(jnp.float32),
        lax.psum(moe_gain_grad.astype(jnp.bfloat16), "wide").astype(jnp.float32),
        lax.psum(moe_shift_grad.astype(jnp.bfloat16), "wide").astype(jnp.float32),
        lax.psum(router_grad.astype(jnp.bfloat16), "wide").astype(jnp.float32),
    )
    return (
        (block_out, tokens_grad)
        + tuple(shared)
        + (expert_in_grad, expert_in_bias_grad, expert_out_grad, expert_out_bias_grad)
    )


def solution(mesh):
    body = functools.partial(shards, mesh.shape["wide"]) if mesh.shape["tensor"] == 2 else plain
    return jax.shard_map(
        body,
        mesh=mesh,
        in_specs=(
            P("wide", None), P(), P(), P(None, None, "tensor"), P(None, "tensor"), P("tensor", None), P(), P(), P(),
            P(None, "tensor"), P("tensor"), P("tensor", None), P(), P(), P(), P(),
            P("wide", None, "tensor"), P("wide", "tensor"), P("wide", "tensor", None), P("wide", None),
            P("wide", None), P("wide", None), P("wide", None),
        ),
        out_specs=(
            P("wide", None), P("wide", None), P(), P(), P(None, None, "tensor"), P(None, "tensor"), P("tensor", None),
            P(), P(), P(), P(None, "tensor"), P("tensor"), P("tensor", None), P(), P(), P(), P(),
            P("wide", None, "tensor"), P("wide", "tensor"), P("wide", "tensor", None), P("wide", None),
        ),
        check_vma=False,
    )
```

```python
import functools

import jax
import jax.numpy as jnp
from jax import lax
from jax.experimental import pallas as pl
from jax.experimental.pallas import tpu as pltpu
from jax.sharding import PartitionSpec as P

HEAD_DIM = 64
PATCHES = 144
BF16 = jnp.bfloat16
F32 = jnp.float32
HIGHEST = lax.Precision.HIGHEST
MESH = pl.DeviceIdType.MESH
VMEM_BYTES = 60 * 1024 * 1024


def dot(left, right):
    return jnp.dot(left, right, preferred_element_type=F32)


def dot_rows(left, right):
    return lax.dot_general(left, right, (((1,), (1,)), ((), ())), preferred_element_type=F32)


def dot_columns(left, right, precision=None):
    return lax.dot_general(
        left, right, (((0,), (0,)), ((), ())), precision=precision, preferred_element_type=F32
    )


def normalized(values):
    centered = values - jnp.mean(values, axis=-1, keepdims=True)
    variance = jnp.mean(centered * centered, axis=-1, keepdims=True)
    scale = lax.rsqrt(variance + 1e-06)
    return centered * scale, scale


def norm_back(rows, scale, gain, upstream):
    scaled = upstream * gain
    inward = jnp.mean(scaled, axis=-1, keepdims=True)
    along = jnp.mean(scaled * rows, axis=-1, keepdims=True)
    return scale * (scaled - inward - rows * along)


def gelu_parts(inner):
    square = inner * inner
    bend = jnp.tanh(0.7978845608028654 * inner * (1.0 + 0.044715 * square))
    half = 0.5 * (1.0 + bend)
    slope = half + (0.5 * 0.7978845608028654) * inner * (1.0 - bend * bend) * (
        1.0 + 0.134145 * square
    )
    return inner * half, slope


def gelu(inner):
    return inner * (0.5 * (1.0 + jnp.tanh(0.7978845608028654 * inner * (1.0 + 0.044715 * inner * inner))))


def softmax_rows(scores, scale):
    peak = jnp.max(scores, axis=-1, keepdims=True)
    weights = jnp.exp((scores - peak) * scale)
    return weights * (1.0 / jnp.sum(weights, axis=-1, keepdims=True))


def spots(places):
    lane = lax.broadcasted_iota(jnp.int32, (places.shape[0], 128), 1)
    return [(lane == places[:, j : j + 1]).astype(F32) for j in range(2)]


def bits_of(index, wide):
    return [lax.rem(lax.div(index, 1 << k), 2) for k in range(wide.bit_length() - 1)]


class Sums:
    def __init__(self, wide, orders, totals, sends, lands, gathers, send_sems, recv_sems):
        me, self.plane = lax.axis_index("wide"), lax.axis_index("tensor")
        self.bits = bits_of(me, wide)
        self.partners = [me + (1 - 2 * bit) * (1 << k) for k, bit in enumerate(self.bits)]
        self.steps = len(self.bits)
        self.orders, self.totals, self.sends, self.lands, self.gathers = orders, totals, sends, lands, gathers
        self.send_sems, self.recv_sems = send_sems, recv_sems

    def piece(self, i, step):
        rows = self.gathers[i].shape[0]
        base = 0
        for s in range(step):
            base = base + self.bits[self.orders[i][s]] * (rows >> (s + 1))
        length = rows >> (step + 1)
        bit = self.bits[self.orders[i][step]]
        return pl.multiple_of(base + bit * length, 16), pl.multiple_of(base + (1 - bit) * length, 16), length

    def staged(self, i, step):
        rows = self.gathers[i].shape[0]
        return rows - (rows >> step)

    def transfer(self, i, k):
        step = k if k < self.steps else 2 * self.steps - 1 - k
        kept, _, length = self.piece(i, step)
        if k < self.steps:
            at = self.staged(i, step)
            source, target = self.sends[i].at[pl.ds(at, length)], self.lands[i].at[pl.ds(at, length)]
        else:
            source = target = self.gathers[i].at[pl.ds(kept, length)]
        return pltpu.make_async_remote_copy(
            source, target, self.send_sems.at[i, k], self.recv_sems.at[i, k],
            device_id=(self.partners[self.orders[i][step]], self.plane), device_id_type=MESH,
        )

    def begin(self, i, k):
        if k < self.steps:
            _, other, length = self.piece(i, k)
            at = self.staged(i, k)
            self.sends[i][at : at + length, :] = self.totals[i][pl.ds(other, length), :].astype(BF16)
        self.transfer(i, k).start()

    def advance(self, i, k):
        self.transfer(i, k).wait()
        if k < self.steps:
            kept, _, length = self.piece(i, k)
            at = self.staged(i, k)
            value = self.totals[i][pl.ds(kept, length), :] + self.lands[i][at : at + length, :].astype(F32)
            if k + 1 < self.steps:
                self.totals[i][pl.ds(kept, length), :] = value
            else:
                self.gathers[i][pl.ds(kept, length), :] = value.astype(BF16)
        if k + 1 < 2 * self.steps:
            self.begin(i, k + 1)


def greet(wide):
    me, plane = lax.axis_index("wide"), lax.axis_index("tensor")
    barrier = pltpu.get_barrier_semaphore()

    def hail(d, carry):
        pl.semaphore_signal(barrier, inc=1, device_id=(lax.rem(me + d, wide), plane), device_id_type=MESH)
        return carry

    lax.fori_loop(1, wide, hail, 0)
    pl.semaphore_signal(barrier, inc=1, device_id=(me, 1 - plane), device_id_type=MESH)
    pl.semaphore_wait(barrier, wide)


def put_row(small, at, row):
    for c in range(row.shape[1] // 128):
        small[at + c : at + c + 1, :] = row[:, 128 * c : 128 * (c + 1)]
    return at + row.shape[1] // 128


def get_row(small, at, width):
    return jnp.concatenate([small[at + c : at + c + 1, :] for c in range(width // 128)], axis=1)


def image_back(heads, qkv, context_grad):
    width = heads * HEAD_DIM
    scale = HEAD_DIM**-0.5
    parts = [[], [], []]
    for head in range(heads):
        h = head * HEAD_DIM
        query = qkv[:, h : h + HEAD_DIM]
        keys = qkv[:, width + h : width + h + HEAD_DIM]
        values = qkv[:, 2 * width + h : 2 * width + h + HEAD_DIM]
        upstream = context_grad[:, h : h + HEAD_DIM]
        scores = dot_rows(keys, query)
        weights = jnp.exp((scores - jnp.max(scores, axis=0, keepdims=True)) * scale)
        probs = weights * (1.0 / jnp.sum(weights, axis=0, keepdims=True))
        prob_grad = dot_rows(values, upstream)
        inward = jnp.sum(probs * prob_grad, axis=0, keepdims=True)
        score_grad = (probs * (prob_grad - inward)).astype(BF16)
        parts[0].append(dot_columns(score_grad, keys) * scale)
        parts[1].append(dot(score_grad, query) * scale)
        parts[2].append(dot(probs.astype(BF16), upstream))
    return jnp.concatenate(parts[0] + parts[1] + parts[2], axis=1).astype(BF16)


def column_dots(left, right, put, tile=256):
    def body(i, carry):
        at = pl.multiple_of(i * tile, tile)
        put(at, tile, dot_columns(left[:, pl.ds(at, tile)], right[...]))
        return carry

    lax.fori_loop(0, left.shape[1] // tile, body, 0)


def image_forward(heads, qkv):
    width = heads * HEAD_DIM
    parts = []
    for head in range(heads):
        h = head * HEAD_DIM
        probs = softmax_rows(
            dot_rows(qkv[:, h : h + HEAD_DIM], qkv[:, width + h : width + h + HEAD_DIM]), HEAD_DIM**-0.5
        )
        parts.append(dot(probs.astype(BF16), qkv[:, 2 * width + h : 2 * width + h + HEAD_DIM]))
    return jnp.concatenate(parts, axis=1).astype(BF16)


def token_hits(choices, slots):
    slot = lax.broadcasted_iota(jnp.int32, (choices.shape[0], slots), 1)
    return [slot == choices[:, j : j + 1] for j in range(2)]


def slot_hits(first, count, targets):
    slot = first + lax.broadcasted_iota(jnp.int32, (count, targets.shape[1]), 0)
    return ((slot == targets[0:1, :]) | (slot == targets[1:2, :])).astype(BF16)


def count_slots(ids, priority, experts, capacity, room):
    tokens = ids.shape[1]
    wide_rows = jnp.concatenate([ids, priority, jnp.zeros((5, tokens), jnp.int32)], axis=0)
    eye = lax.broadcasted_iota(jnp.int32, (8, 8), 0) == lax.broadcasted_iota(jnp.int32, (8, 8), 1)
    turned = dot_columns(wide_rows.astype(F32), eye.astype(F32), HIGHEST).astype(jnp.int32)
    rank, ranks = turned[:, 2:3], priority

    def fold(numbers, own, before, axis):
        later = [jnp.where(numbers == own[0], before, 0.0), jnp.where(numbers == own[1] + experts, before, 0.0)]
        return [jnp.sum(part, axis=axis, keepdims=True) for part in later]

    def finish(own, counts, firsts):
        counts = [counts[0], counts[1] + firsts]
        places = [count.astype(jnp.int32) for count in counts]
        kept = [place < capacity for place in places]
        return (
            [jnp.where(keep, choice * room + place, -1) for keep, choice, place in zip(kept, own, places)],
            [jnp.where(keep, choice, -1) for keep, choice in zip(kept, own)],
            [jnp.where(keep, place, -1) for keep, place in zip(kept, places)],
        )

    number = lax.broadcasted_iota(jnp.int32, (2 * experts, tokens), 0)
    by_row = [ids[0:1, :], ids[1:2, :]]
    held = ((number == by_row[0]) | (number == by_row[1] + experts)).astype(BF16)
    before = dot(held, (rank < ranks).astype(BF16))
    first_counts = jnp.sum(held.astype(F32), axis=1, keepdims=True)
    firsts = jnp.sum(jnp.where(number == by_row[1], first_counts, 0.0), axis=0, keepdims=True)
    targets, _, _ = finish(by_row, fold(number, by_row, before, 0), firsts)

    number = lax.broadcasted_iota(jnp.int32, (tokens, 2 * experts), 1)
    by_token = [turned[:, 0:1], turned[:, 1:2]]
    held_by_token = ((number == by_token[0]) | (number == by_token[1] + experts)).astype(BF16)
    before = dot((ranks < rank).astype(BF16), held_by_token)
    first_counts = jnp.sum(held_by_token.astype(F32), axis=0, keepdims=True)
    firsts = jnp.sum(jnp.where(number == by_token[1], first_counts, 0.0), axis=1, keepdims=True)
    groups = finish(by_token, fold(number, by_token, before, 1), firsts)
    choices = jnp.concatenate([part for group in groups for part in group], axis=1)
    return jnp.concatenate(targets, axis=0), choices


def front(
    wide, room, group, heads, rows, experts,
    tokens_h, cotangent_h, weight_qkv_h, projection_h, hidden_h, output_h, weight_in_h, weight_out_h,
    ids, priority, pre_gain, pre_shift, qv_bias, proj_bias, mid_gain, mid_shift, hidden_bias, output_bias,
    moe_gain, moe_shift, router, bias_in, bias_out,
    qkv_h, context_h, first_h, second_h, info_h, result_h, in_grad_h, out_grad_h, fed_h, slope_h, lowered_h, own_home, peer_home,
    gate_home, in_bias_grad, out_bias_grad,
    tokens, cotangent, weight_qkv, projection, hidden, output, weight_in, weight_out,
    qkv, context, first, second, info, result, in_grad, out_grad, fed, slopes_kept, lowered_mid,
    targets, table, raised_placed, upstream, projection_peer, context_peer, partial_own, partial_peer,
    columns, other_columns, placed, other_placed, rows_own, rows_peer, act, inner_grad, slot_grad, grad_kept, grad_sent, grad_landed,
    grad_back, gate_sent, gate_arrived, gate_back, gate_own, gate_peer,
    sems, load_sems, chunk_sems, store_sems, group_sems,
):
    me, plane = lax.axis_index("wide"), lax.axis_index("tensor")
    chunks, groups = tokens.shape[0] // rows, wide // group
    mine = lax.div(me, group)
    block = group * room
    width = heads * HEAD_DIM
    half = columns.shape[1]
    capacity = tokens.shape[0] // experts
    row_at, gate_at, home_at, back_at, up_at = 0, wide, 2 * wide, 3 * wide, 4 * wide
    grad_at, share_at, join_at = 5 * wide, 5 * wide + groups, 5 * wide + 2 * groups
    context_at = 5 * wide + 3 * groups
    partial_at, last_at = context_at + chunks, context_at + 2 * chunks
    other_at = last_at + 2

    def rows_of(index):
        return pl.ds(pl.multiple_of(index * room, 16), room)

    def rows_of_group(index):
        return pl.ds(pl.multiple_of(index * block, 16), block)

    def chunk_of(index):
        return pl.ds(pl.multiple_of(index * rows, 16), rows)

    def load_tokens(c):
        return pltpu.make_async_copy(tokens_h.at[chunk_of(c)], tokens.at[chunk_of(c)], chunk_sems.at[c])

    def start_tokens(c, carry):
        load_tokens(c).start()
        return carry

    loads = [
        pltpu.make_async_copy(source, target, load_sems.at[i])
        for i, (source, target) in enumerate(
            [(weight_qkv_h, weight_qkv), (projection_h, projection), (hidden_h, hidden), (output_h, output),
             (cotangent_h, cotangent), (weight_in_h, weight_in), (weight_out_h, weight_out)]
        )
    ]
    loads[0].start()
    lax.fori_loop(0, chunks, start_tokens, 0)
    for load in loads[1:]:
        load.start()

    def store(kind, source, target, c):
        return pltpu.make_async_copy(source.at[chunk_of(c)], target.at[chunk_of(c)], store_sems.at[kind, c])

    stores = [(qkv, qkv_h), (context, context_h), (first, first_h), (second, second_h), (info, info_h), (fed, fed_h), (slopes_kept, slope_h),
              (lowered_mid, lowered_h)]
    greet(wide)

    def move(source, target, base, sent, landed, device):
        return pltpu.make_async_remote_copy(
            source, target, sems.at[0, base + sent], sems.at[1, base + landed], device_id=device, device_id_type=MESH
        )

    def across_chunk(source, target, base, index):
        there = chunk_of(index)
        return move(source.at[there], target.at[there], base, index, index, (me, 1 - plane))

    def up_copy(other, sender):
        return move(raised_placed.at[rows_of(other)], upstream.at[rows_of(sender)], up_at, other, sender, (other, plane))

    weights = move(projection_h, projection_peer, last_at, 0, 0, (me, 1 - plane))
    weights.start()
    first_plane = plane == 0
    table[...] = jnp.zeros_like(table)
    in_bias_grad[...] = jnp.zeros_like(in_bias_grad)
    out_bias_grad[...] = jnp.zeros_like(out_bias_grad)

    def attend_chunk(c):
        there = chunk_of(c)
        load_tokens(c).wait()
        normed, _ = normalized(tokens[there, :].astype(F32))
        lowered = (normed * pre_gain[...] + pre_shift[...]).astype(BF16)
        parts = [dot(lowered, weight_qkv[s]) for s in range(3)]
        parts = [parts[0] + qv_bias[0:1, :], parts[1], parts[2] + qv_bias[1:2, :]]
        value = jnp.concatenate(parts, axis=1).astype(BF16)
        qkv[there, :] = value
        contexts = [
            image_forward(heads, value[image * PATCHES : (image + 1) * PATCHES]) for image in range(rows // PATCHES)
        ]
        context[there, :] = jnp.concatenate(contexts, axis=0)
        across_chunk(context, context_peer, context_at, c).start()
        store(0, qkv, qkv_h, c).start()
        store(1, context, context_h, c).start()

    def find_slots():
        by_row, choices = count_slots(ids[...], priority[...], experts, capacity, room)
        targets[0:2, :] = by_row
        info[:, experts : experts + 6] = choices.astype(F32)

    def raise_group(k):
        q = lax.rem(mine + k, groups)
        hits = slot_hits(q * block, block, targets)
        raised_placed[rows_of_group(q), :] = dot(hits, cotangent[...].astype(BF16)).astype(BF16)
        for j in range(group):
            e = q * group + j

            @pl.when(e != me)
            def _(e=e):
                up_copy(e, me).start()

            @pl.when(e == me)
            def _(e=e):
                upstream[rows_of(e), :] = raised_placed[rows_of(e), :]

    def feed_chunk(c):
        there = chunk_of(c)
        across_chunk(context, context_peer, context_at, c).wait()
        branch = dot(context[there, :], projection[...]) + dot(context_peer[there, :], projection_peer[...])
        value = tokens[there, :].astype(F32) + branch + proj_bias[...]
        first[there, :] = value
        normed, _ = normalized(value)
        lowered = (normed * mid_gain[...] + mid_shift[...]).astype(BF16)
        activated, slope = gelu_parts(dot(lowered, hidden[...]) + hidden_bias[...])
        activated = activated.astype(BF16)
        partial_own[there, :] = dot(activated, output[...]).astype(BF16)
        across_chunk(partial_own, partial_peer, partial_at, c).start()
        fed[there, :] = activated
        slopes_kept[there, :] = slope.astype(BF16)
        lowered_mid[there, :] = lowered
        for kind in (5, 6, 7):
            store(kind, *stores[kind], c).start()
        store(2, first, first_h, c).start()

    def route_chunk(c):
        there = chunk_of(c)
        across_chunk(partial_own, partial_peer, partial_at, c).wait()
        partial = partial_own[there, :].astype(F32) + partial_peer[there, :].astype(F32)
        value = first[there, :] + partial + output_bias[...]
        second[there, :] = value
        normed, _ = normalized(value)
        normed = normed * moe_gain[...] + moe_shift[...]
        columns[there, :] = jnp.where(first_plane, normed[:, :half], normed[:, half:]).astype(BF16)
        other_columns[there, :] = jnp.where(first_plane, normed[:, half:], normed[:, :half]).astype(BF16)
        logits = lax.dot_general(
            normed, router[...], (((1,), (1,)), ((), ())), precision=HIGHEST, preferred_element_type=F32
        )
        grown = jnp.exp(logits - jnp.max(logits, axis=-1, keepdims=True))
        route = grown / jnp.sum(grown, axis=-1, keepdims=True)
        info[there, 0:experts] = route
        number = lax.broadcasted_iota(jnp.int32, route.shape, 1)
        picks = info[there, experts : experts + 6].astype(jnp.int32)
        for j, spot in enumerate(spots(picks[:, 4:6])):
            table[...] += dot_columns(jnp.where(number == picks[:, 2 + j : 3 + j], route, 0.0), spot, HIGHEST)
        store(3, second, second_h, c).start()
        store(4, info, info_h, c).start()

    def turn(c, carry):
        @pl.when(c < chunks)
        def _():
            attend_chunk(c)

        @pl.when(c == 0)
        def _():
            loads[4].wait()
            find_slots()

        @pl.when(c < chunks)
        def _():
            for part in range(groups // chunks):
                raise_group(c * (groups // chunks) + part)

        @pl.when(c == 1)
        def _():
            weights.wait()
            for load in loads[1:4]:
                load.wait()

        @pl.when((c >= 1) & (c <= chunks))
        def _():
            feed_chunk(c - 1)

        @pl.when(c >= 2)
        def _():
            route_chunk(c - 2)

        return carry

    info[...] = jnp.zeros_like(info)
    loads[0].wait()
    lax.fori_loop(0, chunks + 2, turn, 0)

    def row_copy(other, sender):
        return move(placed.at[rows_of(other)], rows_own.at[rows_of(sender)], row_at, other, sender, (other, plane))

    def other_copy(other, sender):
        return move(other_placed.at[rows_of(other)], rows_peer.at[rows_of(sender)], other_at, other, sender, (other, plane))

    near_groups = groups // 2
    sides = groups // 4

    def turned(k, sign):
        turn, side = lax.div(k, sides), lax.rem(mine + k, sides)
        place = lax.div(mine, sides)
        pair = lax.rem(lax.div(place, 2) + sign * lax.div(turn, 2) + 2, 2)
        return sides * (2 * pair + lax.rem(place + turn, 2)) + side, k < near_groups

    def gate_copy(other, sender):
        return move(gate_sent.at[other], gate_arrived.at[sender], gate_at, other, sender, (other, plane))

    def home_copy(other, sender):
        return move(grad_back.at[rows_of(other)], own_home.at[rows_of(sender)], home_at, other, sender, (other, plane))

    def back_copy(other, sender):
        return move(gate_back.at[other], gate_own.at[sender], back_at, other, sender, (other, plane))

    def across(source, target, base, index):
        there = rows_of_group(index)
        return move(source.at[there], target.at[there], base, index, index, (me, 1 - plane))

    own_half = pl.ds(pl.multiple_of(plane * half, 16), half)
    peer_half = pl.ds(pl.multiple_of((1 - plane) * half, 16), half)
    for e in range(wide):
        gate_sent[e] = jnp.broadcast_to(table[e : e + 1, :], gate_sent.shape[1:])

    def place_group(k, carry):
        q, near = turned(k, 1)
        hits = slot_hits(q * block, block, targets)
        placed[rows_of_group(q), :] = dot(hits, columns[...]).astype(BF16)

        @pl.when(near)
        def _():
            other_placed[rows_of_group(q), :] = dot(hits, other_columns[...]).astype(BF16)

        for j in range(group):
            e = q * group + j

            @pl.when(e != me)
            def _(e=e):
                row_copy(e, me).start()
                gate_copy(e, me).start()

            @pl.when((e != me) & near)
            def _(e=e):
                other_copy(e, me).start()

            @pl.when(e == me)
            def _(e=e):
                rows_own[rows_of(e), :] = placed[rows_of(e), :]
                rows_peer[rows_of(e), :] = other_placed[rows_of(e), :]
                gate_arrived[e] = gate_sent[e]

        return carry

    lax.fori_loop(0, groups, place_group, 0)
    loads[5].wait()
    loads[6].wait()
    diagonal = lax.broadcasted_iota(jnp.int32, (room, 128), 0) == lax.broadcasted_iota(jnp.int32, (room, 128), 1)

    def store_result(p):
        there = rows_of_group(p)
        return pltpu.make_async_copy(result.at[there], result_h.at[there], group_sems.at[p])

    def join_group(k):
        p, near = turned(k, -1)
        for j in range(group):
            w = p * group + j

            @pl.when(w != me)
            def _(w=w):
                row_copy(w, w).wait_recv()
                gate_copy(w, w).wait_recv()

        @pl.when(jnp.logical_not(near))
        def _():
            across(rows_own, rows_peer, join_at, p).start()

        for j in range(group):
            w = p * group + j

            @pl.when((w != me) & near)
            def _(w=w):
                other_copy(w, w).wait_recv()

            @pl.when(w != me)
            def _(w=w):
                up_copy(w, w).wait_recv()

    def expert_group(k):
        p, near = turned(k, -1)
        there = rows_of_group(p)

        @pl.when(jnp.logical_not(near))
        def _():
            across(rows_own, rows_peer, join_at, p).wait()

        gates = jnp.concatenate(
            [
                jnp.sum(jnp.where(diagonal, gate_arrived[p * group + j][0:1, :], 0.0), axis=1, keepdims=True)
                for j in range(group)
            ],
            axis=0,
        )
        inner = dot(rows_own[there, :], weight_in[own_half, :]) + dot(rows_peer[there, :], weight_in[peer_half, :])
        acted, slope = gelu_parts(inner + bias_in[...])
        acted = acted.astype(BF16)
        act[there, :] = acted
        raised = upstream[there, :].astype(F32)
        slot = (raised * gates).astype(BF16)
        slot_grad[there, :] = slot
        inward = (dot_rows(slot, weight_out[...]) * slope).astype(BF16)
        inner_grad[there, :] = inward
        grad_sent[there, :] = dot_rows(inward, weight_in[peer_half, :]).astype(BF16)
        across(grad_sent, grad_landed, grad_at, p).start()
        grad_kept[there, :] = dot_rows(inward, weight_in[own_half, :])

    def result_group(k, carry):
        p, _ = turned(k, -1)
        there = rows_of_group(p)
        value = dot(act[there, :], weight_out[...]) + bias_out[...] * jnp.where(first_plane, 1.0, 0.0)
        result[there, :] = value.astype(BF16)
        store_result(p).start()
        out_bias_grad[0:1, :] += jnp.sum(slot_grad[there, :].astype(F32), axis=0, keepdims=True)
        in_bias_grad[0:1, :] += jnp.sum(inner_grad[there, :].astype(F32), axis=0, keepdims=True)
        slopes = jnp.sum(upstream[there, :].astype(F32) * value, axis=1, keepdims=True)
        for j in range(group):
            w = p * group + j
            row = jnp.sum(
                jnp.where(diagonal, slopes[j * room : (j + 1) * room], 0.0), axis=0, keepdims=True
            )
            gate_back[w] = jnp.broadcast_to(row, gate_back.shape[1:])

            @pl.when(w != me)
            def _(w=w):
                back_copy(w, me).start()

            @pl.when(w == me)
            def _(w=w):
                gate_own[w] = gate_back[w]

        return carry

    own_rows = pltpu.make_async_copy(grad_back.at[rows_of(me)], own_home.at[rows_of(me)], group_sems.at[groups])

    def give_back(k):
        p, _ = turned(k, -1)
        across(grad_sent, grad_landed, grad_at, p).wait()
        there = rows_of_group(p)
        grad_back[there, :] = (grad_kept[there, :] + grad_landed[there, :].astype(F32)).astype(BF16)
        for j in range(group):
            w = p * group + j

            @pl.when(w != me)
            def _(w=w):
                home_copy(w, me).start()

            @pl.when(w == me)
            def _(w=w):
                own_rows.start()

    def share_group(k, carry):
        q, _ = turned(k, 1)
        for j in range(group):
            e = q * group + j

            @pl.when(e != me)
            def _(e=e):
                home_copy(e, e).wait_recv()

            @pl.when(e == me)
            def _():
                own_rows.wait()

        across(own_home, peer_home, share_at, q).start()
        return carry

    def expert_turn(s, carry):
        @pl.when(s < groups)
        def _():
            join_group(s)

        @pl.when(s < near_groups)
        def _():
            expert_group(s)

        @pl.when((s > near_groups) & (s <= groups))
        def _():
            expert_group(s - 1)

        @pl.when((s >= 1) & (s <= near_groups))
        def _():
            give_back(s - 1)

        @pl.when(s >= near_groups + 2)
        def _():
            give_back(s - 2)
            share_group(s - near_groups - 2, 0)

        return carry

    lax.fori_loop(0, groups + 2, expert_turn, 0)
    lax.fori_loop(0, groups, result_group, 0)
    lax.fori_loop(near_groups, groups, share_group, 0)

    def put_out(at, tile, value):
        out_grad[pl.ds(at, tile), :] = value.astype(BF16)

    column_dots(act, slot_grad, put_out)
    out_store = pltpu.make_async_copy(out_grad, out_grad_h, load_sems.at[7])
    out_store.start()

    def take_gates(d, carry):
        other = lax.rem(me + d, wide)
        back_copy(other, other).wait_recv()
        return carry

    lax.fori_loop(1, wide, take_gates, 0)
    tables = move(gate_own, gate_peer, last_at, 1, 1, (me, 1 - plane))
    tables.start()
    in_grad[own_half, :] = dot_columns(rows_own[...], inner_grad[...]).astype(BF16)
    in_grad[peer_half, :] = dot_columns(rows_peer[...], inner_grad[...]).astype(BF16)
    in_store = pltpu.make_async_copy(in_grad, in_grad_h, load_sems.at[8])
    in_store.start()

    def end_sends(d, carry):
        other = lax.rem(me + d, wide)
        up_copy(other, me).wait_send()
        row_copy(other, me).wait_send()
        gate_copy(other, me).wait_send()
        home_copy(other, me).wait_send()
        back_copy(other, me).wait_send()
        return carry

    lax.fori_loop(1, wide, end_sends, 0)

    def end_others(k, carry):
        q, _ = turned(k, 1)
        for j in range(group):
            e = q * group + j

            @pl.when(e != me)
            def _(e=e):
                other_copy(e, me).wait_send()

        return carry

    lax.fori_loop(0, near_groups, end_others, 0)

    def end_stores(c, carry):
        for kind, (source, target) in enumerate(stores):
            store(kind, source, target, c).wait()
        return carry

    lax.fori_loop(0, chunks, end_stores, 0)
    tables.wait()
    for e in range(wide):
        gate_home[e : e + 1, :] = gate_own[e][0:1, :] + gate_peer[e][0:1, :]

    def end_groups(q, carry):
        store_result(q).wait()
        across(own_home, peer_home, share_at, q).wait()
        return carry

    lax.fori_loop(0, groups, end_groups, 0)
    out_store.wait()
    in_store.wait()


def backward(
    wide, room, heads, layout, orders, rows,
    second_h, cotangent_h, info_h, first_h, tokens_h, qkv_h, context_h, hidden_h, output_h, projection_h, weight_qkv_h,
    row_own_h, row_peer_h, act_h, slope_h, lowered_h, result,
    moe_gain, moe_shift, router, gate_grads, mid_gain, pre_gain, pre_shift,
    block_h, grad_h, hidden_out_h, output_out_h, qkv_out_h, proj_out_h, *rest,
):
    vectors_out, pre_out, rest = rest[: len(layout)], rest[len(layout)], rest[len(layout) + 1 :]
    (second, cotangent, info, first, tokens, qkv, context, hidden, output, projection, weight_qkv, row_own, row_peer,
     act, slopes, lowered_mid, block_out, grad_out, hidden_out, output_out, qkv_out, proj_out), rest = rest[:22], rest[22:]
    load_sems, chunk_sems, store_sems, rest = rest[-3], rest[-2], rest[-1], rest[:-3]
    (inner_grad, mid_own, mid_peer, branch, qkv_grad, lowered_pre, pre_peer, result_own, blend_peer,
     pre_tile, pre_tiles, pre_total, pre_other, moe_sums, router_sums, mid_sums, hidden_sums, qkv_sums, pre_sums, small_sums) = rest[:20]
    hidden_total, output_total, qkv_total, proj_total, small = rest[20:25]
    sends, lands = rest[25:31], rest[31:37]
    mid_sems, pre_sems, blend_sems, result_sems, send_sems, recv_sems = rest[37:]
    blend_own = lowered_mid
    me, plane = lax.axis_index("wide"), lax.axis_index("tensor")
    chunks = tokens.shape[0] // rows
    model = tokens.shape[1]
    width = heads * HEAD_DIM
    split = qkv_total.shape[0] // 2
    totals = (
        hidden_total, output_total, qkv_total.at[pl.ds(0, split)], qkv_total.at[pl.ds(split, split)], proj_total, small
    )
    gathers = (
        hidden_out, output_out, qkv_out.at[pl.ds(0, split)], qkv_out.at[pl.ds(split, split)], proj_out, small_sums
    )

    def chunk_of(index):
        return pl.ds(pl.multiple_of(index * rows, 16), rows)

    early = [(info_h, info), (second_h, second), (cotangent_h, cotangent), (slope_h, slopes)]
    late = [(tokens_h, tokens), (qkv_h, qkv), (first_h, first)]
    middle = [(lowered_h, lowered_mid), (act_h, act)]

    def load(kind, pair, c):
        return pltpu.make_async_copy(pair[0].at[chunk_of(c)], pair[1].at[chunk_of(c)], chunk_sems.at[kind, c])

    def start_early(c, carry):
        for kind, pair in enumerate(early):
            load(kind, pair, c).start()
        return carry

    def start_late(c, carry):
        for kind, pair in enumerate(late):
            load(len(early) + kind, pair, c).start()
        return carry

    middle_loads = [
        pltpu.make_async_copy(source, target, load_sems.at[12 + i]) for i, (source, target) in enumerate(middle)
    ]
    loads = [
        pltpu.make_async_copy(source, target, load_sems.at[i])
        for i, (source, target) in enumerate(
            [(row_own_h, row_own), (row_peer_h, row_peer), (hidden_h, hidden), (output_h, output),
             (projection_h, projection), (weight_qkv_h, weight_qkv), (context_h, context)]
        )
    ]
    for part in loads[:2]:
        part.start()
    start_early(0, 0)
    for part in loads[2:4]:
        part.start()
    lax.fori_loop(1, chunks, start_early, 0)
    for part in loads[4:]:
        part.start()
    for part in middle_loads:
        part.start()
    lax.fori_loop(0, chunks, start_late, 0)
    whole_stores = [
        pltpu.make_async_copy(source, target, load_sems.at[len(loads) + i])
        for i, (source, target) in enumerate(
            [(hidden_out, hidden_out_h), (output_out, output_out_h), (qkv_out, qkv_out_h), (proj_out, proj_out_h)]
        )
    ]

    def store(kind, source, target, c):
        return pltpu.make_async_copy(source.at[chunk_of(c)], target.at[chunk_of(c)], store_sems.at[kind, c])

    greet(wide)
    sums = Sums(wide, orders, totals, sends, lands, gathers, send_sems, recv_sems)

    def rows_of(index):
        return pl.ds(pl.multiple_of(index * room, 16), room)

    def result_copy(other, sender):
        return pltpu.make_async_remote_copy(
            result.at[rows_of(other)], result_own.at[rows_of(sender)], result_sems.at[0, other],
            result_sems.at[1, sender], device_id=(other, plane), device_id_type=MESH,
        )

    def send_result(d, carry):
        result_copy(lax.rem(me + d, wide), me).start()
        return carry

    lax.fori_loop(1, wide, send_result, 0)
    own_rows = pltpu.make_async_copy(
        result.at[rows_of(me)], result_own.at[rows_of(me)], load_sems.at[len(loads) + len(whole_stores)]
    )
    own_rows.start()

    def across(own, peer, sems, chunk):
        at = pl.multiple_of(chunk * rows, rows)
        return pltpu.make_async_remote_copy(
            own.at[pl.ds(at, rows)], peer.at[pl.ds(at, rows)], sems.at[0, chunk], sems.at[1, chunk],
            device_id=(me, 1 - plane), device_id_type=MESH,
        )

    for vector in (moe_sums, router_sums, mid_sums, hidden_sums, qkv_sums, pre_sums):
        vector[...] = jnp.zeros_like(vector)
    first_plane = plane == 0

    def ordered(own, peer):
        return jnp.concatenate([jnp.where(first_plane, own, peer), jnp.where(first_plane, peer, own)], axis=1)

    def settle(here):
        experts = router.shape[0]
        picks = info[here, experts : experts + 6].astype(jnp.int32)
        hits = token_hits(picks, row_own.shape[0])
        table = (hits[0] | hits[1]).astype(BF16)
        moe_grad = ordered(dot(table, row_own[...]), dot(table, row_peer[...]))
        chances = info[here, 0:experts]
        number = lax.broadcasted_iota(jnp.int32, chances.shape, 1)
        route_grad = jnp.zeros_like(chances)
        for j, spot in enumerate(spots(picks[:, 4:6])):
            at_place = dot_rows(spot.astype(BF16), gate_grads[...].astype(BF16))
            route_grad = route_grad + jnp.where(number == picks[:, 2 + j : 3 + j], at_place, 0.0)
        logit_grad = chances * (route_grad - jnp.sum(chances * route_grad, axis=1, keepdims=True))
        normed, scale = normalized(second[here, :])
        logit_grad = logit_grad.astype(BF16)
        router_sums[...] += dot_columns(logit_grad, (normed * moe_gain[...] + moe_shift[...]).astype(BF16))
        moe_grad = moe_grad + dot(logit_grad, router[...].astype(BF16))
        grad = cotangent[here, :] + norm_back(normed, scale, moe_gain[...], moe_grad)
        grad_out[here, :] = grad
        branch[here, :] = grad.astype(BF16)
        moe_sums[0:1, :] += jnp.sum(moe_grad * normed, axis=0, keepdims=True)
        moe_sums[1:2, :] += jnp.sum(moe_grad, axis=0, keepdims=True)
        moe_sums[2:3, :] += jnp.sum(grad, axis=0, keepdims=True)

    def feed_chunk(chunk, carry):
        here = chunk_of(chunk)
        for kind, pair in enumerate(early):
            load(kind, pair, chunk).wait()
        settle(here)

        @pl.when(chunk == 0)
        def _():
            loads[2].wait()
            loads[3].wait()

        inward = (dot_rows(branch[here, :], output[...]) * slopes[here, :].astype(F32)).astype(BF16)
        inner_grad[here, :] = inward
        hidden_sums[0:1, :] += jnp.sum(inward.astype(F32), axis=0, keepdims=True)
        mid_own[here, :] = dot_rows(inward, hidden[...]).astype(BF16)
        across(mid_own, mid_peer, mid_sems, chunk).start()
        return carry

    loads[0].wait()
    loads[1].wait()
    lax.fori_loop(0, chunks, feed_chunk, 0)

    def put_in(total):
        def put(at, tile, value):
            total[pl.ds(at, tile), :] = value

        return put

    for part in middle_loads:
        part.wait()
    column_dots(lowered_mid, inner_grad, put_in(hidden_total))
    sums.begin(0, 0)
    column_dots(act, branch, put_in(output_total))
    sums.begin(1, 0)

    images = rows // PATCHES
    taken = ((3, 7), (3, 7))

    def attend_chunk(chunk, carry):
        here = pl.ds(pl.multiple_of(chunk * rows, rows), rows)
        for kind, pair in enumerate(late):
            load(len(early) + kind, pair, chunk).wait()
        across(mid_own, mid_peer, mid_sems, chunk).wait()
        mid_grad = mid_own[here, :].astype(F32) + mid_peer[here, :].astype(F32)
        normed, scale = normalized(first[here, :])
        first_grad = grad_out[here, :] + norm_back(normed, scale, mid_gain[...], mid_grad)
        grad_out[here, :] = first_grad
        lowered_grad = first_grad.astype(BF16)
        branch[here, :] = lowered_grad
        mid_sums[0:1, :] += jnp.sum(mid_grad * normed, axis=0, keepdims=True)
        mid_sums[1:2, :] += jnp.sum(mid_grad, axis=0, keepdims=True)
        mid_sums[2:3, :] += jnp.sum(first_grad, axis=0, keepdims=True)
        normed, _ = normalized(tokens[here, :].astype(F32))
        lowered_pre[here, :] = (normed * pre_gain[...] + pre_shift[...]).astype(BF16)
        context_grad = dot_rows(lowered_grad, projection[...]).astype(BF16)
        for image in range(rows // PATCHES):
            at = pl.multiple_of(chunk * rows + image * PATCHES, PATCHES)
            block = qkv[pl.ds(at, PATCHES), :]
            grad = image_back(heads, block, context_grad[image * PATCHES : (image + 1) * PATCHES])
            qkv_grad[pl.ds(at, PATCHES), :] = grad
            pre = sum(dot_rows(grad[:, s * width : (s + 1) * width], weight_qkv[s]) for s in range(3))
            pre = pre.astype(BF16)
            mid_own[pl.ds(at, PATCHES), :] = pre
            pre = pre.astype(F32)
            pre_sums[0:1, :] += jnp.sum(pre * normed[image * PATCHES : (image + 1) * PATCHES], axis=0, keepdims=True)
            pre_sums[1:2, :] += jnp.sum(pre, axis=0, keepdims=True)
            qkv_sums[0:1, :] += jnp.sum(grad.astype(F32), axis=0, keepdims=True)
            for i, steps in enumerate(taken):
                for k, boundary in enumerate(steps):
                    if boundary % images == image:

                        @pl.when(chunk == boundary // images)
                        def _(i=i, k=k):
                            sums.advance(i, k)

        across(mid_own, pre_peer, pre_sems, chunk).start()
        return carry

    loads[4].wait()
    loads[5].wait()
    lax.fori_loop(0, chunks, attend_chunk, 0)
    loads[6].wait()

    put_row(pre_tile, put_row(pre_tile, 0, pre_sums[0:1, :]), pre_sums[1:2, :])

    def pre_copy(other, sender):
        return pltpu.make_async_remote_copy(
            pre_tile, pre_tiles.at[sender], result_sems.at[0, wide + other], result_sems.at[1, wide + sender],
            device_id=(other, plane), device_id_type=MESH,
        )

    def send_pre(d, carry):
        pre_copy(lax.rem(me + d, wide), me).start()
        return carry

    lax.fori_loop(1, wide, send_pre, 0)
    pre_tiles[me] = pre_tile[...]

    def put_thirds(at, tile, value):
        for s in range(3):
            there = pl.ds(pl.multiple_of(s * model + at, 16), tile)
            qkv_total[there, :] = value[:, s * width : (s + 1) * width]

    column_dots(lowered_pre, qkv_grad, put_thirds)
    sums.begin(2, 0)
    sums.begin(3, 0)
    column_dots(context, branch, put_in(proj_total))
    sums.begin(4, 0)
    small[...] = jnp.zeros_like(small)
    at = 0
    for vector, picked in zip((mid_sums, moe_sums, hidden_sums, qkv_sums, router_sums), layout):
        for r in picked:
            at = put_row(small, at, vector[r : r + 1, :])
    sums.begin(5, 0)

    def finish_chunk(chunk, carry):
        here = pl.ds(pl.multiple_of(chunk * rows, rows), rows)
        across(mid_own, pre_peer, pre_sems, chunk).wait()
        upstream = mid_own[here, :].astype(F32) + pre_peer[here, :].astype(F32)
        normed, scale = normalized(tokens[here, :].astype(F32))
        grad_out[here, :] += norm_back(normed, scale, pre_gain[...], upstream)
        store(0, grad_out, grad_h, chunk).start()
        return carry

    def take_result(d, carry):
        other = lax.rem(me + d, wide)
        result_copy(other, other).wait_recv()
        result_copy(other, me).wait_send()
        return carry

    lax.fori_loop(1, wide, take_result, 0)
    own_rows.wait()

    def blend(chunk, carry):
        here = pl.ds(pl.multiple_of(chunk * rows, rows), rows)
        experts = router.shape[0]
        picks, chances = info[here, experts : experts + 6].astype(jnp.int32), info[here, 0:experts]
        number = lax.broadcasted_iota(jnp.int32, chances.shape, 1)
        gates = [
            jnp.sum(jnp.where(number == picks[:, 2 + j : 3 + j], chances, 0.0), axis=1, keepdims=True)
            for j in range(2)
        ]
        hits = token_hits(picks, result_own.shape[0])
        table = jnp.where(hits[0], gates[0], jnp.where(hits[1], gates[1], 0.0)).astype(BF16)
        blend_own[here, :] = dot(table, result_own[...]).astype(BF16)
        across(blend_own, blend_peer, blend_sems, chunk).start()
        return carry

    def blend_end(chunk, carry):
        here = pl.ds(pl.multiple_of(chunk * rows, rows), rows)
        across(blend_own, blend_peer, blend_sems, chunk).wait()
        mixture = blend_own[here, :].astype(F32) + blend_peer[here, :].astype(F32)
        block_out[here, :] = (second[here, :] + mixture).astype(BF16)
        store(1, block_out, block_h, chunk).start()
        return carry

    def take_pre(d, carry):
        other = lax.rem(me + d, wide)
        pre_copy(other, other).wait_recv()
        pre_copy(other, me).wait_send()
        return carry

    pre_share = pltpu.make_async_remote_copy(
        pre_total, pre_other, result_sems.at[0, 2 * wide], result_sems.at[1, 2 * wide],
        device_id=(me, 1 - plane), device_id_type=MESH,
    )
    ends = (4, 5, 6, 7)
    for k in range(2 * sums.steps):
        for i in (0, 1):
            if len(taken[i]) + k < 2 * sums.steps:
                sums.advance(i, len(taken[i]) + k)
        for i in (5, 4, 2, 3):
            sums.advance(i, k)
        if k < chunks:
            blend(k, 0)
        if k in ends:
            finish_chunk(ends.index(k), 0)
        if k == sums.steps - 1:
            lax.fori_loop(1, wide, take_pre, 0)
            pre_total[...] = sum(pre_tiles[w] for w in range(wide))
            pre_share.start()
    for part in whole_stores:
        part.start()
    lax.fori_loop(0, chunks, blend_end, 0)
    pre_share.wait()
    pre_tile[...] = pre_total[...] + pre_other[...]
    pre_out[0:1, :] = get_row(pre_tile, 0, model)
    pre_out[1:2, :] = get_row(pre_tile, model // 128, model)
    at = 0
    for out, picked in zip(vectors_out, layout):
        for i in range(len(picked)):
            out[i : i + 1, :] = get_row(small_sums, at, out.shape[1]).astype(F32)
            at += out.shape[1] // 128

    def end_stores(c, carry):
        store(0, grad_out, grad_h, c).wait()
        store(1, block_out, block_h, c).wait()
        return carry

    lax.fori_loop(0, chunks, end_stores, 0)
    for part in whole_stores:
        part.wait()


def widen(pairs, layout, *refs):
    ins, outs = refs[: pairs + len(layout)], refs[pairs + len(layout) :]
    for source, out in zip(ins[:pairs], outs[:pairs]):
        out[...] = source[...].astype(out.dtype)
    outs = iter(outs[pairs:])
    for source, picked in zip(ins[pairs:], layout):
        for r in picked:
            out = next(outs)
            if out.shape[0] == 2:
                out[0:1, :] = source[0:1, : out.shape[1]]
                out[1:2, :] = source[0:1, 2 * out.shape[1] :]
            else:
                out[...] = source[r : r + out.shape[0], : out.shape[1]]


def shards(
    wide,
    tokens_in, pre_gain, pre_shift, qkv_weight, qv_bias, proj_weight, proj_bias, mid_gain, mid_shift,
    hidden_weight, hidden_bias, output_weight, output_bias, moe_gain, moe_shift, router_weight,
    expert_in, expert_in_bias, expert_out, expert_out_bias, expert_ids, priority, cotangent,
):
    tokens, model = tokens_in.shape
    width = qkv_weight.shape[2]
    heads = width // HEAD_DIM
    hidden = hidden_weight.shape[1]
    count = router_weight.shape[1]
    capacity = tokens // count
    room = -(-capacity // 16) * 16
    slots = count * room
    half = model // 2
    lanes = 3 * width
    rows = 2 * PATCHES
    chunks = tokens // rows
    group = 2
    steps = wide.bit_length() - 1

    def row(vector):
        return vector.reshape(1, -1)

    def remote(kernel, name, identity, far_ins, ins, far_outs, outs, scratch):
        far, near = pl.BlockSpec(memory_space=pl.ANY), pl.BlockSpec(memory_space=pltpu.VMEM)
        return pl.pallas_call(
            kernel,
            out_shape=[jax.ShapeDtypeStruct(shape, dtype) for shape, dtype in far_outs + outs],
            in_specs=[far] * len(far_ins) + [near] * len(ins),
            out_specs=[far] * len(far_outs) + [near] * len(outs),
            scratch_shapes=scratch,
            compiler_params=pltpu.CompilerParams(
                vmem_limit_bytes=VMEM_BYTES, collective_id=identity, has_side_effects=True
            ),
            name=name,
        )(*far_ins, *ins)

    def room_for(local):
        return [pltpu.VMEM(shape, dtype) for shape, dtype in local]

    pre_gain, pre_shift, proj_bias = row(pre_gain), row(pre_shift), row(proj_bias)
    mid_gain, mid_shift, hidden_bias = row(mid_gain), row(mid_shift), row(hidden_bias)
    output_bias, moe_gain, moe_shift = row(output_bias), row(moe_gain), row(moe_shift)
    weight_qkv = qkv_weight.transpose(1, 0, 2)
    router = router_weight.T
    groups = wide // group
    kept = [
        ((tokens, lanes), BF16), ((tokens, width), BF16), ((tokens, model), F32), ((tokens, model), F32),
        ((tokens, 128), F32), ((slots, model), BF16), ((model, hidden), BF16), ((hidden, model), BF16),
        ((tokens, hidden), BF16), ((tokens, hidden), BF16), ((tokens, model), BF16),
    ]
    homes = [((slots, half), BF16), ((slots, half), BF16)]
    images = tokens // PATCHES
    fetched = [tokens_in, cotangent, weight_qkv, proj_weight, hidden_weight, output_weight, expert_in[0], expert_out[0]]
    tables = [((count, 8, 128), F32)] * 5
    (qkv, context, first, second, info, result, in_grad, out_grad, fed, slopes, lowered, row_own, row_peer, gate_grads,
     in_bias, out_bias) = remote(
        functools.partial(front, wide, room, group, heads, PATCHES, count), "front", 1,
        fetched,
        [expert_ids.T, priority, pre_gain, pre_shift, qv_bias, proj_bias, mid_gain, mid_shift, hidden_bias, output_bias,
         moe_gain, moe_shift, router, expert_in_bias, expert_out_bias],
        kept + homes,
        [((count, 128), F32), ((8, hidden), F32), ((8, model), F32)],
        room_for([(array.shape, array.dtype) for array in fetched] + kept
                 + [((8, tokens), jnp.int32), ((count, 128), F32), ((slots, model), BF16), ((slots, model), BF16),
                    ((width, model), BF16), ((tokens, width), BF16), ((tokens, model), BF16), ((tokens, model), BF16),
                    ((tokens, half), BF16), ((tokens, half), BF16), ((slots, half), BF16), ((slots, half), BF16),
                    ((slots, half), BF16), ((slots, half), BF16),
                    ((slots, hidden), BF16), ((slots, hidden), BF16), ((slots, model), BF16), ((slots, half), F32),
                    ((slots, half), BF16), ((slots, half), BF16), ((slots, half), BF16)] + tables)
        + [pltpu.SemaphoreType.DMA((2, 6 * wide + 3 * groups + 2 * images + 2)), pltpu.SemaphoreType.DMA((9,)),
           pltpu.SemaphoreType.DMA((images,)), pltpu.SemaphoreType.DMA((8, images)), pltpu.SemaphoreType.DMA((groups + 1,))],
    )

    layout = [(0, 1, 2), (0, 1, 2), (0,), (0,), tuple(range(count))]
    vectors = [((8, model), F32), ((8, model), F32), ((8, hidden), F32), ((8, lanes), F32), ((count, model), F32)]
    near, far = tuple(range(steps)), (0,) + tuple(range(2, steps)) + (1,)
    summed = [(model, hidden), (hidden, model), (3 * model // 2, width), (3 * model // 2, width), (width, model), (16 * wide, 128)]
    fetched = [second, cotangent, info, first, tokens_in, qkv, context, hidden_weight, output_weight, proj_weight, weight_qkv, row_own, row_peer,
               fed, slopes, lowered]
    given = [
        ((tokens, model), BF16), ((tokens, model), F32), ((model, hidden), BF16), ((hidden, model), BF16),
        ((3 * model, width), BF16), ((width, model), BF16),
    ]
    tile = (2 * model // 128, 128)
    block_out, grad, hidden_g, output_g, qkv_g, proj_g, *sums = remote(
        functools.partial(backward, wide, room, heads, layout, (near, far, near, far, near, far), rows), "backward", 2,
        fetched + [result],
        [moe_gain, moe_shift, router, gate_grads, mid_gain, pre_gain, pre_shift],
        given, vectors + [((8, model), F32)],
        room_for([(array.shape, array.dtype) for array in fetched] + given
                 + [((tokens, hidden), BF16), ((tokens, model), BF16),
                    ((tokens, model), BF16), ((tokens, model), BF16), ((tokens, lanes), BF16), ((tokens, model), BF16),
                    ((tokens, model), BF16), ((slots, model), BF16), ((tokens, model), BF16),
                    (tile, F32), ((wide,) + tile, F32), (tile, F32), (tile, F32), ((8, model), F32), ((count, model), F32),
                    ((8, model), F32), ((8, hidden), F32), ((8, lanes), F32), ((8, model), F32), (summed[-1], BF16),
                    (summed[0], F32), (summed[1], F32), ((3 * model, width), F32), (summed[4], F32), (summed[5], F32)]
                 + [(shape, BF16) for shape in summed] * 2)
        + [pltpu.SemaphoreType.DMA((2, chunks))] * 3 + [pltpu.SemaphoreType.DMA((2, 2 * wide + 1))]
        + [pltpu.SemaphoreType.DMA((len(summed), 2 * steps))] * 2
        + [pltpu.SemaphoreType.DMA((14,)), pltpu.SemaphoreType.DMA((7, chunks)), pltpu.SemaphoreType.DMA((2, chunks))],
    )

    pairs = [
        (block_out, BF16), (grad, F32), (hidden_g, F32), (output_g, F32), (qkv_g.reshape(3, model, width), F32),
        (proj_g, F32), (in_grad, F32), (out_grad, F32),
    ]
    singles = [(0, 1), (0, 1, 2), (0, 1, 2), (0,), (0,), (0,), (0,), (0,)]
    sources = [sums[-1]] + list(sums[:-1]) + [in_bias, out_bias]
    sizes = [(1, model)] * 8 + [(1, hidden), (2, width), (count, model), (1, hidden), (1, model)]
    parts = 2

    def spec(shape):
        if len(shape) == 3:
            return pl.BlockSpec((shape[0], shape[1] // parts, shape[2]), lambda i: (0, i, 0))
        return pl.BlockSpec((shape[0] // parts, shape[1]), lambda i: (i, 0))

    def whole(shape):
        return pl.BlockSpec(shape, lambda i: (0, 0))

    outs = pl.pallas_call(
        functools.partial(widen, len(pairs), singles),
        grid=(parts,),
        in_specs=[spec(source.shape) for source, _ in pairs] + [whole(source.shape) for source in sources],
        out_specs=[spec(source.shape) for source, _ in pairs] + [whole(size) for size in sizes],
        out_shape=[jax.ShapeDtypeStruct(source.shape, dtype) for source, dtype in pairs]
        + [jax.ShapeDtypeStruct(size, F32) for size in sizes],
        compiler_params=pltpu.CompilerParams(vmem_limit_bytes=VMEM_BYTES),
        name="widen",
    )(*[source for source, _ in pairs], *sources)
    block_out, grad, hidden_g, output_g, qkv_g, proj_g, in_grad, out_grad = outs[:8]
    pre_gain_g, pre_shift_g, mid_gain_g, mid_shift_g, proj_bias_g, moe_gain_g, moe_shift_g, output_bias_g = (
        vector.reshape(model) for vector in outs[8:16]
    )
    hidden_bias_g, qkv_bias_g, router_g, in_bias_g, out_bias_g = outs[16:]
    return (
        block_out, grad, pre_gain_g, pre_shift_g, qkv_g.transpose(1, 0, 2),
        qkv_bias_g, proj_g, proj_bias_g, mid_gain_g,
        mid_shift_g, hidden_g, hidden_bias_g.reshape(hidden), output_g, output_bias_g, moe_gain_g, moe_shift_g,
        router_g.T, in_grad[None], in_bias_g, out_grad[None], out_bias_g,
    )


def layer_norm(values, gain, shift):
    centered = values - jnp.mean(values, axis=-1, keepdims=True)
    variance = jnp.mean(centered * centered, axis=-1, keepdims=True)
    return centered * lax.rsqrt(variance + 1e-06) * gain + shift


def norm_grad(values, gain, shift, upstream):
    _, pullback = jax.vjp(layer_norm, values, gain, shift)
    return pullback(upstream)


def gelu_grad(inner, upstream):
    _, pullback = jax.vjp(jax.nn.gelu, inner)
    return pullback(upstream)[0]


def slot_tables(choice_ids, ranks, capacity, experts):
    count = choice_ids.shape[0]
    order_keys = jnp.concatenate([ranks, ranks + count])
    flat_ids = jnp.concatenate([choice_ids[:, 0], choice_ids[:, 1]])
    earlier = (order_keys[None, :] < order_keys[:, None]) & (flat_ids[None, :] == flat_ids[:, None])
    position = jnp.sum(earlier.astype(jnp.int32), axis=1)
    kept = position < capacity
    position = position.reshape(2, count)
    kept = kept.reshape(2, count)
    columns = jnp.arange(experts * capacity, dtype=jnp.int32)
    target = choice_ids.T * capacity + position
    tables = (target[:, :, None] == columns[None, None, :]) & kept[:, :, None]
    return (tables, kept)


def plain(
    tokens_in,
    pre_gain,
    pre_shift,
    qkv_weight,
    qv_bias,
    proj_weight,
    proj_bias,
    mid_gain,
    mid_shift,
    hidden_weight,
    hidden_bias,
    output_weight,
    output_bias,
    moe_gain,
    moe_shift,
    router_weight,
    expert_in,
    expert_in_bias,
    expert_out,
    expert_out_bias,
    expert_ids,
    priority,
    cotangent,
):
    tokens = tokens_in.shape[0]
    model_width = tokens_in.shape[1]
    local_heads = qkv_weight.shape[2] // HEAD_DIM
    images = tokens // PATCHES
    experts = router_weight.shape[1]
    capacity = tokens // experts
    score_scale = float(HEAD_DIM) ** (-0.5)
    highest = lax.Precision.HIGHEST
    residual = tokens_in.astype(jnp.float32)
    normed_pre = layer_norm(residual, pre_gain, pre_shift)
    lowered_pre = normed_pre.astype(jnp.bfloat16)
    blank = jnp.zeros_like(qv_bias[0])
    qkv_shift = jnp.stack([qv_bias[0], blank, qv_bias[1]])
    qkv = (
        jnp.einsum("td,dsk->tsk", lowered_pre, qkv_weight, preferred_element_type=jnp.float32)
        + qkv_shift
    ).astype(jnp.bfloat16)
    grid = qkv.reshape(images, PATCHES, 3, local_heads, HEAD_DIM)
    query, keys, values = (grid[:, :, 0], grid[:, :, 1], grid[:, :, 2])
    scores = (
        jnp.einsum("bqhd,bkhd->bhqk", query, keys, preferred_element_type=jnp.float32) * score_scale
    )
    log_total = jax.nn.logsumexp(scores, axis=-1, keepdims=True)
    weights = jnp.exp(scores - log_total).astype(jnp.bfloat16)
    context = jnp.einsum("bhqk,bkhd->bqhd", weights, values, preferred_element_type=jnp.float32)
    context = context.astype(jnp.bfloat16).reshape(tokens, local_heads * HEAD_DIM)
    branch = lax.psum(jnp.dot(context, proj_weight, preferred_element_type=jnp.float32), "tensor")
    first = residual + branch + proj_bias
    normed_mid = layer_norm(first, mid_gain, mid_shift)
    lowered_mid = normed_mid.astype(jnp.bfloat16)
    inner = jnp.dot(lowered_mid, hidden_weight, preferred_element_type=jnp.float32) + hidden_bias
    activated = jax.nn.gelu(inner).astype(jnp.bfloat16)
    partial_out = jnp.dot(activated, output_weight, preferred_element_type=jnp.float32)
    second = first + lax.psum(partial_out, "tensor") + output_bias
    normed_moe = layer_norm(second, moe_gain, moe_shift)
    lowered_moe = normed_moe.astype(jnp.bfloat16)
    route = jax.nn.softmax(jnp.dot(normed_moe, router_weight, precision=highest), axis=-1)
    tables, kept = slot_tables(expert_ids, priority[0], capacity, experts)
    tables = tables.astype(jnp.bfloat16)
    dispatch = tables[0] + tables[1]
    buffers = jnp.einsum("tk,td->kd", dispatch, lowered_moe, preferred_element_type=jnp.float32)
    buffers = buffers.astype(jnp.bfloat16).reshape(experts, capacity, model_width)
    arrived = lax.all_to_all(buffers, "wide", split_axis=0, concat_axis=1, tiled=True)
    expert_inner = (
        jnp.einsum("erd,edf->erf", arrived, expert_in, preferred_element_type=jnp.float32)
        + expert_in_bias[:, None, :]
    )
    expert_act = jax.nn.gelu(expert_inner).astype(jnp.bfloat16)
    expert_partial = jnp.einsum(
        "erf,efd->erd", expert_act, expert_out, preferred_element_type=jnp.float32
    )
    expert_result = (
        lax.psum(expert_partial.astype(jnp.bfloat16), "tensor").astype(jnp.float32)
        + expert_out_bias[:, None, :]
    ).astype(jnp.bfloat16)
    returned = lax.all_to_all(
        expert_result, "wide", split_axis=1, concat_axis=0, tiled=True
    ).reshape(experts * capacity, model_width)
    picked = jnp.einsum("jtk,kd->jtd", tables, returned, preferred_element_type=jnp.float32)
    expert_range = jnp.arange(experts, dtype=jnp.int32)
    chosen = (expert_ids.T[:, :, None] == expert_range[None, None, :]).astype(jnp.float32) * kept[
        :, :, None
    ].astype(jnp.float32)
    gates = jnp.sum(chosen * route[None], axis=-1)
    mixture = jnp.sum(gates[:, :, None] * picked, axis=0)
    block_out = (second + mixture).astype(jnp.bfloat16)
    gate_grad = jnp.sum(picked * cotangent[None], axis=-1)
    weighted = (gates[:, :, None] * cotangent[None]).astype(jnp.bfloat16)
    slot_grad = jnp.einsum("jtk,jtd->kd", tables, weighted, preferred_element_type=jnp.float32)
    slot_grad = slot_grad.astype(jnp.bfloat16).reshape(experts, capacity, model_width)
    result_grad = lax.all_to_all(slot_grad, "wide", split_axis=0, concat_axis=1, tiled=True)
    expert_out_bias_grad = jnp.sum(result_grad.astype(jnp.float32), axis=1)
    expert_out_grad = jnp.einsum(
        "erf,erd->efd", expert_act, result_grad, preferred_element_type=jnp.float32
    )
    act_grad = jnp.einsum(
        "erd,efd->erf", result_grad, expert_out, preferred_element_type=jnp.float32
    )
    expert_inner_grad = gelu_grad(expert_inner, act_grad).astype(jnp.bfloat16)
    expert_in_bias_grad = jnp.sum(expert_inner_grad.astype(jnp.float32), axis=1)
    expert_in_grad = jnp.einsum(
        "erd,erf->edf", arrived, expert_inner_grad, preferred_element_type=jnp.float32
    )
    arrived_partial = jnp.einsum(
        "erf,edf->erd", expert_inner_grad, expert_in, preferred_element_type=jnp.float32
    )
    arrived_grad = lax.psum(arrived_partial.astype(jnp.bfloat16), "tensor")
    buffer_grad = lax.all_to_all(
        arrived_grad, "wide", split_axis=1, concat_axis=0, tiled=True
    ).reshape(experts * capacity, model_width)
    moe_input_grad = jnp.dot(dispatch, buffer_grad, preferred_element_type=jnp.float32)
    route_grad = jnp.sum(gate_grad[:, :, None] * chosen, axis=0)
    logit_grad = route * (route_grad - jnp.sum(route * route_grad, axis=-1, keepdims=True))
    router_grad = jnp.einsum("td,te->de", normed_moe, logit_grad, precision=highest)
    moe_input_grad = moe_input_grad + jnp.einsum(
        "te,de->td", logit_grad, router_weight, precision=highest
    )
    second_part, moe_gain_grad, moe_shift_grad = norm_grad(
        second, moe_gain, moe_shift, moe_input_grad
    )
    second_grad = cotangent + second_part
    lowered_second = second_grad.astype(jnp.bfloat16)
    output_bias_grad = jnp.sum(second_grad, axis=0)
    output_weight_grad = jnp.einsum(
        "tf,td->fd", activated, lowered_second, preferred_element_type=jnp.float32
    )
    activated_grad = jnp.einsum(
        "td,fd->tf", lowered_second, output_weight, preferred_element_type=jnp.float32
    )
    inner_grad = gelu_grad(inner, activated_grad).astype(jnp.bfloat16)
    hidden_bias_grad = jnp.sum(inner_grad.astype(jnp.float32), axis=0)
    hidden_weight_grad = jnp.einsum(
        "td,tf->df", lowered_mid, inner_grad, preferred_element_type=jnp.float32
    )
    mid_partial = jnp.einsum(
        "tf,df->td", inner_grad, hidden_weight, preferred_element_type=jnp.float32
    )
    mid_grad = lax.psum(mid_partial, "tensor")
    first_part, mid_gain_grad, mid_shift_grad = norm_grad(first, mid_gain, mid_shift, mid_grad)
    first_grad = second_grad + first_part
    proj_bias_grad = jnp.sum(first_grad, axis=0)
    branch_grad = first_grad.astype(jnp.bfloat16)
    proj_weight_grad = jnp.einsum(
        "tk,td->kd", context, branch_grad, preferred_element_type=jnp.float32
    )
    context_grad = jnp.einsum(
        "td,kd->tk", branch_grad, proj_weight, preferred_element_type=jnp.float32
    )
    context_grad = context_grad.astype(jnp.bfloat16).reshape(images, PATCHES, local_heads, HEAD_DIM)
    scores = (
        jnp.einsum("bqhd,bkhd->bhqk", query, keys, preferred_element_type=jnp.float32) * score_scale
    )
    probs = jnp.exp(scores - log_total)
    weights = probs.astype(jnp.bfloat16)
    value_grad = jnp.einsum(
        "bhqk,bqhd->bkhd", weights, context_grad, preferred_element_type=jnp.float32
    )
    prob_grad = jnp.einsum(
        "bqhd,bkhd->bhqk", context_grad, values, preferred_element_type=jnp.float32
    )
    score_grad = (probs * (prob_grad - jnp.sum(probs * prob_grad, axis=-1, keepdims=True))).astype(
        jnp.bfloat16
    )
    query_grad = (
        jnp.einsum("bhqk,bkhd->bqhd", score_grad, keys, preferred_element_type=jnp.float32)
        * score_scale
    )
    key_grad = (
        jnp.einsum("bhqk,bqhd->bkhd", score_grad, query, preferred_element_type=jnp.float32)
        * score_scale
    )
    qkv_grad = jnp.stack([query_grad, key_grad, value_grad], axis=2).astype(jnp.bfloat16)
    qkv_grad = qkv_grad.reshape(tokens, 3, local_heads * HEAD_DIM)
    qkv_sums = jnp.sum(qkv_grad.astype(jnp.float32), axis=0)
    qv_bias_grad = jnp.stack([qkv_sums[0], qkv_sums[2]])
    qkv_weight_grad = jnp.einsum(
        "td,tsk->dsk", lowered_pre, qkv_grad, preferred_element_type=jnp.float32
    )
    pre_partial = jnp.einsum(
        "tsk,dsk->td", qkv_grad, qkv_weight, preferred_element_type=jnp.float32
    )
    pre_grad = lax.psum(pre_partial.astype(jnp.bfloat16), "tensor").astype(jnp.float32)
    input_part, pre_gain_grad, pre_shift_grad = norm_grad(residual, pre_gain, pre_shift, pre_grad)
    tokens_grad = first_grad + input_part
    shared = (
        lax.psum(pre_gain_grad.astype(jnp.bfloat16), "wide").astype(jnp.float32),
        lax.psum(pre_shift_grad.astype(jnp.bfloat16), "wide").astype(jnp.float32),
        lax.psum(qkv_weight_grad.astype(jnp.bfloat16), "wide").astype(jnp.float32),
        lax.psum(qv_bias_grad.astype(jnp.bfloat16), "wide").astype(jnp.float32),
        lax.psum(proj_weight_grad.astype(jnp.bfloat16), "wide").astype(jnp.float32),
        lax.psum(proj_bias_grad.astype(jnp.bfloat16), "wide").astype(jnp.float32),
        lax.psum(mid_gain_grad.astype(jnp.bfloat16), "wide").astype(jnp.float32),
        lax.psum(mid_shift_grad.astype(jnp.bfloat16), "wide").astype(jnp.float32),
        lax.psum(hidden_weight_grad.astype(jnp.bfloat16), "wide").astype(jnp.float32),
        lax.psum(hidden_bias_grad.astype(jnp.bfloat16), "wide").astype(jnp.float32),
        lax.psum(output_weight_grad.astype(jnp.bfloat16), "wide").astype(jnp.float32),
        lax.psum(output_bias_grad.astype(jnp.bfloat16), "wide").astype(jnp.float32),
        lax.psum(moe_gain_grad.astype(jnp.bfloat16), "wide").astype(jnp.float32),
        lax.psum(moe_shift_grad.astype(jnp.bfloat16), "wide").astype(jnp.float32),
        lax.psum(router_grad.astype(jnp.bfloat16), "wide").astype(jnp.float32),
    )
    return (
        (block_out, tokens_grad)
        + tuple(shared)
        + (expert_in_grad, expert_in_bias_grad, expert_out_grad, expert_out_bias_grad)
    )


def solution(mesh):
    body = functools.partial(shards, mesh.shape["wide"]) if mesh.shape["tensor"] == 2 else plain
    return jax.shard_map(
        body,
        mesh=mesh,
        in_specs=(
            P("wide", None), P(), P(), P(None, None, "tensor"), P(None, "tensor"), P("tensor", None), P(), P(), P(),
            P(None, "tensor"), P("tensor"), P("tensor", None), P(), P(), P(), P(),
            P("wide", None, "tensor"), P("wide", "tensor"), P("wide", "tensor", None), P("wide", None),
            P("wide", None), P("wide", None), P("wide", None),
        ),
        out_specs=(
            P("wide", None), P("wide", None), P(), P(), P(None, None, "tensor"), P(None, "tensor"), P("tensor", None),
            P(), P(), P(), P(None, "tensor"), P("tensor"), P("tensor", None), P(), P(), P(), P(),
            P("wide", None, "tensor"), P("wide", "tensor"), P("wide", "tensor", None), P("wide", None),
        ),
        check_vma=False,
    )
```
